32 devices in a mesh: seq: 8 (over y, x, core), tp: 4 (over z).
Axes of the slice: x: 2, y: 2, z: 4, core: 2. Of those that a mesh axis runs over, the one named last changes fastest.
Arguments:
- tokens: bfloat16 [8192, 2048], P(('seq', 'tp')), may hold values from -6 to 6
- lengths: int32 [7], replicated, may hold values from 1 to 7296, as said below
- cotangent: bfloat16 [8192, 2048], P(('seq', 'tp')), may hold values from -6 to 6
- first_gain: float32 [2048], replicated, may hold values from 0.5 to 1.5
- query_weight: bfloat16 [2048, 2048], P(None, 'tp'), may hold values from -0.125 to 0.125
- forget_weight: bfloat16 [2048, 2048], P(None, 'tp'), may hold values from -0.125 to 0.125
- input_weight: bfloat16 [2048, 2048], P(None, 'tp'), may hold values from -0.125 to 0.125
- swish_weight: bfloat16 [2048, 2048], P(None, 'tp'), may hold values from -0.125 to 0.125
- bound_logit: float32 [16, 128], P('tp'), as said below
- group_gain: float32 [16, 128], P('tp'), may hold values from 0.5 to 1.5
- out_weight: bfloat16 [2048, 2048], P('tp'), may hold values from -0.125 to 0.125
- second_gain: float32 [2048], replicated, may hold values from 0.5 to 1.5
- gate_weight: bfloat16 [2048, 5632], P(None, 'tp'), may hold values from -0.125 to 0.125
- up_weight: bfloat16 [2048, 5632], P(None, 'tp'), may hold values from -0.125 to 0.125
- down_weight: bfloat16 [5632, 2048], P('tp'), may hold values from -0.078125 to 0.078125
Outputs:
- output: bfloat16 [8192, 2048], P(('seq', 'tp'))
- tokens_grad: float32 [8192, 2048], P(('seq', 'tp'))
- first_gain_grad: float32 [2048], P(('seq', 'tp'))
- query_grad: float32 [2048, 2048], P('seq', 'tp')
- forget_grad: float32 [2048, 2048], P('seq', 'tp')
- input_grad: float32 [2048, 2048], P('seq', 'tp')
- swish_grad: float32 [2048, 2048], P('seq', 'tp')
- bound_grad: float32 [16, 128], P('tp', 'seq')
- group_gain_grad: float32 [16, 128], P('tp', 'seq')
- out_grad: float32 [2048, 2048], P('tp', 'seq')
- second_gain_grad: float32 [2048], P(('seq', 'tp'))
- gate_grad: float32 [2048, 5632], P('seq', 'tp')
- up_grad: float32 [2048, 5632], P('seq', 'tp')
- down_grad: float32 [5632, 2048], P('tp', 'seq')
The draws below stay inside these ranges and needn't reach their ends.
Inputs may be any that keep to these rules, and one draw needn't show every extreme that they name: lengths of the packed sequences in order; the fourth is the longest, their sum is under 8192, and rows from the sum on are padding. `bound_logit`: logits of the lower bounds, each at least 0 and under ln(16384).
All inputs are finite; a program needn't handle non-finite values.
Results may differ from the reference program's by a relative error of at most 0.014.
Values may be sent and summed in bfloat16 or wider, within the bound.
A program may use at most 256 MiB of HBM per device.

```python
import jax
import jax.numpy as jnp
from jax import lax

D = 2048
HEADS = 16
HEAD = 128
FF = 5632
BLOCK = 64
TOKENS = 8192
SHORT = 128


def draw_lengths(key, part):
    key = jax.random.fold_in(key, 11)
    first_key, second_key = jax.random.split(key, 2)
    leading = jax.random.randint(first_key, (3,), 1, SHORT + 1)
    trailing = jax.random.randint(second_key, (3,), 1, SHORT + 1)
    longest = jnp.full((1,), TOKENS - 7 * SHORT, jnp.int32)
    return jnp.concatenate([leading.astype(jnp.int32), longest, trailing.astype(jnp.int32)]).astype(jnp.int32)


def draw_bound_logit(key, part):
    key = jax.random.fold_in(key, 23)
    order_key, quick_key, rate_key = jax.random.split(key, 3)
    ranks = jax.random.permutation(order_key, HEADS)
    slow_count = HEADS // 2
    slow_head = (ranks < slow_count).astype(jnp.float32)[:, None]
    quick_logit = jax.random.uniform(quick_key, (HEADS, HEAD), jnp.float32, 0.0, 3.0)
    rate = jnp.exp(jax.random.uniform(rate_key, (HEADS, HEAD), jnp.float32, jnp.log(0.4), jnp.log(2.0)))
    slow_logit = jnp.log(TOKENS / (2.0 * rate) - 1.0)
    return (slow_head * slow_logit + (1.0 - slow_head) * quick_logit).astype(jnp.float32)


def block_levels(key, shape, cuts, least, high):
    def one(position, shards_of):
        draws = jax.random.uniform(jax.random.fold_in(jax.random.fold_in(key, 6), position), (shards_of,), jnp.float32, least / len(cuts), high / len(cuts))
        return jnp.repeat(jnp.exp(draws), shape[position] // shards_of).reshape((-1,) + (1,) * (len(shape) - position - 1))

    level = one(*cuts[0])
    for cut in cuts[1:]:
        level = level * one(*cut)
    return level


def centred(stream_key, dims, deviation, limit, shards=(), kind=jnp.bfloat16):
    values = jax.random.normal(stream_key, dims, jnp.float32) * deviation
    if len(shards) > 0:
        values = block_levels(stream_key, dims, shards, -0.22, 0.18) * values
    return jnp.clip(values, min=-limit, max=limit).astype(kind)


def setup_inputs(seed: int = 0) -> dict:
    keys = jax.random.split(jax.random.key(seed), 16)
    return {
        "tokens": centred(keys[0], (TOKENS, D), 1.0, 6.0, ((0, 32),)),
        "lengths": draw_lengths(jax.random.fold_in(keys[15], 71), 0),
        "cotangent": centred(keys[2], (TOKENS, D), 1.0, 6.0, ((0, 32),)),
        "first_gain": jnp.clip(1.0 + 0.1 * jax.random.normal(keys[3], (D,), jnp.float32), 0.5, 1.5),
        "query_weight": centred(keys[4], (D, D), D ** -0.5, 0.125, ((1, 4),)),
        "forget_weight": centred(keys[5], (D, D), D ** -0.5, 0.125, ((1, 4),)),
        "input_weight": centred(keys[6], (D, D), D ** -0.5, 0.125, ((1, 4),)),
        "swish_weight": centred(keys[7], (D, D), D ** -0.5, 0.125, ((1, 4),)),
        "bound_logit": draw_bound_logit(jax.random.fold_in(keys[15], 71), 0),
        "group_gain": jnp.clip(1.0 + 0.1 * jax.random.normal(keys[9], (HEADS, HEAD), jnp.float32), 0.5, 1.5),
        "out_weight": centred(keys[10], (D, D), D ** -0.5, 0.125, ((0, 4),)),
        "second_gain": jnp.clip(1.0 + 0.1 * jax.random.normal(keys[11], (D,), jnp.float32), 0.5, 1.5),
        "gate_weight": centred(keys[12], (D, FF), D ** -0.5, 0.125, ((1, 4),)),
        "up_weight": centred(keys[13], (D, FF), D ** -0.5, 0.125, ((1, 4),)),
        "down_weight": centred(keys[14], (FF, D), FF ** -0.5, 0.078125, ((0, 4),)),
    }


epsilon = 1e-05
highest = lax.Precision.HIGHEST

@jax.custom_vjp
def low(v):
    return lax.optimization_barrier(v.astype(jnp.bfloat16)).astype(jnp.float32)

@jax.custom_vjp
def low_back(v):
    return v

def low_keep(v):
    return (low(v), None)

def low_pass(kept, grad):
    return (grad,)

def back_keep(v):
    return (v, None)

def back_low(kept, grad):
    return (low(grad),)
low.defvjp(low_keep, low_pass)
low_back.defvjp(back_keep, back_low)

def product(left, right):
    return jnp.dot(left, right, precision=highest, preferred_element_type=jnp.float32)

def doc_layout(positions, lengths):
    seq_ends = jnp.cumsum(lengths).astype(jnp.int32)
    doc_ids = lax.optimization_barrier(jnp.sum((positions[:, None] >= seq_ends[None, :]).astype(jnp.int32), axis=1)).astype(jnp.int32)
    shifted = positions - 1
    earlier_ids = lax.optimization_barrier(jnp.sum((shifted[:, None] >= seq_ends[None, :]).astype(jnp.int32), axis=1)).astype(jnp.int32)
    prev_ids = jnp.where(shifted >= 0, earlier_ids, -1).astype(jnp.int32)
    valid_rows = (positions < seq_ends[-1]).astype(jnp.float32)
    return (doc_ids, prev_ids, valid_rows)

def rms_norm(rows_in, gain_vector):
    inv_scale = lax.rsqrt(lax.optimization_barrier(jnp.mean(rows_in * rows_in, axis=-1, keepdims=True)) + epsilon)
    return rows_in * inv_scale * gain_vector

def gate_values(query_pre, forget_pre, input_pre, bound_logit):
    lower_bound = jax.nn.sigmoid(bound_logit).reshape(-1)
    forget = lower_bound + (1.0 - lower_bound) * jax.nn.sigmoid(forget_pre)
    return (jax.nn.silu(query_pre), jnp.log(forget), 1.0 - forget, input_pre)

def group_out(valid_rows, recurrent_out, swish_pre, group_gain):
    head_count, head_width = group_gain.shape
    split_heads = recurrent_out.reshape(recurrent_out.shape[0], head_count, head_width)
    inv_scale = lax.rsqrt(lax.optimization_barrier(jnp.mean(split_heads * split_heads, axis=-1, keepdims=True)) + epsilon)
    normed = (split_heads * inv_scale * group_gain).reshape(recurrent_out.shape)
    return normed * jax.nn.silu(swish_pre) * valid_rows[:, None]

def block_run(queries, log_forget, key_rows, values, doc_ids, prev_ids, carried):
    head_count, head_width = (carried.shape[0], carried.shape[1])
    blocks = queries.shape[0] // BLOCK
    layout = (blocks, BLOCK, head_count, head_width)
    query_blocks = queries.reshape(layout)
    key_blocks = key_rows.reshape(layout)
    value_blocks = values.reshape(layout)
    cum_log = jnp.cumsum(log_forget.reshape(layout), axis=1)
    last_log = cum_log[:, -1]
    block_ids = doc_ids.reshape(blocks, BLOCK)
    before = prev_ids.reshape(blocks, BLOCK)[:, 0]
    query_decay = query_blocks * jnp.exp(cum_log)
    key_decay = key_blocks * jnp.exp(-cum_log)
    lower_mask = jnp.tril(jnp.ones((BLOCK, BLOCK), jnp.float32))
    same_doc = (block_ids[:, :, None] == block_ids[:, None, :]).astype(jnp.float32) * lower_mask
    scores = jnp.einsum('nthd,nshd->nhts', query_decay, key_decay, precision=highest) * same_doc[:, None]
    within = jnp.einsum('nhts,nshe->nthe', scores, value_blocks, precision=highest)
    carry_in = (block_ids == before[:, None]).astype(jnp.float32)
    tail_keep = (block_ids == block_ids[:, -1:]).astype(jnp.float32)
    key_tail = key_blocks * jnp.exp(last_log[:, None] - cum_log) * tail_keep[:, :, None, None]
    state_adds = jnp.einsum('nshd,nshe->nhde', key_tail, value_blocks, precision=highest)
    decays = jnp.exp(last_log) * carry_in[:, -1][:, None, None]

    def advance(state_now, pieces):
        return (pieces[0][:, :, None] * state_now + pieces[1], state_now)
    closing, starts = lax.scan(advance, carried, (decays, state_adds))
    across = jnp.einsum('nthd,nhde->nthe', query_decay * carry_in[:, :, None, None], starts, precision=highest)
    return ((within + across).reshape(queries.shape), closing)

def reference(tokens, lengths, cotangent, first_gain, query_weight, forget_weight, input_weight, swish_weight, bound_logit, group_gain, out_weight, second_gain, gate_weight, up_weight, down_weight):
    positions = jnp.arange(TOKENS, dtype=jnp.int32)
    doc_ids, prev_ids, valid_rows = doc_layout(positions, lengths)

    def forward(input_rows, first_gain, query_weight, forget_weight, input_weight, swish_weight, bound_logit, group_gain, out_weight, second_gain, gate_weight, up_weight, down_weight):
        normed_a = low(rms_norm(input_rows, first_gain))
        query_pre = low_back(product(normed_a, query_weight))
        forget_pre = low_back(product(normed_a, forget_weight))
        input_pre = low_back(product(normed_a, input_weight))
        swish_pre = low_back(product(normed_a, swish_weight))
        queries, log_forget, key_rows, values = gate_values(query_pre, forget_pre, input_pre, bound_logit)
        empty_state = jnp.zeros((HEADS, HEAD, HEAD), jnp.float32)
        recurrent_out, closing = block_run(queries, log_forget, key_rows, values, doc_ids, prev_ids, empty_state)
        gated = low(group_out(valid_rows, recurrent_out, swish_pre, group_gain))
        residual = input_rows + low_back(product(gated, out_weight))
        normed_b = low(rms_norm(residual, second_gain))
        gate_rows = low_back(product(normed_b, gate_weight))
        up_rows = low_back(product(normed_b, up_weight))
        hidden = low(jax.nn.silu(gate_rows) * up_rows)
        return residual + product(hidden, down_weight)
    result, pullback = jax.vjp(forward, tokens.astype(jnp.float32), first_gain, query_weight.astype(jnp.float32), forget_weight.astype(jnp.float32), input_weight.astype(jnp.float32), swish_weight.astype(jnp.float32), bound_logit, group_gain, out_weight.astype(jnp.float32), second_gain, gate_weight.astype(jnp.float32), up_weight.astype(jnp.float32), down_weight.astype(jnp.float32))
    gradients = pullback(cotangent.astype(jnp.float32))
    return (result.astype(jnp.bfloat16), gradients[0], gradients[1], gradients[2], gradients[3], gradients[4], gradients[5], gradients[6], gradients[7], gradients[8], gradients[9], gradients[10], gradients[11], gradients[12])
```

```python
from functools import partial

import jax
import jax.numpy as jnp
from jax import lax
from jax.sharding import PartitionSpec as P

BLOCK = 64


epsilon = 1e-05
highest = lax.Precision.HIGHEST


def entering(value, axis, combine, identity):
    size, here = (lax.axis_size(axis), lax.axis_index(axis))
    everything = jax.tree.map(lambda part: lax.all_gather(part, axis), value)
    start = jax.tree.map(
        lambda part, zero: jnp.broadcast_to(jnp.asarray(zero, part.dtype), part.shape),
        value,
        identity,
    )

    def lap(k, before):
        reached = k < here
        new = combine(before, jax.tree.map(lambda part: part[k], everything))
        return jax.tree.map(lambda a, b: jnp.where(reached, a, b), new, before)

    return lax.fori_loop(0, size, lap, start)


def entering_2(value, axis, combine, identity):
    size, here = (lax.axis_size(axis), lax.axis_index(axis))
    everything = jax.tree.map(
        lambda part, kind: lax.all_gather(part.astype(kind), axis),
        value,
        jax.tree.map(lambda a: jnp.bfloat16 if a.dtype == jnp.float32 else a.dtype, value),
    )
    start = jax.tree.map(
        lambda part, zero: jnp.broadcast_to(jnp.asarray(zero, part.dtype), part.shape),
        value,
        identity,
    )

    def lap(k, before):
        at = size - 1 - k
        reached = at > here
        new = combine(
            before, jax.tree.map(lambda part, own: part[at].astype(own.dtype), everything, value)
        )
        return jax.tree.map(lambda a, b: jnp.where(reached, a, b), new, before)

    return lax.fori_loop(0, size, lap, start)


def sum_groups(part, dimension):
    low = part.astype(jnp.bfloat16)
    total = lax.psum_scatter(low, "seq", scatter_dimension=dimension, tiled=True)
    return total.astype(jnp.float32)


def doc_layout(positions, lengths):
    seq_ends = jnp.cumsum(lengths)
    doc_ids = jnp.sum((positions[:, None] >= seq_ends[None, :]).astype(jnp.int32), axis=1)
    shifted = positions - 1
    earlier_ids = jnp.sum((shifted[:, None] >= seq_ends[None, :]).astype(jnp.int32), axis=1)
    prev_ids = jnp.where(shifted >= 0, earlier_ids, -1)
    valid_rows = (positions < seq_ends[-1]).astype(jnp.float32)
    return (doc_ids, prev_ids, valid_rows)


def rms_norm(rows_in, gain_vector):
    inv_scale = lax.rsqrt(jnp.mean(rows_in * rows_in, axis=-1, keepdims=True) + epsilon)
    return rows_in * inv_scale * gain_vector


def gate_values(query_pre, forget_pre, input_pre, bound_logit):
    lower_bound = jax.nn.sigmoid(bound_logit).reshape(-1)
    forget = lower_bound + (1.0 - lower_bound) * jax.nn.sigmoid(forget_pre)
    return (jax.nn.silu(query_pre), jnp.log(forget), 1.0 - forget, input_pre)


def group_out(valid_rows, recurrent_out, swish_pre, group_gain):
    head_count, head_width = group_gain.shape
    split_heads = recurrent_out.reshape(recurrent_out.shape[0], head_count, head_width)
    inv_scale = lax.rsqrt(jnp.mean(split_heads * split_heads, axis=-1, keepdims=True) + epsilon)
    normed = (split_heads * inv_scale * group_gain).reshape(recurrent_out.shape)
    return normed * jax.nn.silu(swish_pre) * valid_rows[:, None]


def swiglu_mix(gate_up):
    gate_rows, up_rows = jnp.split(gate_up, 2, axis=1)
    return jax.nn.silu(gate_rows) * up_rows


def block_run(queries, log_forget, key_rows, values, doc_ids, prev_ids, carried):
    head_count, head_width = (carried.shape[0], carried.shape[1])
    blocks = queries.shape[0] // BLOCK
    layout = (blocks, BLOCK, head_count, head_width)
    query_blocks = queries.reshape(layout)
    key_blocks = key_rows.reshape(layout)
    value_blocks = values.reshape(layout)
    cum_log = jnp.cumsum(log_forget.reshape(layout), axis=1)
    last_log = cum_log[:, -1]
    block_ids = doc_ids.reshape(blocks, BLOCK)
    before = prev_ids.reshape(blocks, BLOCK)[:, 0]
    query_decay = query_blocks * jnp.exp(cum_log)
    key_decay = key_blocks * jnp.exp(-cum_log)
    lower_mask = jnp.tril(jnp.ones((BLOCK, BLOCK), jnp.float32))
    same_doc = (block_ids[:, :, None] == block_ids[:, None, :]).astype(jnp.float32) * lower_mask
    scores = (
        jnp.einsum("nthd,nshd->nhts", query_decay, key_decay, precision=highest) * same_doc[:, None]
    )
    within = jnp.einsum("nhts,nshe->nthe", scores, value_blocks, precision=highest)
    carry_in = (block_ids == before[:, None]).astype(jnp.float32)
    tail_keep = (block_ids == block_ids[:, -1:]).astype(jnp.float32)
    key_tail = key_blocks * jnp.exp(last_log[:, None] - cum_log) * tail_keep[:, :, None, None]
    state_adds = jnp.einsum("nshd,nshe->nhde", key_tail, value_blocks, precision=highest)
    decays = jnp.exp(last_log) * carry_in[:, -1][:, None, None]

    def advance(state_now, pieces):
        return (pieces[0][:, :, None] * state_now + pieces[1], state_now)

    closing, starts = lax.scan(advance, carried, (decays, state_adds))
    across = jnp.einsum(
        "nthd,nhde->nthe", query_decay * carry_in[:, :, None, None], starts, precision=highest
    )
    return ((within + across).reshape(queries.shape), closing)


def reach_rows(queries, log_forget, doc_ids, first_prev):
    blocks = queries.shape[0] // BLOCK
    cum_log = jnp.cumsum(log_forget.reshape(blocks, BLOCK, -1), axis=1)
    totals = cum_log[:, -1]
    before = jnp.concatenate([jnp.zeros_like(totals[:1]), jnp.cumsum(totals, axis=0)[:-1]], axis=0)
    factor = jnp.exp(cum_log + before[:, None]).reshape(queries.shape)
    kept = (doc_ids == first_prev).astype(jnp.float32)
    return queries * factor * kept[:, None]


def mixer_local(doc_ids, prev_ids, query_pre, forget_pre, input_pre, bound_logit):
    queries, log_forget, key_rows, values = gate_values(
        query_pre, forget_pre, input_pre, bound_logit
    )
    head_count, head_width = bound_logit.shape
    empty_state = jnp.zeros((head_count, head_width, head_width), jnp.float32)
    own_part, state_adds = block_run(
        queries, log_forget, key_rows, values, doc_ids, prev_ids, empty_state
    )
    whole_doc = jnp.all(doc_ids == prev_ids[0]).astype(jnp.float32)
    decays = jnp.exp(jnp.sum(log_forget, axis=0)).reshape(head_count, head_width) * whole_doc
    entry_rows = reach_rows(queries, log_forget, doc_ids, prev_ids[0])
    return (own_part, state_adds, decays, entry_rows)


def combine_maps(earlier, latter):
    return (earlier[0] * latter[0], latter[0][:, :, None] * earlier[1] + latter[1])


def per_device(
    tokens,
    lengths,
    cotangent,
    first_gain,
    query_weight,
    forget_weight,
    input_weight,
    swish_weight,
    bound_logit,
    group_gain,
    out_weight,
    second_gain,
    gate_weight,
    up_weight,
    down_weight,
):
    input_rows = tokens.astype(jnp.float32)
    first_norm, first_back = jax.vjp(rms_norm, input_rows, first_gain)
    gathered = lax.all_gather(first_norm.astype(jnp.bfloat16), "tp", axis=0, tiled=True)
    group_rows = gathered.shape[0]
    positions = lax.axis_index("seq") * group_rows + jnp.arange(group_rows, dtype=jnp.int32)
    doc_ids, prev_ids, valid_rows = doc_layout(positions, lengths)
    mix_weights = jnp.concatenate([query_weight, forget_weight, input_weight, swish_weight], axis=1)
    projected = jnp.dot(gathered, mix_weights, preferred_element_type=jnp.float32)
    query_pre, forget_pre, input_pre, swish_pre = jnp.split(projected, 4, axis=1)
    pieces, mixer_back = jax.vjp(
        partial(mixer_local, doc_ids, prev_ids), query_pre, forget_pre, input_pre, bound_logit
    )
    own_part, state_adds, decays, entry_rows = pieces
    identity = (jnp.ones_like(decays), jnp.zeros_like(state_adds))
    arrived = entering((decays, state_adds), "seq", combine_maps, identity)[1]
    head_count, head_width = bound_logit.shape
    entry_heads = entry_rows.reshape(group_rows, head_count, head_width)
    carried_out = jnp.einsum("thd,hde->the", entry_heads, arrived, precision=highest)
    recurrent_out = own_part + carried_out.reshape(own_part.shape)
    gated, group_back = jax.vjp(
        partial(group_out, valid_rows), recurrent_out, swish_pre, group_gain
    )
    gated_low = gated.astype(jnp.bfloat16)
    piece = gated_low
    residual = input_rows + lax.psum_scatter(
        jnp.dot(piece, out_weight, preferred_element_type=jnp.float32).astype(jnp.bfloat16),
        "tp",
        scatter_dimension=0,
        tiled=True,
    ).astype(jnp.float32)
    second_norm, second_back = jax.vjp(rms_norm, residual, second_gain)
    ffn_rows = lax.all_gather(second_norm.astype(jnp.bfloat16), "tp", axis=0, tiled=True)
    glu_weights = jnp.concatenate([gate_weight, up_weight], axis=1)
    gate_up = jnp.dot(ffn_rows, glu_weights, preferred_element_type=jnp.float32)
    hidden, glu_back = jax.vjp(swiglu_mix, gate_up)
    hidden_low = hidden.astype(jnp.bfloat16)
    piece = hidden_low
    result = residual + lax.psum_scatter(
        jnp.dot(piece, down_weight, preferred_element_type=jnp.float32).astype(jnp.bfloat16),
        "tp",
        scatter_dimension=0,
        tiled=True,
    ).astype(jnp.float32)
    output = result.astype(jnp.bfloat16)
    cot_rows = lax.all_gather(cotangent, "tp", axis=0, tiled=True)
    down_grad = jnp.dot(hidden_low.T, cot_rows, preferred_element_type=jnp.float32)
    hidden_grad = jnp.dot(cot_rows, down_weight.T, preferred_element_type=jnp.float32)
    gate_up_grad = glu_back(hidden_grad)[0].astype(jnp.bfloat16)
    glu_grad = jnp.dot(ffn_rows.T, gate_up_grad, preferred_element_type=jnp.float32)
    gate_grad, up_grad = jnp.split(glu_grad, 2, axis=1)
    piece = gate_up_grad
    second_norm_grad = lax.psum_scatter(
        jnp.dot(piece, glu_weights.T, preferred_element_type=jnp.float32).astype(jnp.bfloat16),
        "tp",
        scatter_dimension=0,
        tiled=True,
    ).astype(jnp.float32)
    residual_norm_grad, second_gain_grad = second_back(second_norm_grad)
    residual_grad = cotangent.astype(jnp.float32) + residual_norm_grad
    branch_rows = lax.all_gather(residual_grad.astype(jnp.bfloat16), "tp", axis=0, tiled=True)
    out_grad = jnp.dot(gated_low.T, branch_rows, preferred_element_type=jnp.float32)
    gated_grad = jnp.dot(branch_rows, out_weight.T, preferred_element_type=jnp.float32)
    recurrent_grad, swish_back, group_gain_grad = group_back(gated_grad)
    recurrent_heads = recurrent_grad.reshape(group_rows, head_count, head_width)
    pulled = jnp.einsum("thd,the->hde", entry_heads, recurrent_heads, precision=highest)
    later_grad = entering_2((decays, pulled), "seq", combine_maps, identity)[1]
    entry_grad = jnp.einsum("the,hde->thd", recurrent_heads, arrived, precision=highest).reshape(
        entry_rows.shape
    )
    decay_grad = jnp.sum(later_grad * arrived, axis=-1)
    query_back, forget_back, input_back, bound_grad = mixer_back(
        (recurrent_grad, later_grad, decay_grad, entry_grad)
    )
    pre_grad = jnp.concatenate([query_back, forget_back, input_back, swish_back], axis=1).astype(
        jnp.bfloat16
    )
    mix_grad = jnp.dot(gathered.T, pre_grad, preferred_element_type=jnp.float32)
    piece = pre_grad
    first_norm_grad = lax.psum_scatter(
        jnp.dot(piece, mix_weights.T, preferred_element_type=jnp.float32).astype(jnp.bfloat16),
        "tp",
        scatter_dimension=0,
        tiled=True,
    ).astype(jnp.float32)
    input_norm_grad, first_gain_grad = first_back(first_norm_grad)
    tokens_grad = residual_grad + input_norm_grad
    query_grad, forget_grad, input_grad, swish_grad = jnp.split(mix_grad, 4, axis=1)
    (
        query_grad,
        forget_grad,
        input_grad,
        swish_grad,
        bound_grad,
        group_gain_grad,
        out_grad,
        gate_grad,
        up_grad,
        down_grad,
    ) = (
        sum_groups(query_grad, 0),
        sum_groups(forget_grad, 0),
        sum_groups(input_grad, 0),
        sum_groups(swish_grad, 0),
        lax.psum_scatter(bound_grad, "seq", scatter_dimension=1, tiled=True),
        lax.psum_scatter(group_gain_grad, "seq", scatter_dimension=1, tiled=True),
        sum_groups(out_grad, 1),
        sum_groups(gate_grad, 0),
        sum_groups(up_grad, 0),
        sum_groups(down_grad, 1),
    )
    first_gain_grad, second_gain_grad = (
        lax.psum_scatter(first_gain_grad, ("seq", "tp"), scatter_dimension=0, tiled=True),
        lax.psum_scatter(second_gain_grad, ("seq", "tp"), scatter_dimension=0, tiled=True),
    )
    return (
        output,
        tokens_grad,
        first_gain_grad,
        query_grad,
        forget_grad,
        input_grad,
        swish_grad,
        bound_grad,
        group_gain_grad,
        out_grad,
        second_gain_grad,
        gate_grad,
        up_grad,
        down_grad,
    )


def solution(mesh):
    in_specs = (
        P(("seq", "tp"), None),
        P(),
        P(("seq", "tp"), None),
        P(),
        P(None, "tp"),
        P(None, "tp"),
        P(None, "tp"),
        P(None, "tp"),
        P("tp", None),
        P("tp", None),
        P("tp", None),
        P(),
        P(None, "tp"),
        P(None, "tp"),
        P("tp", None),
    )
    out_specs = (
        P(("seq", "tp"), None),
        P(("seq", "tp"), None),
        P(("seq", "tp")),
        P("seq", "tp"),
        P("seq", "tp"),
        P("seq", "tp"),
        P("seq", "tp"),
        P("tp", "seq"),
        P("tp", "seq"),
        P("tp", "seq"),
        P(("seq", "tp")),
        P("seq", "tp"),
        P("seq", "tp"),
        P("tp", "seq"),
    )
    return jax.shard_map(
        per_device, mesh=mesh, in_specs=in_specs, out_specs=out_specs, check_vma=False
    )
```

```python
from functools import partial

import jax
import jax.numpy as jnp
from jax import lax
from jax.experimental import pallas as pl
from jax.experimental.pallas import tpu as pltpu
from jax.sharding import PartitionSpec as P

WIDTH = 128
ROUNDS = 4
MIB = 1 << 20
epsilon = 1e-05

f32 = jnp.float32
bf16 = jnp.bfloat16
NN = (((1,), (0,)), ((), ()))
NT = (((1,), (1,)), ((), ()))
TN = (((0,), (0,)), ((), ()))
VM = pltpu.VMEM
DMA = pltpu.SemaphoreType.DMA
MESH = pl.DeviceIdType.MESH


def mul(left, right, dims):
    return lax.dot_general(left, right, dims, preferred_element_type=f32)


def silu_slope(value):
    gate = jax.nn.sigmoid(value)
    return gate * (1.0 + value * (1.0 - gate))


def remote(src, dst, send, recv, axis, peer):
    return pltpu.make_async_remote_copy(
        src_ref=src,
        dst_ref=dst,
        send_sem=send,
        recv_sem=recv,
        device_id={axis: peer},
        device_id_type=MESH,
    )


def greet(peers, count):
    barrier = pltpu.get_barrier_semaphore()
    for axis, peer, wanted in peers:

        @pl.when(wanted)
        def _():
            pl.semaphore_signal(barrier, inc=1, device_id={axis: peer}, device_id_type=MESH)

    pl.semaphore_wait(barrier, count)


def line_peers(size):
    me = lax.axis_index("tp")
    peers = [("tp", lax.rem(me + 1, size), me < size - 1), ("tp", lax.rem(me + size - 1, size), me > 0)]
    return peers, jnp.where(me < size - 1, 1, 0) + jnp.where(me > 0, 1, 0)


def group_peers(size, axis):
    me = lax.axis_index(axis)
    return [(axis, lax.rem(me + k, size), True) for k in range(1, size)], size - 1


class Line:
    def __init__(self, size, send, recv):
        self.size = size
        self.me = lax.axis_index("tp")
        self.right = lax.rem(self.me + 1, size)
        self.left = lax.rem(self.me + size - 1, size)
        self.send, self.recv = send, recv

    def hop(self, way, src, dst, j, at):
        peer = self.right if way == 0 else self.left
        return remote(src, dst, self.send.at[way, j, at], self.recv.at[way, j, at], "tp", peer)


class Scatter(Line):
    def __init__(self, size, send, recv, part, land, total):
        super().__init__(size, send, recv)
        self.part, self.land, self.total = part, land, total

    def copy(self, way, j, to):
        return self.hop(way, self.part.at[j, to], self.land.at[way, j, to], j, to)

    def start(self, j):
        last = self.size - 1

        @pl.when(self.me == 0)
        def _():
            for to in range(last, 0, -1):
                self.copy(0, j, to).start()

        @pl.when(self.me == last)
        def _():
            for to in range(last):
                self.copy(1, j, to).start()

    def step(self, j, t):
        last = self.size - 1
        for way in (0, 1):
            place = self.me if way == 0 else last - self.me
            to = last - t + place
            to = to if way == 0 else last - to

            @pl.when((place >= 1) & (place <= t))
            def _():
                copy = self.copy(way, j, to)
                copy.wait_recv()
                self.add(self.part.at[j, to], self.land.at[way, j, to])
                copy.start()

    def add(self, into, more):
        rows = into.shape[0]

        @pl.loop(0, rows // 16)
        def _(g):
            r = pl.ds(pl.multiple_of(g * 16, 16), 16)
            into[r, :] = (into[r, :].astype(f32) + more[r, :].astype(f32)).astype(bf16)

    def finish(self, j):
        me, last = self.me, self.size - 1
        rows = self.total.shape[0]

        def over(body):
            @pl.loop(0, rows // 16)
            def _(g):
                body(pl.ds(pl.multiple_of(g * 16, 16), 16))

        def first(r):
            self.total[r, :] = self.part[j, me, r, :].astype(f32)

        over(first)
        for way, there in ((0, me >= 1), (1, me < last)):

            @pl.when(there)
            def _():
                self.copy(way, j, me).wait_recv()

                def more(r):
                    self.total[r, :] = self.total[r, :] + self.land[way, j, me, r, :].astype(f32)

                over(more)

    def drain(self, j):
        for to in range(self.size):

            @pl.when(self.me < to)
            def _():
                self.copy(0, j, to).wait_send()

            @pl.when(self.me > to)
            def _():
                self.copy(1, j, to).wait_send()


class Gather(Line):
    def __init__(self, size, send, recv, whole):
        super().__init__(size, send, recv)
        self.whole = whole

    def copy(self, way, j, source):
        block = self.whole.at[source, j]
        return self.hop(way, block, block, j, source)

    def start(self, j):
        @pl.when(self.me < self.size - 1)
        def _():
            self.copy(0, j, self.me).start()

        @pl.when(self.me > 0)
        def _():
            self.copy(1, j, self.me).start()

    def step(self, j, t):
        last = self.size - 1

        @pl.when(self.me >= t)
        def _():
            copy = self.copy(0, j, self.me - t)
            copy.wait_recv()

            @pl.when(self.me < last)
            def _():
                copy.start()

        @pl.when(self.me + t <= last)
        def _():
            copy = self.copy(1, j, self.me + t)
            copy.wait_recv()

            @pl.when(self.me > 0)
            def _():
                copy.start()

    def drain(self, j):
        last = self.size - 1
        for source in range(self.size):

            @pl.when((self.me >= source) & (self.me < last))
            def _():
                self.copy(0, j, source).wait_send()

            @pl.when((self.me <= source) & (self.me > 0))
            def _():
                self.copy(1, j, source).wait_send()


class GroupSum:
    def __init__(self, size, grad, own, got, land, out, sems):
        self.half = size // 2
        here = lax.axis_index("seq")
        self.side = lax.rem(here, 2)
        self.mine = here // 2
        self.sibling = here + 1 - 2 * self.side
        self.grad, self.own, self.got, self.land, self.out = grad, own, got, land, out
        self.pair_sems, self.send, self.recv = sems

    def near(self):
        return remote(
            self.grad.at[:, 1 - self.side], self.got, self.pair_sems.at[0], self.pair_sems.at[1], "seq", self.sibling
        )

    def load(self):
        return pltpu.make_async_copy(self.grad.at[:, self.side], self.own, self.pair_sems.at[2])

    def far(self, k):
        return remote(
            self.own.at[k], self.land.at[self.mine], self.send.at[k], self.recv.at[self.mine], "seq", 2 * k + self.side
        )

    def arrival(self, k):
        return remote(
            self.own.at[k], self.land.at[k], self.send.at[k], self.recv.at[k], "seq", 2 * k + self.side
        )

    def start(self):
        self.near().start()
        self.load().start()

    def over(self, body):
        rows = self.own.shape[1]

        @pl.loop(0, rows // 16)
        def _(g):
            body(pl.ds(pl.multiple_of(g * 16, 16), 16))

    def middle(self):
        self.load().wait()
        self.near().wait_recv()
        for k in range(self.half):

            def both(r):
                self.own[k, r, :] = (self.own[k, r, :].astype(f32) + self.got[k, r, :].astype(f32)).astype(bf16)

            self.over(both)

            @pl.when(k != self.mine)
            def _():
                self.far(k).start()

    def finish(self):
        def first(r):
            self.out[r, :] = self.own[self.mine, r, :].astype(f32)

        self.over(first)
        for k in range(self.half):

            @pl.when(k != self.mine)
            def _():
                self.arrival(k).wait_recv()

                def more(r):
                    self.out[r, :] = self.out[r, :] + self.land[k, r, :].astype(f32)

                self.over(more)

    def drain(self):
        self.near().wait_send()
        for k in range(self.half):

            @pl.when(k != self.mine)
            def _():
                self.far(k).wait_send()


def group_sums(size, grads, outs, take):
    sums = []
    for grad, out in zip(grads, outs):
        own, got, land, *sems = take(6)
        sums.append(GroupSum(size, grad, own, got, land, out, sems))
    return sums


def group_sums_scratch(grads):
    scratch = []
    for grad in grads:
        half = grad.shape[0] // 2
        shape = (half,) + grad.shape[1:]
        scratch += [VM(shape, bf16), VM(shape, bf16), VM(shape, bf16), DMA((3,)), DMA((half,)), DMA((half,))]
    return scratch


def in_pairs(grad):
    return grad.reshape((grad.shape[0] // 2, 2) + grad.shape[1:])


def taker(refs):
    refs = list(refs)

    def take(count):
        taken, refs[:count] = refs[:count], []
        return taken

    return take


def project_kernel(size, rounds, x_ref, gain_ref, wq, wf, wi, ws, a_ref, q_ref, f_ref, i_ref, s_ref, send, recv):
    greet(*line_peers(size))
    line = Gather(size, send, recv, a_ref)
    gain = gain_ref[...]
    m, d = x_ref.shape[1:]

    @pl.loop(0, rounds)
    def _(j):
        @pl.loop(0, m // 16)
        def _(g):
            r = pl.ds(pl.multiple_of(g * 16, 16), 16)
            x = x_ref[j, r, :].astype(f32)
            scale = lax.rsqrt(jnp.mean(x * x, axis=-1, keepdims=True) + epsilon)
            a_ref[line.me, j, r, :] = (x * scale * gain).astype(bf16)

        line.start(j)

    def products(j):
        rows = a_ref[:, j].reshape(size * m, d)
        for weight, out in ((wq, q_ref), (wf, f_ref), (wi, i_ref), (ws, s_ref)):
            out[:, j] = mul(rows, weight[...], NN).reshape(size, m, weight.shape[1])

    @pl.loop(0, rounds)
    def _(j):
        for t in range(1, size):
            line.step(j, t)
        products(j)

    @pl.loop(0, rounds)
    def _(j):
        line.drain(j)


def project(size, rounds, tokens, first_gain, wq, wf, wi, ws):
    rows, d = tokens.shape
    m = rows // rounds
    c = wq.shape[1]
    shape = (size, rounds, m)
    out = pl.pallas_call(
        partial(project_kernel, size, rounds),
        out_shape=[jax.ShapeDtypeStruct(shape + (d,), bf16)] + [jax.ShapeDtypeStruct(shape + (c,), f32)] * 4,
        in_specs=[pl.BlockSpec(memory_space=VM)] * 6,
        out_specs=[pl.BlockSpec(memory_space=VM)] * 5,
        scratch_shapes=[DMA((2, rounds, size)), DMA((2, rounds, size))],
        compiler_params=pltpu.CompilerParams(collective_id=0, has_side_effects=True, vmem_limit_bytes=48 * MIB),
        cost_estimate=pl.CostEstimate(flops=8 * size * rows * d * c, bytes_accessed=32 * MIB, transcendentals=0),
        name="project",
    )(tokens.reshape(rounds, m, d), first_gain.reshape(1, d), wq, wf, wi, ws)
    total = size * rows
    return [out[0].reshape(total, d)] + [part.reshape(total, c) for part in out[1:]]


def document(rows, ends_ref):
    total = jnp.where(rows >= ends_ref[0], 1, 0)
    for k in range(1, ends_ref.shape[0]):
        total = total + jnp.where(rows >= ends_ref[k], 1, 0)
    return total


def block_masks(first, ends_ref):
    shape = (WIDTH, WIDTH)
    down = lax.broadcasted_iota(jnp.int32, shape, 0)
    along = lax.broadcasted_iota(jnp.int32, shape, 1)
    docs = document(first + down, ends_ref)
    same = (docs == document(first + along, ends_ref)) & (down >= along)
    before = jnp.where(first > 0, document(first - 1, ends_ref), -1)
    final = document(first + WIDTH - 1, ends_ref)
    carry = jnp.where(docs == before, 1.0, 0.0)
    tail = jnp.where(docs == final, 1.0, 0.0)
    keep = jnp.where(final == before, 1.0, 0.0)
    return same, carry, tail, keep


def running(log_forget):
    shape = (WIDTH, WIDTH)
    lower = lax.broadcasted_iota(jnp.int32, shape, 0) >= lax.broadcasted_iota(jnp.int32, shape, 1)
    ones = jnp.where(lower, 1.0, 0.0).astype(bf16)
    high = log_forget.astype(bf16)
    low = (log_forget - high.astype(f32)).astype(bf16)
    return mul(ones, high, NN) + mul(ones, low, NN)


def decay_parts(forget_pre, bound):
    away = jax.nn.sigmoid(-forget_pre)
    key = jax.nn.sigmoid(-bound) * away
    return key, running(jnp.log(1.0 - key)), away


class States:
    def __init__(self, size, out_state, out_decay, land_state, land_decay, sems):
        self.size = size
        self.here = lax.axis_index("seq")
        self.out_state, self.out_decay = out_state, out_decay
        self.land_state, self.land_decay = land_state, land_decay
        self.sems = sems

    def pair(self, slot, peer):
        s = self.sems
        return (
            remote(self.out_state, self.land_state.at[slot], s.at[0, peer], s.at[1, slot], "seq", peer),
            remote(self.out_decay, self.land_decay.at[slot], s.at[2, peer], s.at[3, slot], "seq", peer),
        )

    def sends(self, later):
        for k in range(self.size):
            yield k, (self.here < k if later else self.here > k)

    def start(self, later):
        for k, wanted in self.sends(later):

            @pl.when(wanted)
            def _():
                for copy in self.pair(self.here, k):
                    copy.start()

    def compose(self, later, state):
        state[...] = jnp.zeros_like(state)
        order = range(self.size) if later else range(self.size - 1, -1, -1)
        for k in order:

            @pl.when(self.here > k if later else self.here < k)
            def _():
                for copy in self.pair(k, k):
                    copy.wait_recv()
                for h in range(state.shape[0]):
                    decay = self.land_decay[k, h : h + 1, :]
                    state[h] = decay * state[h] + self.land_state[k, h].astype(f32)

    def drain(self, later):
        for k, wanted in self.sends(later):

            @pl.when(wanted)
            def _():
                for copy in self.pair(self.here, k):
                    copy.wait_send()


def states_scratch(size, heads):
    return [
        VM((heads, WIDTH, WIDTH), f32),
        VM((heads, WIDTH, WIDTH), bf16),
        VM((8, WIDTH), f32),
        VM((size, heads, WIDTH, WIDTH), bf16),
        VM((size, 8, WIDTH), f32),
        DMA((4, size)),
    ]


def scan_kernel(
    size,
    ends_ref,
    q_ref,
    f_ref,
    i_ref,
    s_ref,
    bound_ref,
    gain_ref,
    o_ref,
    u_ref,
    starts_ref,
    qd_ref,
    kd_ref,
    qe_ref,
    adds,
    decays,
    state,
    out_state,
    out_decay,
    land_state,
    land_decay,
    sems,
):
    greet(*group_peers(size, "seq"))
    rows, c = q_ref.shape
    blocks, heads = rows // WIDTH, c // WIDTH
    base = lax.axis_index("seq") * rows
    states = States(size, out_state, out_decay, land_state, land_decay, sems)
    state[...] = jnp.zeros_like(state)
    out_decay[...] = jnp.ones_like(out_decay)

    @pl.loop(0, blocks)
    def _(b):
        r = pl.ds(pl.multiple_of(b * WIDTH, WIDTH), WIDTH)
        same, carry, tail, keep = block_masks(base + b * WIDTH, ends_ref)
        for h in range(heads):
            cols = slice(h * WIDTH, (h + 1) * WIDTH)
            q = q_ref[r, cols]
            q = q * jax.nn.sigmoid(q)
            key, run, _ = decay_parts(f_ref[r, cols], bound_ref[:, cols])
            middle, last = run[WIDTH // 2 - 1 : WIDTH // 2, :], run[WIDTH - 1 :, :]
            qd_ref[r, cols] = (q * jnp.exp(run - middle)).astype(bf16)
            kd_ref[r, cols] = (key * jnp.exp(middle - run)).astype(bf16)
            qe_ref[r, cols] = (q * jnp.exp(run) * carry).astype(bf16)
            key_tail = (key * jnp.exp(last - run) * tail).astype(bf16)
            add = mul(i_ref[r, cols].astype(bf16), key_tail, TN)
            decay = jnp.exp(last) * keep
            adds[b, h] = add
            decays[b, h : h + 1, :] = decay
            state[h] = decay * state[h] + add
            out_decay[h : h + 1, :] = out_decay[h : h + 1, :] * decay

    out_state[...] = state[...].astype(bf16)
    states.start(True)

    @pl.loop(0, blocks)
    def _(b):
        r = pl.ds(pl.multiple_of(b * WIDTH, WIDTH), WIDTH)
        same, carry, tail, keep = block_masks(base + b * WIDTH, ends_ref)
        for h in range(heads):
            cols = slice(h * WIDTH, (h + 1) * WIDTH)
            scores = jnp.where(same, mul(qd_ref[r, cols], kd_ref[r, cols], NT), 0.0).astype(bf16)
            o_ref[r, cols] = mul(scores, i_ref[r, cols].astype(bf16), NN)

    states.compose(True, state)

    @pl.loop(0, blocks)
    def _(b):
        r = pl.ds(pl.multiple_of(b * WIDTH, WIDTH), WIDTH)
        places = base + b * WIDTH + lax.broadcasted_iota(jnp.int32, (WIDTH, WIDTH), 0)
        valid = jnp.where(places < ends_ref[ends_ref.shape[0] - 1], 1.0, 0.0)
        for h in range(heads):
            cols = slice(h * WIDTH, (h + 1) * WIDTH)
            low = state[h].astype(bf16)
            starts_ref[b, h] = low
            o = o_ref[r, cols] + mul(qe_ref[r, cols], low, NT)
            o_ref[r, cols] = o
            state[h] = decays[b, h : h + 1, :] * state[h] + adds[b, h]
            scale = lax.rsqrt(jnp.mean(o * o, axis=-1, keepdims=True) + epsilon)
            s = s_ref[r, cols]
            z = s * jax.nn.sigmoid(s) * valid
            u_ref[r, cols] = (o * scale * gain_ref[:, cols] * z).astype(bf16)

    states.drain(True)


def scan_forward(size, ends, q, f, i, s, bound, gain):
    rows, c = q.shape
    blocks, heads = rows // WIDTH, c // WIDTH
    low = VM((rows, c), bf16)
    return pl.pallas_call(
        partial(scan_kernel, size),
        out_shape=[
            jax.ShapeDtypeStruct((rows, c), f32),
            jax.ShapeDtypeStruct((rows, c), bf16),
            jax.ShapeDtypeStruct((blocks, heads, WIDTH, WIDTH), bf16),
        ],
        in_specs=[pl.BlockSpec(memory_space=pltpu.SMEM)] + [pl.BlockSpec(memory_space=VM)] * 6,
        out_specs=[pl.BlockSpec(memory_space=VM)] * 3,
        scratch_shapes=[
            low,
            low,
            low,
            VM((blocks, heads, WIDTH, WIDTH), f32),
            VM((blocks, 8, WIDTH), f32),
        ]
        + states_scratch(size, heads),
        compiler_params=pltpu.CompilerParams(collective_id=1, has_side_effects=True, vmem_limit_bytes=48 * MIB),
        cost_estimate=pl.CostEstimate(flops=20 * rows * c * WIDTH, bytes_accessed=14 * MIB, transcendentals=8 * rows * c),
        name="scan_forward",
    )(ends, q, f, i, s, bound, gain)


def scan_back_kernel(size, count, *refs):
    take = taker(refs)
    ends_ref, q_ref, f_ref, i_ref, s_ref, bound_ref, gain_ref, o_ref, starts_ref, ub_ref = take(10)
    grads = take(count)
    dq_ref, df_ref, di_ref, ds_ref, small_ref = take(5)
    grad_outs = take(count)
    qd_ref, kd_ref, qe_ref, kt_ref, do_ref, run_ref, adds, decays = take(8)
    state, out_state, out_decay, land_state, land_decay, sems = take(6)
    sums = group_sums(size, grads, grad_outs, take)
    greet(*group_peers(size, "seq"))
    rows, c = q_ref.shape
    blocks, heads = rows // WIDTH, c // WIDTH
    base = lax.axis_index("seq") * rows
    states = States(size, out_state, out_decay, land_state, land_decay, sems)
    for each in sums:
        each.start()
    state[...] = jnp.zeros_like(state)
    out_decay[...] = jnp.ones_like(out_decay)
    small_ref[...] = jnp.zeros_like(small_ref)

    @pl.loop(0, blocks)
    def _(back):
        b = blocks - 1 - back
        r = pl.ds(pl.multiple_of(b * WIDTH, WIDTH), WIDTH)
        same, carry, tail, keep = block_masks(base + b * WIDTH, ends_ref)
        places = base + b * WIDTH + lax.broadcasted_iota(jnp.int32, (WIDTH, WIDTH), 0)
        valid = jnp.where(places < ends_ref[ends_ref.shape[0] - 1], 1.0, 0.0)
        for h in range(heads):
            cols = slice(h * WIDTH, (h + 1) * WIDTH)
            o, s, ub, gain = o_ref[r, cols], s_ref[r, cols], ub_ref[r, cols], gain_ref[:, cols]
            scale = lax.rsqrt(jnp.mean(o * o, axis=-1, keepdims=True) + epsilon)
            normed = o * scale
            gate = jax.nn.sigmoid(s)
            uz = ub * (s * gate * valid)
            small_ref[heads + h : heads + h + 1, :] += jnp.sum(uz * normed, axis=0, keepdims=True)
            nb = uz * gain
            ds_ref[r, cols] = (ub * normed * gain * valid * (gate * (1.0 + s * (1.0 - gate)))).astype(bf16)
            do = (scale * (nb - normed * jnp.mean(nb * normed, axis=-1, keepdims=True))).astype(bf16)
            do_ref[r, cols] = do
            q = q_ref[r, cols]
            q = q * jax.nn.sigmoid(q)
            key, run, _ = decay_parts(f_ref[r, cols], bound_ref[:, cols])
            middle, last = run[WIDTH // 2 - 1 : WIDTH // 2, :], run[WIDTH - 1 :, :]
            run_ref[r, cols] = run
            qd_ref[r, cols] = (q * jnp.exp(run - middle)).astype(bf16)
            kd_ref[r, cols] = (key * jnp.exp(middle - run)).astype(bf16)
            kt_ref[r, cols] = (key * jnp.exp(last - run) * tail).astype(bf16)
            qe = (q * jnp.exp(run) * carry).astype(bf16)
            qe_ref[r, cols] = qe
            add = mul(do, qe, TN)
            decay = jnp.exp(last) * keep
            adds[b, h] = add
            decays[b, h : h + 1, :] = decay
            state[h] = decay * state[h] + add
            out_decay[h : h + 1, :] = out_decay[h : h + 1, :] * decay

    out_state[...] = state[...].astype(bf16)
    states.start(False)

    for each in sums:
        each.middle()

    states.compose(False, state)

    @pl.loop(0, blocks)
    def _(back):
        b = blocks - 1 - back
        r = pl.ds(pl.multiple_of(b * WIDTH, WIDTH), WIDTH)
        same, carry, tail, keep = block_masks(base + b * WIDTH, ends_ref)
        shape = (WIDTH, WIDTH)
        down, along = lax.broadcasted_iota(jnp.int32, shape, 0), lax.broadcasted_iota(jnp.int32, shape, 1)
        from_here = jnp.where(along >= down, 1.0, 0.0).astype(bf16)
        ahead = jnp.where(along < down, 1.0, 0.0).astype(bf16)
        for h in range(heads):
            cols = slice(h * WIDTH, (h + 1) * WIDTH)
            do, v = do_ref[r, cols], i_ref[r, cols].astype(bf16)
            low, start = state[h].astype(bf16), starts_ref[b, h]
            dq_state = mul(do, start, NN)
            dk_state = mul(v, low, NN)
            kt = kt_ref[r, cols]
            qd, kd = qd_ref[r, cols], kd_ref[r, cols]
            scores = jnp.where(same, mul(qd, kd, NT), 0.0).astype(bf16)
            slopes = jnp.where(same, mul(do, v, NT), 0.0).astype(bf16)
            dq_near = mul(slopes, kd, NN)
            dk_near = mul(slopes, qd, TN)
            di_ref[r, cols] = (mul(scores, do, TN) + mul(kt, low, NT)).astype(bf16)
            run = run_ref[r, cols]
            middle, last = run[WIDTH // 2 - 1 : WIDTH // 2, :], run[WIDTH - 1 :, :]
            q_back = dq_near * jnp.exp(run - middle) + dq_state * (jnp.exp(run) * carry)
            k_back = dk_near * jnp.exp(middle - run) + dk_state * (jnp.exp(last - run) * tail)
            later = (
                qe_ref[r, cols].astype(f32) * dq_state
                + qd.astype(f32) * dq_near
                - kd.astype(f32) * dk_near
            )
            earlier = kt.astype(f32) * dk_state
            decay = decays[b, h : h + 1, :]
            log_back = decay * jnp.sum(low.astype(f32) * start.astype(f32), axis=0, keepdims=True)
            for ones, part in ((from_here, later), (ahead, earlier)):
                high = part.astype(bf16)
                log_back = log_back + mul(ones, high, NN)
                log_back = log_back + mul(ones, (part - high.astype(f32)).astype(bf16), NN)
            f_pre = f_ref[r, cols]
            away, near = jax.nn.sigmoid(-f_pre), jax.nn.sigmoid(f_pre)
            upper = jax.nn.sigmoid(-bound_ref[:, cols])
            lower = jax.nn.sigmoid(bound_ref[:, cols])
            forget_back = log_back / (1.0 - upper * away) - k_back
            slope = forget_back * away * upper
            df_ref[r, cols] = (slope * near).astype(bf16)
            small_ref[h : h + 1, :] += jnp.sum(slope, axis=0, keepdims=True) * lower
            dq_ref[r, cols] = (q_back * silu_slope(q_ref[r, cols])).astype(bf16)
            state[h] = adds[b, h] + decay * state[h]

    for each in sums:
        each.finish()
    states.drain(False)
    for each in sums:
        each.drain()


def scan_backward(size, ends, q, f, i, s, bound, gain, o, starts, ub, grads):
    rows, c = q.shape
    blocks, heads = rows // WIDTH, c // WIDTH
    low, wide = VM((rows, c), bf16), VM((rows, c), f32)
    spec = pl.BlockSpec(memory_space=VM)
    return pl.pallas_call(
        partial(scan_back_kernel, size, len(grads)),
        out_shape=[jax.ShapeDtypeStruct((rows, c), bf16)] * 4
        + [jax.ShapeDtypeStruct((2 * heads, WIDTH), f32)]
        + [jax.ShapeDtypeStruct(grad.shape[1:], f32) for grad in grads],
        in_specs=[pl.BlockSpec(memory_space=pltpu.SMEM)]
        + [spec] * 9
        + [pl.BlockSpec(memory_space=pl.ANY)] * len(grads),
        out_specs=[spec] * (5 + len(grads)),
        scratch_shapes=[low] * 5
        + [wide, VM((blocks, heads, WIDTH, WIDTH), f32), VM((blocks, 8, WIDTH), f32)]
        + states_scratch(size, heads)
        + group_sums_scratch(grads),
        compiler_params=pltpu.CompilerParams(collective_id=2, has_side_effects=True, vmem_limit_bytes=60 * MIB),
        cost_estimate=pl.CostEstimate(flops=40 * rows * c * WIDTH, bytes_accessed=20 * MIB, transcendentals=16 * rows * c),
        name="scan_backward",
    )(ends, q, f, i, s, bound, gain, o, starts, ub, *[in_pairs(grad) for grad in grads])


def middle_kernel(
    size,
    rounds,
    u_ref,
    x_ref,
    cot_ref,
    gain_ref,
    out_w,
    gate_w,
    up_w,
    down_w,
    res_ref,
    back_ref,
    b_ref,
    e_ref,
    ub_ref,
    second_ref,
    hidden_out,
    gate_out,
    up_out,
    part,
    land,
    total,
    hidden,
    gate_back,
    up_back,
    keep_sems,
    s_send,
    s_recv,
    g_send,
    g_recv,
    s_send2,
    s_recv2,
    g_send2,
    g_recv2,
):
    greet(*line_peers(size))
    me = lax.axis_index("tp")
    m, d = x_ref.shape[1:]
    ff = gate_w.shape[1]
    scatter = Scatter(size, s_send, s_recv, part, land, total)
    gather = Gather(size, g_send, g_recv, b_ref)
    scatter_back = Scatter(size, s_send2, s_recv2, part, land, total)
    gather_back = Gather(size, g_send2, g_recv2, e_ref)
    gain = gain_ref[...]
    second_ref[...] = jnp.zeros_like(second_ref)
    tile = min(512, d)

    def project_out(j):
        rows = u_ref[:, j].reshape(size * m, u_ref.shape[3])

        @pl.loop(0, d // tile)
        def _(n):
            cols = pl.ds(pl.multiple_of(n * tile, tile), tile)
            part[j, :, :, cols] = mul(rows, out_w[:, cols], NN).astype(bf16).reshape(size, m, tile)

        scatter.start(j)

    def norm(j):
        @pl.loop(0, m // 16)
        def _(g):
            r = pl.ds(pl.multiple_of(g * 16, 16), 16)
            residual = x_ref[j, r, :].astype(f32) + total[r, :]
            res_ref[j, r, :] = residual
            scale = lax.rsqrt(jnp.mean(residual * residual, axis=-1, keepdims=True) + epsilon)
            b_ref[me, j, r, :] = (residual * scale * gain).astype(bf16)

        gather.start(j)

    def kept(j):
        return [
            pltpu.make_async_copy(src, dst.at[:, j], keep_sems.at[k])
            for k, (src, dst) in enumerate(((hidden, hidden_out), (gate_back, gate_out), (up_back, up_out)))
        ]

    def feed(j):
        @pl.when(j > 0)
        def _():
            for copy in kept(j - 1):
                copy.wait()

        rows = b_ref[:, j].reshape(size * m, d)
        cot = cot_ref[:, j].reshape(size * m, d)
        step = 512
        for low in range(0, ff, step):
            cols = slice(low, min(low + step, ff))
            width = cols.stop - cols.start
            gate = mul(rows, gate_w[:, cols], NN)
            up = mul(rows, up_w[:, cols], NN)
            hb = mul(cot, down_w[cols, :], NT)
            sig = jax.nn.sigmoid(gate)
            act = gate * sig
            shape = (size, m, width)
            hidden[:, :, cols] = (act * up).astype(bf16).reshape(shape)
            up_back[:, :, cols] = (hb * act).astype(bf16).reshape(shape)
            gate_back[:, :, cols] = (hb * up * (sig * (1.0 + gate * (1.0 - sig)))).astype(bf16).reshape(shape)
        for copy in kept(j):
            copy.start()

    def feed_back(j):
        scatter.drain(j)
        gates = gate_back[...].reshape(size * m, ff)
        ups = up_back[...].reshape(size * m, ff)

        @pl.loop(0, d // tile)
        def _(n):
            cols = pl.ds(pl.multiple_of(n * tile, tile), tile)
            sums = mul(gates, gate_w[cols, :], NT) + mul(ups, up_w[cols, :], NT)
            part[j, :, :, cols] = sums.astype(bf16).reshape(size, m, tile)

        scatter_back.start(j)

    def norm_back(j):
        @pl.loop(0, m // 16)
        def _(g):
            r = pl.ds(pl.multiple_of(g * 16, 16), 16)
            b_back, residual = total[r, :], res_ref[j, r, :]
            scale = lax.rsqrt(jnp.mean(residual * residual, axis=-1, keepdims=True) + epsilon)
            normed = residual * scale
            second_ref[...] += jnp.sum(b_back * normed, axis=0, keepdims=True)
            inner = b_back * gain
            back = cot_ref[me, j, r, :].astype(f32) + scale * (
                inner - normed * jnp.mean(inner * normed, axis=-1, keepdims=True)
            )
            back_ref[j, r, :] = back
            e_ref[me, j, r, :] = back.astype(bf16)

        gather_back.start(j)

    def unproject(j):
        rows = e_ref[:, j].reshape(size * m, d)
        ub_ref[:, j] = mul(rows, out_w[...], NT).reshape(size, m, out_w.shape[0])

    @pl.loop(0, rounds + 4)
    def _(i):
        def stage(lag, body):
            @pl.when((i >= lag) & (i < rounds + lag))
            def _():
                body(i - lag)

        stage(0, project_out)
        for t in range(1, size):
            stage(1, lambda j: scatter.step(j, t) if t < size - 1 else scatter.finish(j))
            if t == size - 1:
                stage(1, norm)
            stage(2, lambda j: gather.step(j, t))
            stage(3, lambda j: scatter_back.step(j, t) if t < size - 1 else scatter_back.finish(j))
            if t == size - 1:
                stage(3, norm_back)
            stage(4, lambda j: gather_back.step(j, t))
        stage(2, feed)
        stage(2, feed_back)
        stage(4, unproject)

    for copy in kept(rounds - 1):
        copy.wait()

    @pl.loop(0, rounds)
    def _(j):
        gather.drain(j)
        scatter_back.drain(j)
        gather_back.drain(j)


def middle(size, rounds, u, x, cot, gain, out_w, gate_w, up_w, down_w):
    rows, d = x.shape
    m = rows // rounds
    c, ff = out_w.shape[0], gate_w.shape[1]
    shape = (size, rounds, m)
    sems = DMA((2, rounds, size))
    wide = VM((size, m, ff), bf16)
    outs = pl.pallas_call(
        partial(middle_kernel, size, rounds),
        out_shape=[
            jax.ShapeDtypeStruct((rounds, m, d), f32),
            jax.ShapeDtypeStruct((rounds, m, d), f32),
            jax.ShapeDtypeStruct(shape + (d,), bf16),
            jax.ShapeDtypeStruct(shape + (d,), bf16),
            jax.ShapeDtypeStruct(shape + (c,), f32),
            jax.ShapeDtypeStruct((1, d), f32),
        ]
        + [jax.ShapeDtypeStruct(shape + (ff,), bf16)] * 3,
        in_specs=[pl.BlockSpec(memory_space=VM)] * 8,
        out_specs=[pl.BlockSpec(memory_space=VM)] * 6 + [pl.BlockSpec(memory_space=pl.ANY)] * 3,
        scratch_shapes=[
            VM((rounds, size, m, d), bf16),
            VM((2, rounds, size, m, d), bf16),
            VM((m, d), f32),
            wide,
            wide,
            wide,
            DMA((3,)),
        ]
        + [sems] * 8,
        compiler_params=pltpu.CompilerParams(collective_id=3, has_side_effects=True, vmem_limit_bytes=63 * MIB),
        cost_estimate=pl.CostEstimate(
            flops=2 * size * rows * d * (2 * c + 5 * ff), bytes_accessed=56 * MIB, transcendentals=size * rows * ff
        ),
        name="middle",
    )(
        u.reshape(shape + (c,)),
        x.reshape(rounds, m, d),
        cot.reshape(shape + (d,)),
        gain.reshape(1, d),
        out_w,
        gate_w,
        up_w,
        down_w,
    )
    res, back, b, e, ub, second, hidden, gates, ups = outs
    total = size * rows
    return (
        res.reshape(rows, d),
        back.reshape(rows, d),
        b.reshape(total, d),
        e.reshape(total, d),
        ub.reshape(total, c),
        second,
        hidden.reshape(total, ff),
        gates.reshape(total, ff),
        ups.reshape(total, ff),
    )


class Everyone:
    def __init__(self, size, axis, mine, land, sems):
        self.size, self.axis = size, axis
        self.here = lax.axis_index(axis)
        self.mine, self.land, self.sems = mine, land, sems

    def copy(self, slot, peer):
        return remote(self.mine, self.land.at[slot], self.sems.at[0, peer], self.sems.at[1, slot], self.axis, peer)

    def others(self):
        for k in range(self.size):
            yield k, self.here != k

    def start(self):
        for k, other in self.others():

            @pl.when(other)
            def _():
                self.copy(self.here, k).start()

    def finish(self, out):
        out[...] = self.mine[...]
        for k, other in self.others():

            @pl.when(other)
            def _():
                self.copy(k, k).wait_recv()
                out[...] = out[...] + self.land[k]

    def drain(self):
        for k, other in self.others():

            @pl.when(other)
            def _():
                self.copy(self.here, k).wait_send()


def everyone_scratch(size, rows):
    return [VM((rows, WIDTH), f32), VM((size, rows, WIDTH), f32), DMA((2, size))]


def stack(vector, into, at):
    for k in range(vector.shape[1] // WIDTH):
        into[at + k : at + k + 1, :] = vector[:, k * WIDTH : (k + 1) * WIDTH]


def last_kernel(size, groups, rounds, count, *refs):
    take = taker(refs)
    backs, weights = take(4), take(4)
    x_ref, back_ref, gain_ref, second_ref, small_ref = take(5)
    grads = take(count)
    tokens_out, second_out, first_out, small_out = take(4)
    grad_outs = take(count)
    part, land, total, first, s_send, s_recv = take(6)
    small_seq, gain_seq, second_tp, first_tp = (take(3) for _ in range(4))
    sums = group_sums(groups, grads, grad_outs, take)

    seq, seq_count = group_peers(groups, "seq")
    tp, tp_count = group_peers(size, "tp")
    greet(seq + tp, seq_count + tp_count)

    for each in sums:
        each.start()

    m, d = x_ref.shape[1:]
    scatter = Scatter(size, s_send, s_recv, part, land, total)
    gain = gain_ref[...]
    first[...] = jnp.zeros_like(first)
    tile = min(512, d)

    seq_small = Everyone(groups, "seq", *small_seq)
    seq_first = Everyone(groups, "seq", *gain_seq)
    tp_second = Everyone(size, "tp", *second_tp)
    tp_first = Everyone(size, "tp", *first_tp)
    lines, smalls = d // WIDTH, small_ref.shape[0]
    stack(second_ref[...], small_seq[0], 0)
    small_seq[0][lines : lines + smalls, :] = small_ref[...]
    seq_small.start()

    def products(j):
        @pl.loop(0, d // tile)
        def _(n):
            cols = pl.ds(pl.multiple_of(n * tile, tile), tile)
            acc = None
            for back, weight in zip(backs, weights):
                term = mul(back[:, j].reshape(size * m, back.shape[3]), weight[cols, :], NT)
                acc = term if acc is None else acc + term
            part[j, :, :, cols] = acc.astype(bf16).reshape(size, m, tile)

        scatter.start(j)

    def norm_back(j):
        @pl.loop(0, m // 16)
        def _(g):
            r = pl.ds(pl.multiple_of(g * 16, 16), 16)
            a_back, x = total[r, :], x_ref[j, r, :].astype(f32)
            scale = lax.rsqrt(jnp.mean(x * x, axis=-1, keepdims=True) + epsilon)
            normed = x * scale
            first[...] += jnp.sum(a_back * normed, axis=0, keepdims=True)
            inner = a_back * gain
            tokens_out[j, r, :] = back_ref[j, r, :] + scale * (
                inner - normed * jnp.mean(inner * normed, axis=-1, keepdims=True)
            )

    @pl.loop(0, rounds)
    def _(j):
        products(j)

    for each in sums[: count // 2]:
        each.middle()

    seq_small.finish(small_out)
    second_tp[0][...] = small_out[:lines, :]
    tp_second.start()

    for each in sums[count // 2 :]:
        each.middle()

    @pl.loop(0, rounds)
    def _(j):
        for t in range(1, size):
            if t < size - 1:
                scatter.step(j, t)
            else:
                scatter.finish(j)
        norm_back(j)

    stack(first[...], gain_seq[0], 0)
    seq_first.start()
    tp_second.finish(second_out)
    for each in sums[: count // 2]:
        each.finish()
    seq_first.finish(first_tp[0])
    tp_first.start()
    for each in sums[count // 2 :]:
        each.finish()
    tp_first.finish(first_out)

    for each in sums + [seq_small, seq_first, tp_second, tp_first]:
        each.drain()

    @pl.loop(0, rounds)
    def _(j):
        scatter.drain(j)


def last(size, groups, rounds, backs, weights, x, back, gain, second, small, grads):
    rows, d = x.shape
    m = rows // rounds
    c = weights[0].shape[1]
    shape = (size, rounds, m)
    lines = d // WIDTH
    sems = DMA((2, rounds, size))
    spec = pl.BlockSpec(memory_space=VM)
    small_rows = lines + small.shape[0]
    outs = pl.pallas_call(
        partial(last_kernel, size, groups, rounds, len(grads)),
        out_shape=[
            jax.ShapeDtypeStruct((rounds, m, d), f32),
            jax.ShapeDtypeStruct((lines, WIDTH), f32),
            jax.ShapeDtypeStruct((lines, WIDTH), f32),
            jax.ShapeDtypeStruct((small_rows, WIDTH), f32),
        ]
        + [jax.ShapeDtypeStruct(grad.shape[1:], f32) for grad in grads],
        in_specs=[spec] * 13 + [pl.BlockSpec(memory_space=pl.ANY)] * len(grads),
        out_specs=[spec] * (4 + len(grads)),
        scratch_shapes=[
            VM((rounds, size, m, d), bf16),
            VM((2, rounds, size, m, d), bf16),
            VM((m, d), f32),
            VM((1, d), f32),
            sems,
            sems,
        ]
        + everyone_scratch(groups, small_rows)
        + everyone_scratch(groups, lines)
        + everyone_scratch(size, lines)
        + everyone_scratch(size, lines)
        + group_sums_scratch(grads),
        compiler_params=pltpu.CompilerParams(collective_id=4, has_side_effects=True, vmem_limit_bytes=63 * MIB),
        cost_estimate=pl.CostEstimate(flops=8 * size * rows * d * c, bytes_accessed=56 * MIB, transcendentals=0),
        name="last",
    )(
        *[part.reshape(shape + (c,)) for part in backs],
        *weights,
        x.reshape(rounds, m, d),
        back.reshape(rounds, m, d),
        gain.reshape(1, d),
        second,
        small,
        *[in_pairs(grad) for grad in grads],
    )
    return (outs[0].reshape(rows, d), outs[1], outs[2], outs[3][lines:]) + tuple(outs[4:])


def per_device(
    size,
    groups,
    tokens,
    lengths,
    cotangent,
    first_gain,
    query_weight,
    forget_weight,
    input_weight,
    swish_weight,
    bound_logit,
    group_gain,
    out_weight,
    second_gain,
    gate_weight,
    up_weight,
    down_weight,
):
    weights = (query_weight, forget_weight, input_weight, swish_weight)
    ends = jnp.cumsum(lengths).astype(jnp.int32)
    bound, head_gain = bound_logit.reshape(1, -1), group_gain.reshape(1, -1)
    a, q, f, i, s = project(size, ROUNDS, tokens, first_gain, *weights)
    cot_own, q = lax.optimization_barrier((cotangent, q))
    cot = lax.all_gather(cot_own, "tp", axis=0, tiled=True)
    o, u, starts = scan_forward(groups, ends, q, f, i, s, bound, head_gain)
    residual, back, b, e, ub, second, hidden, gates, ups = middle(
        size, ROUNDS, u, tokens, cot, second_gain, out_weight, gate_weight, up_weight, down_weight
    )
    hidden_2, ub = lax.optimization_barrier((hidden, ub))
    down = jnp.dot(hidden_2, down_weight, preferred_element_type=f32).astype(bf16)
    down = lax.psum_scatter(down, "tp", scatter_dimension=0, tiled=True)
    output = (residual + down.astype(f32)).astype(bf16)
    total, d = b.shape

    def by_rows(left, right):
        grad = lax.dot_general(left, right, TN, preferred_element_type=f32).astype(bf16)
        return grad.reshape(groups, grad.shape[0] // groups, grad.shape[1])

    narrow = d // groups < WIDTH

    def by_cols(left, right):
        if narrow:
            return by_rows(right, left)
        right = right.reshape(total, groups, right.shape[1] // groups)
        return jnp.einsum("tf,tnc->nfc", left, right, preferred_element_type=f32).astype(bf16)

    glu = [by_rows(b, gates), by_rows(b, ups)]
    dq, df, di, ds, small, gate_grad, up_grad = scan_backward(
        groups, ends, q, f, i, s, bound, head_gain, o, starts, ub, glu
    )
    others = [by_cols(hidden, cot), by_cols(u, e)]
    mix = [by_rows(a, part) for part in (dq, df, di, ds)]
    tokens_grad, second_sum, first_sum, small_sum, *sums = last(
        size, groups, ROUNDS, (dq, df, di, ds), weights, tokens, back, first_gain, second, small, others + mix
    )
    heads = bound_logit.shape[0]
    here = lax.axis_index("seq")
    place = here * size + lax.axis_index("tp")
    each = d // (groups * size)
    wide = WIDTH // groups
    first_grad = lax.dynamic_slice_in_dim(first_sum.reshape(-1), place * each, each)
    second_grad = lax.dynamic_slice_in_dim(second_sum.reshape(-1), place * each, each)
    bound_grad = lax.dynamic_slice_in_dim(small_sum[:heads], here * wide, wide, axis=1)
    head_grad = lax.dynamic_slice_in_dim(small_sum[heads:], here * wide, wide, axis=1)
    down_grad, out_grad, query_grad, forget_grad, input_grad, swish_grad = sums
    if narrow:
        down_grad, out_grad = down_grad.T, out_grad.T
    return (
        output,
        tokens_grad,
        first_grad,
        query_grad,
        forget_grad,
        input_grad,
        swish_grad,
        bound_grad,
        head_grad,
        out_grad,
        second_grad,
        gate_grad,
        up_grad,
        down_grad,
    )


def solution(mesh):
    rows, both, cols, lines = P(("seq", "tp"), None), P(("seq", "tp")), P(None, "tp"), P("tp", None)
    in_specs = (rows, P(), rows, P(), cols, cols, cols, cols, lines, lines, lines, P(), cols, cols, lines)
    down, across = P("seq", "tp"), P("tp", "seq")
    out_specs = (rows, rows, both, down, down, down, down, across, across, across, both, down, down, across)
    return jax.shard_map(
        partial(per_device, mesh.shape["tp"], mesh.shape["seq"]),
        mesh=mesh,
        in_specs=in_specs,
        out_specs=out_specs,
        check_vma=False,
    )
```

```python
from functools import partial

import jax
import jax.numpy as jnp
from jax import lax
from jax.experimental import pallas as pl
from jax.experimental.pallas import tpu as pltpu
from jax.sharding import PartitionSpec as P

WIDTH = 128
ROUNDS = 4
MIB = 1 << 20
epsilon = 1e-05

f32 = jnp.float32
bf16 = jnp.bfloat16
NN = (((1,), (0,)), ((), ()))
NT = (((1,), (1,)), ((), ()))
TN = (((0,), (0,)), ((), ()))
VM = pltpu.VMEM
DMA = pltpu.SemaphoreType.DMA
MESH = pl.DeviceIdType.MESH


def mul(left, right, dims):
    return lax.dot_general(left, right, dims, preferred_element_type=f32)


def silu_slope(value):
    gate = jax.nn.sigmoid(value)
    return gate * (1.0 + value * (1.0 - gate))


def remote(src, dst, send, recv, axis, peer):
    return pltpu.make_async_remote_copy(
        src_ref=src,
        dst_ref=dst,
        send_sem=send,
        recv_sem=recv,
        device_id={axis: peer},
        device_id_type=MESH,
    )


def greet(peers, count):
    barrier = pltpu.get_barrier_semaphore()
    for axis, peer, wanted in peers:

        @pl.when(wanted)
        def _():
            pl.semaphore_signal(barrier, inc=1, device_id={axis: peer}, device_id_type=MESH)

    pl.semaphore_wait(barrier, count)


def line_peers(size):
    me = lax.axis_index("tp")
    peers = [("tp", lax.rem(me + 1, size), me < size - 1), ("tp", lax.rem(me + size - 1, size), me > 0)]
    return peers, jnp.where(me < size - 1, 1, 0) + jnp.where(me > 0, 1, 0)


def group_peers(size, axis):
    me = lax.axis_index(axis)
    return [(axis, lax.rem(me + k, size), True) for k in range(1, size)], size - 1


class Line:
    def __init__(self, size, send, recv):
        self.size = size
        self.me = lax.axis_index("tp")
        self.right = lax.rem(self.me + 1, size)
        self.left = lax.rem(self.me + size - 1, size)
        self.send, self.recv = send, recv

    def hop(self, way, src, dst, j, at):
        peer = self.right if way == 0 else self.left
        return remote(src, dst, self.send.at[way, j, at], self.recv.at[way, j, at], "tp", peer)


class Scatter(Line):
    def __init__(self, size, send, recv, part, land, total):
        super().__init__(size, send, recv)
        self.part, self.land, self.total = part, land, total

    def copy(self, way, j, to):
        return self.hop(way, self.part.at[j, to], self.slot(way, j, to), j, to)

    def slot(self, way, j, to):
        return self.land.at[way, j, to - 1 + way]

    def start(self, j):
        last = self.size - 1

        @pl.when(self.me == 0)
        def _():
            for to in range(last, 0, -1):
                self.copy(0, j, to).start()

        @pl.when(self.me == last)
        def _():
            for to in range(last):
                self.copy(1, j, to).start()

    def step(self, j, t):
        last = self.size - 1
        for way in (0, 1):
            place = self.me if way == 0 else last - self.me
            to = last - t + place
            to = to if way == 0 else last - to

            @pl.when((place >= 1) & (place <= t))
            def _():
                copy = self.copy(way, j, to)
                copy.wait_recv()
                self.add(self.part.at[j, to], self.slot(way, j, to))
                copy.start()

    def add(self, into, more):
        rows = into.shape[0]

        @pl.loop(0, rows // 16)
        def _(g):
            r = pl.ds(pl.multiple_of(g * 16, 16), 16)
            into[r, :] = (into[r, :].astype(f32) + more[r, :].astype(f32)).astype(bf16)

    def finish(self, j):
        me, last = self.me, self.size - 1
        rows = self.total.shape[0]

        def over(body):
            @pl.loop(0, rows // 16)
            def _(g):
                body(pl.ds(pl.multiple_of(g * 16, 16), 16))

        def first(r):
            self.total[r, :] = self.part[j, me, r, :].astype(f32)

        over(first)
        for way, there in ((0, me >= 1), (1, me < last)):

            @pl.when(there)
            def _():
                self.copy(way, j, me).wait_recv()

                def more(r):
                    self.total[r, :] = self.total[r, :] + self.land[way, j, me - 1 + way, r, :].astype(f32)

                over(more)

    def drain(self, j):
        for to in range(self.size):

            @pl.when(self.me < to)
            def _():
                self.copy(0, j, to).wait_send()

            @pl.when(self.me > to)
            def _():
                self.copy(1, j, to).wait_send()


class Gather(Line):
    def __init__(self, size, send, recv, whole):
        super().__init__(size, send, recv)
        self.whole = whole

    def copy(self, way, j, source):
        block = self.whole.at[source, j]
        return self.hop(way, block, block, j, source)

    def start(self, j):
        @pl.when(self.me < self.size - 1)
        def _():
            self.copy(0, j, self.me).start()

        @pl.when(self.me > 0)
        def _():
            self.copy(1, j, self.me).start()

    def step(self, j, t):
        last = self.size - 1

        @pl.when(self.me >= t)
        def _():
            copy = self.copy(0, j, self.me - t)
            copy.wait_recv()

            @pl.when(self.me < last)
            def _():
                copy.start()

        @pl.when(self.me + t <= last)
        def _():
            copy = self.copy(1, j, self.me + t)
            copy.wait_recv()

            @pl.when(self.me > 0)
            def _():
                copy.start()

    def drain(self, j):
        last = self.size - 1
        for source in range(self.size):

            @pl.when((self.me >= source) & (self.me < last))
            def _():
                self.copy(0, j, source).wait_send()

            @pl.when((self.me <= source) & (self.me > 0))
            def _():
                self.copy(1, j, source).wait_send()


def add_rows(into, left, right):
    rows = into.shape[0]

    @pl.loop(0, rows // 16)
    def _(g):
        r = pl.ds(pl.multiple_of(g * 16, 16), 16)
        into[r, :] = (left[r, :].astype(f32) + right[r, :].astype(f32)).astype(bf16)


class GroupSum:
    refs = 6

    def __init__(self, size, grad, out, own, got, land, *sems):
        self.half = size // 2
        here = lax.axis_index("seq")
        self.side = lax.rem(here, 2)
        self.mine = here // 2
        self.sibling = here + 1 - 2 * self.side
        self.grad, self.own, self.got, self.land, self.out = grad, own, got, land, out
        self.near_sems, *self.sems = sems
        self.loads = len(grad.shape) == 4
        self.turned = out.shape != own.shape[1:]

    @staticmethod
    def scratch(shape):
        half = shape[0]
        return [VM(shape, bf16)] * 3 + [DMA((3, half)), DMA((half,)), DMA((half,))]

    def near(self, k):
        sems = self.near_sems
        source = self.grad.at[k, 1 - self.side] if self.loads else self.grad.at[k]
        return remote(source, self.got.at[k], sems.at[0, k], sems.at[1, k], "seq", self.sibling)

    def load(self, k):
        return pltpu.make_async_copy(self.grad.at[k, self.side], self.own.at[k], self.near_sems.at[2, k])

    def start(self):
        for k in range(self.half):
            self.near(k).start()
            if self.loads:
                self.load(k).start()

    def pair(self, k, into):
        if self.loads:
            self.load(k).wait()
        self.near(k).wait_recv()
        add_rows(into, self.own.at[k], self.got.at[k])

    def far(self, k):
        send, recv = self.sems
        return remote(self.own.at[k], self.land.at[self.mine], send.at[k], recv.at[self.mine], "seq", 2 * k + self.side)

    def arrival(self, k):
        send, recv = self.sems
        return remote(self.own.at[k], self.land.at[k], send.at[k], recv.at[k], "seq", 2 * k + self.side)

    def middle(self):
        for k in range(self.half):

            @pl.when(k == self.mine)
            def _():
                self.pair(k, self.land.at[k])

            @pl.when(k != self.mine)
            def _():
                self.pair(k, self.own.at[k])
                self.far(k).start()

    def relay(self):
        pass

    def arrive(self):
        for k in range(self.half):

            @pl.when(k != self.mine)
            def _():
                self.arrival(k).wait_recv()

    def terms(self):
        return [self.land.at[k] for k in range(self.half)]

    def finish(self):
        self.arrive()
        rows, cols = self.own.shape[1:]

        def total(r, c):
            acc = None
            for term in self.terms():
                part = term[r, c].astype(f32)
                acc = part if acc is None else acc + part
            return acc

        if self.turned:

            @pl.loop(0, cols // WIDTH)
            def _(g):
                c = pl.ds(pl.multiple_of(g * WIDTH, WIDTH), WIDTH)
                self.out[c, :] = total(slice(None), c).T

        else:

            @pl.loop(0, rows // 16)
            def _(g):
                r = pl.ds(pl.multiple_of(g * 16, 16), 16)
                self.out[r, :] = total(r, slice(None))

    def drain(self):
        for k in range(self.half):
            self.near(k).wait_send()
        self.drain_far()

    def drain_far(self):
        for k in range(self.half):

            @pl.when(k != self.mine)
            def _():
                self.far(k).wait_send()


class SquareSum(GroupSum):
    refs = 6

    def __init__(self, *args):
        super().__init__(*args)
        self.hop, self.far_sems = self.sems
        x, y = lax.rem(self.mine, 2), self.mine // 2
        self.beside = (2 * y + 1 - x, 2 * (1 - y) + x)
        self.opposite = 2 * (1 - y) + 1 - x
        rows = self.own.shape[1] // 2
        self.halves = (pl.ds(0, rows), pl.ds(rows, rows))

    @staticmethod
    def scratch(shape):
        half, rows, cols = shape
        return [
            VM(shape, bf16),
            VM(shape, bf16),
            VM((2, rows, cols), bf16),
            DMA((3, half)),
            VM((2, rows // 2, cols), bf16),
            DMA((2, 6)),
        ]

    def over(self, way, at, source, target):
        sems = self.far_sems
        return remote(source, target, sems.at[0, at], sems.at[1, at], "seq", 2 * self.beside[way] + self.side)

    def pass_on(self, way):
        return self.over(way, way, self.own.at[self.opposite, self.halves[way]], self.hop.at[way])

    def deliver(self, way, half):
        source = self.own.at[self.beside[way], self.halves[half]]
        return self.over(way, 2 + 2 * way + half, source, self.land.at[way, self.halves[half]])

    def middle(self):
        self.pair(self.opposite, self.own.at[self.opposite])
        for way in (0, 1):
            self.pass_on(way).start()
        for way in (0, 1):
            self.pair(self.beside[way], self.own.at[self.beside[way]])
            self.deliver(way, way).start()
        self.pair(self.mine, self.own.at[self.mine])

    def relay(self):
        for way in (0, 1):
            self.pass_on(way).wait_recv()
            into = self.own.at[self.beside[1 - way], self.halves[way]]
            add_rows(into, into, self.hop.at[way])
            self.deliver(1 - way, way).start()

    def arrive(self):
        for way in (0, 1):
            for half in (0, 1):
                self.deliver(way, half).wait_recv()

    def terms(self):
        return [self.own.at[self.mine], self.land.at[0], self.land.at[1]]

    def drain_far(self):
        for way in (0, 1):
            self.pass_on(way).wait_send()
            for half in (0, 1):
                self.deliver(way, half).wait_send()


def summer(size):
    return SquareSum if size == 8 else GroupSum


def group_sums(size, grads, outs, take):
    kind = summer(size)
    return [kind(size, grad, out, *take(kind.refs)) for grad, out in zip(grads, outs)]


def group_sums_scratch(shapes):
    scratch = []
    for size, rows, cols in shapes:
        scratch += summer(size).scratch((size // 2, rows, cols))
    return scratch


def sum_shapes(shapes, turned):
    shapes = [shape[:0:-1] if turn else shape[1:] for shape, turn in zip(shapes, turned)]
    return [jax.ShapeDtypeStruct(shape, f32) for shape in shapes]


def in_pairs(grad):
    return grad.reshape((grad.shape[0] // 2, 2) + grad.shape[1:])


def taker(refs):
    refs = list(refs)

    def take(count):
        taken, refs[:count] = refs[:count], []
        return taken

    return take


def project_kernel(size, rounds, x_ref, gain_ref, wq, wf, wi, ws, a_ref, q_ref, f_ref, i_ref, s_ref, send, recv):
    greet(*line_peers(size))
    line = Gather(size, send, recv, a_ref)
    gain = gain_ref[...]
    m, d = x_ref.shape[1:]

    @pl.loop(0, rounds)
    def _(j):
        @pl.loop(0, m // 16)
        def _(g):
            r = pl.ds(pl.multiple_of(g * 16, 16), 16)
            x = x_ref[j, r, :].astype(f32)
            scale = lax.rsqrt(jnp.mean(x * x, axis=-1, keepdims=True) + epsilon)
            a_ref[line.me, j, r, :] = (x * scale * gain).astype(bf16)

        line.start(j)

    def products(j):
        rows = a_ref[:, j].reshape(size * m, d)
        for weight, out in ((wq, q_ref), (wf, f_ref), (wi, i_ref), (ws, s_ref)):
            out[:, j] = mul(rows, weight[...], NN).reshape(size, m, weight.shape[1])

    @pl.loop(0, rounds)
    def _(j):
        for t in range(1, size):
            line.step(j, t)
        products(j)

    @pl.loop(0, rounds)
    def _(j):
        line.drain(j)


def project(size, rounds, tokens, first_gain, wq, wf, wi, ws):
    rows, d = tokens.shape
    m = rows // rounds
    c = wq.shape[1]
    shape = (size, rounds, m)
    out = pl.pallas_call(
        partial(project_kernel, size, rounds),
        out_shape=[jax.ShapeDtypeStruct(shape + (d,), bf16)] + [jax.ShapeDtypeStruct(shape + (c,), f32)] * 4,
        in_specs=[pl.BlockSpec(memory_space=VM)] * 6,
        out_specs=[pl.BlockSpec(memory_space=VM)] * 5,
        scratch_shapes=[DMA((2, rounds, size)), DMA((2, rounds, size))],
        compiler_params=pltpu.CompilerParams(collective_id=0, has_side_effects=True, vmem_limit_bytes=48 * MIB),
        cost_estimate=pl.CostEstimate(flops=8 * size * rows * d * c, bytes_accessed=32 * MIB, transcendentals=0),
        name="project",
    )(tokens.reshape(rounds, m, d), first_gain.reshape(1, d), wq, wf, wi, ws)
    total = size * rows
    return [out[0].reshape(total, d)] + [part.reshape(total, c) for part in out[1:]]


def document(rows, ends_ref):
    total = jnp.where(rows >= ends_ref[0], 1, 0)
    for k in range(1, ends_ref.shape[0]):
        total = total + jnp.where(rows >= ends_ref[k], 1, 0)
    return total


def block_masks(first, ends_ref):
    shape = (WIDTH, WIDTH)
    down = lax.broadcasted_iota(jnp.int32, shape, 0)
    along = lax.broadcasted_iota(jnp.int32, shape, 1)
    docs = document(first + down, ends_ref)
    same = (docs == document(first + along, ends_ref)) & (down >= along)
    before = jnp.where(first > 0, document(first - 1, ends_ref), -1)
    final = document(first + WIDTH - 1, ends_ref)
    carry = jnp.where(docs == before, 1.0, 0.0)
    tail = jnp.where(docs == final, 1.0, 0.0)
    keep = jnp.where(final == before, 1.0, 0.0)
    return same, carry, tail, keep


def running(log_forget):
    shape = (WIDTH, WIDTH)
    lower = lax.broadcasted_iota(jnp.int32, shape, 0) >= lax.broadcasted_iota(jnp.int32, shape, 1)
    ones = jnp.where(lower, 1.0, 0.0).astype(bf16)
    high = log_forget.astype(bf16)
    low = (log_forget - high.astype(f32)).astype(bf16)
    return mul(ones, high, NN) + mul(ones, low, NN)


def decay_parts(forget_pre, bound):
    away = jax.nn.sigmoid(-forget_pre)
    key = jax.nn.sigmoid(-bound) * away
    return key, running(jnp.log(1.0 - key)), away


class States:
    def __init__(self, size, out_state, out_decay, land_state, land_decay, sems):
        self.size = size
        self.here = lax.axis_index("seq")
        self.out_state, self.out_decay = out_state, out_decay
        self.land_state, self.land_decay = land_state, land_decay
        self.sems = sems

    def pair(self, slot, peer):
        s = self.sems
        return (
            remote(self.out_state, self.land_state.at[slot], s.at[0, peer], s.at[1, slot], "seq", peer),
            remote(self.out_decay, self.land_decay.at[slot], s.at[2, peer], s.at[3, slot], "seq", peer),
        )

    def sends(self, later):
        for k in range(self.size):
            yield k, (self.here < k if later else self.here > k)

    def start(self, later):
        for k, wanted in self.sends(later):

            @pl.when(wanted)
            def _():
                for copy in self.pair(self.here, k):
                    copy.start()

    def compose(self, later, state):
        state[...] = jnp.zeros_like(state)
        order = range(self.size) if later else range(self.size - 1, -1, -1)
        for k in order:

            @pl.when(self.here > k if later else self.here < k)
            def _():
                for copy in self.pair(k, k):
                    copy.wait_recv()
                for h in range(state.shape[0]):
                    decay = self.land_decay[k, h : h + 1, :]
                    state[h] = decay * state[h] + self.land_state[k, h].astype(f32)

    def drain(self, later):
        for k, wanted in self.sends(later):

            @pl.when(wanted)
            def _():
                for copy in self.pair(self.here, k):
                    copy.wait_send()


def states_scratch(size, heads):
    return [
        VM((heads, WIDTH, WIDTH), f32),
        VM((heads, WIDTH, WIDTH), bf16),
        VM((8, WIDTH), f32),
        VM((size, heads, WIDTH, WIDTH), bf16),
        VM((size, 8, WIDTH), f32),
        DMA((4, size)),
    ]


def scan_kernel(
    size,
    ends_ref,
    q_ref,
    f_ref,
    i_ref,
    s_ref,
    bound_ref,
    gain_ref,
    o_ref,
    u_ref,
    starts_ref,
    qd_ref,
    kd_ref,
    qe_ref,
    adds,
    decays,
    state,
    out_state,
    out_decay,
    land_state,
    land_decay,
    sems,
):
    greet(*group_peers(size, "seq"))
    rows, c = q_ref.shape
    blocks, heads = rows // WIDTH, c // WIDTH
    base = lax.axis_index("seq") * rows
    states = States(size, out_state, out_decay, land_state, land_decay, sems)
    state[...] = jnp.zeros_like(state)
    out_decay[...] = jnp.ones_like(out_decay)

    @pl.loop(0, blocks)
    def _(b):
        r = pl.ds(pl.multiple_of(b * WIDTH, WIDTH), WIDTH)
        same, carry, tail, keep = block_masks(base + b * WIDTH, ends_ref)
        for h in range(heads):
            cols = slice(h * WIDTH, (h + 1) * WIDTH)
            q = q_ref[r, cols]
            q = q * jax.nn.sigmoid(q)
            key, run, _ = decay_parts(f_ref[r, cols], bound_ref[:, cols])
            middle, last = run[WIDTH // 2 - 1 : WIDTH // 2, :], run[WIDTH - 1 :, :]
            qd_ref[r, cols] = (q * jnp.exp(run - middle)).astype(bf16)
            kd_ref[r, cols] = (key * jnp.exp(middle - run)).astype(bf16)
            qe_ref[r, cols] = (q * jnp.exp(run) * carry).astype(bf16)
            key_tail = (key * jnp.exp(last - run) * tail).astype(bf16)
            add = mul(i_ref[r, cols].astype(bf16), key_tail, TN)
            decay = jnp.exp(last) * keep
            adds[b, h] = add
            decays[b, h : h + 1, :] = decay
            state[h] = decay * state[h] + add
            out_decay[h : h + 1, :] = out_decay[h : h + 1, :] * decay

    out_state[...] = state[...].astype(bf16)
    states.start(True)

    @pl.loop(0, blocks)
    def _(b):
        r = pl.ds(pl.multiple_of(b * WIDTH, WIDTH), WIDTH)
        same, carry, tail, keep = block_masks(base + b * WIDTH, ends_ref)
        for h in range(heads):
            cols = slice(h * WIDTH, (h + 1) * WIDTH)
            scores = jnp.where(same, mul(qd_ref[r, cols], kd_ref[r, cols], NT), 0.0).astype(bf16)
            o_ref[r, cols] = mul(scores, i_ref[r, cols].astype(bf16), NN)

    states.compose(True, state)

    @pl.loop(0, blocks)
    def _(b):
        r = pl.ds(pl.multiple_of(b * WIDTH, WIDTH), WIDTH)
        places = base + b * WIDTH + lax.broadcasted_iota(jnp.int32, (WIDTH, WIDTH), 0)
        valid = jnp.where(places < ends_ref[ends_ref.shape[0] - 1], 1.0, 0.0)
        for h in range(heads):
            cols = slice(h * WIDTH, (h + 1) * WIDTH)
            low = state[h].astype(bf16)
            starts_ref[b, h] = low
            o = o_ref[r, cols] + mul(qe_ref[r, cols], low, NT)
            o_ref[r, cols] = o
            state[h] = decays[b, h : h + 1, :] * state[h] + adds[b, h]
            scale = lax.rsqrt(jnp.mean(o * o, axis=-1, keepdims=True) + epsilon)
            s = s_ref[r, cols]
            z = s * jax.nn.sigmoid(s) * valid
            u_ref[r, cols] = (o * scale * gain_ref[:, cols] * z).astype(bf16)

    states.drain(True)


def scan_forward(size, ends, q, f, i, s, bound, gain):
    rows, c = q.shape
    blocks, heads = rows // WIDTH, c // WIDTH
    low = VM((rows, c), bf16)
    return pl.pallas_call(
        partial(scan_kernel, size),
        out_shape=[
            jax.ShapeDtypeStruct((rows, c), f32),
            jax.ShapeDtypeStruct((rows, c), bf16),
            jax.ShapeDtypeStruct((blocks, heads, WIDTH, WIDTH), bf16),
        ],
        in_specs=[pl.BlockSpec(memory_space=pltpu.SMEM)] + [pl.BlockSpec(memory_space=VM)] * 6,
        out_specs=[pl.BlockSpec(memory_space=VM)] * 3,
        scratch_shapes=[
            low,
            low,
            low,
            VM((blocks, heads, WIDTH, WIDTH), f32),
            VM((blocks, 8, WIDTH), f32),
        ]
        + states_scratch(size, heads),
        compiler_params=pltpu.CompilerParams(collective_id=1, has_side_effects=True, vmem_limit_bytes=48 * MIB),
        cost_estimate=pl.CostEstimate(flops=20 * rows * c * WIDTH, bytes_accessed=14 * MIB, transcendentals=8 * rows * c),
        name="scan_forward",
    )(ends, q, f, i, s, bound, gain)


def scan_back_kernel(size, count, *refs):
    take = taker(refs)
    ends_ref, q_ref, f_ref, i_ref, s_ref, bound_ref, gain_ref, o_ref, starts_ref, ub_ref = take(10)
    grads = take(count)
    dq_ref, df_ref, di_ref, ds_ref, small_ref = take(5)
    grad_outs = take(count)
    qd_ref, kd_ref, qe_ref, kt_ref, do_ref, run_ref, adds, decays = take(8)
    state, out_state, out_decay, land_state, land_decay, sems = take(6)
    sums = group_sums(size, grads, grad_outs, take)
    greet(*group_peers(size, "seq"))
    rows, c = q_ref.shape
    blocks, heads = rows // WIDTH, c // WIDTH
    base = lax.axis_index("seq") * rows
    states = States(size, out_state, out_decay, land_state, land_decay, sems)
    for each in sums:
        each.start()
    state[...] = jnp.zeros_like(state)
    out_decay[...] = jnp.ones_like(out_decay)
    small_ref[...] = jnp.zeros_like(small_ref)

    @pl.loop(0, blocks)
    def _(back):
        for order, each in enumerate(sums):

            @pl.when(back == min(order + 1, blocks - 1))
            def _():
                each.middle()

            @pl.when(back == blocks - 1)
            def _():
                each.relay()

        b = blocks - 1 - back
        r = pl.ds(pl.multiple_of(b * WIDTH, WIDTH), WIDTH)
        same, carry, tail, keep = block_masks(base + b * WIDTH, ends_ref)
        places = base + b * WIDTH + lax.broadcasted_iota(jnp.int32, (WIDTH, WIDTH), 0)
        valid = jnp.where(places < ends_ref[ends_ref.shape[0] - 1], 1.0, 0.0)
        for h in range(heads):
            cols = slice(h * WIDTH, (h + 1) * WIDTH)
            o, s, ub, gain = o_ref[r, cols], s_ref[r, cols], ub_ref[r, cols], gain_ref[:, cols]
            scale = lax.rsqrt(jnp.mean(o * o, axis=-1, keepdims=True) + epsilon)
            normed = o * scale
            gate = jax.nn.sigmoid(s)
            uz = ub * (s * gate * valid)
            small_ref[heads + h : heads + h + 1, :] += jnp.sum(uz * normed, axis=0, keepdims=True)
            nb = uz * gain
            ds_ref[r, cols] = (ub * normed * gain * valid * (gate * (1.0 + s * (1.0 - gate)))).astype(bf16)
            do = (scale * (nb - normed * jnp.mean(nb * normed, axis=-1, keepdims=True))).astype(bf16)
            do_ref[r, cols] = do
            q = q_ref[r, cols]
            q = q * jax.nn.sigmoid(q)
            key, run, _ = decay_parts(f_ref[r, cols], bound_ref[:, cols])
            middle, last = run[WIDTH // 2 - 1 : WIDTH // 2, :], run[WIDTH - 1 :, :]
            run_ref[r, cols] = run
            qd_ref[r, cols] = (q * jnp.exp(run - middle)).astype(bf16)
            kd_ref[r, cols] = (key * jnp.exp(middle - run)).astype(bf16)
            kt_ref[r, cols] = (key * jnp.exp(last - run) * tail).astype(bf16)
            qe = (q * jnp.exp(run) * carry).astype(bf16)
            qe_ref[r, cols] = qe
            add = mul(do, qe, TN)
            decay = jnp.exp(last) * keep
            adds[b, h] = add
            decays[b, h : h + 1, :] = decay
            state[h] = decay * state[h] + add
            out_decay[h : h + 1, :] = out_decay[h : h + 1, :] * decay

    out_state[...] = state[...].astype(bf16)
    states.start(False)

    states.compose(False, state)

    @pl.loop(0, blocks)
    def _(back):
        b = blocks - 1 - back
        r = pl.ds(pl.multiple_of(b * WIDTH, WIDTH), WIDTH)
        same, carry, tail, keep = block_masks(base + b * WIDTH, ends_ref)
        shape = (WIDTH, WIDTH)
        down, along = lax.broadcasted_iota(jnp.int32, shape, 0), lax.broadcasted_iota(jnp.int32, shape, 1)
        from_here = jnp.where(along >= down, 1.0, 0.0).astype(bf16)
        ahead = jnp.where(along < down, 1.0, 0.0).astype(bf16)
        for h in range(heads):
            cols = slice(h * WIDTH, (h + 1) * WIDTH)
            do, v = do_ref[r, cols], i_ref[r, cols].astype(bf16)
            low, start = state[h].astype(bf16), starts_ref[b, h]
            dq_state = mul(do, start, NN)
            dk_state = mul(v, low, NN)
            kt = kt_ref[r, cols]
            qd, kd = qd_ref[r, cols], kd_ref[r, cols]
            scores = jnp.where(same, mul(qd, kd, NT), 0.0).astype(bf16)
            slopes = jnp.where(same, mul(do, v, NT), 0.0).astype(bf16)
            dq_near = mul(slopes, kd, NN)
            dk_near = mul(slopes, qd, TN)
            di_ref[r, cols] = (mul(scores, do, TN) + mul(kt, low, NT)).astype(bf16)
            run = run_ref[r, cols]
            middle, last = run[WIDTH // 2 - 1 : WIDTH // 2, :], run[WIDTH - 1 :, :]
            q_back = dq_near * jnp.exp(run - middle) + dq_state * (jnp.exp(run) * carry)
            k_back = dk_near * jnp.exp(middle - run) + dk_state * (jnp.exp(last - run) * tail)
            later = (
                qe_ref[r, cols].astype(f32) * dq_state
                + qd.astype(f32) * dq_near
                - kd.astype(f32) * dk_near
            )
            earlier = kt.astype(f32) * dk_state
            decay = decays[b, h : h + 1, :]
            log_back = decay * jnp.sum(low.astype(f32) * start.astype(f32), axis=0, keepdims=True)
            for ones, part in ((from_here, later), (ahead, earlier)):
                high = part.astype(bf16)
                log_back = log_back + mul(ones, high, NN)
                log_back = log_back + mul(ones, (part - high.astype(f32)).astype(bf16), NN)
            f_pre = f_ref[r, cols]
            away, near = jax.nn.sigmoid(-f_pre), jax.nn.sigmoid(f_pre)
            upper = jax.nn.sigmoid(-bound_ref[:, cols])
            lower = jax.nn.sigmoid(bound_ref[:, cols])
            forget_back = log_back / (1.0 - upper * away) - k_back
            slope = forget_back * away * upper
            df_ref[r, cols] = (slope * near).astype(bf16)
            small_ref[h : h + 1, :] += jnp.sum(slope, axis=0, keepdims=True) * lower
            dq_ref[r, cols] = (q_back * silu_slope(q_ref[r, cols])).astype(bf16)
            state[h] = adds[b, h] + decay * state[h]

    for each in sums:
        each.finish()
    states.drain(False)
    for each in sums:
        each.drain()


def scan_backward(size, ends, q, f, i, s, bound, gain, o, starts, ub, grads):
    rows, c = q.shape
    blocks, heads = rows // WIDTH, c // WIDTH
    low, wide = VM((rows, c), bf16), VM((rows, c), f32)
    spec = pl.BlockSpec(memory_space=VM)
    return pl.pallas_call(
        partial(scan_back_kernel, size, len(grads)),
        out_shape=[jax.ShapeDtypeStruct((rows, c), bf16)] * 4
        + [jax.ShapeDtypeStruct((2 * heads, WIDTH), f32)]
        + sum_shapes([grad.shape for grad in grads], [False] * len(grads)),
        in_specs=[pl.BlockSpec(memory_space=pltpu.SMEM)]
        + [spec] * 9
        + [pl.BlockSpec(memory_space=pl.ANY)] * len(grads),
        out_specs=[spec] * (5 + len(grads)),
        scratch_shapes=[low] * 5
        + [wide, VM((blocks, heads, WIDTH, WIDTH), f32), VM((blocks, 8, WIDTH), f32)]
        + states_scratch(size, heads)
        + group_sums_scratch([grad.shape for grad in grads]),
        compiler_params=pltpu.CompilerParams(collective_id=2, has_side_effects=True, vmem_limit_bytes=60 * MIB),
        cost_estimate=pl.CostEstimate(flops=40 * rows * c * WIDTH, bytes_accessed=20 * MIB, transcendentals=16 * rows * c),
        name="scan_backward",
    )(ends, q, f, i, s, bound, gain, o, starts, ub, *[in_pairs(grad) for grad in grads])


def middle_kernel(size, rounds, *refs):
    take = taker(refs)
    u_ref, x_ref, gain_ref, out_w, *loaded = take(8)
    res_out, back_out, e_out, ub_out, second_ref, down_out, *grad_outs = take(9)
    gate_w, up_w, down_w, cot_ref = weights = take(4)
    b_ref, e_ref, res_ref, back_ref, ub_ref, part, land, total = take(8)
    wide = take(3)
    down_ref, *tiles = take(4)
    load_sems, res_sems, back_sems, e_sems, ub_sem, down_sem, tile_sems = take(7)
    lines = [take(2) for _ in range(4)]
    hidden, gate_back, up_back = wide
    me = lax.axis_index("tp")
    m, d = x_ref.shape[1:]
    ff = gate_w.shape[1]
    group = size * m
    scatter = Scatter(size, *lines[0], part, land, total)
    gather = Gather(size, *lines[1], b_ref)
    scatter_back = Scatter(size, *lines[2], part, land, total)
    gather_back = Gather(size, *lines[3], e_ref)
    gain = gain_ref[...]
    tile = min(512, d)
    local = pltpu.make_async_copy
    loads = [local(src, dst, load_sems.at[k]) for k, (src, dst) in enumerate(zip(loaded, weights))]
    for load in loads:
        load.start()
    second_ref[...] = jnp.zeros_like(second_ref)
    greet(*line_peers(size))

    def project_out(j):
        rows = u_ref[:, j].reshape(group, u_ref.shape[3])

        @pl.loop(0, d // tile)
        def _(n):
            cols = pl.ds(pl.multiple_of(n * tile, tile), tile)
            part[j, :, :, cols] = mul(rows, out_w[:, cols], NN).astype(bf16).reshape(size, m, tile)

        scatter.start(j)

    def res_copy(j):
        return local(res_ref.at[j], res_out.at[j], res_sems.at[j])

    def back_copy(j):
        return local(back_ref.at[j], back_out.at[j], back_sems.at[j])

    def e_copy(j):
        return local(e_ref.at[:, j], e_out.at[:, j], e_sems.at[j])

    def ub_copy(j):
        return local(ub_ref, ub_out.at[:, j], ub_sem.at[0])

    def down_copy(j):
        return local(down_ref, down_out.at[:, j], down_sem.at[0])

    def norm(j):
        @pl.loop(0, m // 16)
        def _(g):
            r = pl.ds(pl.multiple_of(g * 16, 16), 16)
            residual = x_ref[j, r, :].astype(f32) + total[r, :]
            res_ref[j, r, :] = residual
            scale = lax.rsqrt(jnp.mean(residual * residual, axis=-1, keepdims=True) + epsilon)
            b_ref[me, j, r, :] = (residual * scale * gain).astype(bf16)

        gather.start(j)
        res_copy(j).start()

    def feed(j):
        @pl.when(j == 0)
        def _():
            for load in loads:
                load.wait()

        rows = b_ref[:, j].reshape(group, d)
        cot = cot_ref[:, j].reshape(group, d)
        step = 256
        for low in range(0, ff, step):
            cols = slice(low, min(low + step, ff))
            width = cols.stop - cols.start
            gate = mul(rows, gate_w[:, cols], NN)
            up = mul(rows, up_w[:, cols], NN)
            hb = mul(cot, down_w[cols, :], NT)
            sig = jax.nn.sigmoid(gate)
            act = gate * sig
            shape = (size, m, width)
            hidden[:, j, :, cols] = (act * up).astype(bf16).reshape(shape)
            up_back[:, j, :, cols] = (hb * act).astype(bf16).reshape(shape)
            gate_back[:, j, :, cols] = (hb * up * (sig * (1.0 + gate * (1.0 - sig)))).astype(bf16).reshape(shape)

    def feed_back(j):
        scatter.drain(j)
        gates = gate_back[:, j].reshape(group, ff)
        ups = up_back[:, j].reshape(group, ff)

        @pl.loop(0, d // tile)
        def _(n):
            cols = pl.ds(pl.multiple_of(n * tile, tile), tile)
            sums = mul(gates, gate_w[cols, :], NT) + mul(ups, up_w[cols, :], NT)
            part[j, :, :, cols] = sums.astype(bf16).reshape(size, m, tile)

        scatter_back.start(j)

    def feed_out(j):
        @pl.when(j > 0)
        def _():
            down_copy(j - 1).wait()

        rows = hidden[:, j].reshape(group, ff)

        @pl.loop(0, d // tile)
        def _(n):
            cols = pl.ds(pl.multiple_of(n * tile, tile), tile)
            down_ref[:, :, cols] = mul(rows, down_w[:, cols], NN).astype(bf16).reshape(size, m, tile)

        down_copy(j).start()

    def norm_back(j):
        @pl.loop(0, m // 16)
        def _(g):
            r = pl.ds(pl.multiple_of(g * 16, 16), 16)
            b_back, residual = total[r, :], res_ref[j, r, :]
            scale = lax.rsqrt(jnp.mean(residual * residual, axis=-1, keepdims=True) + epsilon)
            normed = residual * scale
            second_ref[...] += jnp.sum(b_back * normed, axis=0, keepdims=True)
            inner = b_back * gain
            back = cot_ref[me, j, r, :].astype(f32) + scale * (
                inner - normed * jnp.mean(inner * normed, axis=-1, keepdims=True)
            )
            back_ref[j, r, :] = back
            e_ref[me, j, r, :] = back.astype(bf16)

        gather_back.start(j)
        back_copy(j).start()

    def unproject(j, wait):
        e_copy(j).start()

        @pl.when(wait)
        def _():
            ub_copy(j - 1).wait()

        rows = e_ref[:, j].reshape(group, d)
        ub_ref[...] = mul(rows, out_w[...], NT).reshape(size, m, out_w.shape[0])
        ub_copy(j).start()

    depth = tiles[0].shape[0]
    count = d // depth

    def tile_copies(n):
        rows = pl.ds(pl.multiple_of(n * depth, depth), depth)
        return [local(src, dst.at[rows, :], tile_sems.at[k]) for k, (src, dst) in enumerate(zip(tiles, grad_outs))]

    def weight_tiles(low, high):
        @pl.loop(low, high)
        def _(n):
            @pl.when(n > 0)
            def _():
                for copy in tile_copies(n - 1):
                    copy.wait()

            cols = pl.ds(pl.multiple_of(n * depth, depth), depth)
            for left, right, out in zip((b_ref, b_ref, cot_ref), (gate_back, up_back, hidden), tiles):
                rows = left[:, :, :, cols].reshape(rounds * group, depth)
                out[...] = mul(rows, right[...].reshape(rounds * group, ff), TN).astype(bf16)
            for copy in tile_copies(n):
                copy.start()

    final = rounds - 1

    @pl.loop(0, rounds + 2)
    def _(i):
        def stage(lag, body):
            @pl.when((i >= lag) & (i < rounds + lag))
            def _():
                body(i - lag)

        stage(0, project_out)
        for t in range(1, size):
            stage(1, lambda j: scatter.step(j, t) if t < size - 1 else scatter.finish(j))
            if t == size - 1:
                stage(1, norm)
            stage(2, lambda j: gather.step(j, t))
            stage(3, lambda j: scatter_back.step(j, t) if t < size - 1 else scatter_back.finish(j))
            if t == size - 1:
                stage(3, norm_back)
            stage(4, lambda j: gather_back.step(j, t))
        stage(2, feed)
        stage(2, feed_back)
        stage(2, feed_out)
        stage(4, lambda j: unproject(j, j > 0))

    shares = [count * k // 5 for k in range(6)]
    for t in range(1, size):
        if t < size - 1:
            scatter_back.step(final, t)
        else:
            scatter_back.finish(final)
            norm_back(final)
        gather_back.step(final - 1, t)
        if t < size - 1:
            weight_tiles(shares[t - 1], shares[t])
    unproject(final - 1, True)
    weight_tiles(shares[2], shares[3])
    for t in range(1, size):
        gather_back.step(final, t)
        if t < size - 1:
            weight_tiles(shares[t + 2], shares[t + 3])
    unproject(final, True)

    for copy in tile_copies(count - 1):
        copy.wait()
    ub_copy(final).wait()
    down_copy(final).wait()

    @pl.loop(0, rounds)
    def _(j):
        res_copy(j).wait()
        back_copy(j).wait()
        e_copy(j).wait()
        gather.drain(j)
        scatter_back.drain(j)
        gather_back.drain(j)


def middle(size, rounds, u, x, cot, gain, out_w, gate_w, up_w, down_w):
    rows, d = x.shape
    m = rows // rounds
    c, ff = out_w.shape[0], gate_w.shape[1]
    shape = (size, rounds, m)
    sems = DMA((2, rounds, size))
    spec, far = pl.BlockSpec(memory_space=VM), pl.BlockSpec(memory_space=pl.ANY)
    depth = min(256, d)
    outs = pl.pallas_call(
        partial(middle_kernel, size, rounds),
        out_shape=[
            jax.ShapeDtypeStruct((rounds, m, d), f32),
            jax.ShapeDtypeStruct((rounds, m, d), f32),
            jax.ShapeDtypeStruct(shape + (d,), bf16),
            jax.ShapeDtypeStruct(shape + (c,), f32),
            jax.ShapeDtypeStruct((1, d), f32),
            jax.ShapeDtypeStruct(shape + (d,), bf16),
        ]
        + [jax.ShapeDtypeStruct((d, ff), bf16)] * 3,
        in_specs=[spec] * 4 + [far] * 4,
        out_specs=[far] * 4 + [spec] + [far] * 4,
        scratch_shapes=[
            VM(gate_w.shape, bf16),
            VM(up_w.shape, bf16),
            VM(down_w.shape, bf16),
            VM(shape + (d,), bf16),
            VM(shape + (d,), bf16),
            VM(shape + (d,), bf16),
            VM((rounds, m, d), f32),
            VM((rounds, m, d), f32),
            VM((size, m, c), f32),
            VM((rounds, size, m, d), bf16),
            VM((2, rounds, size - 1, m, d), bf16),
            VM((m, d), f32),
        ]
        + [VM(shape + (ff,), bf16)] * 3
        + [VM((size, m, d), bf16)]
        + [VM((depth, ff), bf16)] * 3
        + [DMA((4,)), DMA((rounds,)), DMA((rounds,)), DMA((rounds,)), DMA((1,)), DMA((1,)), DMA((3,))]
        + [sems] * 8,
        compiler_params=pltpu.CompilerParams(collective_id=3, has_side_effects=True, vmem_limit_bytes=63 * MIB),
        cost_estimate=pl.CostEstimate(
            flops=2 * size * rows * d * (2 * c + 9 * ff), bytes_accessed=56 * MIB, transcendentals=size * rows * ff
        ),
        name="middle",
    )(
        u.reshape(shape + (c,)),
        x.reshape(rounds, m, d),
        gain.reshape(1, d),
        out_w,
        gate_w,
        up_w,
        down_w,
        cot.reshape(shape + (d,)),
    )
    res, back, e, ub, second, down, *grads = outs
    total = size * rows
    return (
        res.reshape(rows, d),
        back.reshape(rows, d),
        e.reshape(total, d),
        ub.reshape(total, c),
        second,
        down.reshape(total, d),
        *grads,
    )


class Everyone:
    def __init__(self, size, axis, mine, land, sems):
        self.size, self.axis = size, axis
        self.here = lax.axis_index(axis)
        self.mine, self.land, self.sems = mine, land, sems

    def copy(self, slot, peer):
        return remote(self.mine, self.land.at[slot], self.sems.at[0, peer], self.sems.at[1, slot], self.axis, peer)

    def others(self):
        for k in range(self.size):
            yield k, self.here != k

    def start(self):
        for k, other in self.others():

            @pl.when(other)
            def _():
                self.copy(self.here, k).start()

    def finish(self, out):
        out[...] = self.mine[...]
        for k, other in self.others():

            @pl.when(other)
            def _():
                self.copy(k, k).wait_recv()
                out[...] = out[...] + self.land[k]

    def drain(self):
        for k, other in self.others():

            @pl.when(other)
            def _():
                self.copy(self.here, k).wait_send()


def everyone_scratch(size, rows):
    return [VM((rows, WIDTH), f32), VM((size, rows, WIDTH), f32), DMA((2, size))]


def stack(vector, into, at):
    for k in range(vector.shape[1] // WIDTH):
        into[at + k : at + k + 1, :] = vector[:, k * WIDTH : (k + 1) * WIDTH]


def last_kernel(size, groups, rounds, count, mixed, *refs):
    take = taker(refs)
    backs, weights = take(4), take(4)
    x_ref, gain_ref, second_ref, small_ref, back_in = take(5)
    a_in = take(1 if mixed else 0)
    grads = take(count)
    tokens_out, second_out, first_out, small_out = take(4)
    grad_outs = take(count + (4 if mixed else 0))
    part, land, total, first, s_send, s_recv = take(6)
    small_seq, gain_seq, second_tp, first_tp = (take(3) for _ in range(4))
    nears, a_refs = take(4 if mixed else 0), take(1 if mixed else 0)
    load_sems = take(1)[0]
    sums = group_sums(groups, grads + nears, grad_outs, take)
    early, late = sums[:2], sums[2:]

    seq, seq_count = group_peers(groups, "seq")
    tp, tp_count = group_peers(size, "tp")
    greet(seq + tp, seq_count + tp_count)

    for each in sums[:count]:
        each.start()
    loads = [
        pltpu.make_async_copy(source, target, load_sems.at[k])
        for k, (source, target) in enumerate(zip([back_in, *a_in], [tokens_out, *a_refs]))
    ]
    for load in loads:
        load.start()

    m, d = x_ref.shape[1:]
    group = size * m
    scatter = Scatter(size, s_send, s_recv, part, land, total)
    gain = gain_ref[...]
    first[...] = jnp.zeros_like(first)
    tile = min(512, d)

    seq_small = Everyone(groups, "seq", *small_seq)
    seq_first = Everyone(groups, "seq", *gain_seq)
    tp_second = Everyone(size, "tp", *second_tp)
    tp_first = Everyone(size, "tp", *first_tp)
    lines, smalls = d // WIDTH, small_ref.shape[0]
    stack(second_ref[...], small_seq[0], 0)
    small_seq[0][lines : lines + smalls, :] = small_ref[...]
    seq_small.start()

    def products(j):
        @pl.loop(0, d // tile)
        def _(n):
            cols = pl.ds(pl.multiple_of(n * tile, tile), tile)
            acc = None
            for back, weight in zip(backs, weights):
                term = mul(back[:, j].reshape(group, back.shape[3]), weight[cols, :], NT)
                acc = term if acc is None else acc + term
            part[j, :, :, cols] = acc.astype(bf16).reshape(size, m, tile)

        scatter.start(j)

    def mix(back, each):
        rows = back[...].reshape(rounds * group, back.shape[3])
        depth = each.own.shape[1]
        for side, into in ((1 - each.side, each.grad), (each.side, each.own)):

            @pl.loop(0, each.half)
            def _(k):
                cols = pl.ds(pl.multiple_of((2 * k + side) * depth, depth), depth)
                left = a_refs[0][:, :, :, cols].reshape(rounds * group, depth)
                into[k] = mul(left, rows, TN).astype(bf16)

            if into is each.grad:
                each.start()

    def norm_back(j):
        @pl.loop(0, m // 16)
        def _(g):
            r = pl.ds(pl.multiple_of(g * 16, 16), 16)
            a_back, x = total[r, :], x_ref[j, r, :].astype(f32)
            scale = lax.rsqrt(jnp.mean(x * x, axis=-1, keepdims=True) + epsilon)
            normed = x * scale
            first[...] += jnp.sum(a_back * normed, axis=0, keepdims=True)
            inner = a_back * gain
            tokens_out[j, r, :] = tokens_out[j, r, :] + scale * (
                inner - normed * jnp.mean(inner * normed, axis=-1, keepdims=True)
            )

    def steps(j, low, high):
        for t in range(low, high):
            if t < size - 1:
                scatter.step(j, t)
            else:
                scatter.finish(j)
                norm_back(j)

    for j in range(rounds):
        products(j)
        if j < len(early):
            early[j].middle()
    for load in loads:
        load.wait()
    if mixed:
        for at, (back, each) in enumerate(zip(backs, late)):
            mix(back, each)
            steps(0, 1, 2) if at == 1 else None
            steps(0, 2, 3) if at == 3 else None
    else:
        steps(0, 1, 3)
    for each in early:
        each.relay()
    for each in late:
        each.middle()
    seq_small.finish(small_out)
    second_tp[0][...] = small_out[:lines, :]
    tp_second.start()
    steps(0, 3, size)
    for j in range(1, rounds):
        steps(j, 1, size)
        if j == 1:
            for each in late[:2]:
                each.relay()
        if j == 2:
            for each in late[2:]:
                each.relay()
            early[0].finish()

    stack(first[...], gain_seq[0], 0)
    seq_first.start()
    tp_second.finish(second_out)
    for each in early[1:]:
        each.finish()
    seq_first.finish(first_tp[0])
    tp_first.start()
    for each in late:
        each.finish()
    tp_first.finish(first_out)

    for each in sums + [seq_small, seq_first, tp_second, tp_first]:
        each.drain()

    @pl.loop(0, rounds)
    def _(j):
        scatter.drain(j)


def last(size, groups, rounds, backs, weights, a, x, back, gain, second, small, grads, turned):
    rows, d = x.shape
    m = rows // rounds
    c = weights[0].shape[1]
    shape = (size, rounds, m)
    lines = d // WIDTH
    sems = DMA((2, rounds, size))
    spec = pl.BlockSpec(memory_space=VM)
    small_rows = lines + small.shape[0]
    mixed = a is not None
    shapes = [grad.shape for grad in grads] + ([(groups, d // groups, c)] * 4 if mixed else [])
    outs = pl.pallas_call(
        partial(last_kernel, size, groups, rounds, len(grads), mixed),
        out_shape=[
            jax.ShapeDtypeStruct((rounds, m, d), f32),
            jax.ShapeDtypeStruct((lines, WIDTH), f32),
            jax.ShapeDtypeStruct((lines, WIDTH), f32),
            jax.ShapeDtypeStruct((small_rows, WIDTH), f32),
        ]
        + sum_shapes(shapes, turned),
        in_specs=[spec] * 12 + [pl.BlockSpec(memory_space=pl.ANY)] * (1 + mixed + len(grads)),
        out_specs=[spec] * (4 + len(shapes)),
        scratch_shapes=[
            VM((rounds, size, m, d), bf16),
            VM((2, rounds, size - 1, m, d), bf16),
            VM((m, d), f32),
            VM((1, d), f32),
            sems,
            sems,
        ]
        + everyone_scratch(groups, small_rows)
        + everyone_scratch(groups, lines)
        + everyone_scratch(size, lines)
        + everyone_scratch(size, lines)
        + ([VM((groups // 2, d // groups, c), bf16)] * 4 + [VM(shape + (d,), bf16)] if mixed else [])
        + [DMA((2,))]
        + group_sums_scratch(shapes),
        compiler_params=pltpu.CompilerParams(collective_id=4, has_side_effects=True, vmem_limit_bytes=63 * MIB),
        cost_estimate=pl.CostEstimate(flops=16 * size * rows * d * c, bytes_accessed=56 * MIB, transcendentals=0),
        name="last",
    )(
        *[part.reshape(shape + (c,)) for part in backs],
        *weights,
        x.reshape(rounds, m, d),
        gain.reshape(1, d),
        second,
        small,
        back.reshape(rounds, m, d),
        *([a.reshape(shape + (d,))] if mixed else []),
        *[in_pairs(grad) for grad in grads],
    )
    return (outs[0].reshape(rows, d), outs[1], outs[2], outs[3][lines:]) + tuple(outs[4:])


def per_device(
    size,
    groups,
    tokens,
    lengths,
    cotangent,
    first_gain,
    query_weight,
    forget_weight,
    input_weight,
    swish_weight,
    bound_logit,
    group_gain,
    out_weight,
    second_gain,
    gate_weight,
    up_weight,
    down_weight,
):
    weights = (query_weight, forget_weight, input_weight, swish_weight)
    ends = jnp.cumsum(lengths).astype(jnp.int32)
    bound, head_gain = bound_logit.reshape(1, -1), group_gain.reshape(1, -1)
    a, q, f, i, s = project(size, ROUNDS, tokens, first_gain, *weights)
    cot_own, q = lax.optimization_barrier((cotangent, q))
    cot = lax.all_gather(cot_own, "tp", axis=0, tiled=True)
    o, u, starts = scan_forward(groups, ends, q, f, i, s, bound, head_gain)
    residual, back, e, ub, second, down, *glu = middle(
        size, ROUNDS, u, tokens, cot, second_gain, out_weight, gate_weight, up_weight, down_weight
    )
    down, ub = lax.optimization_barrier((down, ub))
    down = lax.psum_scatter(down, "tp", scatter_dimension=0, tiled=True)
    output = (residual + down.astype(f32)).astype(bf16)
    d = tokens.shape[1]

    def chunks(grad):
        return grad.reshape(groups, grad.shape[0] // groups, grad.shape[1])

    def grad_of(left, right):
        return chunks(lax.dot_general(left, right, TN, preferred_element_type=f32).astype(bf16))

    gates, ups, downs = (chunks(grad) for grad in glu)
    dq, df, di, ds, small, gate_grad, up_grad = scan_backward(
        groups, ends, q, f, i, s, bound, head_gain, o, starts, ub, [gates, ups]
    )
    back_rows = (dq, df, di, ds)
    here_too = groups == 8
    others = [downs, grad_of(e, u)] + ([] if here_too else [grad_of(a, part) for part in back_rows])
    tokens_grad, second_sum, first_sum, small_sum, *sums = last(
        size,
        groups,
        ROUNDS,
        back_rows,
        weights,
        a if here_too else None,
        tokens,
        back,
        first_gain,
        second,
        small,
        others,
        [True, True] + [False] * 4,
    )
    down_grad, out_grad, query_grad, forget_grad, input_grad, swish_grad = sums
    heads = bound_logit.shape[0]
    here = lax.axis_index("seq")
    place = here * size + lax.axis_index("tp")
    each = d // (groups * size)
    wide = WIDTH // groups
    first_grad = lax.dynamic_slice_in_dim(first_sum.reshape(-1), place * each, each)
    second_grad = lax.dynamic_slice_in_dim(second_sum.reshape(-1), place * each, each)
    bound_grad = lax.dynamic_slice_in_dim(small_sum[:heads], here * wide, wide, axis=1)
    head_grad = lax.dynamic_slice_in_dim(small_sum[heads:], here * wide, wide, axis=1)
    return (
        output,
        tokens_grad,
        first_grad,
        query_grad,
        forget_grad,
        input_grad,
        swish_grad,
        bound_grad,
        head_grad,
        out_grad,
        second_grad,
        gate_grad,
        up_grad,
        down_grad,
    )


def solution(mesh):
    rows, both, cols, lines = P(("seq", "tp"), None), P(("seq", "tp")), P(None, "tp"), P("tp", None)
    in_specs = (rows, P(), rows, P(), cols, cols, cols, cols, lines, lines, lines, P(), cols, cols, lines)
    down, across = P("seq", "tp"), P("tp", "seq")
    out_specs = (rows, rows, both, down, down, down, down, across, across, across, both, down, down, across)
    return jax.shard_map(
        partial(per_device, mesh.shape["tp"], mesh.shape["seq"]),
        mesh=mesh,
        in_specs=in_specs,
        out_specs=out_specs,
        check_vma=False,
    )
```

```python
from functools import partial

import jax
import jax.numpy as jnp
from jax import lax
from jax.experimental import pallas as pl
from jax.experimental.pallas import tpu as pltpu
from jax.sharding import PartitionSpec as P

WIDTH = 128
ROUNDS = 4
MIB = 1 << 20
epsilon = 1e-05

f32 = jnp.float32
bf16 = jnp.bfloat16
NN = (((1,), (0,)), ((), ()))
NT = (((1,), (1,)), ((), ()))
TN = (((0,), (0,)), ((), ()))
VM = pltpu.VMEM
DMA = pltpu.SemaphoreType.DMA
MESH = pl.DeviceIdType.MESH


def mul(left, right, dims):
    return lax.dot_general(left, right, dims, preferred_element_type=f32)


def silu_slope(value):
    gate = jax.nn.sigmoid(value)
    return gate * (1.0 + value * (1.0 - gate))


def remote(src, dst, send, recv, axis, peer):
    return pltpu.make_async_remote_copy(
        src_ref=src,
        dst_ref=dst,
        send_sem=send,
        recv_sem=recv,
        device_id={axis: peer},
        device_id_type=MESH,
    )


def greet(peers, count):
    barrier = pltpu.get_barrier_semaphore()
    for axis, peer, wanted in peers:

        @pl.when(wanted)
        def _():
            pl.semaphore_signal(barrier, inc=1, device_id={axis: peer}, device_id_type=MESH)

    pl.semaphore_wait(barrier, count)


def line_peers(size):
    me = lax.axis_index("tp")
    peers = [("tp", lax.rem(me + 1, size), me < size - 1), ("tp", lax.rem(me + size - 1, size), me > 0)]
    return peers, jnp.where(me < size - 1, 1, 0) + jnp.where(me > 0, 1, 0)


def group_peers(size, axis):
    me = lax.axis_index(axis)
    return [(axis, lax.rem(me + k, size), True) for k in range(1, size)], size - 1


class Line:
    def __init__(self, size, send, recv):
        self.size = size
        self.me = lax.axis_index("tp")
        self.right = lax.rem(self.me + 1, size)
        self.left = lax.rem(self.me + size - 1, size)
        self.send, self.recv = send, recv

    def hop(self, way, src, dst, j, at):
        peer = self.right if way == 0 else self.left
        return remote(src, dst, self.send.at[way, j, at], self.recv.at[way, j, at], "tp", peer)


class Scatter(Line):
    def __init__(self, size, send, recv, part, land, total):
        super().__init__(size, send, recv)
        self.part, self.land, self.total = part, land, total

    def copy(self, way, j, to):
        return self.hop(way, self.part.at[j, to], self.slot(way, j, to), j, to)

    def slot(self, way, j, to):
        return self.land.at[way, j, to - 1 + way]

    def start(self, j):
        last = self.size - 1

        @pl.when(self.me == 0)
        def _():
            for to in range(last, 0, -1):
                self.copy(0, j, to).start()

        @pl.when(self.me == last)
        def _():
            for to in range(last):
                self.copy(1, j, to).start()

    def step(self, j, t):
        last = self.size - 1
        for way in (0, 1):
            place = self.me if way == 0 else last - self.me
            to = last - t + place
            to = to if way == 0 else last - to

            @pl.when((place >= 1) & (place <= t))
            def _():
                copy = self.copy(way, j, to)
                copy.wait_recv()
                self.add(self.part.at[j, to], self.slot(way, j, to))
                copy.start()

    def add(self, into, more):
        rows = into.shape[0]

        @pl.loop(0, rows // 16)
        def _(g):
            r = pl.ds(pl.multiple_of(g * 16, 16), 16)
            into[r, :] = (into[r, :].astype(f32) + more[r, :].astype(f32)).astype(bf16)

    def finish(self, j):
        me, last = self.me, self.size - 1
        rows = self.total.shape[0]

        def over(body):
            @pl.loop(0, rows // 16)
            def _(g):
                body(pl.ds(pl.multiple_of(g * 16, 16), 16))

        def first(r):
            self.total[r, :] = self.part[j, me, r, :].astype(f32)

        over(first)
        for way, there in ((0, me >= 1), (1, me < last)):

            @pl.when(there)
            def _():
                self.copy(way, j, me).wait_recv()

                def more(r):
                    self.total[r, :] = self.total[r, :] + self.land[way, j, me - 1 + way, r, :].astype(f32)

                over(more)

    def drain(self, j):
        for to in range(self.size):

            @pl.when(self.me < to)
            def _():
                self.copy(0, j, to).wait_send()

            @pl.when(self.me > to)
            def _():
                self.copy(1, j, to).wait_send()


class Gather(Line):
    def __init__(self, size, send, recv, whole):
        super().__init__(size, send, recv)
        self.whole = whole

    def copy(self, way, j, source):
        block = self.whole.at[source, j]
        return self.hop(way, block, block, j, source)

    def start(self, j):
        @pl.when(self.me < self.size - 1)
        def _():
            self.copy(0, j, self.me).start()

        @pl.when(self.me > 0)
        def _():
            self.copy(1, j, self.me).start()

    def step(self, j, t):
        last = self.size - 1

        @pl.when(self.me >= t)
        def _():
            copy = self.copy(0, j, self.me - t)
            copy.wait_recv()

            @pl.when(self.me < last)
            def _():
                copy.start()

        @pl.when(self.me + t <= last)
        def _():
            copy = self.copy(1, j, self.me + t)
            copy.wait_recv()

            @pl.when(self.me > 0)
            def _():
                copy.start()

    def drain(self, j):
        last = self.size - 1
        for source in range(self.size):

            @pl.when((self.me >= source) & (self.me < last))
            def _():
                self.copy(0, j, source).wait_send()

            @pl.when((self.me <= source) & (self.me > 0))
            def _():
                self.copy(1, j, source).wait_send()


def add_rows(into, left, right):
    rows = into.shape[0]

    @pl.loop(0, rows // 16)
    def _(g):
        r = pl.ds(pl.multiple_of(g * 16, 16), 16)
        into[r, :] = (left[r, :].astype(f32) + right[r, :].astype(f32)).astype(bf16)


class GroupSum:
    refs = 6

    def __init__(self, size, grad, out, own, got, land, *sems):
        self.half = size // 2
        here = lax.axis_index("seq")
        self.side = lax.rem(here, 2)
        self.mine = here // 2
        self.sibling = here + 1 - 2 * self.side
        self.grad, self.own, self.got, self.land, self.out = grad, own, got, land, out
        self.near_sems, *self.sems = sems
        self.loads = len(grad.shape) == 4
        self.turned = out.shape != own.shape[1:]

    @staticmethod
    def scratch(shape):
        half = shape[0]
        return [VM(shape, bf16)] * 3 + [DMA((3, half)), DMA((half,)), DMA((half,))]

    def near(self, k):
        sems = self.near_sems
        source = self.grad.at[k, 1 - self.side] if self.loads else self.grad.at[k]
        return remote(source, self.got.at[k], sems.at[0, k], sems.at[1, k], "seq", self.sibling)

    def load(self, k):
        return pltpu.make_async_copy(self.grad.at[k, self.side], self.own.at[k], self.near_sems.at[2, k])

    def start(self):
        for k in range(self.half):
            self.near(k).start()
            if self.loads:
                self.load(k).start()

    def pair(self, k, into):
        if self.loads:
            self.load(k).wait()
        self.near(k).wait_recv()
        add_rows(into, self.own.at[k], self.got.at[k])

    def far(self, k):
        send, recv = self.sems
        return remote(self.own.at[k], self.land.at[self.mine], send.at[k], recv.at[self.mine], "seq", 2 * k + self.side)

    def arrival(self, k):
        send, recv = self.sems
        return remote(self.own.at[k], self.land.at[k], send.at[k], recv.at[k], "seq", 2 * k + self.side)

    def middle(self):
        for k in range(self.half):

            @pl.when(k == self.mine)
            def _():
                self.pair(k, self.land.at[k])

            @pl.when(k != self.mine)
            def _():
                self.pair(k, self.own.at[k])
                self.far(k).start()

    def relay(self):
        pass

    def arrive(self):
        for k in range(self.half):

            @pl.when(k != self.mine)
            def _():
                self.arrival(k).wait_recv()

    def terms(self):
        return [self.land.at[k] for k in range(self.half)]

    def finish(self):
        self.arrive()
        rows, cols = self.own.shape[1:]

        def total(r, c):
            acc = None
            for term in self.terms():
                part = term[r, c].astype(f32)
                acc = part if acc is None else acc + part
            return acc

        if self.turned:

            @pl.loop(0, cols // WIDTH)
            def _(g):
                c = pl.ds(pl.multiple_of(g * WIDTH, WIDTH), WIDTH)
                self.out[c, :] = total(slice(None), c).T

        else:

            @pl.loop(0, rows // 16)
            def _(g):
                r = pl.ds(pl.multiple_of(g * 16, 16), 16)
                self.out[r, :] = total(r, slice(None))

    def drain(self):
        for k in range(self.half):
            self.near(k).wait_send()
        self.drain_far()

    def drain_far(self):
        for k in range(self.half):

            @pl.when(k != self.mine)
            def _():
                self.far(k).wait_send()


class SquareSum(GroupSum):
    refs = 6

    def __init__(self, *args):
        super().__init__(*args)
        self.hop, self.far_sems = self.sems
        x, y = lax.rem(self.mine, 2), self.mine // 2
        self.beside = (2 * y + 1 - x, 2 * (1 - y) + x)
        self.opposite = 2 * (1 - y) + 1 - x
        rows = self.own.shape[1] // 2
        self.halves = (pl.ds(0, rows), pl.ds(rows, rows))

    @staticmethod
    def scratch(shape):
        half, rows, cols = shape
        return [
            VM(shape, bf16),
            VM(shape, bf16),
            VM((2, rows, cols), bf16),
            DMA((3, half)),
            VM((2, rows // 2, cols), bf16),
            DMA((2, 6)),
        ]

    def over(self, way, at, source, target):
        sems = self.far_sems
        return remote(source, target, sems.at[0, at], sems.at[1, at], "seq", 2 * self.beside[way] + self.side)

    def pass_on(self, way):
        return self.over(way, way, self.own.at[self.opposite, self.halves[way]], self.hop.at[way])

    def deliver(self, way, half):
        source = self.own.at[self.beside[way], self.halves[half]]
        return self.over(way, 2 + 2 * way + half, source, self.land.at[way, self.halves[half]])

    def middle(self):
        self.pair(self.opposite, self.own.at[self.opposite])
        for way in (0, 1):
            self.pass_on(way).start()
        for way in (0, 1):
            self.pair(self.beside[way], self.own.at[self.beside[way]])
            self.deliver(way, way).start()
        self.pair(self.mine, self.own.at[self.mine])

    def relay(self):
        for way in (0, 1):
            self.pass_on(way).wait_recv()
            into = self.own.at[self.beside[1 - way], self.halves[way]]
            add_rows(into, into, self.hop.at[way])
            self.deliver(1 - way, way).start()

    def arrive(self):
        for way in (0, 1):
            for half in (0, 1):
                self.deliver(way, half).wait_recv()

    def terms(self):
        return [self.own.at[self.mine], self.land.at[0], self.land.at[1]]

    def drain_far(self):
        for way in (0, 1):
            self.pass_on(way).wait_send()
            for half in (0, 1):
                self.deliver(way, half).wait_send()


def summer(size):
    return SquareSum if size == 8 else GroupSum


def group_sums(size, grads, outs, take):
    kind = summer(size)
    return [kind(size, grad, out, *take(kind.refs)) for grad, out in zip(grads, outs)]


def group_sums_scratch(shapes):
    scratch = []
    for size, rows, cols in shapes:
        scratch += summer(size).scratch((size // 2, rows, cols))
    return scratch


def sum_shapes(shapes, turned):
    shapes = [shape[:0:-1] if turn else shape[1:] for shape, turn in zip(shapes, turned)]
    return [jax.ShapeDtypeStruct(shape, f32) for shape in shapes]


def in_pairs(grad):
    return grad.reshape((grad.shape[0] // 2, 2) + grad.shape[1:])


def taker(refs):
    refs = list(refs)

    def take(count):
        taken, refs[:count] = refs[:count], []
        return taken

    return take


def document(rows, ends_ref):
    total = jnp.where(rows >= ends_ref[0], 1, 0)
    for k in range(1, ends_ref.shape[0]):
        total = total + jnp.where(rows >= ends_ref[k], 1, 0)
    return total


def block_masks(first, ends_ref):
    shape = (WIDTH, WIDTH)
    down = lax.broadcasted_iota(jnp.int32, shape, 0)
    along = lax.broadcasted_iota(jnp.int32, shape, 1)
    docs = document(first + down, ends_ref)
    same = (docs == document(first + along, ends_ref)) & (down >= along)
    before = jnp.where(first > 0, document(first - 1, ends_ref), -1)
    final = document(first + WIDTH - 1, ends_ref)
    carry = jnp.where(docs == before, 1.0, 0.0)
    tail = jnp.where(docs == final, 1.0, 0.0)
    keep = jnp.where(final == before, 1.0, 0.0)
    return same, carry, tail, keep


def running(log_forget):
    shape = (WIDTH, WIDTH)
    lower = lax.broadcasted_iota(jnp.int32, shape, 0) >= lax.broadcasted_iota(jnp.int32, shape, 1)
    ones = jnp.where(lower, 1.0, 0.0).astype(bf16)
    high = log_forget.astype(bf16)
    low = (log_forget - high.astype(f32)).astype(bf16)
    return mul(ones, high, NN) + mul(ones, low, NN)


def decay_parts(forget_pre, bound):
    away = jax.nn.sigmoid(-forget_pre)
    key = jax.nn.sigmoid(-bound) * away
    return key, running(jnp.log(1.0 - key)), away


class States:
    def __init__(self, size, out_state, out_decay, land_state, land_decay, sems):
        self.size = size
        self.here = lax.axis_index("seq")
        self.out_state, self.out_decay = out_state, out_decay
        self.land_state, self.land_decay = land_state, land_decay
        self.sems = sems

    def pair(self, slot, peer):
        s = self.sems
        return (
            remote(self.out_state, self.land_state.at[slot], s.at[0, peer], s.at[1, slot], "seq", peer),
            remote(self.out_decay, self.land_decay.at[slot], s.at[2, peer], s.at[3, slot], "seq", peer),
        )

    def sends(self, later):
        for k in range(self.size):
            yield k, (self.here < k if later else self.here > k)

    def start(self, later):
        for k, wanted in self.sends(later):

            @pl.when(wanted)
            def _():
                for copy in self.pair(self.here, k):
                    copy.start()

    def compose(self, later, state):
        state[...] = jnp.zeros_like(state)
        order = range(self.size) if later else range(self.size - 1, -1, -1)
        for k in order:

            @pl.when(self.here > k if later else self.here < k)
            def _():
                for copy in self.pair(k, k):
                    copy.wait_recv()
                for h in range(state.shape[0]):
                    decay = self.land_decay[k, h : h + 1, :]
                    state[h] = decay * state[h] + self.land_state[k, h].astype(f32)

    def drain(self, later):
        for k, wanted in self.sends(later):

            @pl.when(wanted)
            def _():
                for copy in self.pair(self.here, k):
                    copy.wait_send()


def states_scratch(size, heads):
    return [
        VM((heads, WIDTH, WIDTH), f32),
        VM((heads, WIDTH, WIDTH), bf16),
        VM((8, WIDTH), f32),
        VM((size, heads, WIDTH, WIDTH), bf16),
        VM((size, 8, WIDTH), f32),
        DMA((4, size)),
    ]


def front_kernel(size, groups, rounds, *refs):
    take = taker(refs)
    ends_ref, x_ref, norm_gain_ref, bound_ref, gain_ref, cot_in, *loaded = take(10)
    a_out, q_out, f_out, i_out, s_out, cot_out, o_ref, u_ref, starts_ref = take(9)
    *weights, a_ref, q_ref, f_ref, i_ref, s_ref, cot_ref = take(10)
    qd_ref, kd_ref, qe_ref, adds, decays = take(5)
    state, out_state, out_decay, land_state, land_decay, sems = take(6)
    load_sems, store_sems, a_send, a_recv, c_send, c_recv = take(6)
    me = lax.axis_index("tp")
    m, d = x_ref.shape[1:]
    known = cot_ref.shape[1]
    local = pltpu.make_async_copy
    cot_load = local(cot_in.at[:known], cot_ref.at[me], load_sems.at[4])
    cot_load.start()
    loads = [local(source, target, load_sems.at[k]) for k, (source, target) in enumerate(zip(loaded, weights))]
    for load in loads:
        load.start()
    line, line_count = line_peers(size)
    seq, seq_count = group_peers(groups, "seq")
    greet(line + seq, line_count + seq_count)

    gather = Gather(size, a_send, a_recv, a_ref)
    gather_cot = Gather(size, c_send, c_recv, cot_ref)
    norm_gain = norm_gain_ref[...]

    @pl.loop(0, rounds)
    def _(j):
        @pl.loop(0, m // 16)
        def _(g):
            r = pl.ds(pl.multiple_of(g * 16, 16), 16)
            x = x_ref[j, r, :].astype(f32)
            scale = lax.rsqrt(jnp.mean(x * x, axis=-1, keepdims=True) + epsilon)
            a_ref[me, j, r, :] = (x * scale * norm_gain).astype(bf16)

        gather.start(j)

    for load in loads:
        load.wait()
    cot_load.wait()
    pres = (q_ref, f_ref, i_ref, s_ref)

    @pl.loop(0, rounds)
    def _(j):
        for t in range(1, size):
            gather.step(j, t)

        @pl.when(j >= rounds - known)
        def _():
            gather_cot.start(j - (rounds - known))

        rows = a_ref[:, j].reshape(size * m, d)
        for weight, out in zip(weights, pres):
            product = mul(rows, weight[...], NN)
            for z in range(size):
                at = pl.multiple_of(z * rounds * m + j * m, 16)
                out[pl.ds(at, m), :] = product[z * m : (z + 1) * m]

    stores = [
        local(source, target, store_sems.at[k])
        for k, (source, target) in enumerate(zip((a_ref, *pres), (a_out, q_out, f_out, i_out, s_out)))
    ]
    for store in stores:
        store.start()

    rows, c = q_ref.shape
    blocks, heads = rows // WIDTH, c // WIDTH
    base = lax.axis_index("seq") * rows
    states = States(groups, out_state, out_decay, land_state, land_decay, sems)
    state[...] = jnp.zeros_like(state)
    out_decay[...] = jnp.ones_like(out_decay)

    def cot_steps(t):
        @pl.loop(0, known)
        def _(j):
            gather_cot.step(j, t)

    @pl.loop(0, blocks)
    def _(b):
        r = pl.ds(pl.multiple_of(b * WIDTH, WIDTH), WIDTH)
        same, carry, tail, keep = block_masks(base + b * WIDTH, ends_ref)
        for h in range(heads):
            cols = slice(h * WIDTH, (h + 1) * WIDTH)
            q = q_ref[r, cols]
            q = q * jax.nn.sigmoid(q)
            key, run, _ = decay_parts(f_ref[r, cols], bound_ref[:, cols])
            middle, last = run[WIDTH // 2 - 1 : WIDTH // 2, :], run[WIDTH - 1 :, :]
            qd_ref[r, cols] = (q * jnp.exp(run - middle)).astype(bf16)
            kd_ref[r, cols] = (key * jnp.exp(middle - run)).astype(bf16)
            qe_ref[r, cols] = (q * jnp.exp(run) * carry).astype(bf16)
            key_tail = (key * jnp.exp(last - run) * tail).astype(bf16)
            add = mul(i_ref[r, cols].astype(bf16), key_tail, TN)
            decay = jnp.exp(last) * keep
            adds[b, h] = add
            decays[b, h : h + 1, :] = decay
            state[h] = decay * state[h] + add
            out_decay[h : h + 1, :] = out_decay[h : h + 1, :] * decay

    out_state[...] = state[...].astype(bf16)
    states.start(True)
    cot_steps(1)

    @pl.loop(0, blocks)
    def _(b):
        r = pl.ds(pl.multiple_of(b * WIDTH, WIDTH), WIDTH)
        same, carry, tail, keep = block_masks(base + b * WIDTH, ends_ref)
        for h in range(heads):
            cols = slice(h * WIDTH, (h + 1) * WIDTH)
            scores = jnp.where(same, mul(qd_ref[r, cols], kd_ref[r, cols], NT), 0.0).astype(bf16)
            o_ref[r, cols] = mul(scores, i_ref[r, cols].astype(bf16), NN)

    states.compose(True, state)
    for t in range(2, size - 1):
        cot_steps(t)

    @pl.loop(0, blocks)
    def _(b):
        r = pl.ds(pl.multiple_of(b * WIDTH, WIDTH), WIDTH)
        places = base + b * WIDTH + lax.broadcasted_iota(jnp.int32, (WIDTH, WIDTH), 0)
        valid = jnp.where(places < ends_ref[ends_ref.shape[0] - 1], 1.0, 0.0)
        for h in range(heads):
            cols = slice(h * WIDTH, (h + 1) * WIDTH)
            low = state[h].astype(bf16)
            starts_ref[b, h] = low
            o = o_ref[r, cols] + mul(qe_ref[r, cols], low, NT)
            o_ref[r, cols] = o
            state[h] = decays[b, h : h + 1, :] * state[h] + adds[b, h]
            scale = lax.rsqrt(jnp.mean(o * o, axis=-1, keepdims=True) + epsilon)
            s = s_ref[r, cols]
            z = s * jax.nn.sigmoid(s) * valid
            u_ref[r, cols] = (o * scale * gain_ref[:, cols] * z).astype(bf16)

    cot_steps(size - 1)
    cot_store = local(cot_ref, cot_out, load_sems.at[4])
    cot_store.start()
    states.drain(True)

    @pl.loop(0, rounds)
    def _(j):
        gather.drain(j)

    @pl.loop(0, known)
    def _(j):
        gather_cot.drain(j)

    for store in stores:
        store.wait()
    cot_store.wait()


def front(size, groups, rounds, tokens, cot, norm_gain, weights, ends, bound, gain):
    own, d = tokens.shape
    m, c = own // rounds, weights[0].shape[1]
    rows = size * own
    blocks, heads = rows // WIDTH, c // WIDTH
    known = max(1, rounds // 2)
    shape, some = (size, rounds, m, d), (size, known, m, d)
    wide, low = jax.ShapeDtypeStruct((rows, c), f32), VM((rows, c), bf16)
    spec, far = pl.BlockSpec(memory_space=VM), pl.BlockSpec(memory_space=pl.ANY)
    sems = DMA((2, rounds, size))
    outs = pl.pallas_call(
        partial(front_kernel, size, groups, rounds),
        out_shape=[
            jax.ShapeDtypeStruct(shape, bf16),
            wide,
            wide,
            wide,
            wide,
            jax.ShapeDtypeStruct(some, bf16),
            wide,
            jax.ShapeDtypeStruct((rows, c), bf16),
            jax.ShapeDtypeStruct((blocks, heads, WIDTH, WIDTH), bf16),
        ],
        in_specs=[pl.BlockSpec(memory_space=pltpu.SMEM)] + [spec] * 4 + [far] * 5,
        out_specs=[far] * 6 + [spec] * 3,
        scratch_shapes=[VM((d, c), bf16)] * 4
        + [VM(shape, bf16)]
        + [VM((rows, c), f32)] * 4
        + [VM(some, bf16)]
        + [low] * 3
        + [VM((blocks, heads, WIDTH, WIDTH), f32), VM((blocks, 8, WIDTH), f32)]
        + states_scratch(groups, heads)
        + [DMA((5,)), DMA((5,)), sems, sems, sems, sems],
        compiler_params=pltpu.CompilerParams(collective_id=0, has_side_effects=True, vmem_limit_bytes=60 * MIB),
        cost_estimate=pl.CostEstimate(flops=8 * rows * d * c, bytes_accessed=36 * MIB, transcendentals=8 * rows * c),
        name="front",
    )(
        ends,
        tokens.reshape(rounds, m, d),
        norm_gain.reshape(1, d),
        bound,
        gain,
        cot.reshape(rounds, m, d),
        *weights,
    )
    return [outs[0].reshape(rows, d)] + list(outs[1:])


def scan_back_kernel(size, count, *refs):
    take = taker(refs)
    ends_ref, bound_ref, gain_ref, *loaded = take(10)
    grads = take(count)
    dq_ref, df_ref, di_ref, ds_ref, small_ref = take(5)
    grad_outs = take(count)
    qd_ref, kd_ref, qe_ref, kt_ref, do_ref, run_ref, adds, decays = take(8)
    state, out_state, out_decay, land_state, land_decay, sems = take(6)
    *inputs, load_sems = take(8)
    q_ref, f_ref, i_ref, s_ref, o_ref, ub_ref, starts_ref = inputs
    loads = [
        pltpu.make_async_copy(source, target, load_sems.at[k]) for k, (source, target) in enumerate(zip(loaded, inputs))
    ]
    for load in loads:
        load.start()
    sums = group_sums(size, grads, grad_outs, take)
    greet(*group_peers(size, "seq"))
    rows, c = q_ref.shape
    blocks, heads = rows // WIDTH, c // WIDTH
    base = lax.axis_index("seq") * rows
    states = States(size, out_state, out_decay, land_state, land_decay, sems)
    for each in sums:
        each.start()
    state[...] = jnp.zeros_like(state)
    out_decay[...] = jnp.ones_like(out_decay)
    small_ref[...] = jnp.zeros_like(small_ref)
    for load in loads:
        load.wait()

    @pl.loop(0, blocks)
    def _(back):
        for each in sums[:1]:

            @pl.when(back == 1)
            def _():
                each.middle()

        b = blocks - 1 - back
        r = pl.ds(pl.multiple_of(b * WIDTH, WIDTH), WIDTH)
        same, carry, tail, keep = block_masks(base + b * WIDTH, ends_ref)
        places = base + b * WIDTH + lax.broadcasted_iota(jnp.int32, (WIDTH, WIDTH), 0)
        valid = jnp.where(places < ends_ref[ends_ref.shape[0] - 1], 1.0, 0.0)
        for h in range(heads):
            cols = slice(h * WIDTH, (h + 1) * WIDTH)
            o, s, ub, gain = o_ref[r, cols], s_ref[r, cols], ub_ref[r, cols], gain_ref[:, cols]
            scale = lax.rsqrt(jnp.mean(o * o, axis=-1, keepdims=True) + epsilon)
            normed = o * scale
            gate = jax.nn.sigmoid(s)
            uz = ub * (s * gate * valid)
            small_ref[heads + h : heads + h + 1, :] += jnp.sum(uz * normed, axis=0, keepdims=True)
            nb = uz * gain
            ds_ref[r, cols] = (ub * normed * gain * valid * (gate * (1.0 + s * (1.0 - gate)))).astype(bf16)
            do = (scale * (nb - normed * jnp.mean(nb * normed, axis=-1, keepdims=True))).astype(bf16)
            do_ref[r, cols] = do
            q = q_ref[r, cols]
            q = q * jax.nn.sigmoid(q)
            key, run, _ = decay_parts(f_ref[r, cols], bound_ref[:, cols])
            middle, last = run[WIDTH // 2 - 1 : WIDTH // 2, :], run[WIDTH - 1 :, :]
            run_ref[r, cols] = run
            qd_ref[r, cols] = (q * jnp.exp(run - middle)).astype(bf16)
            kd_ref[r, cols] = (key * jnp.exp(middle - run)).astype(bf16)
            kt_ref[r, cols] = (key * jnp.exp(last - run) * tail).astype(bf16)
            qe = (q * jnp.exp(run) * carry).astype(bf16)
            qe_ref[r, cols] = qe
            add = mul(do, qe, TN)
            decay = jnp.exp(last) * keep
            adds[b, h] = add
            decays[b, h : h + 1, :] = decay
            state[h] = decay * state[h] + add
            out_decay[h : h + 1, :] = out_decay[h : h + 1, :] * decay

    out_state[...] = state[...].astype(bf16)
    states.start(False)
    for each in sums[:1]:
        each.relay()
    for each in sums[1:]:
        each.middle()
    states.compose(False, state)

    @pl.loop(0, blocks)
    def _(back):
        for each in sums[1:]:

            @pl.when(back == blocks // 2)
            def _():
                each.relay()
        b = blocks - 1 - back
        r = pl.ds(pl.multiple_of(b * WIDTH, WIDTH), WIDTH)
        same, carry, tail, keep = block_masks(base + b * WIDTH, ends_ref)
        shape = (WIDTH, WIDTH)
        down, along = lax.broadcasted_iota(jnp.int32, shape, 0), lax.broadcasted_iota(jnp.int32, shape, 1)
        from_here = jnp.where(along >= down, 1.0, 0.0).astype(bf16)
        ahead = jnp.where(along < down, 1.0, 0.0).astype(bf16)
        for h in range(heads):
            cols = slice(h * WIDTH, (h + 1) * WIDTH)
            do, v = do_ref[r, cols], i_ref[r, cols].astype(bf16)
            low, start = state[h].astype(bf16), starts_ref[b, h]
            dq_state = mul(do, start, NN)
            dk_state = mul(v, low, NN)
            kt = kt_ref[r, cols]
            qd, kd = qd_ref[r, cols], kd_ref[r, cols]
            scores = jnp.where(same, mul(qd, kd, NT), 0.0).astype(bf16)
            slopes = jnp.where(same, mul(do, v, NT), 0.0).astype(bf16)
            dq_near = mul(slopes, kd, NN)
            dk_near = mul(slopes, qd, TN)
            di_ref[r, cols] = (mul(scores, do, TN) + mul(kt, low, NT)).astype(bf16)
            run = run_ref[r, cols]
            middle, last = run[WIDTH // 2 - 1 : WIDTH // 2, :], run[WIDTH - 1 :, :]
            q_back = dq_near * jnp.exp(run - middle) + dq_state * (jnp.exp(run) * carry)
            k_back = dk_near * jnp.exp(middle - run) + dk_state * (jnp.exp(last - run) * tail)
            later = (
                qe_ref[r, cols].astype(f32) * dq_state
                + qd.astype(f32) * dq_near
                - kd.astype(f32) * dk_near
            )
            earlier = kt.astype(f32) * dk_state
            decay = decays[b, h : h + 1, :]
            log_back = decay * jnp.sum(low.astype(f32) * start.astype(f32), axis=0, keepdims=True)
            for ones, part in ((from_here, later), (ahead, earlier)):
                high = part.astype(bf16)
                log_back = log_back + mul(ones, high, NN)
                log_back = log_back + mul(ones, (part - high.astype(f32)).astype(bf16), NN)
            f_pre = f_ref[r, cols]
            away, near = jax.nn.sigmoid(-f_pre), jax.nn.sigmoid(f_pre)
            upper = jax.nn.sigmoid(-bound_ref[:, cols])
            lower = jax.nn.sigmoid(bound_ref[:, cols])
            forget_back = log_back / (1.0 - upper * away) - k_back
            slope = forget_back * away * upper
            df_ref[r, cols] = (slope * near).astype(bf16)
            small_ref[h : h + 1, :] += jnp.sum(slope, axis=0, keepdims=True) * lower
            dq_ref[r, cols] = (q_back * silu_slope(q_ref[r, cols])).astype(bf16)
            state[h] = adds[b, h] + decay * state[h]

    for each in sums:
        each.finish()
    states.drain(False)
    for each in sums:
        each.drain()


def scan_backward(size, ends, bound, gain, q, f, i, s, o, ub, starts, grads):
    rows, c = q.shape
    blocks, heads = rows // WIDTH, c // WIDTH
    low, wide = VM((rows, c), bf16), VM((rows, c), f32)
    spec = pl.BlockSpec(memory_space=VM)
    return pl.pallas_call(
        partial(scan_back_kernel, size, len(grads)),
        out_shape=[jax.ShapeDtypeStruct((rows, c), bf16)] * 4
        + [jax.ShapeDtypeStruct((2 * heads, WIDTH), f32)]
        + sum_shapes([grad.shape for grad in grads], [False] * len(grads)),
        in_specs=[pl.BlockSpec(memory_space=pltpu.SMEM)]
        + [spec] * 2
        + [pl.BlockSpec(memory_space=pl.ANY)] * (7 + len(grads)),
        out_specs=[spec] * (5 + len(grads)),
        scratch_shapes=[low] * 5
        + [wide, VM((blocks, heads, WIDTH, WIDTH), f32), VM((blocks, 8, WIDTH), f32)]
        + states_scratch(size, heads)
        + [wide] * 6
        + [VM(starts.shape, bf16), DMA((7,))]
        + group_sums_scratch([grad.shape for grad in grads]),
        compiler_params=pltpu.CompilerParams(collective_id=2, has_side_effects=True, vmem_limit_bytes=60 * MIB),
        cost_estimate=pl.CostEstimate(flops=40 * rows * c * WIDTH, bytes_accessed=20 * MIB, transcendentals=16 * rows * c),
        name="scan_backward",
    )(ends, bound, gain, q, f, i, s, o, ub, starts, *[in_pairs(grad) for grad in grads])


def middle_kernel(size, rounds, *refs):
    take = taker(refs)
    u_ref, x_ref, gain_ref, out_w, *loaded, cot_some, cot_own = take(9)
    res_out, back_out, e_out, ub_out, second_ref, down_out, out_grad, *grad_outs = take(10)
    gate_w, up_w, down_w = weights = take(3)
    cot_ref = take(1)[0]
    b_ref, e_ref, res_ref, back_ref, ub_ref, part, land, total = take(8)
    wide = take(3)
    down_ref, *tiles = take(4)
    load_sems, res_sems, back_sems, e_sems, ub_sem, down_sem, tile_sems = take(7)
    lines = [take(2) for _ in range(5)]
    hidden, gate_back, up_back = wide
    me = lax.axis_index("tp")
    m, d = x_ref.shape[1:]
    ff = gate_w.shape[1]
    group = size * m
    scatter = Scatter(size, *lines[0], part, land, total)
    gather = Gather(size, *lines[1], b_ref)
    scatter_back = Scatter(size, *lines[2], part, land, total)
    gather_back = Gather(size, *lines[3], e_ref)
    gather_cot = Gather(size, *lines[4], cot_ref)
    known = cot_some.shape[1]
    gain = gain_ref[...]
    tile = min(512, d)
    local = pltpu.make_async_copy
    loads = [local(src, dst, load_sems.at[k]) for k, (src, dst) in enumerate(zip(loaded, weights))]
    loads.append(local(cot_some, cot_ref.at[:, :known], load_sems.at[3]))
    cot_load = local(cot_own.at[known:], cot_ref.at[me, known:], load_sems.at[4])
    cot_load.start()
    for load in loads:
        load.start()
    second_ref[...] = jnp.zeros_like(second_ref)
    greet(*line_peers(size))

    def project_out(j):
        rows = u_ref[:, j].reshape(group, u_ref.shape[3])

        @pl.loop(0, d // tile)
        def _(n):
            cols = pl.ds(pl.multiple_of(n * tile, tile), tile)
            part[j, :, :, cols] = mul(rows, out_w[:, cols], NN).astype(bf16).reshape(size, m, tile)

        scatter.start(j)

    def res_copy(j):
        return local(res_ref.at[j], res_out.at[j], res_sems.at[j])

    def back_copy(j):
        return local(back_ref, back_out.at[j], back_sems.at[0])

    def e_copy(j):
        return local(e_ref.at[:, j], e_out.at[:, j], e_sems.at[j])

    def ub_copy(j):
        return local(ub_ref, ub_out.at[:, j], ub_sem.at[0])

    def down_copy(j):
        return local(down_ref, down_out.at[:, j], down_sem.at[0])

    def norm(j):
        @pl.loop(0, m // 16)
        def _(g):
            r = pl.ds(pl.multiple_of(g * 16, 16), 16)
            residual = x_ref[j, r, :].astype(f32) + total[r, :]
            res_ref[j, r, :] = residual
            scale = lax.rsqrt(jnp.mean(residual * residual, axis=-1, keepdims=True) + epsilon)
            b_ref[me, j, r, :] = (residual * scale * gain).astype(bf16)

        gather.start(j)
        res_copy(j).start()

    def feed(j):
        @pl.when(j == 0)
        def _():
            for load in loads:
                load.wait()

        rows = b_ref[:, j].reshape(group, d)
        cot = cot_ref[:, j].reshape(group, d)
        step = 256
        for low in range(0, ff, step):
            cols = slice(low, min(low + step, ff))
            width = cols.stop - cols.start
            gate = mul(rows, gate_w[:, cols], NN)
            up = mul(rows, up_w[:, cols], NN)
            hb = mul(cot, down_w[cols, :], NT)
            sig = jax.nn.sigmoid(gate)
            act = gate * sig
            shape = (size, m, width)
            hidden[:, j, :, cols] = (act * up).astype(bf16).reshape(shape)
            up_back[:, j, :, cols] = (hb * act).astype(bf16).reshape(shape)
            gate_back[:, j, :, cols] = (hb * up * (sig * (1.0 + gate * (1.0 - sig)))).astype(bf16).reshape(shape)

    def feed_back(j):
        scatter.drain(j)
        gates = gate_back[:, j].reshape(group, ff)
        ups = up_back[:, j].reshape(group, ff)

        @pl.loop(0, d // tile)
        def _(n):
            cols = pl.ds(pl.multiple_of(n * tile, tile), tile)
            sums = mul(gates, gate_w[cols, :], NT) + mul(ups, up_w[cols, :], NT)
            part[j, :, :, cols] = sums.astype(bf16).reshape(size, m, tile)

        scatter_back.start(j)

    def feed_out(j):
        @pl.when(j > 0)
        def _():
            down_copy(j - 1).wait()

        rows = hidden[:, j].reshape(group, ff)

        @pl.loop(0, d // tile)
        def _(n):
            cols = pl.ds(pl.multiple_of(n * tile, tile), tile)
            down_ref[:, :, cols] = mul(rows, down_w[:, cols], NN).astype(bf16).reshape(size, m, tile)

        down_copy(j).start()

    def norm_back(j, again):
        @pl.when(again)
        def _():
            back_copy(j - 1).wait()

        @pl.loop(0, m // 16)
        def _(g):
            r = pl.ds(pl.multiple_of(g * 16, 16), 16)
            b_back, residual = total[r, :], res_ref[j, r, :]
            scale = lax.rsqrt(jnp.mean(residual * residual, axis=-1, keepdims=True) + epsilon)
            normed = residual * scale
            second_ref[...] += jnp.sum(b_back * normed, axis=0, keepdims=True)
            inner = b_back * gain
            back = cot_ref[me, j, r, :].astype(f32) + scale * (
                inner - normed * jnp.mean(inner * normed, axis=-1, keepdims=True)
            )
            back_ref[r, :] = back
            e_ref[me, j, r, :] = back.astype(bf16)

        gather_back.start(j)
        back_copy(j).start()

    def unproject(j, wait):
        e_copy(j).start()

        @pl.when(wait)
        def _():
            ub_copy(j - 1).wait()

        rows = e_ref[:, j].reshape(group, d)
        ub_ref[...] = mul(rows, out_w[...], NT).reshape(size, m, out_w.shape[0])
        ub_copy(j).start()

    depth = tiles[0].shape[0]
    count = d // depth

    def tile_copies(n):
        rows = pl.ds(pl.multiple_of(n * depth, depth), depth)
        return [local(src, dst.at[rows, :], tile_sems.at[k]) for k, (src, dst) in enumerate(zip(tiles, grad_outs))]

    def weight_tiles(low, high):
        @pl.loop(low, high)
        def _(n):
            @pl.when(n > 0)
            def _():
                for copy in tile_copies(n - 1):
                    copy.wait()

            cols = pl.ds(pl.multiple_of(n * depth, depth), depth)
            for left, right, out in zip((b_ref, b_ref, cot_ref), (gate_back, up_back, hidden), tiles):
                rows = left[:, :, :, cols].reshape(rounds * group, depth)
                out[...] = mul(rows, right[...].reshape(rounds * group, ff), TN).astype(bf16)
            for copy in tile_copies(n):
                copy.start()

    final = rounds - 1
    cot_load.wait()

    @pl.loop(0, rounds + 2)
    def _(i):
        def stage(lag, body):
            @pl.when((i >= lag) & (i < rounds + lag))
            def _():
                body(i - lag)

        stage(0, project_out)

        @pl.when(i < rounds - known)
        def _():
            gather_cot.start(known + i)

        for t in range(1, size):

            @pl.when((i > 0) & (i <= rounds - known))
            def _():
                gather_cot.step(known + i - 1, t)

            stage(1, lambda j: scatter.step(j, t) if t < size - 1 else scatter.finish(j))
            if t == size - 1:
                stage(1, norm)
            stage(2, lambda j: gather.step(j, t))
            stage(3, lambda j: scatter_back.step(j, t) if t < size - 1 else scatter_back.finish(j))
            if t == size - 1:
                stage(3, lambda j: norm_back(j, j > 0))
            stage(4, lambda j: gather_back.step(j, t))
        stage(2, feed)
        stage(2, feed_back)
        stage(2, feed_out)
        stage(4, lambda j: unproject(j, j > 0))

    shares = [count * k // 5 for k in range(6)]
    for t in range(1, size):
        if t < size - 1:
            scatter_back.step(final, t)
        else:
            scatter_back.finish(final)
            norm_back(final, True)
        gather_back.step(final - 1, t)
        if t < size - 1:
            weight_tiles(shares[t - 1], shares[t])
    unproject(final - 1, True)
    weight_tiles(shares[2], shares[3])
    for t in range(1, size):
        gather_back.step(final, t)
        if t < size - 1:
            weight_tiles(shares[t + 2], shares[t + 3])
    unproject(final, True)
    for copy in tile_copies(count - 1):
        copy.wait()
    width = u_ref.shape[3]

    def out_tile(n, slot):
        rows = pl.ds(pl.multiple_of(n * depth, depth), depth)
        source = tiles[slot].at[:, pl.ds(0, width)]
        return local(source, out_grad.at[rows, :], tile_sems.at[slot])

    slots = len(tiles) - 1

    @pl.loop(0, count // slots)
    def _(n):
        for slot in range(slots):
            at = n * slots + slot

            @pl.when(n > 0)
            def _():
                out_tile(at - slots, slot).wait()

            cols = pl.ds(pl.multiple_of(at * depth, depth), depth)
            rows = e_ref[:, :, :, cols].reshape(rounds * group, depth)
            tiles[slot][:, :width] = mul(rows, u_ref[...].reshape(rounds * group, width), TN).astype(bf16)
            out_tile(at, slot).start()

    for slot in range(slots):
        out_tile(count - slots + slot, slot).wait()
    ub_copy(final).wait()
    back_copy(final).wait()
    down_copy(final).wait()

    @pl.loop(0, rounds)
    def _(j):
        res_copy(j).wait()
        e_copy(j).wait()

        @pl.when(j >= known)
        def _():
            gather_cot.drain(j)

        gather.drain(j)
        scatter_back.drain(j)
        gather_back.drain(j)


def middle(size, rounds, u, x, cot_some, cot, gain, out_w, gate_w, up_w, down_w):
    rows, d = x.shape
    m = rows // rounds
    c, ff = out_w.shape[0], gate_w.shape[1]
    shape = (size, rounds, m)
    sems = DMA((2, rounds, size))
    spec, far = pl.BlockSpec(memory_space=VM), pl.BlockSpec(memory_space=pl.ANY)
    depth = min(256, d)
    outs = pl.pallas_call(
        partial(middle_kernel, size, rounds),
        out_shape=[
            jax.ShapeDtypeStruct((rounds, m, d), f32),
            jax.ShapeDtypeStruct((rounds, m, d), f32),
            jax.ShapeDtypeStruct(shape + (d,), bf16),
            jax.ShapeDtypeStruct(shape + (c,), f32),
            jax.ShapeDtypeStruct((1, d), f32),
            jax.ShapeDtypeStruct(shape + (d,), bf16),
            jax.ShapeDtypeStruct((d, c), bf16),
        ]
        + [jax.ShapeDtypeStruct((d, ff), bf16)] * 3,
        in_specs=[spec] * 4 + [far] * 5,
        out_specs=[far] * 4 + [spec] + [far] * 5,
        scratch_shapes=[
            VM(gate_w.shape, bf16),
            VM(up_w.shape, bf16),
            VM(down_w.shape, bf16),
            VM(shape + (d,), bf16),
            VM(shape + (d,), bf16),
            VM(shape + (d,), bf16),
            VM((rounds, m, d), f32),
            VM((m, d), f32),
            VM((size, m, c), f32),
            VM((rounds, size, m, d), bf16),
            VM((2, rounds, size - 1, m, d), bf16),
            VM((m, d), f32),
        ]
        + [VM(shape + (ff,), bf16)] * 3
        + [VM((size, m, d), bf16)]
        + [VM((depth, ff), bf16)] * 3
        + [DMA((5,)), DMA((rounds,)), DMA((1,)), DMA((rounds,)), DMA((1,)), DMA((1,)), DMA((3,))]
        + [sems] * 10,
        compiler_params=pltpu.CompilerParams(collective_id=3, has_side_effects=True, vmem_limit_bytes=63 * MIB),
        cost_estimate=pl.CostEstimate(
            flops=2 * size * rows * d * (2 * c + 9 * ff), bytes_accessed=56 * MIB, transcendentals=size * rows * ff
        ),
        name="middle",
    )(
        u.reshape(shape + (c,)),
        x.reshape(rounds, m, d),
        gain.reshape(1, d),
        out_w,
        gate_w,
        up_w,
        down_w,
        cot_some,
        cot.reshape(rounds, m, d),
    )
    res, back, e, ub, second, down, *grads = outs
    total = size * rows
    return (
        res.reshape(rows, d),
        back.reshape(rows, d),
        ub.reshape(total, c),
        second,
        down.reshape(total, d),
        *grads,
    )


class Everyone:
    def __init__(self, size, axis, mine, land, sems):
        self.size, self.axis = size, axis
        self.here = lax.axis_index(axis)
        self.mine, self.land, self.sems = mine, land, sems

    def copy(self, slot, peer):
        return remote(self.mine, self.land.at[slot], self.sems.at[0, peer], self.sems.at[1, slot], self.axis, peer)

    def others(self):
        for k in range(self.size):
            yield k, self.here != k

    def start(self):
        for k, other in self.others():

            @pl.when(other)
            def _():
                self.copy(self.here, k).start()

    def finish(self, out):
        out[...] = self.mine[...]
        for k, other in self.others():

            @pl.when(other)
            def _():
                self.copy(k, k).wait_recv()
                out[...] = out[...] + self.land[k]

    def drain(self):
        for k, other in self.others():

            @pl.when(other)
            def _():
                self.copy(self.here, k).wait_send()


def everyone_scratch(size, rows):
    return [VM((rows, WIDTH), f32), VM((size, rows, WIDTH), f32), DMA((2, size))]


def stack(vector, into, at):
    for k in range(vector.shape[1] // WIDTH):
        into[at + k : at + k + 1, :] = vector[:, k * WIDTH : (k + 1) * WIDTH]


def last_kernel(size, groups, rounds, count, mixed, *refs):
    take = taker(refs)
    backs, weights = take(4), take(4)
    x_ref, gain_ref, second_ref, small_ref, back_in = take(5)
    a_in = take(1 if mixed else 0)
    grads = take(count)
    tokens_out, second_out, first_out, small_out = take(4)
    grad_outs = take(count + (4 if mixed else 0))
    part, land, total, first, s_send, s_recv = take(6)
    small_seq, gain_seq, second_tp, first_tp = (take(3) for _ in range(4))
    nears, a_refs = take(4 if mixed else 0), take(1 if mixed else 0)
    load_sems = take(1)[0]
    sums = group_sums(groups, grads + nears, grad_outs, take)
    early, late = sums[:2], sums[2:]

    seq, seq_count = group_peers(groups, "seq")
    tp, tp_count = group_peers(size, "tp")
    greet(seq + tp, seq_count + tp_count)

    for each in sums[:count]:
        each.start()
    loads = [
        pltpu.make_async_copy(source, target, load_sems.at[k])
        for k, (source, target) in enumerate(zip([back_in, *a_in], [tokens_out, *a_refs]))
    ]
    for load in loads:
        load.start()

    m, d = x_ref.shape[1:]
    group = size * m
    scatter = Scatter(size, s_send, s_recv, part, land, total)
    gain = gain_ref[...]
    first[...] = jnp.zeros_like(first)
    tile = min(512, d)

    seq_small = Everyone(groups, "seq", *small_seq)
    seq_first = Everyone(groups, "seq", *gain_seq)
    tp_second = Everyone(size, "tp", *second_tp)
    tp_first = Everyone(size, "tp", *first_tp)
    lines, smalls = d // WIDTH, small_ref.shape[0]
    stack(second_ref[...], small_seq[0], 0)
    small_seq[0][lines : lines + smalls, :] = small_ref[...]
    seq_small.start()

    def products(j):
        @pl.loop(0, d // tile)
        def _(n):
            cols = pl.ds(pl.multiple_of(n * tile, tile), tile)
            acc = None
            for back, weight in zip(backs, weights):
                term = mul(back[:, j].reshape(group, back.shape[3]), weight[cols, :], NT)
                acc = term if acc is None else acc + term
            part[j, :, :, cols] = acc.astype(bf16).reshape(size, m, tile)

        scatter.start(j)

    def mix(back, each):
        rows = back[...].reshape(rounds * group, back.shape[3])
        depth = each.own.shape[1]
        for side, into in ((1 - each.side, each.grad), (each.side, each.own)):

            @pl.loop(0, each.half)
            def _(k):
                cols = pl.ds(pl.multiple_of((2 * k + side) * depth, depth), depth)
                left = a_refs[0][:, :, :, cols].reshape(rounds * group, depth)
                into[k] = mul(left, rows, TN).astype(bf16)

            if into is each.grad:
                each.start()

    def norm_back(j):
        @pl.loop(0, m // 16)
        def _(g):
            r = pl.ds(pl.multiple_of(g * 16, 16), 16)
            a_back, x = total[r, :], x_ref[j, r, :].astype(f32)
            scale = lax.rsqrt(jnp.mean(x * x, axis=-1, keepdims=True) + epsilon)
            normed = x * scale
            first[...] += jnp.sum(a_back * normed, axis=0, keepdims=True)
            inner = a_back * gain
            tokens_out[j, r, :] = tokens_out[j, r, :] + scale * (
                inner - normed * jnp.mean(inner * normed, axis=-1, keepdims=True)
            )

    def steps(j, low, high):
        for t in range(low, high):
            if t < size - 1:
                scatter.step(j, t)
            else:
                scatter.finish(j)
                norm_back(j)

    for j in range(rounds):
        products(j)
        if j < len(early):
            early[j].middle()
    for load in loads:
        load.wait()
    if mixed:
        for at, (back, each) in enumerate(zip(backs, late)):
            mix(back, each)
            steps(0, 1, 2) if at == 1 else None
            steps(0, 2, 3) if at == 3 else None
    else:
        steps(0, 1, 3)
    for each in early:
        each.relay()
    for each in late:
        each.middle()
    seq_small.finish(small_out)
    second_tp[0][...] = small_out[:lines, :]
    tp_second.start()
    steps(0, 3, size)
    for j in range(1, rounds):
        steps(j, 1, size)
        if j == 1:
            for each in late[:2]:
                each.relay()
        if j == 2:
            for each in late[2:]:
                each.relay()
            early[0].finish()

    stack(first[...], gain_seq[0], 0)
    seq_first.start()
    tp_second.finish(second_out)
    for each in early[1:]:
        each.finish()
    seq_first.finish(first_tp[0])
    tp_first.start()
    for each in late:
        each.finish()
    tp_first.finish(first_out)

    for each in sums + [seq_small, seq_first, tp_second, tp_first]:
        each.drain()

    @pl.loop(0, rounds)
    def _(j):
        scatter.drain(j)


def last(size, groups, rounds, backs, weights, a, x, back, gain, second, small, grads, turned):
    rows, d = x.shape
    m = rows // rounds
    c = weights[0].shape[1]
    shape = (size, rounds, m)
    lines = d // WIDTH
    sems = DMA((2, rounds, size))
    spec = pl.BlockSpec(memory_space=VM)
    small_rows = lines + small.shape[0]
    mixed = a is not None
    shapes = [grad.shape for grad in grads] + ([(groups, d // groups, c)] * 4 if mixed else [])
    outs = pl.pallas_call(
        partial(last_kernel, size, groups, rounds, len(grads), mixed),
        out_shape=[
            jax.ShapeDtypeStruct((rounds, m, d), f32),
            jax.ShapeDtypeStruct((lines, WIDTH), f32),
            jax.ShapeDtypeStruct((lines, WIDTH), f32),
            jax.ShapeDtypeStruct((small_rows, WIDTH), f32),
        ]
        + sum_shapes(shapes, turned),
        in_specs=[spec] * 12 + [pl.BlockSpec(memory_space=pl.ANY)] * (1 + mixed + len(grads)),
        out_specs=[spec] * (4 + len(shapes)),
        scratch_shapes=[
            VM((rounds, size, m, d), bf16),
            VM((2, rounds, size - 1, m, d), bf16),
            VM((m, d), f32),
            VM((1, d), f32),
            sems,
            sems,
        ]
        + everyone_scratch(groups, small_rows)
        + everyone_scratch(groups, lines)
        + everyone_scratch(size, lines)
        + everyone_scratch(size, lines)
        + ([VM((groups // 2, d // groups, c), bf16)] * 4 + [VM(shape + (d,), bf16)] if mixed else [])
        + [DMA((2,))]
        + group_sums_scratch(shapes),
        compiler_params=pltpu.CompilerParams(collective_id=4, has_side_effects=True, vmem_limit_bytes=63 * MIB),
        cost_estimate=pl.CostEstimate(flops=16 * size * rows * d * c, bytes_accessed=56 * MIB, transcendentals=0),
        name="last",
    )(
        *[part.reshape(shape + (c,)) for part in backs],
        *weights,
        x.reshape(rounds, m, d),
        gain.reshape(1, d),
        second,
        small,
        back.reshape(rounds, m, d),
        *([a.reshape(shape + (d,))] if mixed else []),
        *[in_pairs(grad) for grad in grads],
    )
    return (outs[0].reshape(rows, d), outs[1], outs[2], outs[3][lines:]) + tuple(outs[4:])


def per_device(
    size,
    groups,
    tokens,
    lengths,
    cotangent,
    first_gain,
    query_weight,
    forget_weight,
    input_weight,
    swish_weight,
    bound_logit,
    group_gain,
    out_weight,
    second_gain,
    gate_weight,
    up_weight,
    down_weight,
):
    weights = (query_weight, forget_weight, input_weight, swish_weight)
    ends = jnp.cumsum(lengths).astype(jnp.int32)
    bound, head_gain = bound_logit.reshape(1, -1), group_gain.reshape(1, -1)
    a, q, f, i, s, cot_some, o, u, starts = front(
        size, groups, ROUNDS, tokens, cotangent, first_gain, weights, ends, bound, head_gain
    )
    residual, back, ub, second, down, *wide = middle(
        size, ROUNDS, u, tokens, cot_some, cotangent, second_gain, out_weight, gate_weight, up_weight, down_weight
    )
    down, ub = lax.optimization_barrier((down, ub))
    down = lax.psum_scatter(down, "tp", scatter_dimension=0, tiled=True)
    output = (residual + down.astype(f32)).astype(bf16)
    d = tokens.shape[1]

    def chunks(grad):
        return grad.reshape(groups, grad.shape[0] // groups, grad.shape[1])

    def grad_of(left, right):
        return chunks(lax.dot_general(left, right, TN, preferred_element_type=f32).astype(bf16))

    outs, gates, ups, downs = (chunks(grad) for grad in wide)
    dq, df, di, ds, small, gate_grad, up_grad = scan_backward(
        groups, ends, bound, head_gain, q, f, i, s, o, ub, starts, [gates, ups]
    )
    back_rows = (dq, df, di, ds)
    here_too = groups == 8
    others = [downs, outs] + ([] if here_too else [grad_of(a, part) for part in back_rows])
    tokens_grad, second_sum, first_sum, small_sum, *sums = last(
        size,
        groups,
        ROUNDS,
        back_rows,
        weights,
        a if here_too else None,
        tokens,
        back,
        first_gain,
        second,
        small,
        others,
        [True, True] + [False] * 4,
    )
    down_grad, out_grad, query_grad, forget_grad, input_grad, swish_grad = sums
    heads = bound_logit.shape[0]
    here = lax.axis_index("seq")
    place = here * size + lax.axis_index("tp")
    each = d // (groups * size)
    wide = WIDTH // groups
    first_grad = lax.dynamic_slice_in_dim(first_sum.reshape(-1), place * each, each)
    second_grad = lax.dynamic_slice_in_dim(second_sum.reshape(-1), place * each, each)
    bound_grad = lax.dynamic_slice_in_dim(small_sum[:heads], here * wide, wide, axis=1)
    head_grad = lax.dynamic_slice_in_dim(small_sum[heads:], here * wide, wide, axis=1)
    return (
        output,
        tokens_grad,
        first_grad,
        query_grad,
        forget_grad,
        input_grad,
        swish_grad,
        bound_grad,
        head_grad,
        out_grad,
        second_grad,
        gate_grad,
        up_grad,
        down_grad,
    )


def solution(mesh):
    rows, both, cols, lines = P(("seq", "tp"), None), P(("seq", "tp")), P(None, "tp"), P("tp", None)
    in_specs = (rows, P(), rows, P(), cols, cols, cols, cols, lines, lines, lines, P(), cols, cols, lines)
    down, across = P("seq", "tp"), P("tp", "seq")
    out_specs = (rows, rows, both, down, down, down, down, across, across, across, both, down, down, across)
    return jax.shard_map(
        partial(per_device, mesh.shape["tp"], mesh.shape["seq"]),
        mesh=mesh,
        in_specs=in_specs,
        out_specs=out_specs,
        check_vma=False,
    )
```

```python
from functools import partial

import jax
import jax.numpy as jnp
from jax import lax
from jax.experimental import pallas as pl
from jax.experimental.pallas import tpu as pltpu
from jax.sharding import PartitionSpec as P

WIDTH = 128
ROUNDS = 4
KNOWN = 1
PIECES = 3
STEPS = (
    "C10", "C11", "C20", "A0", "C12", "C13", "A1", "C21", "C22", "C23", "S01", "C30", "S11", "S02", "S03", "A2",
    "A3", "C31", "C32", "C33", "G01", "G02", "S21", "S22", "S12", "S23", "G03", "F00", "F01", "F02", "O0", "S13",
    "B0", "S31", "G11", "T01", "T02", "G12", "G13", "F10", "F11", "F12", "O1", "G21", "T03", "B1", "S32", "G22",
    "G23", "F20", "E01", "F21", "F22", "E02", "E03", "S33", "T11", "T12", "T13", "G31", "O2", "E11", "B2", "U0",
    "T21", "G32", "G33", "F30", "F31", "T22", "F32", "O3", "E12", "T23", "B3", "W0", "E21", "T31", "T32", "E22",
    "W1", "W2", "T33", "W3", "E23", "W5", "E31", "E13", "U1", "W6", "W4", "U2", "W7", "E32", "E33", "U3",
)
MIB = 1 << 20
epsilon = 1e-05

f32 = jnp.float32
bf16 = jnp.bfloat16
NN = (((1,), (0,)), ((), ()))
NT = (((1,), (1,)), ((), ()))
TN = (((0,), (0,)), ((), ()))
VM = pltpu.VMEM
DMA = pltpu.SemaphoreType.DMA
MESH = pl.DeviceIdType.MESH


def mul(left, right, dims):
    return lax.dot_general(left, right, dims, preferred_element_type=f32)


def silu_slope(value):
    gate = jax.nn.sigmoid(value)
    return gate * (1.0 + value * (1.0 - gate))


def remote(src, dst, send, recv, axis, peer):
    return pltpu.make_async_remote_copy(
        src_ref=src,
        dst_ref=dst,
        send_sem=send,
        recv_sem=recv,
        device_id={axis: peer},
        device_id_type=MESH,
    )


def greet(peers, count):
    barrier = pltpu.get_barrier_semaphore()
    for axis, peer, wanted in peers:

        @pl.when(wanted)
        def _():
            pl.semaphore_signal(barrier, inc=1, device_id={axis: peer}, device_id_type=MESH)

    pl.semaphore_wait(barrier, count)


def line_peers(size):
    me = lax.axis_index("tp")
    peers = [("tp", lax.rem(me + 1, size), me < size - 1), ("tp", lax.rem(me + size - 1, size), me > 0)]
    return peers, jnp.where(me < size - 1, 1, 0) + jnp.where(me > 0, 1, 0)


def group_peers(size, axis):
    me = lax.axis_index(axis)
    return [(axis, lax.rem(me + k, size), True) for k in range(1, size)], size - 1


class Line:
    def __init__(self, size, send, recv):
        self.size = size
        self.me = lax.axis_index("tp")
        self.right = lax.rem(self.me + 1, size)
        self.left = lax.rem(self.me + size - 1, size)
        self.send, self.recv = send, recv

    def hop(self, way, src, dst, j, at):
        peer = self.right if way == 0 else self.left
        return remote(src, dst, self.send.at[way, j, at], self.recv.at[way, j, at], "tp", peer)


class Scatter(Line):
    def __init__(self, size, send, recv, part, land, total):
        super().__init__(size, send, recv)
        self.part, self.land, self.total = part, land, total

    def copy(self, way, j, to):
        return self.hop(way, self.part.at[j, to], self.slot(way, j, to), j, to)

    def slot(self, way, j, to):
        return self.land.at[way, j, to - 1 + way]

    def start(self, j):
        last = self.size - 1

        @pl.when(self.me == 0)
        def _():
            for to in range(last, 0, -1):
                self.copy(0, j, to).start()

        @pl.when(self.me == last)
        def _():
            for to in range(last):
                self.copy(1, j, to).start()

    def step(self, j, t):
        last = self.size - 1
        for way in (0, 1):
            place = self.me if way == 0 else last - self.me
            to = last - t + place
            to = to if way == 0 else last - to

            @pl.when((place >= 1) & (place <= t))
            def _():
                copy = self.copy(way, j, to)
                copy.wait_recv()
                self.add(self.part.at[j, to], self.slot(way, j, to))
                copy.start()

    def add(self, into, more):
        rows = into.shape[0]

        @pl.loop(0, rows // 16)
        def _(g):
            r = pl.ds(pl.multiple_of(g * 16, 16), 16)
            into[r, :] = (into[r, :].astype(f32) + more[r, :].astype(f32)).astype(bf16)

    def finish(self, j):
        me, last = self.me, self.size - 1
        rows = self.total.shape[0]

        def over(body):
            @pl.loop(0, rows // 16)
            def _(g):
                body(pl.ds(pl.multiple_of(g * 16, 16), 16))

        def first(r):
            self.total[r, :] = self.part[j, me, r, :].astype(f32)

        over(first)
        for way, there in ((0, me >= 1), (1, me < last)):

            @pl.when(there)
            def _():
                self.copy(way, j, me).wait_recv()

                def more(r):
                    self.total[r, :] = self.total[r, :] + self.land[way, j, me - 1 + way, r, :].astype(f32)

                over(more)

    def drain(self, j):
        for to in range(self.size):

            @pl.when(self.me < to)
            def _():
                self.copy(0, j, to).wait_send()

            @pl.when(self.me > to)
            def _():
                self.copy(1, j, to).wait_send()


class Gather(Line):
    def __init__(self, size, send, recv, whole):
        super().__init__(size, send, recv)
        self.whole = whole

    def copy(self, way, j, source):
        block = self.whole.at[source, j]
        return self.hop(way, block, block, j, source)

    def start(self, j):
        @pl.when(self.me < self.size - 1)
        def _():
            self.copy(0, j, self.me).start()

        @pl.when(self.me > 0)
        def _():
            self.copy(1, j, self.me).start()

    def step(self, j, t):
        last = self.size - 1

        @pl.when(self.me >= t)
        def _():
            copy = self.copy(0, j, self.me - t)
            copy.wait_recv()

            @pl.when(self.me < last)
            def _():
                copy.start()

        @pl.when(self.me + t <= last)
        def _():
            copy = self.copy(1, j, self.me + t)
            copy.wait_recv()

            @pl.when(self.me > 0)
            def _():
                copy.start()

    def drain(self, j):
        last = self.size - 1
        for source in range(self.size):

            @pl.when((self.me >= source) & (self.me < last))
            def _():
                self.copy(0, j, source).wait_send()

            @pl.when((self.me <= source) & (self.me > 0))
            def _():
                self.copy(1, j, source).wait_send()


def add_rows(into, left, right):
    rows = into.shape[0]

    @pl.loop(0, rows // 16)
    def _(g):
        r = pl.ds(pl.multiple_of(g * 16, 16), 16)
        into[r, :] = (left[r, :].astype(f32) + right[r, :].astype(f32)).astype(bf16)


class GroupSum:
    refs = 6

    def __init__(self, size, grad, out, own, got, land, *sems):
        self.half = size // 2
        here = lax.axis_index("seq")
        self.side = lax.rem(here, 2)
        self.mine = here // 2
        self.sibling = here + 1 - 2 * self.side
        self.grad, self.own, self.got, self.land, self.out = grad, own, got, land, out
        self.near_sems, *self.sems = sems
        self.loads = len(grad.shape) == 4
        self.turned = out.shape != own.shape[1:]

    @staticmethod
    def scratch(shape):
        half = shape[0]
        return [VM(shape, bf16)] * 3 + [DMA((3, half)), DMA((half,)), DMA((half,))]

    def near(self, k):
        sems = self.near_sems
        source = self.grad.at[k, 1 - self.side] if self.loads else self.grad.at[k]
        return remote(source, self.got.at[k], sems.at[0, k], sems.at[1, k], "seq", self.sibling)

    def load(self, k):
        return pltpu.make_async_copy(self.grad.at[k, self.side], self.own.at[k], self.near_sems.at[2, k])

    def start(self):
        for k in range(self.half):
            self.near(k).start()
            if self.loads:
                self.load(k).start()

    def pair(self, k, into):
        if self.loads:
            self.load(k).wait()
        self.near(k).wait_recv()
        add_rows(into, self.own.at[k], self.got.at[k])

    def far(self, k):
        send, recv = self.sems
        return remote(self.own.at[k], self.land.at[self.mine], send.at[k], recv.at[self.mine], "seq", 2 * k + self.side)

    def arrival(self, k):
        send, recv = self.sems
        return remote(self.own.at[k], self.land.at[k], send.at[k], recv.at[k], "seq", 2 * k + self.side)

    def middle(self):
        for k in range(self.half):

            @pl.when(k == self.mine)
            def _():
                self.pair(k, self.land.at[k])

            @pl.when(k != self.mine)
            def _():
                self.pair(k, self.own.at[k])
                self.far(k).start()

    def relay(self):
        pass

    def arrive(self):
        for k in range(self.half):

            @pl.when(k != self.mine)
            def _():
                self.arrival(k).wait_recv()

    def terms(self):
        return [self.land.at[k] for k in range(self.half)]

    def finish(self):
        self.arrive()
        rows, cols = self.own.shape[1:]

        def total(r, c):
            acc = None
            for term in self.terms():
                part = term[r, c].astype(f32)
                acc = part if acc is None else acc + part
            return acc

        if self.turned:

            @pl.loop(0, cols // WIDTH)
            def _(g):
                c = pl.ds(pl.multiple_of(g * WIDTH, WIDTH), WIDTH)
                self.out[c, :] = total(slice(None), c).T

        else:

            @pl.loop(0, rows // 16)
            def _(g):
                r = pl.ds(pl.multiple_of(g * 16, 16), 16)
                self.out[r, :] = total(r, slice(None))

    def drain(self):
        for k in range(self.half):
            self.near(k).wait_send()
        self.drain_far()

    def drain_far(self):
        for k in range(self.half):

            @pl.when(k != self.mine)
            def _():
                self.far(k).wait_send()


class SquareSum(GroupSum):
    refs = 6

    def __init__(self, *args):
        super().__init__(*args)
        self.hop, self.far_sems = self.sems
        x, y = lax.rem(self.mine, 2), self.mine // 2
        self.beside = (2 * y + 1 - x, 2 * (1 - y) + x)
        self.opposite = 2 * (1 - y) + 1 - x
        rows = self.own.shape[1] // 2
        self.halves = (pl.ds(0, rows), pl.ds(rows, rows))

    @staticmethod
    def scratch(shape):
        half, rows, cols = shape
        return [
            VM(shape, bf16),
            VM(shape, bf16),
            VM((2, rows, cols), bf16),
            DMA((3, half)),
            VM((2, rows // 2, cols), bf16),
            DMA((2, 6)),
        ]

    def over(self, way, at, source, target):
        sems = self.far_sems
        return remote(source, target, sems.at[0, at], sems.at[1, at], "seq", 2 * self.beside[way] + self.side)

    def pass_on(self, way):
        return self.over(way, way, self.own.at[self.opposite, self.halves[way]], self.hop.at[way])

    def deliver(self, way, half):
        source = self.own.at[self.beside[way], self.halves[half]]
        return self.over(way, 2 + 2 * way + half, source, self.land.at[way, self.halves[half]])

    def middle(self):
        self.pair(self.opposite, self.own.at[self.opposite])
        for way in (0, 1):
            self.pass_on(way).start()
        for way in (0, 1):
            self.pair(self.beside[way], self.own.at[self.beside[way]])
            self.deliver(way, way).start()
        self.pair(self.mine, self.own.at[self.mine])

    def relay(self):
        for way in (0, 1):
            self.pass_on(way).wait_recv()
            into = self.own.at[self.beside[1 - way], self.halves[way]]
            add_rows(into, into, self.hop.at[way])
            self.deliver(1 - way, way).start()

    def arrive(self):
        for way in (0, 1):
            for half in (0, 1):
                self.deliver(way, half).wait_recv()

    def terms(self):
        return [self.own.at[self.mine], self.land.at[0], self.land.at[1]]

    def drain_far(self):
        for way in (0, 1):
            self.pass_on(way).wait_send()
            for half in (0, 1):
                self.deliver(way, half).wait_send()


def summer(size):
    return SquareSum if size == 8 else GroupSum


def group_sums(size, grads, outs, take):
    kind = summer(size)
    return [kind(size, grad, out, *take(kind.refs)) for grad, out in zip(grads, outs)]


def group_sums_scratch(shapes):
    scratch = []
    for size, rows, cols in shapes:
        scratch += summer(size).scratch((size // 2, rows, cols))
    return scratch


def sum_shapes(shapes, turned):
    shapes = [shape[:0:-1] if turn else shape[1:] for shape, turn in zip(shapes, turned)]
    return [jax.ShapeDtypeStruct(shape, f32) for shape in shapes]


def in_pairs(grad):
    return grad.reshape((grad.shape[0] // 2, 2) + grad.shape[1:])


def taker(refs):
    refs = list(refs)

    def take(count):
        taken, refs[:count] = refs[:count], []
        return taken

    return take


def document(rows, ends_ref):
    total = jnp.where(rows >= ends_ref[0], 1, 0)
    for k in range(1, ends_ref.shape[0]):
        total = total + jnp.where(rows >= ends_ref[k], 1, 0)
    return total


def block_masks(first, ends_ref):
    shape = (WIDTH, WIDTH)
    down = lax.broadcasted_iota(jnp.int32, shape, 0)
    along = lax.broadcasted_iota(jnp.int32, shape, 1)
    docs = document(first + down, ends_ref)
    same = (docs == document(first + along, ends_ref)) & (down >= along)
    before = jnp.where(first > 0, document(first - 1, ends_ref), -1)
    final = document(first + WIDTH - 1, ends_ref)
    carry = jnp.where(docs == before, 1.0, 0.0)
    tail = jnp.where(docs == final, 1.0, 0.0)
    keep = jnp.where(final == before, 1.0, 0.0)
    return same, carry, tail, keep


def running(log_forget):
    shape = (WIDTH, WIDTH)
    lower = lax.broadcasted_iota(jnp.int32, shape, 0) >= lax.broadcasted_iota(jnp.int32, shape, 1)
    ones = jnp.where(lower, 1.0, 0.0).astype(bf16)
    high = log_forget.astype(bf16)
    low = (log_forget - high.astype(f32)).astype(bf16)
    return mul(ones, high, NN) + mul(ones, low, NN)


def decay_parts(forget_pre, bound):
    away = jax.nn.sigmoid(-forget_pre)
    key = jax.nn.sigmoid(-bound) * away
    return key, running(jnp.log(1.0 - key)), away


class States:
    def __init__(self, size, out_state, out_decay, land_state, land_decay, sems):
        self.size = size
        self.here = lax.axis_index("seq")
        self.out_state, self.out_decay = out_state, out_decay
        self.land_state, self.land_decay = land_state, land_decay
        self.sems = sems

    def pair(self, slot, peer):
        s = self.sems
        return (
            remote(self.out_state, self.land_state.at[slot], s.at[0, peer], s.at[1, slot], "seq", peer),
            remote(self.out_decay, self.land_decay.at[slot], s.at[2, peer], s.at[3, slot], "seq", peer),
        )

    def sends(self, later):
        for k in range(self.size):
            yield k, (self.here < k if later else self.here > k)

    def start(self, later):
        for k, wanted in self.sends(later):

            @pl.when(wanted)
            def _():
                for copy in self.pair(self.here, k):
                    copy.start()

    def compose(self, later, state):
        state[...] = jnp.zeros_like(state)
        order = range(self.size) if later else range(self.size - 1, -1, -1)
        for k in order:

            @pl.when(self.here > k if later else self.here < k)
            def _():
                for copy in self.pair(k, k):
                    copy.wait_recv()
                for h in range(state.shape[0]):
                    decay = self.land_decay[k, h : h + 1, :]
                    state[h] = decay * state[h] + self.land_state[k, h].astype(f32)

    def drain(self, later):
        for k, wanted in self.sends(later):

            @pl.when(wanted)
            def _():
                for copy in self.pair(self.here, k):
                    copy.wait_send()


def states_scratch(size, heads):
    return [
        VM((heads, WIDTH, WIDTH), f32),
        VM((heads, WIDTH, WIDTH), bf16),
        VM((8, WIDTH), f32),
        VM((size, heads, WIDTH, WIDTH), bf16),
        VM((size, 8, WIDTH), f32),
        DMA((4, size)),
    ]


def front_kernel(size, groups, rounds, *refs):
    take = taker(refs)
    ends_ref, x_ref, norm_gain_ref, bound_ref, gain_ref, cot_in, *loaded = take(10)
    a_out, q_out, f_out, i_out, s_out, cot_out, o_ref, u_ref, starts_ref = take(9)
    *weights, a_ref, q_ref, f_ref, i_ref, s_ref, cot_ref = take(10)
    qd_ref, kd_ref, qe_ref, adds, decays = take(5)
    state, out_state, out_decay, land_state, land_decay, sems = take(6)
    load_sems, store_sems, a_send, a_recv, c_send, c_recv = take(6)
    me = lax.axis_index("tp")
    m, d = x_ref.shape[1:]
    known = cot_ref.shape[1]
    local = pltpu.make_async_copy
    cot_load = local(cot_in.at[:known], cot_ref.at[me], load_sems.at[4])
    cot_load.start()
    loads = [local(source, target, load_sems.at[k]) for k, (source, target) in enumerate(zip(loaded, weights))]
    for load in loads:
        load.start()
    line, line_count = line_peers(size)
    seq, seq_count = group_peers(groups, "seq")
    greet(line + seq, line_count + seq_count)

    gather = Gather(size, a_send, a_recv, a_ref)
    gather_cot = Gather(size, c_send, c_recv, cot_ref)
    norm_gain = norm_gain_ref[...]

    @pl.loop(0, rounds)
    def _(j):
        @pl.loop(0, m // 16)
        def _(g):
            r = pl.ds(pl.multiple_of(g * 16, 16), 16)
            x = x_ref[j, r, :].astype(f32)
            scale = lax.rsqrt(jnp.mean(x * x, axis=-1, keepdims=True) + epsilon)
            a_ref[me, j, r, :] = (x * scale * norm_gain).astype(bf16)

        gather.start(j)

    for load in loads:
        load.wait()
    cot_load.wait()
    pres = (q_ref, f_ref, i_ref, s_ref)

    @pl.loop(0, rounds)
    def _(j):
        for t in range(1, size):
            gather.step(j, t)

        @pl.when(j >= rounds - known)
        def _():
            gather_cot.start(j - (rounds - known))

        rows = a_ref[:, j].reshape(size * m, d)
        for weight, out in zip(weights, pres):
            product = mul(rows, weight[...], NN)
            for z in range(size):
                at = pl.multiple_of(z * rounds * m + j * m, 16)
                out[pl.ds(at, m), :] = product[z * m : (z + 1) * m]

    stores = [
        local(source, target, store_sems.at[k])
        for k, (source, target) in enumerate(zip((a_ref, *pres), (a_out, q_out, f_out, i_out, s_out)))
    ]
    for store in stores:
        store.start()

    rows, c = q_ref.shape
    blocks, heads = rows // WIDTH, c // WIDTH
    base = lax.axis_index("seq") * rows
    states = States(groups, out_state, out_decay, land_state, land_decay, sems)
    state[...] = jnp.zeros_like(state)
    out_decay[...] = jnp.ones_like(out_decay)

    def cot_steps(t):
        @pl.loop(0, known)
        def _(j):
            gather_cot.step(j, t)

    @pl.loop(0, blocks)
    def _(b):
        r = pl.ds(pl.multiple_of(b * WIDTH, WIDTH), WIDTH)
        same, carry, tail, keep = block_masks(base + b * WIDTH, ends_ref)
        for h in range(heads):
            cols = slice(h * WIDTH, (h + 1) * WIDTH)
            q = q_ref[r, cols]
            q = q * jax.nn.sigmoid(q)
            key, run, _ = decay_parts(f_ref[r, cols], bound_ref[:, cols])
            middle, last = run[WIDTH // 2 - 1 : WIDTH // 2, :], run[WIDTH - 1 :, :]
            qd_ref[r, cols] = (q * jnp.exp(run - middle)).astype(bf16)
            kd_ref[r, cols] = (key * jnp.exp(middle - run)).astype(bf16)
            qe_ref[r, cols] = (q * jnp.exp(run) * carry).astype(bf16)
            key_tail = (key * jnp.exp(last - run) * tail).astype(bf16)
            add = mul(i_ref[r, cols].astype(bf16), key_tail, TN)
            decay = jnp.exp(last) * keep
            adds[b, h] = add
            decays[b, h : h + 1, :] = decay
            state[h] = decay * state[h] + add
            out_decay[h : h + 1, :] = out_decay[h : h + 1, :] * decay

    out_state[...] = state[...].astype(bf16)
    states.start(True)
    cot_steps(1)

    @pl.loop(0, blocks)
    def _(b):
        r = pl.ds(pl.multiple_of(b * WIDTH, WIDTH), WIDTH)
        same, carry, tail, keep = block_masks(base + b * WIDTH, ends_ref)
        for h in range(heads):
            cols = slice(h * WIDTH, (h + 1) * WIDTH)
            scores = jnp.where(same, mul(qd_ref[r, cols], kd_ref[r, cols], NT), 0.0).astype(bf16)
            o_ref[r, cols] = mul(scores, i_ref[r, cols].astype(bf16), NN)

    states.compose(True, state)
    for t in range(2, size - 1):
        cot_steps(t)

    @pl.loop(0, blocks)
    def _(b):
        r = pl.ds(pl.multiple_of(b * WIDTH, WIDTH), WIDTH)
        places = base + b * WIDTH + lax.broadcasted_iota(jnp.int32, (WIDTH, WIDTH), 0)
        valid = jnp.where(places < ends_ref[ends_ref.shape[0] - 1], 1.0, 0.0)
        for h in range(heads):
            cols = slice(h * WIDTH, (h + 1) * WIDTH)
            low = state[h].astype(bf16)
            starts_ref[b, h] = low
            o = o_ref[r, cols] + mul(qe_ref[r, cols], low, NT)
            o_ref[r, cols] = o
            state[h] = decays[b, h : h + 1, :] * state[h] + adds[b, h]
            scale = lax.rsqrt(jnp.mean(o * o, axis=-1, keepdims=True) + epsilon)
            s = s_ref[r, cols]
            z = s * jax.nn.sigmoid(s) * valid
            u_ref[r, cols] = (o * scale * gain_ref[:, cols] * z).astype(bf16)

    cot_steps(size - 1)
    cot_store = local(cot_ref, cot_out, load_sems.at[4])
    cot_store.start()
    states.drain(True)

    @pl.loop(0, rounds)
    def _(j):
        gather.drain(j)

    @pl.loop(0, known)
    def _(j):
        gather_cot.drain(j)

    for store in stores:
        store.wait()
    cot_store.wait()


def front(size, groups, rounds, tokens, cot, norm_gain, weights, ends, bound, gain):
    own, d = tokens.shape
    m, c = own // rounds, weights[0].shape[1]
    rows = size * own
    blocks, heads = rows // WIDTH, c // WIDTH
    known = KNOWN
    shape, some = (size, rounds, m, d), (size, known, m, d)
    wide, low = jax.ShapeDtypeStruct((rows, c), f32), VM((rows, c), bf16)
    spec, far = pl.BlockSpec(memory_space=VM), pl.BlockSpec(memory_space=pl.ANY)
    sems = DMA((2, rounds, size))
    outs = pl.pallas_call(
        partial(front_kernel, size, groups, rounds),
        out_shape=[
            jax.ShapeDtypeStruct(shape, bf16),
            wide,
            wide,
            wide,
            wide,
            jax.ShapeDtypeStruct(some, bf16),
            wide,
            jax.ShapeDtypeStruct((rows, c), bf16),
            jax.ShapeDtypeStruct((blocks, heads, WIDTH, WIDTH), bf16),
        ],
        in_specs=[pl.BlockSpec(memory_space=pltpu.SMEM)] + [spec] * 4 + [far] * 5,
        out_specs=[far] * 6 + [spec] * 3,
        scratch_shapes=[VM((d, c), bf16)] * 4
        + [VM(shape, bf16)]
        + [VM((rows, c), f32)] * 4
        + [VM(some, bf16)]
        + [low] * 3
        + [VM((blocks, heads, WIDTH, WIDTH), f32), VM((blocks, 8, WIDTH), f32)]
        + states_scratch(groups, heads)
        + [DMA((5,)), DMA((5,)), sems, sems, sems, sems],
        compiler_params=pltpu.CompilerParams(collective_id=0, has_side_effects=True, vmem_limit_bytes=60 * MIB),
        cost_estimate=pl.CostEstimate(flops=8 * rows * d * c, bytes_accessed=36 * MIB, transcendentals=8 * rows * c),
        name="front",
    )(
        ends,
        tokens.reshape(rounds, m, d),
        norm_gain.reshape(1, d),
        bound,
        gain,
        cot.reshape(rounds, m, d),
        *weights,
    )
    return [outs[0].reshape(rows, d)] + list(outs[1:])


def scan_back_kernel(size, count, *refs):
    take = taker(refs)
    ends_ref, bound_ref, gain_ref, *loaded = take(10)
    grads = take(count)
    dq_ref, df_ref, di_ref, ds_ref, small_ref = take(5)
    grad_outs = take(count)
    qd_ref, kd_ref, qe_ref, kt_ref, do_ref, run_ref, adds, decays = take(8)
    state, out_state, out_decay, land_state, land_decay, sems = take(6)
    *inputs, load_sems = take(8)
    q_ref, f_ref, i_ref, s_ref, o_ref, ub_ref, starts_ref = inputs
    loads = [
        pltpu.make_async_copy(source, target, load_sems.at[k]) for k, (source, target) in enumerate(zip(loaded, inputs))
    ]
    for load in loads:
        load.start()
    sums = group_sums(size, grads, grad_outs, take)
    greet(*group_peers(size, "seq"))
    rows, c = q_ref.shape
    blocks, heads = rows // WIDTH, c // WIDTH
    base = lax.axis_index("seq") * rows
    states = States(size, out_state, out_decay, land_state, land_decay, sems)
    for each in sums:
        each.start()
    state[...] = jnp.zeros_like(state)
    out_decay[...] = jnp.ones_like(out_decay)
    small_ref[...] = jnp.zeros_like(small_ref)
    for load in loads:
        load.wait()

    @pl.loop(0, blocks)
    def _(back):
        for each in sums[:1]:

            @pl.when(back == 1)
            def _():
                each.middle()

        b = blocks - 1 - back
        r = pl.ds(pl.multiple_of(b * WIDTH, WIDTH), WIDTH)
        same, carry, tail, keep = block_masks(base + b * WIDTH, ends_ref)
        places = base + b * WIDTH + lax.broadcasted_iota(jnp.int32, (WIDTH, WIDTH), 0)
        valid = jnp.where(places < ends_ref[ends_ref.shape[0] - 1], 1.0, 0.0)
        for h in range(heads):
            cols = slice(h * WIDTH, (h + 1) * WIDTH)
            o, s, ub, gain = o_ref[r, cols], s_ref[r, cols], ub_ref[r, cols], gain_ref[:, cols]
            scale = lax.rsqrt(jnp.mean(o * o, axis=-1, keepdims=True) + epsilon)
            normed = o * scale
            gate = jax.nn.sigmoid(s)
            uz = ub * (s * gate * valid)
            small_ref[heads + h : heads + h + 1, :] += jnp.sum(uz * normed, axis=0, keepdims=True)
            nb = uz * gain
            ds_ref[r, cols] = (ub * normed * gain * valid * (gate * (1.0 + s * (1.0 - gate)))).astype(bf16)
            do = (scale * (nb - normed * jnp.mean(nb * normed, axis=-1, keepdims=True))).astype(bf16)
            do_ref[r, cols] = do
            q = q_ref[r, cols]
            q = q * jax.nn.sigmoid(q)
            key, run, _ = decay_parts(f_ref[r, cols], bound_ref[:, cols])
            middle, last = run[WIDTH // 2 - 1 : WIDTH // 2, :], run[WIDTH - 1 :, :]
            run_ref[r, cols] = run
            qd_ref[r, cols] = (q * jnp.exp(run - middle)).astype(bf16)
            kd_ref[r, cols] = (key * jnp.exp(middle - run)).astype(bf16)
            kt_ref[r, cols] = (key * jnp.exp(last - run) * tail).astype(bf16)
            qe = (q * jnp.exp(run) * carry).astype(bf16)
            qe_ref[r, cols] = qe
            add = mul(do, qe, TN)
            decay = jnp.exp(last) * keep
            adds[b, h] = add
            decays[b, h : h + 1, :] = decay
            state[h] = decay * state[h] + add
            out_decay[h : h + 1, :] = out_decay[h : h + 1, :] * decay

    out_state[...] = state[...].astype(bf16)
    states.start(False)
    for each in sums[:1]:
        each.relay()
    for each in sums[1:]:
        each.middle()
    states.compose(False, state)

    @pl.loop(0, blocks)
    def _(back):
        for each in sums[1:]:

            @pl.when(back == blocks // 2)
            def _():
                each.relay()
        b = blocks - 1 - back
        r = pl.ds(pl.multiple_of(b * WIDTH, WIDTH), WIDTH)
        same, carry, tail, keep = block_masks(base + b * WIDTH, ends_ref)
        shape = (WIDTH, WIDTH)
        down, along = lax.broadcasted_iota(jnp.int32, shape, 0), lax.broadcasted_iota(jnp.int32, shape, 1)
        from_here = jnp.where(along >= down, 1.0, 0.0).astype(bf16)
        ahead = jnp.where(along < down, 1.0, 0.0).astype(bf16)
        for h in range(heads):
            cols = slice(h * WIDTH, (h + 1) * WIDTH)
            do, v = do_ref[r, cols], i_ref[r, cols].astype(bf16)
            low, start = state[h].astype(bf16), starts_ref[b, h]
            dq_state = mul(do, start, NN)
            dk_state = mul(v, low, NN)
            kt = kt_ref[r, cols]
            qd, kd = qd_ref[r, cols], kd_ref[r, cols]
            scores = jnp.where(same, mul(qd, kd, NT), 0.0).astype(bf16)
            slopes = jnp.where(same, mul(do, v, NT), 0.0).astype(bf16)
            dq_near = mul(slopes, kd, NN)
            dk_near = mul(slopes, qd, TN)
            di_ref[r, cols] = (mul(scores, do, TN) + mul(kt, low, NT)).astype(bf16)
            run = run_ref[r, cols]
            middle, last = run[WIDTH // 2 - 1 : WIDTH // 2, :], run[WIDTH - 1 :, :]
            q_back = dq_near * jnp.exp(run - middle) + dq_state * (jnp.exp(run) * carry)
            k_back = dk_near * jnp.exp(middle - run) + dk_state * (jnp.exp(last - run) * tail)
            later = (
                qe_ref[r, cols].astype(f32) * dq_state
                + qd.astype(f32) * dq_near
                - kd.astype(f32) * dk_near
            )
            earlier = kt.astype(f32) * dk_state
            decay = decays[b, h : h + 1, :]
            log_back = decay * jnp.sum(low.astype(f32) * start.astype(f32), axis=0, keepdims=True)
            for ones, part in ((from_here, later), (ahead, earlier)):
                high = part.astype(bf16)
                log_back = log_back + mul(ones, high, NN)
                log_back = log_back + mul(ones, (part - high.astype(f32)).astype(bf16), NN)
            f_pre = f_ref[r, cols]
            away, near = jax.nn.sigmoid(-f_pre), jax.nn.sigmoid(f_pre)
            upper = jax.nn.sigmoid(-bound_ref[:, cols])
            lower = jax.nn.sigmoid(bound_ref[:, cols])
            forget_back = log_back / (1.0 - upper * away) - k_back
            slope = forget_back * away * upper
            df_ref[r, cols] = (slope * near).astype(bf16)
            small_ref[h : h + 1, :] += jnp.sum(slope, axis=0, keepdims=True) * lower
            dq_ref[r, cols] = (q_back * silu_slope(q_ref[r, cols])).astype(bf16)
            state[h] = adds[b, h] + decay * state[h]

    for each in sums:
        each.finish()
    states.drain(False)
    for each in sums:
        each.drain()


def scan_backward(size, ends, bound, gain, q, f, i, s, o, ub, starts, grads):
    rows, c = q.shape
    blocks, heads = rows // WIDTH, c // WIDTH
    low, wide = VM((rows, c), bf16), VM((rows, c), f32)
    spec = pl.BlockSpec(memory_space=VM)
    return pl.pallas_call(
        partial(scan_back_kernel, size, len(grads)),
        out_shape=[jax.ShapeDtypeStruct((rows, c), bf16)] * 4
        + [jax.ShapeDtypeStruct((2 * heads, WIDTH), f32)]
        + sum_shapes([grad.shape for grad in grads], [False] * len(grads)),
        in_specs=[pl.BlockSpec(memory_space=pltpu.SMEM)]
        + [spec] * 2
        + [pl.BlockSpec(memory_space=pl.ANY)] * (7 + len(grads)),
        out_specs=[spec] * (5 + len(grads)),
        scratch_shapes=[low] * 5
        + [wide, VM((blocks, heads, WIDTH, WIDTH), f32), VM((blocks, 8, WIDTH), f32)]
        + states_scratch(size, heads)
        + [wide] * 6
        + [VM(starts.shape, bf16), DMA((7,))]
        + group_sums_scratch([grad.shape for grad in grads]),
        compiler_params=pltpu.CompilerParams(collective_id=2, has_side_effects=True, vmem_limit_bytes=60 * MIB),
        cost_estimate=pl.CostEstimate(flops=40 * rows * c * WIDTH, bytes_accessed=20 * MIB, transcendentals=16 * rows * c),
        name="scan_backward",
    )(ends, bound, gain, q, f, i, s, o, ub, starts, *[in_pairs(grad) for grad in grads])


def middle_kernel(size, rounds, *refs):
    take = taker(refs)
    u_ref, x_ref, gain_ref, out_w, *loaded, cot_some, cot_own = take(9)
    res_out, back_out, e_out, ub_out, second_ref, down_out, out_grad, *grad_outs = take(10)
    gate_w, up_w, down_w = weights = take(3)
    cot_ref = take(1)[0]
    b_ref, e_ref, res_ref, back_ref, ub_ref, part, land, total = take(8)
    wide = take(3)
    down_ref, *tiles = take(4)
    load_sems, res_sems, back_sems, e_sems, ub_sem, down_sem, tile_sems = take(7)
    lines = [take(2) for _ in range(5)]
    hidden, gate_back, up_back = wide
    me = lax.axis_index("tp")
    m, d = x_ref.shape[1:]
    ff = gate_w.shape[1]
    group = size * m
    scatter = Scatter(size, *lines[0], part, land, total)
    gather = Gather(size, *lines[1], b_ref)
    scatter_back = Scatter(size, *lines[2], part, land, total)
    gather_back = Gather(size, *lines[3], e_ref)
    gather_cot = Gather(size, *lines[4], cot_ref)
    known = cot_some.shape[1]
    gain = gain_ref[...]
    tile = min(512, d)
    local = pltpu.make_async_copy
    loads = [local(src, dst, load_sems.at[k]) for k, (src, dst) in enumerate(zip(loaded, weights))]
    loads.append(local(cot_some, cot_ref.at[:, :known], load_sems.at[3]))
    cot_load = local(cot_own.at[known:], cot_ref.at[me, known:], load_sems.at[4])
    cot_load.start()
    for load in loads:
        load.start()
    second_ref[...] = jnp.zeros_like(second_ref)
    greet(*line_peers(size))

    def project_out(j):
        rows = u_ref[:, j].reshape(group, u_ref.shape[3])

        @pl.loop(0, d // tile)
        def _(n):
            cols = pl.ds(pl.multiple_of(n * tile, tile), tile)
            part[j, :, :, cols] = mul(rows, out_w[:, cols], NN).astype(bf16).reshape(size, m, tile)

        scatter.start(j)

    def res_copy(j):
        return local(res_ref.at[j], res_out.at[j], res_sems.at[j])

    def back_copy(j):
        return local(back_ref, back_out.at[j], back_sems.at[0])

    def e_copy(j):
        return local(e_ref.at[:, j], e_out.at[:, j], e_sems.at[j])

    def ub_copy(j):
        return local(ub_ref, ub_out.at[:, j], ub_sem.at[0])

    def down_copy(j):
        return local(down_ref, down_out.at[:, j], down_sem.at[0])

    def norm(j):
        @pl.loop(0, m // 16)
        def _(g):
            r = pl.ds(pl.multiple_of(g * 16, 16), 16)
            residual = x_ref[j, r, :].astype(f32) + total[r, :]
            res_ref[j, r, :] = residual
            scale = lax.rsqrt(jnp.mean(residual * residual, axis=-1, keepdims=True) + epsilon)
            b_ref[me, j, r, :] = (residual * scale * gain).astype(bf16)

        gather.start(j)
        res_copy(j).start()

    def feed(j, piece):
        rows = b_ref[:, j].reshape(group, d)
        cot = cot_ref[:, j].reshape(group, d)
        step = 256
        starts = list(range(0, ff, step))
        for low in starts[len(starts) * piece // PIECES : len(starts) * (piece + 1) // PIECES]:
            cols = slice(low, min(low + step, ff))
            width = cols.stop - cols.start
            gate = mul(rows, gate_w[:, cols], NN)
            up = mul(rows, up_w[:, cols], NN)
            hb = mul(cot, down_w[cols, :], NT)
            sig = jax.nn.sigmoid(gate)
            act = gate * sig
            shape = (size, m, width)
            hidden[:, j, :, cols] = (act * up).astype(bf16).reshape(shape)
            up_back[:, j, :, cols] = (hb * act).astype(bf16).reshape(shape)
            gate_back[:, j, :, cols] = (hb * up * (sig * (1.0 + gate * (1.0 - sig)))).astype(bf16).reshape(shape)

    def feed_back(j):
        scatter.drain(j)
        gates = gate_back[:, j].reshape(group, ff)
        ups = up_back[:, j].reshape(group, ff)

        @pl.loop(0, d // tile)
        def _(n):
            cols = pl.ds(pl.multiple_of(n * tile, tile), tile)
            sums = mul(gates, gate_w[cols, :], NT) + mul(ups, up_w[cols, :], NT)
            part[j, :, :, cols] = sums.astype(bf16).reshape(size, m, tile)

        scatter_back.start(j)

    def feed_out(j):
        rows = hidden[:, j].reshape(group, ff)

        @pl.loop(0, d // tile)
        def _(n):
            cols = pl.ds(pl.multiple_of(n * tile, tile), tile)
            down_ref[:, :, cols] = mul(rows, down_w[:, cols], NN).astype(bf16).reshape(size, m, tile)

        down_copy(j).start()

    def norm_back(j):
        @pl.loop(0, m // 16)
        def _(g):
            r = pl.ds(pl.multiple_of(g * 16, 16), 16)
            b_back, residual = total[r, :], res_ref[j, r, :]
            scale = lax.rsqrt(jnp.mean(residual * residual, axis=-1, keepdims=True) + epsilon)
            normed = residual * scale
            second_ref[...] += jnp.sum(b_back * normed, axis=0, keepdims=True)
            inner = b_back * gain
            back = cot_ref[me, j, r, :].astype(f32) + scale * (
                inner - normed * jnp.mean(inner * normed, axis=-1, keepdims=True)
            )
            back_ref[r, :] = back
            e_ref[me, j, r, :] = back.astype(bf16)

        gather_back.start(j)
        back_copy(j).start()

    def unproject(j):
        e_copy(j).start()
        rows = e_ref[:, j].reshape(group, d)
        ub_ref[...] = mul(rows, out_w[...], NT).reshape(size, m, out_w.shape[0])
        ub_copy(j).start()

    depth = tiles[0].shape[0]
    count = d // depth

    def tile_copies(n):
        rows = pl.ds(n * depth, depth)
        return [local(src, dst.at[rows, :], tile_sems.at[k]) for k, (src, dst) in enumerate(zip(tiles, grad_outs))]

    def weight_tile(n):
        cols = pl.ds(n * depth, depth)
        for left, right, out in zip((b_ref, b_ref, cot_ref), (gate_back, up_back, hidden), tiles):
            rows = left[:, :, :, cols].reshape(rounds * group, depth)
            out[...] = mul(rows, right[...].reshape(rounds * group, ff), TN).astype(bf16)
        for copy in tile_copies(n):
            copy.start()

    cot_load.wait()
    held = {}

    def then(kind, copies):
        for copy in held.get(kind, []):
            copy.wait()
        held[kind] = copies

    shares = sum(name[0] == "W" for name in STEPS)
    for name in STEPS:
        kind, j, t = name[0], int(name[1]), int(name[2:] or 0)
        if kind == "A":
            project_out(j)
        elif kind == "C":
            gather_cot.step(j, t) if t else gather_cot.start(j)
        elif kind == "S" and t < size - 1:
            scatter.step(j, t)
        elif kind == "S":
            scatter.finish(j)
            norm(j)
        elif kind == "G":
            gather.step(j, t)
        elif kind == "F":
            then("loads", loads if "loads" not in held else [])
            then("loads", [])
            feed(j, t)
        elif kind == "B":
            feed_back(j)
        elif kind == "O":
            then(kind, [])
            feed_out(j)
            then(kind, [down_copy(j)])
        elif kind == "T" and t < size - 1:
            scatter_back.step(j, t)
        elif kind == "T":
            then(kind, [])
            scatter_back.finish(j)
            norm_back(j)
            then(kind, [back_copy(j)])
        elif kind == "E":
            gather_back.step(j, t)
        elif kind == "U":
            then(kind, [])
            unproject(j)
            then(kind, [ub_copy(j)])
        elif kind == "W":
            for n in range(count * j // shares, count * (j + 1) // shares):
                then(kind, [])
                weight_tile(n)
                then(kind, tile_copies(n))
    for kind in list(held):
        then(kind, [])
    width = u_ref.shape[3]

    def out_tile(n, slot):
        rows = pl.ds(pl.multiple_of(n * depth, depth), depth)
        source = tiles[slot].at[:, pl.ds(0, width)]
        return local(source, out_grad.at[rows, :], tile_sems.at[slot])

    slots = len(tiles) - 1

    @pl.loop(0, count // slots)
    def _(n):
        for slot in range(slots):
            at = n * slots + slot

            @pl.when(n > 0)
            def _():
                out_tile(at - slots, slot).wait()

            cols = pl.ds(pl.multiple_of(at * depth, depth), depth)
            rows = e_ref[:, :, :, cols].reshape(rounds * group, depth)
            tiles[slot][:, :width] = mul(rows, u_ref[...].reshape(rounds * group, width), TN).astype(bf16)
            out_tile(at, slot).start()

    for slot in range(slots):
        out_tile(count - slots + slot, slot).wait()

    @pl.loop(0, rounds)
    def _(j):
        res_copy(j).wait()
        e_copy(j).wait()

        @pl.when(j >= known)
        def _():
            gather_cot.drain(j)

        gather.drain(j)
        scatter_back.drain(j)
        gather_back.drain(j)


def middle(size, rounds, u, x, cot_some, cot, gain, out_w, gate_w, up_w, down_w):
    rows, d = x.shape
    m = rows // rounds
    c, ff = out_w.shape[0], gate_w.shape[1]
    shape = (size, rounds, m)
    sems = DMA((2, rounds, size))
    spec, far = pl.BlockSpec(memory_space=VM), pl.BlockSpec(memory_space=pl.ANY)
    depth = min(256, d)
    outs = pl.pallas_call(
        partial(middle_kernel, size, rounds),
        out_shape=[
            jax.ShapeDtypeStruct((rounds, m, d), f32),
            jax.ShapeDtypeStruct((rounds, m, d), f32),
            jax.ShapeDtypeStruct(shape + (d,), bf16),
            jax.ShapeDtypeStruct(shape + (c,), f32),
            jax.ShapeDtypeStruct((1, d), f32),
            jax.ShapeDtypeStruct(shape + (d,), bf16),
            jax.ShapeDtypeStruct((d, c), bf16),
        ]
        + [jax.ShapeDtypeStruct((d, ff), bf16)] * 3,
        in_specs=[spec] * 4 + [far] * 5,
        out_specs=[far] * 4 + [spec] + [far] * 5,
        scratch_shapes=[
            VM(gate_w.shape, bf16),
            VM(up_w.shape, bf16),
            VM(down_w.shape, bf16),
            VM(shape + (d,), bf16),
            VM(shape + (d,), bf16),
            VM(shape + (d,), bf16),
            VM((rounds, m, d), f32),
            VM((m, d), f32),
            VM((size, m, c), f32),
            VM((rounds, size, m, d), bf16),
            VM((2, rounds, size - 1, m, d), bf16),
            VM((m, d), f32),
        ]
        + [VM(shape + (ff,), bf16)] * 3
        + [VM((size, m, d), bf16)]
        + [VM((depth, ff), bf16)] * 3
        + [DMA((5,)), DMA((rounds,)), DMA((1,)), DMA((rounds,)), DMA((1,)), DMA((1,)), DMA((3,))]
        + [sems] * 10,
        compiler_params=pltpu.CompilerParams(collective_id=3, has_side_effects=True, vmem_limit_bytes=63 * MIB),
        cost_estimate=pl.CostEstimate(
            flops=2 * size * rows * d * (2 * c + 9 * ff), bytes_accessed=56 * MIB, transcendentals=size * rows * ff
        ),
        name="middle",
    )(
        u.reshape(shape + (c,)),
        x.reshape(rounds, m, d),
        gain.reshape(1, d),
        out_w,
        gate_w,
        up_w,
        down_w,
        cot_some,
        cot.reshape(rounds, m, d),
    )
    res, back, e, ub, second, down, *grads = outs
    total = size * rows
    return (
        res.reshape(rows, d),
        back.reshape(rows, d),
        ub.reshape(total, c),
        second,
        down.reshape(total, d),
        *grads,
    )


class Everyone:
    def __init__(self, size, axis, mine, land, sems):
        self.size, self.axis = size, axis
        self.here = lax.axis_index(axis)
        self.mine, self.land, self.sems = mine, land, sems

    def copy(self, slot, peer):
        return remote(self.mine, self.land.at[slot], self.sems.at[0, peer], self.sems.at[1, slot], self.axis, peer)

    def others(self):
        for k in range(self.size):
            yield k, self.here != k

    def start(self):
        for k, other in self.others():

            @pl.when(other)
            def _():
                self.copy(self.here, k).start()

    def finish(self, out):
        out[...] = self.mine[...]
        for k, other in self.others():

            @pl.when(other)
            def _():
                self.copy(k, k).wait_recv()
                out[...] = out[...] + self.land[k]

    def drain(self):
        for k, other in self.others():

            @pl.when(other)
            def _():
                self.copy(self.here, k).wait_send()


def everyone_scratch(size, rows):
    return [VM((rows, WIDTH), f32), VM((size, rows, WIDTH), f32), DMA((2, size))]


def stack(vector, into, at):
    for k in range(vector.shape[1] // WIDTH):
        into[at + k : at + k + 1, :] = vector[:, k * WIDTH : (k + 1) * WIDTH]


def last_kernel(size, groups, rounds, count, mixed, *refs):
    take = taker(refs)
    backs = take(4)
    x_ref, gain_ref, second_ref, small_ref, back_in, a_in, *weights_in = take(10)
    grads = take(count)
    tokens_out, sides_out, small_out = take(3)
    grad_outs = take(count + (4 if mixed else 0))
    part, land, total, first, s_send, s_recv = take(6)
    small_seq, gains_tp = take(3), take(3)
    nears = take(4 if mixed else 0)
    a_ref, *weights, load_sems = take(6)
    sums = group_sums(groups, grads + nears, grad_outs, take)
    early, late = sums[:2], sums[2:]

    seq, seq_count = group_peers(groups, "seq")
    tp, tp_count = group_peers(size, "tp")
    greet(seq + tp, seq_count + tp_count)

    for each in sums[:count]:
        each.start()
    pairs = zip([back_in, a_in, *weights_in], [tokens_out, a_ref, *weights])
    loads = [pltpu.make_async_copy(source, target, load_sems.at[k]) for k, (source, target) in enumerate(pairs)]
    for load in loads[1:] + loads[:1]:
        load.start()

    m, d = x_ref.shape[1:]
    group = size * m
    scatter = Scatter(size, s_send, s_recv, part, land, total)
    gain = gain_ref[...]
    first[...] = jnp.zeros_like(first)
    tile = min(512, d)

    seq_small = Everyone(groups, "seq", *small_seq)
    tp_gains = Everyone(size, "tp", *gains_tp)
    lines, smalls = d // WIDTH, small_ref.shape[0]

    def products(j):
        @pl.loop(0, d // tile)
        def _(n):
            cols = pl.ds(pl.multiple_of(n * tile, tile), tile)
            acc = None
            for back, weight in zip(backs, weights):
                term = mul(back[:, j].reshape(group, back.shape[3]), weight[cols, :], NT)
                acc = term if acc is None else acc + term
            first[:, cols] += jnp.sum(acc * a_ref[:, j, :, cols].reshape(group, tile).astype(f32), axis=0, keepdims=True)
            part[j, :, :, cols] = acc.astype(bf16).reshape(size, m, tile)

        scatter.start(j)

    def mix(back, each):
        rows = back[...].reshape(rounds * group, back.shape[3])
        depth = each.own.shape[1]
        for side, into in ((1 - each.side, each.grad), (each.side, each.own)):

            @pl.loop(0, each.half)
            def _(k):
                cols = pl.ds(pl.multiple_of((2 * k + side) * depth, depth), depth)
                left = a_ref[:, :, :, cols].reshape(rounds * group, depth)
                into[k] = mul(left, rows, TN).astype(bf16)

            if into is each.grad:
                each.start()

    def norm_back(j):
        @pl.loop(0, m // 16)
        def _(g):
            r = pl.ds(pl.multiple_of(g * 16, 16), 16)
            a_back, x = total[r, :], x_ref[j, r, :].astype(f32)
            scale = lax.rsqrt(jnp.mean(x * x, axis=-1, keepdims=True) + epsilon)
            normed = x * scale
            inner = a_back * gain
            tokens_out[j, r, :] = tokens_out[j, r, :] + scale * (
                inner - normed * jnp.mean(inner * normed, axis=-1, keepdims=True)
            )

    def steps(j, low, high):
        for t in range(low, high):
            if t < size - 1:
                scatter.step(j, t)
            else:
                scatter.finish(j)
                norm_back(j)

    for load in loads[1:]:
        load.wait()
    for j in range(rounds):
        products(j)
        if j < len(early):
            early[j].middle()
    stack(second_ref[...], small_seq[0], 0)
    stack(first[...] / gain, small_seq[0], lines)
    small_seq[0][2 * lines : 2 * lines + smalls, :] = small_ref[...]
    seq_small.start()
    steps(0, 1, 2)
    loads[0].wait()
    if mixed:
        for at, (back, each) in enumerate(zip(backs, late)):
            mix(back, each)
            steps(0, 2, 3) if at == 1 else None
    else:
        steps(0, 2, 3)
    for each in early:
        each.relay()
    steps(0, 3, size)
    for each in late:
        each.middle()
    steps(1, 1, 3)
    seq_small.finish(small_out)
    gains_tp[0][...] = small_out[: 2 * lines, :]
    tp_gains.start()
    steps(1, 3, size)
    for each in late[:2]:
        each.relay()
    steps(2, 1, 3)
    for each in late[2:]:
        each.relay()
    steps(2, 3, size)
    for each in early:
        each.finish()
    tp_gains.finish(sides_out)
    for j in range(3, rounds):
        steps(j, 1, size)
    for each in late:
        each.finish()

    for each in sums + [seq_small, tp_gains]:
        each.drain()

    @pl.loop(0, rounds)
    def _(j):
        scatter.drain(j)


def last(size, groups, rounds, backs, weights, a, x, back, gain, second, small, grads, turned):
    mixed = len(turned) > len(grads)
    rows, d = x.shape
    m = rows // rounds
    c = weights[0].shape[1]
    shape = (size, rounds, m)
    lines = d // WIDTH
    sems = DMA((2, rounds, size))
    spec = pl.BlockSpec(memory_space=VM)
    small_rows = 2 * lines + small.shape[0]
    shapes = [grad.shape for grad in grads] + ([(groups, d // groups, c)] * 4 if mixed else [])
    outs = pl.pallas_call(
        partial(last_kernel, size, groups, rounds, len(grads), mixed),
        out_shape=[
            jax.ShapeDtypeStruct((rounds, m, d), f32),
            jax.ShapeDtypeStruct((2 * lines, WIDTH), f32),
            jax.ShapeDtypeStruct((small_rows, WIDTH), f32),
        ]
        + sum_shapes(shapes, turned),
        in_specs=[spec] * 8 + [pl.BlockSpec(memory_space=pl.ANY)] * (6 + len(grads)),
        out_specs=[spec] * (3 + len(shapes)),
        scratch_shapes=[
            VM((rounds, size, m, d), bf16),
            VM((2, rounds, size - 1, m, d), bf16),
            VM((m, d), f32),
            VM((1, d), f32),
            sems,
            sems,
        ]
        + everyone_scratch(groups, small_rows)
        + everyone_scratch(size, 2 * lines)
        + ([VM((groups // 2, d // groups, c), bf16)] * 4 if mixed else [])
        + [VM(shape + (d,), bf16)]
        + [VM((d, c), bf16)] * 4
        + [DMA((6,))]
        + group_sums_scratch(shapes),
        compiler_params=pltpu.CompilerParams(collective_id=4, has_side_effects=True, vmem_limit_bytes=63 * MIB),
        cost_estimate=pl.CostEstimate(flops=16 * size * rows * d * c, bytes_accessed=56 * MIB, transcendentals=0),
        name="last",
    )(
        *[part.reshape(shape + (c,)) for part in backs],
        x.reshape(rounds, m, d),
        gain.reshape(1, d),
        second,
        small,
        back.reshape(rounds, m, d),
        a.reshape(shape + (d,)),
        *weights,
        *[in_pairs(grad) for grad in grads],
    )
    sides = outs[1]
    return (outs[0].reshape(rows, d), sides[:lines], sides[lines:], outs[2][2 * lines :]) + tuple(outs[3:])


def per_device(
    size,
    groups,
    tokens,
    lengths,
    cotangent,
    first_gain,
    query_weight,
    forget_weight,
    input_weight,
    swish_weight,
    bound_logit,
    group_gain,
    out_weight,
    second_gain,
    gate_weight,
    up_weight,
    down_weight,
):
    weights = (query_weight, forget_weight, input_weight, swish_weight)
    ends = jnp.cumsum(lengths).astype(jnp.int32)
    bound, head_gain = bound_logit.reshape(1, -1), group_gain.reshape(1, -1)
    a, q, f, i, s, cot_some, o, u, starts = front(
        size, groups, ROUNDS, tokens, cotangent, first_gain, weights, ends, bound, head_gain
    )
    residual, back, ub, second, down, *wide = middle(
        size, ROUNDS, u, tokens, cot_some, cotangent, second_gain, out_weight, gate_weight, up_weight, down_weight
    )
    down, ub = lax.optimization_barrier((down, ub))
    down = lax.psum_scatter(down, "tp", scatter_dimension=0, tiled=True)
    output = (residual + down.astype(f32)).astype(bf16)
    d = tokens.shape[1]

    def chunks(grad):
        return grad.reshape(groups, grad.shape[0] // groups, grad.shape[1])

    def grad_of(left, right):
        return chunks(lax.dot_general(left, right, TN, preferred_element_type=f32).astype(bf16))

    outs, gates, ups, downs = (chunks(grad) for grad in wide)
    dq, df, di, ds, small, gate_grad, up_grad = scan_backward(
        groups, ends, bound, head_gain, q, f, i, s, o, ub, starts, [gates, ups]
    )
    back_rows = (dq, df, di, ds)
    here_too = groups == 8
    others = [downs, outs] + ([] if here_too else [grad_of(a, part) for part in back_rows])
    tokens_grad, second_sum, first_sum, small_sum, *sums = last(
        size,
        groups,
        ROUNDS,
        back_rows,
        weights,
        a,
        tokens,
        back,
        first_gain,
        second,
        small,
        others,
        [True, True] + [False] * 4,
    )
    down_grad, out_grad, query_grad, forget_grad, input_grad, swish_grad = sums
    heads = bound_logit.shape[0]
    here = lax.axis_index("seq")
    place = here * size + lax.axis_index("tp")
    each = d // (groups * size)
    wide = WIDTH // groups
    first_grad = lax.dynamic_slice_in_dim(first_sum.reshape(-1), place * each, each)
    second_grad = lax.dynamic_slice_in_dim(second_sum.reshape(-1), place * each, each)
    bound_grad = lax.dynamic_slice_in_dim(small_sum[:heads], here * wide, wide, axis=1)
    head_grad = lax.dynamic_slice_in_dim(small_sum[heads:], here * wide, wide, axis=1)
    return (
        output,
        tokens_grad,
        first_grad,
        query_grad,
        forget_grad,
        input_grad,
        swish_grad,
        bound_grad,
        head_grad,
        out_grad,
        second_grad,
        gate_grad,
        up_grad,
        down_grad,
    )


def solution(mesh):
    rows, both, cols, lines = P(("seq", "tp"), None), P(("seq", "tp")), P(None, "tp"), P("tp", None)
    in_specs = (rows, P(), rows, P(), cols, cols, cols, cols, lines, lines, lines, P(), cols, cols, lines)
    down, across = P("seq", "tp"), P("tp", "seq")
    out_specs = (rows, rows, both, down, down, down, down, across, across, across, both, down, down, across)
    return jax.shard_map(
        partial(per_device, mesh.shape["tp"], mesh.shape["seq"]),
        mesh=mesh,
        in_specs=in_specs,
        out_specs=out_specs,
        check_vma=False,
    )
```

```python
from functools import partial

import jax
import jax.numpy as jnp
from jax import lax
from jax.experimental import pallas as pl
from jax.experimental.pallas import tpu as pltpu
from jax.sharding import PartitionSpec as P

WIDTH = 128
ROUNDS = 4
KNOWN = 1
PIECES = 3
STEPS = (
    "C10", "C11", "C20", "A0", "C12", "C13", "A1", "C21", "C22", "C23", "S01", "C30", "S11", "S02", "S03", "A2",
    "A3", "C31", "C32", "C33", "G01", "G02", "S21", "S22", "S12", "S23", "G03", "F00", "F01", "F02", "O0", "S13",
    "B0", "S31", "G11", "T01", "T02", "G12", "G13", "F10", "F11", "F12", "O1", "G21", "T03", "B1", "S32", "G22",
    "G23", "F20", "E01", "F21", "F22", "E02", "E03", "S33", "T11", "T12", "T13", "G31", "O2", "E11", "B2", "U0",
    "T21", "G32", "G33", "F30", "F31", "T22", "F32", "O3", "E12", "T23", "B3", "W0", "E21", "T31", "T32", "E22",
    "W1", "W2", "T33", "W3", "E23", "W5", "E31", "E13", "U1", "W6", "W4", "U2", "W7", "E32", "E33", "U3",
)
MIB = 1 << 20
epsilon = 1e-05

f32 = jnp.float32
bf16 = jnp.bfloat16
NN = (((1,), (0,)), ((), ()))
NT = (((1,), (1,)), ((), ()))
TN = (((0,), (0,)), ((), ()))
VM = pltpu.VMEM
DMA = pltpu.SemaphoreType.DMA
MESH = pl.DeviceIdType.MESH


def mul(left, right, dims):
    return lax.dot_general(left, right, dims, preferred_element_type=f32)


def silu_slope(value):
    gate = jax.nn.sigmoid(value)
    return gate * (1.0 + value * (1.0 - gate))


def remote(src, dst, send, recv, axis, peer):
    return pltpu.make_async_remote_copy(
        src_ref=src,
        dst_ref=dst,
        send_sem=send,
        recv_sem=recv,
        device_id={axis: peer},
        device_id_type=MESH,
    )


def greet(peers, count):
    barrier = pltpu.get_barrier_semaphore()
    for axis, peer, wanted in peers:

        @pl.when(wanted)
        def _():
            pl.semaphore_signal(barrier, inc=1, device_id={axis: peer}, device_id_type=MESH)

    pl.semaphore_wait(barrier, count)


def line_peers(size):
    me = lax.axis_index("tp")
    peers = [("tp", lax.rem(me + 1, size), me < size - 1), ("tp", lax.rem(me + size - 1, size), me > 0)]
    return peers, jnp.where(me < size - 1, 1, 0) + jnp.where(me > 0, 1, 0)


def group_peers(size, axis):
    me = lax.axis_index(axis)
    return [(axis, lax.rem(me + k, size), True) for k in range(1, size)], size - 1


class Line:
    def __init__(self, size, send, recv):
        self.size = size
        self.me = lax.axis_index("tp")
        self.right = lax.rem(self.me + 1, size)
        self.left = lax.rem(self.me + size - 1, size)
        self.send, self.recv = send, recv

    def hop(self, way, src, dst, j, at):
        peer = self.right if way == 0 else self.left
        return remote(src, dst, self.send.at[way, j, at], self.recv.at[way, j, at], "tp", peer)


class Scatter(Line):
    def __init__(self, size, send, recv, part, land, total):
        super().__init__(size, send, recv)
        self.part, self.land, self.total = part, land, total

    def copy(self, way, j, to):
        return self.hop(way, self.part.at[j, to], self.slot(way, j, to), j, to)

    def slot(self, way, j, to):
        return self.land.at[way, j, to - 1 + way]

    def start(self, j):
        last = self.size - 1

        @pl.when(self.me == 0)
        def _():
            for to in range(last, 0, -1):
                self.copy(0, j, to).start()

        @pl.when(self.me == last)
        def _():
            for to in range(last):
                self.copy(1, j, to).start()

    def step(self, j, t):
        last = self.size - 1
        for way in (0, 1):
            place = self.me if way == 0 else last - self.me
            to = last - t + place
            to = to if way == 0 else last - to

            @pl.when((place >= 1) & (place <= t))
            def _():
                copy = self.copy(way, j, to)
                copy.wait_recv()
                self.add(self.part.at[j, to], self.slot(way, j, to))
                copy.start()

    def add(self, into, more):
        rows = into.shape[0]

        @pl.loop(0, rows // 16)
        def _(g):
            r = pl.ds(pl.multiple_of(g * 16, 16), 16)
            into[r, :] = (into[r, :].astype(f32) + more[r, :].astype(f32)).astype(bf16)

    def finish(self, j):
        me, last = self.me, self.size - 1
        rows = self.total.shape[0]

        def over(body):
            @pl.loop(0, rows // 16)
            def _(g):
                body(pl.ds(pl.multiple_of(g * 16, 16), 16))

        def first(r):
            self.total[r, :] = self.part[j, me, r, :].astype(f32)

        over(first)
        for way, there in ((0, me >= 1), (1, me < last)):

            @pl.when(there)
            def _():
                self.copy(way, j, me).wait_recv()

                def more(r):
                    self.total[r, :] = self.total[r, :] + self.land[way, j, me - 1 + way, r, :].astype(f32)

                over(more)

    def drain(self, j):
        for to in range(self.size):

            @pl.when(self.me < to)
            def _():
                self.copy(0, j, to).wait_send()

            @pl.when(self.me > to)
            def _():
                self.copy(1, j, to).wait_send()


class Gather(Line):
    def __init__(self, size, send, recv, whole):
        super().__init__(size, send, recv)
        self.whole = whole

    def copy(self, way, j, source):
        block = self.whole.at[source, j]
        return self.hop(way, block, block, j, source)

    def start(self, j):
        @pl.when(self.me < self.size - 1)
        def _():
            self.copy(0, j, self.me).start()

        @pl.when(self.me > 0)
        def _():
            self.copy(1, j, self.me).start()

    def step(self, j, t):
        last = self.size - 1

        @pl.when(self.me >= t)
        def _():
            copy = self.copy(0, j, self.me - t)
            copy.wait_recv()

            @pl.when(self.me < last)
            def _():
                copy.start()

        @pl.when(self.me + t <= last)
        def _():
            copy = self.copy(1, j, self.me + t)
            copy.wait_recv()

            @pl.when(self.me > 0)
            def _():
                copy.start()

    def drain(self, j):
        last = self.size - 1
        for source in range(self.size):

            @pl.when((self.me >= source) & (self.me < last))
            def _():
                self.copy(0, j, source).wait_send()

            @pl.when((self.me <= source) & (self.me > 0))
            def _():
                self.copy(1, j, source).wait_send()


def add_rows(into, left, right):
    rows = into.shape[0]

    @pl.loop(0, rows // 16)
    def _(g):
        r = pl.ds(pl.multiple_of(g * 16, 16), 16)
        into[r, :] = (left[r, :].astype(f32) + right[r, :].astype(f32)).astype(bf16)


class GroupSum:
    refs = 6

    def __init__(self, size, grad, out, own, got, land, *sems):
        self.half = size // 2
        here = lax.axis_index("seq")
        self.side = lax.rem(here, 2)
        self.mine = here // 2
        self.sibling = here + 1 - 2 * self.side
        self.grad, self.own, self.got, self.land, self.out = grad, own, got, land, out
        self.near_sems, *self.sems = sems
        self.loads = len(grad.shape) == 4
        self.turned = out.shape != own.shape[1:]

    @staticmethod
    def scratch(shape):
        half = shape[0]
        return [VM(shape, bf16)] * 3 + [DMA((3, half)), DMA((half,)), DMA((half,))]

    def near(self, k):
        sems = self.near_sems
        source = self.grad.at[k, 1 - self.side] if self.loads else self.grad.at[k]
        return remote(source, self.got.at[k], sems.at[0, k], sems.at[1, k], "seq", self.sibling)

    def load(self, k):
        return pltpu.make_async_copy(self.grad.at[k, self.side], self.own.at[k], self.near_sems.at[2, k])

    def start(self):
        for k in range(self.half):
            self.near(k).start()
            if self.loads:
                self.load(k).start()

    def pair(self, k, into):
        if self.loads:
            self.load(k).wait()
        self.near(k).wait_recv()
        add_rows(into, self.own.at[k], self.got.at[k])

    def far(self, k):
        send, recv = self.sems
        return remote(self.own.at[k], self.land.at[self.mine], send.at[k], recv.at[self.mine], "seq", 2 * k + self.side)

    def arrival(self, k):
        send, recv = self.sems
        return remote(self.own.at[k], self.land.at[k], send.at[k], recv.at[k], "seq", 2 * k + self.side)

    def middle(self):
        for k in range(self.half):

            @pl.when(k == self.mine)
            def _():
                self.pair(k, self.land.at[k])

            @pl.when(k != self.mine)
            def _():
                self.pair(k, self.own.at[k])
                self.far(k).start()

    def relay(self):
        pass

    def arrive(self):
        for k in range(self.half):

            @pl.when(k != self.mine)
            def _():
                self.arrival(k).wait_recv()

    def terms(self):
        return [self.land.at[k] for k in range(self.half)]

    def finish(self):
        self.arrive()
        rows, cols = self.own.shape[1:]

        def total(r, c):
            acc = None
            for term in self.terms():
                part = term[r, c].astype(f32)
                acc = part if acc is None else acc + part
            return acc

        if self.turned:

            @pl.loop(0, cols // WIDTH)
            def _(g):
                c = pl.ds(pl.multiple_of(g * WIDTH, WIDTH), WIDTH)
                self.out[c, :] = total(slice(None), c).T

        else:

            @pl.loop(0, rows // 16)
            def _(g):
                r = pl.ds(pl.multiple_of(g * 16, 16), 16)
                self.out[r, :] = total(r, slice(None))

    def drain(self):
        for k in range(self.half):
            self.near(k).wait_send()
        self.drain_far()

    def drain_far(self):
        for k in range(self.half):

            @pl.when(k != self.mine)
            def _():
                self.far(k).wait_send()


class SquareSum(GroupSum):
    refs = 6

    def __init__(self, *args):
        super().__init__(*args)
        self.hop, self.far_sems = self.sems
        x, y = lax.rem(self.mine, 2), self.mine // 2
        self.beside = (2 * y + 1 - x, 2 * (1 - y) + x)
        self.opposite = 2 * (1 - y) + 1 - x
        rows = self.own.shape[1] // 2
        self.halves = (pl.ds(0, rows), pl.ds(rows, rows))

    @staticmethod
    def scratch(shape):
        half, rows, cols = shape
        return [
            VM(shape, bf16),
            VM(shape, bf16),
            VM((2, rows, cols), bf16),
            DMA((3, half)),
            VM((2, rows // 2, cols), bf16),
            DMA((2, 6)),
        ]

    def over(self, way, at, source, target):
        sems = self.far_sems
        return remote(source, target, sems.at[0, at], sems.at[1, at], "seq", 2 * self.beside[way] + self.side)

    def pass_on(self, way):
        return self.over(way, way, self.own.at[self.opposite, self.halves[way]], self.hop.at[way])

    def deliver(self, way, half):
        source = self.own.at[self.beside[way], self.halves[half]]
        return self.over(way, 2 + 2 * way + half, source, self.land.at[way, self.halves[half]])

    def middle(self):
        self.pair(self.opposite, self.own.at[self.opposite])
        for way in (0, 1):
            self.pass_on(way).start()
        for way in (0, 1):
            self.pair(self.beside[way], self.own.at[self.beside[way]])
            self.deliver(way, way).start()
        self.pair(self.mine, self.own.at[self.mine])

    def relay(self):
        for way in (0, 1):
            self.pass_on(way).wait_recv()
            into = self.own.at[self.beside[1 - way], self.halves[way]]
            add_rows(into, into, self.hop.at[way])
            self.deliver(1 - way, way).start()

    def arrive(self):
        for way in (0, 1):
            for half in (0, 1):
                self.deliver(way, half).wait_recv()

    def terms(self):
        return [self.own.at[self.mine], self.land.at[0], self.land.at[1]]

    def drain_far(self):
        for way in (0, 1):
            self.pass_on(way).wait_send()
            for half in (0, 1):
                self.deliver(way, half).wait_send()


def summer(size):
    return SquareSum if size == 8 else GroupSum


def group_sums(size, grads, outs, take):
    kind = summer(size)
    return [kind(size, grad, out, *take(kind.refs)) for grad, out in zip(grads, outs)]


def group_sums_scratch(shapes):
    scratch = []
    for size, rows, cols in shapes:
        scratch += summer(size).scratch((size // 2, rows, cols))
    return scratch


def sum_shapes(shapes, turned):
    shapes = [shape[:0:-1] if turn else shape[1:] for shape, turn in zip(shapes, turned)]
    return [jax.ShapeDtypeStruct(shape, f32) for shape in shapes]


def in_pairs(grad):
    return grad.reshape((grad.shape[0] // 2, 2) + grad.shape[1:])


def taker(refs):
    refs = list(refs)

    def take(count):
        taken, refs[:count] = refs[:count], []
        return taken

    return take


def document(rows, ends_ref):
    total = jnp.where(rows >= ends_ref[0], 1, 0)
    for k in range(1, ends_ref.shape[0]):
        total = total + jnp.where(rows >= ends_ref[k], 1, 0)
    return total


def block_masks(first, ends_ref):
    shape = (WIDTH, WIDTH)
    down = lax.broadcasted_iota(jnp.int32, shape, 0)
    along = lax.broadcasted_iota(jnp.int32, shape, 1)
    docs = document(first + down, ends_ref)
    same = (docs == document(first + along, ends_ref)) & (down >= along)
    before = jnp.where(first > 0, document(first - 1, ends_ref), -1)
    final = document(first + WIDTH - 1, ends_ref)
    carry = jnp.where(docs == before, 1.0, 0.0)
    tail = jnp.where(docs == final, 1.0, 0.0)
    keep = jnp.where(final == before, 1.0, 0.0)
    return same, carry, tail, keep


def running(log_forget):
    shape = (WIDTH, WIDTH)
    lower = lax.broadcasted_iota(jnp.int32, shape, 0) >= lax.broadcasted_iota(jnp.int32, shape, 1)
    ones = jnp.where(lower, 1.0, 0.0).astype(bf16)
    high = log_forget.astype(bf16)
    low = (log_forget - high.astype(f32)).astype(bf16)
    return mul(ones, high, NN) + mul(ones, low, NN)


def decay_parts(forget_pre, bound):
    away = jax.nn.sigmoid(-forget_pre)
    key = jax.nn.sigmoid(-bound) * away
    return key, running(jnp.log(1.0 - key)), away


class States:
    def __init__(self, size, out_state, out_decay, land_state, land_decay, sems):
        self.size = size
        self.here = lax.axis_index("seq")
        self.out_state, self.out_decay = out_state, out_decay
        self.land_state, self.land_decay = land_state, land_decay
        self.sems = sems

    def pair(self, slot, peer):
        s = self.sems
        return (
            remote(self.out_state, self.land_state.at[slot], s.at[0, peer], s.at[1, slot], "seq", peer),
            remote(self.out_decay, self.land_decay.at[slot], s.at[2, peer], s.at[3, slot], "seq", peer),
        )

    def sends(self, later):
        for k in range(self.size):
            yield k, (self.here < k if later else self.here > k)

    def start(self, later):
        for k, wanted in self.sends(later):

            @pl.when(wanted)
            def _():
                for copy in self.pair(self.here, k):
                    copy.start()

    def compose(self, later, state):
        state[...] = jnp.zeros_like(state)
        order = range(self.size) if later else range(self.size - 1, -1, -1)
        for k in order:

            @pl.when(self.here > k if later else self.here < k)
            def _():
                for copy in self.pair(k, k):
                    copy.wait_recv()
                for h in range(state.shape[0]):
                    decay = self.land_decay[k, h : h + 1, :]
                    state[h] = decay * state[h] + self.land_state[k, h].astype(f32)

    def drain(self, later):
        for k, wanted in self.sends(later):

            @pl.when(wanted)
            def _():
                for copy in self.pair(self.here, k):
                    copy.wait_send()


def states_scratch(size, heads):
    return [
        VM((heads, WIDTH, WIDTH), f32),
        VM((heads, WIDTH, WIDTH), bf16),
        VM((8, WIDTH), f32),
        VM((size, heads, WIDTH, WIDTH), bf16),
        VM((size, 8, WIDTH), f32),
        DMA((4, size)),
    ]


def front_kernel(size, groups, rounds, *refs):
    take = taker(refs)
    ends_ref, x_ref, norm_gain_ref, bound_ref, gain_ref, cot_in, *loaded = take(10)
    a_out, q_out, f_out, i_out, s_out, cot_out, o_ref, u_ref, starts_ref = take(9)
    *weights, a_ref, q_ref, f_ref, i_ref, s_ref, cot_ref = take(10)
    qd_ref, kd_ref, qe_ref, adds, decays = take(5)
    state, out_state, out_decay, land_state, land_decay, sems = take(6)
    load_sems, store_sems, a_send, a_recv, c_send, c_recv = take(6)
    me = lax.axis_index("tp")
    m, d = x_ref.shape[1:]
    known = cot_ref.shape[1]
    local = pltpu.make_async_copy
    cot_load = local(cot_in.at[:known], cot_ref.at[me], load_sems.at[4])
    cot_load.start()
    loads = [local(source, target, load_sems.at[k]) for k, (source, target) in enumerate(zip(loaded, weights))]
    for load in loads:
        load.start()
    line, line_count = line_peers(size)
    seq, seq_count = group_peers(groups, "seq")
    greet(line + seq, line_count + seq_count)

    gather = Gather(size, a_send, a_recv, a_ref)
    gather_cot = Gather(size, c_send, c_recv, cot_ref)
    norm_gain = norm_gain_ref[...]

    @pl.loop(0, rounds)
    def _(j):
        @pl.loop(0, m // 16)
        def _(g):
            r = pl.ds(pl.multiple_of(g * 16, 16), 16)
            x = x_ref[j, r, :].astype(f32)
            scale = lax.rsqrt(jnp.mean(x * x, axis=-1, keepdims=True) + epsilon)
            a_ref[me, j, r, :] = (x * scale * norm_gain).astype(bf16)

        gather.start(j)

    for load in loads:
        load.wait()
    cot_load.wait()
    pres = (q_ref, f_ref, i_ref, s_ref)

    rows, c = q_ref.shape
    blocks, heads = rows // WIDTH, c // WIDTH
    base = lax.axis_index("seq") * rows
    states = States(groups, out_state, out_decay, land_state, land_decay, sems)
    state[...] = jnp.zeros_like(state)
    out_decay[...] = jnp.ones_like(out_decay)

    def cot_steps(t):
        @pl.loop(0, known)
        def _(j):
            gather_cot.step(j, t)

    def block(b):
        r = pl.ds(pl.multiple_of(b * WIDTH, WIDTH), WIDTH)
        same, carry, tail, keep = block_masks(base + b * WIDTH, ends_ref)
        for h in range(heads):
            cols = slice(h * WIDTH, (h + 1) * WIDTH)
            q = q_ref[r, cols]
            q = q * jax.nn.sigmoid(q)
            key, run, _ = decay_parts(f_ref[r, cols], bound_ref[:, cols])
            middle, last = run[WIDTH // 2 - 1 : WIDTH // 2, :], run[WIDTH - 1 :, :]
            qd_ref[r, cols] = (q * jnp.exp(run - middle)).astype(bf16)
            kd_ref[r, cols] = (key * jnp.exp(middle - run)).astype(bf16)
            qe_ref[r, cols] = (q * jnp.exp(run) * carry).astype(bf16)
            key_tail = (key * jnp.exp(last - run) * tail).astype(bf16)
            adds[b, h] = mul(i_ref[r, cols].astype(bf16), key_tail, TN)
            decays[b, h : h + 1, :] = jnp.exp(last) * keep

    def near_part(b):
        r = pl.ds(pl.multiple_of(b * WIDTH, WIDTH), WIDTH)
        same, carry, tail, keep = block_masks(base + b * WIDTH, ends_ref)
        for h in range(heads):
            cols = slice(h * WIDTH, (h + 1) * WIDTH)
            scores = jnp.where(same, mul(qd_ref[r, cols], kd_ref[r, cols], NT), 0.0).astype(bf16)
            o_ref[r, cols] = mul(scores, i_ref[r, cols].astype(bf16), NN)

    own_rows = rounds * m
    per = own_rows // WIDTH if own_rows % WIDTH == 0 and WIDTH % m == 0 else 0
    early = [z * per + k for z in range(size) for k in range(per - 1)] if per > 1 else []
    late = [b for b in range(blocks) if b not in early]
    ready = (per - 1) * WIDTH // m if early else rounds

    def some_blocks(chosen, body):
        if chosen is early and early:

            @pl.loop(0, size)
            def _(z):
                for k in range(per - 1):
                    body(z * per + k)

        elif early:

            @pl.loop(0, size)
            def _(z):
                body(z * per + per - 1)

        elif chosen is late:
            pl.loop(0, blocks)(body)

    def project(j):
        block_rows = a_ref[:, j].reshape(size * m, d)
        for weight, out in zip(weights, pres):
            product = mul(block_rows, weight[...], NN)
            for z in range(size):
                at = pl.multiple_of(z * own_rows + j * m, 16)
                out[pl.ds(at, m), :] = product[z * m : (z + 1) * m]

    @pl.loop(0, rounds)
    def _(j):
        for t in range(1, size):
            gather.step(j, t)
            if early and t == 1:

                @pl.when(j == ready)
                def _():
                    some_blocks(early, block)

            if early and t == 2:

                @pl.when(j == ready)
                def _():
                    some_blocks(early, near_part)

        @pl.when(j >= rounds - known)
        def _():
            gather_cot.start(j - (rounds - known))

        project(j)

    stores = [
        local(source, target, store_sems.at[k])
        for k, (source, target) in enumerate(zip((a_ref, *pres), (a_out, q_out, f_out, i_out, s_out)))
    ]
    for store in stores:
        store.start()

    some_blocks(late, block)

    @pl.loop(0, blocks)
    def _(b):
        for h in range(heads):
            decay = decays[b, h : h + 1, :]
            state[h] = decay * state[h] + adds[b, h]
            out_decay[h : h + 1, :] = out_decay[h : h + 1, :] * decay

    out_state[...] = state[...].astype(bf16)
    states.start(True)
    cot_steps(1)
    some_blocks(late, near_part)

    states.compose(True, state)
    for t in range(2, size - 1):
        cot_steps(t)

    @pl.loop(0, blocks)
    def _(b):
        r = pl.ds(pl.multiple_of(b * WIDTH, WIDTH), WIDTH)
        places = base + b * WIDTH + lax.broadcasted_iota(jnp.int32, (WIDTH, WIDTH), 0)
        valid = jnp.where(places < ends_ref[ends_ref.shape[0] - 1], 1.0, 0.0)
        for h in range(heads):
            cols = slice(h * WIDTH, (h + 1) * WIDTH)
            low = state[h].astype(bf16)
            starts_ref[b, h] = low
            o = o_ref[r, cols] + mul(qe_ref[r, cols], low, NT)
            o_ref[r, cols] = o
            state[h] = decays[b, h : h + 1, :] * state[h] + adds[b, h]
            scale = lax.rsqrt(jnp.mean(o * o, axis=-1, keepdims=True) + epsilon)
            s = s_ref[r, cols]
            z = s * jax.nn.sigmoid(s) * valid
            u_ref[r, cols] = (o * scale * gain_ref[:, cols] * z).astype(bf16)

    cot_steps(size - 1)
    cot_store = local(cot_ref, cot_out, load_sems.at[4])
    cot_store.start()
    states.drain(True)

    @pl.loop(0, rounds)
    def _(j):
        gather.drain(j)

    @pl.loop(0, known)
    def _(j):
        gather_cot.drain(j)

    for store in stores:
        store.wait()
    cot_store.wait()


def front(size, groups, rounds, tokens, cot, norm_gain, weights, ends, bound, gain):
    own, d = tokens.shape
    m, c = own // rounds, weights[0].shape[1]
    rows = size * own
    blocks, heads = rows // WIDTH, c // WIDTH
    known = KNOWN
    shape, some = (size, rounds, m, d), (size, known, m, d)
    wide, low = jax.ShapeDtypeStruct((rows, c), f32), VM((rows, c), bf16)
    spec, far = pl.BlockSpec(memory_space=VM), pl.BlockSpec(memory_space=pl.ANY)
    sems = DMA((2, rounds, size))
    outs = pl.pallas_call(
        partial(front_kernel, size, groups, rounds),
        out_shape=[
            jax.ShapeDtypeStruct(shape, bf16),
            wide,
            wide,
            wide,
            wide,
            jax.ShapeDtypeStruct(some, bf16),
            wide,
            jax.ShapeDtypeStruct((rows, c), bf16),
            jax.ShapeDtypeStruct((blocks, heads, WIDTH, WIDTH), bf16),
        ],
        in_specs=[pl.BlockSpec(memory_space=pltpu.SMEM)] + [spec] * 4 + [far] * 5,
        out_specs=[far] * 6 + [spec] * 3,
        scratch_shapes=[VM((d, c), bf16)] * 4
        + [VM(shape, bf16)]
        + [VM((rows, c), f32)] * 4
        + [VM(some, bf16)]
        + [low] * 3
        + [VM((blocks, heads, WIDTH, WIDTH), f32), VM((blocks, 8, WIDTH), f32)]
        + states_scratch(groups, heads)
        + [DMA((5,)), DMA((5,)), sems, sems, sems, sems],
        compiler_params=pltpu.CompilerParams(collective_id=0, has_side_effects=True, vmem_limit_bytes=60 * MIB),
        cost_estimate=pl.CostEstimate(flops=8 * rows * d * c, bytes_accessed=36 * MIB, transcendentals=8 * rows * c),
        name="front",
    )(
        ends,
        tokens.reshape(rounds, m, d),
        norm_gain.reshape(1, d),
        bound,
        gain,
        cot.reshape(rounds, m, d),
        *weights,
    )
    return [outs[0].reshape(rows, d)] + list(outs[1:])


def scan_back_kernel(size, line, rounds, count, *refs):
    take = taker(refs)
    ends_ref, bound_ref, gain_ref, norm_gain_ref, *loaded = take(16)
    grads = take(count)
    dq_ref, df_ref, di_ref, ds_ref, small_ref, first_ref, part_out = take(7)
    grad_outs = take(count)
    qd_ref, kd_ref, qe_ref, kt_ref, do_ref, run_ref, adds, decays = take(8)
    state, out_state, out_decay, land_state, land_decay, sems = take(6)
    *inputs, load_sems = take(13)
    q_ref, f_ref, i_ref, s_ref, o_ref, ub_ref, starts_ref, *weights, a_ref = inputs
    *loaded, a_in = loaded
    stage, stage_sems, a_sems = take(3)
    loads = [
        pltpu.make_async_copy(source, target, load_sems.at[k]) for k, (source, target) in enumerate(zip(loaded, inputs))
    ]
    for load in loads:
        load.start()
    sums = group_sums(size, grads, grad_outs, take)
    greet(*group_peers(size, "seq"))
    rows, c = q_ref.shape
    blocks, heads = rows // WIDTH, c // WIDTH
    base = lax.axis_index("seq") * rows
    states = States(size, out_state, out_decay, land_state, land_decay, sems)
    for each in sums:
        each.start()
    state[...] = jnp.zeros_like(state)
    out_decay[...] = jnp.ones_like(out_decay)
    small_ref[...] = jnp.zeros_like(small_ref)
    for load in loads[:7]:
        load.wait()

    @pl.loop(0, blocks)
    def _(back):
        for each in sums[:1]:

            @pl.when(back == 1)
            def _():
                each.middle()

        b = blocks - 1 - back
        r = pl.ds(pl.multiple_of(b * WIDTH, WIDTH), WIDTH)
        same, carry, tail, keep = block_masks(base + b * WIDTH, ends_ref)
        places = base + b * WIDTH + lax.broadcasted_iota(jnp.int32, (WIDTH, WIDTH), 0)
        valid = jnp.where(places < ends_ref[ends_ref.shape[0] - 1], 1.0, 0.0)
        for h in range(heads):
            cols = slice(h * WIDTH, (h + 1) * WIDTH)
            o, s, ub, gain = o_ref[r, cols], s_ref[r, cols], ub_ref[r, cols], gain_ref[:, cols]
            scale = lax.rsqrt(jnp.mean(o * o, axis=-1, keepdims=True) + epsilon)
            normed = o * scale
            gate = jax.nn.sigmoid(s)
            uz = ub * (s * gate * valid)
            small_ref[heads + h : heads + h + 1, :] += jnp.sum(uz * normed, axis=0, keepdims=True)
            nb = uz * gain
            ds_ref[r, cols] = (ub * normed * gain * valid * (gate * (1.0 + s * (1.0 - gate)))).astype(bf16)
            do = (scale * (nb - normed * jnp.mean(nb * normed, axis=-1, keepdims=True))).astype(bf16)
            do_ref[r, cols] = do
            q = q_ref[r, cols]
            q = q * jax.nn.sigmoid(q)
            key, run, _ = decay_parts(f_ref[r, cols], bound_ref[:, cols])
            middle, last = run[WIDTH // 2 - 1 : WIDTH // 2, :], run[WIDTH - 1 :, :]
            run_ref[r, cols] = run
            qd_ref[r, cols] = (q * jnp.exp(run - middle)).astype(bf16)
            kd_ref[r, cols] = (key * jnp.exp(middle - run)).astype(bf16)
            kt_ref[r, cols] = (key * jnp.exp(last - run) * tail).astype(bf16)
            qe = (q * jnp.exp(run) * carry).astype(bf16)
            qe_ref[r, cols] = qe
            add = mul(do, qe, TN)
            decay = jnp.exp(last) * keep
            adds[b, h] = add
            decays[b, h : h + 1, :] = decay
            state[h] = decay * state[h] + add
            out_decay[h : h + 1, :] = out_decay[h : h + 1, :] * decay

    out_state[...] = state[...].astype(bf16)
    states.start(False)
    for each in sums[:1]:
        each.relay()
    for each in sums[1:]:
        each.middle()
    states.compose(False, state)

    @pl.loop(0, blocks)
    def _(back):
        for each in sums[1:]:

            @pl.when(back == blocks // 2)
            def _():
                each.relay()
        b = blocks - 1 - back
        r = pl.ds(pl.multiple_of(b * WIDTH, WIDTH), WIDTH)
        same, carry, tail, keep = block_masks(base + b * WIDTH, ends_ref)
        shape = (WIDTH, WIDTH)
        down, along = lax.broadcasted_iota(jnp.int32, shape, 0), lax.broadcasted_iota(jnp.int32, shape, 1)
        from_here = jnp.where(along >= down, 1.0, 0.0).astype(bf16)
        ahead = jnp.where(along < down, 1.0, 0.0).astype(bf16)
        for h in range(heads):
            cols = slice(h * WIDTH, (h + 1) * WIDTH)
            do, v = do_ref[r, cols], i_ref[r, cols].astype(bf16)
            low, start = state[h].astype(bf16), starts_ref[b, h]
            dq_state = mul(do, start, NN)
            dk_state = mul(v, low, NN)
            kt = kt_ref[r, cols]
            qd, kd = qd_ref[r, cols], kd_ref[r, cols]
            scores = jnp.where(same, mul(qd, kd, NT), 0.0).astype(bf16)
            slopes = jnp.where(same, mul(do, v, NT), 0.0).astype(bf16)
            dq_near = mul(slopes, kd, NN)
            dk_near = mul(slopes, qd, TN)
            di_ref[r, cols] = (mul(scores, do, TN) + mul(kt, low, NT)).astype(bf16)
            run = run_ref[r, cols]
            middle, last = run[WIDTH // 2 - 1 : WIDTH // 2, :], run[WIDTH - 1 :, :]
            q_back = dq_near * jnp.exp(run - middle) + dq_state * (jnp.exp(run) * carry)
            k_back = dk_near * jnp.exp(middle - run) + dk_state * (jnp.exp(last - run) * tail)
            later = (
                qe_ref[r, cols].astype(f32) * dq_state
                + qd.astype(f32) * dq_near
                - kd.astype(f32) * dk_near
            )
            earlier = kt.astype(f32) * dk_state
            decay = decays[b, h : h + 1, :]
            log_back = decay * jnp.sum(low.astype(f32) * start.astype(f32), axis=0, keepdims=True)
            for ones, part in ((from_here, later), (ahead, earlier)):
                high = part.astype(bf16)
                log_back = log_back + mul(ones, high, NN)
                log_back = log_back + mul(ones, (part - high.astype(f32)).astype(bf16), NN)
            f_pre = f_ref[r, cols]
            away, near = jax.nn.sigmoid(-f_pre), jax.nn.sigmoid(f_pre)
            upper = jax.nn.sigmoid(-bound_ref[:, cols])
            lower = jax.nn.sigmoid(bound_ref[:, cols])
            forget_back = log_back / (1.0 - upper * away) - k_back
            slope = forget_back * away * upper
            df_ref[r, cols] = (slope * near).astype(bf16)
            small_ref[h : h + 1, :] += jnp.sum(slope, axis=0, keepdims=True) * lower
            dq_ref[r, cols] = (q_back * silu_slope(q_ref[r, cols])).astype(bf16)
            state[h] = adds[b, h] + decay * state[h]

    for load in loads[7:]:
        load.wait()
    m, d = a_ref.shape[2:]

    def a_load(j):
        slot = lax.rem(j, 2)
        return pltpu.make_async_copy(a_in.at[:, j], a_ref.at[slot], a_sems.at[slot])

    for j in range(min(2, rounds)):
        a_load(j).start()
    tile = min(512, d)
    first_ref[...] = jnp.zeros_like(first_ref)

    def part_copy(j):
        return pltpu.make_async_copy(stage.at[lax.rem(j, 2)], part_out.at[j], stage_sems.at[lax.rem(j, 2)])

    @pl.loop(0, rounds)
    def _(j):
        @pl.when(j > 1)
        def _():
            part_copy(j - 2).wait()

        a_load(j).wait()

        def round_rows(ref):
            places = [pl.multiple_of(z * rounds * m + j * m, 16) for z in range(line)]
            return jnp.concatenate([ref[pl.ds(at, m), :] for at in places], axis=0)

        @pl.loop(0, d // tile)
        def _(n):
            cols = pl.ds(pl.multiple_of(n * tile, tile), tile)
            acc = None
            for back, weight in zip((dq_ref, df_ref, di_ref, ds_ref), weights):
                term = mul(round_rows(back), weight[cols, :], NT)
                acc = term if acc is None else acc + term
            normed = a_ref[lax.rem(j, 2), :, :, cols].reshape(line * m, tile).astype(f32)
            first_ref[:, cols] += jnp.sum(acc * normed, axis=0, keepdims=True)
            stage[lax.rem(j, 2), :, :, cols] = acc.astype(bf16).reshape(line, m, tile)

        part_copy(j).start()

        @pl.when(j + 2 < rounds)
        def _():
            a_load(j + 2).start()

    first_ref[...] = first_ref[...] / norm_gain_ref[...]
    for each in sums:
        each.finish()
    for j in range(max(0, rounds - 2), rounds):
        part_copy(j).wait()
    states.drain(False)
    for each in sums:
        each.drain()


def scan_backward(size, line, rounds, ends, bound, gain, q, f, i, s, o, ub, starts, norm_gain, a, weights, grads):
    rows, c = q.shape
    d = a.shape[1]
    shape = (line, rounds, rows // line // rounds, d)
    part = (rounds, line) + shape[2:]
    blocks, heads = rows // WIDTH, c // WIDTH
    low, wide = VM((rows, c), bf16), VM((rows, c), f32)
    spec = pl.BlockSpec(memory_space=VM)
    return pl.pallas_call(
        partial(scan_back_kernel, size, line, rounds, len(grads)),
        out_shape=[jax.ShapeDtypeStruct((rows, c), bf16)] * 4
        + [jax.ShapeDtypeStruct((2 * heads, WIDTH), f32), jax.ShapeDtypeStruct((1, d), f32)]
        + [jax.ShapeDtypeStruct(part, bf16)]
        + sum_shapes([grad.shape for grad in grads], [False] * len(grads)),
        in_specs=[pl.BlockSpec(memory_space=pltpu.SMEM)]
        + [spec] * 3
        + [pl.BlockSpec(memory_space=pl.ANY)] * (12 + len(grads)),
        out_specs=[spec] * 6 + [pl.BlockSpec(memory_space=pl.ANY)] + [spec] * len(grads),
        scratch_shapes=[low] * 5
        + [wide, VM((blocks, heads, WIDTH, WIDTH), f32), VM((blocks, 8, WIDTH), f32)]
        + states_scratch(size, heads)
        + [wide] * 6
        + [VM(starts.shape, bf16)]
        + [VM((d, c), bf16)] * 4
        + [VM((2,) + part[1:], bf16), DMA((11,)), VM((2,) + part[1:], bf16), DMA((2,)), DMA((2,))]
        + group_sums_scratch([grad.shape for grad in grads]),
        compiler_params=pltpu.CompilerParams(collective_id=2, has_side_effects=True, vmem_limit_bytes=63 * MIB),
        cost_estimate=pl.CostEstimate(flops=8 * rows * c * d, bytes_accessed=40 * MIB, transcendentals=16 * rows * c),
        name="scan_backward",
    )(
        ends,
        bound,
        gain,
        norm_gain.reshape(1, d),
        q,
        f,
        i,
        s,
        o,
        ub,
        starts,
        *weights,
        a.reshape(shape),
        *[in_pairs(grad) for grad in grads],
    )


def middle_kernel(size, rounds, *refs):
    take = taker(refs)
    u_ref, x_ref, gain_ref, out_w, *loaded, cot_some, cot_own = take(9)
    res_out, back_out, e_out, ub_out, second_ref, down_out, out_grad, *grad_outs = take(10)
    gate_w, up_w, down_w = weights = take(3)
    cot_ref = take(1)[0]
    b_ref, e_ref, res_ref, back_ref, ub_ref, part, land, total = take(8)
    wide = take(3)
    down_ref, *tiles = take(4)
    load_sems, res_sems, back_sems, e_sems, ub_sem, down_sem, tile_sems = take(7)
    lines = [take(2) for _ in range(5)]
    hidden, gate_back, up_back = wide
    me = lax.axis_index("tp")
    m, d = x_ref.shape[1:]
    ff = gate_w.shape[1]
    group = size * m
    scatter = Scatter(size, *lines[0], part, land, total)
    gather = Gather(size, *lines[1], b_ref)
    scatter_back = Scatter(size, *lines[2], part, land, total)
    gather_back = Gather(size, *lines[3], e_ref)
    gather_cot = Gather(size, *lines[4], cot_ref)
    known = cot_some.shape[1]
    gain = gain_ref[...]
    tile = min(512, d)
    local = pltpu.make_async_copy
    loads = [local(src, dst, load_sems.at[k]) for k, (src, dst) in enumerate(zip(loaded, weights))]
    loads.append(local(cot_some, cot_ref.at[:, :known], load_sems.at[3]))
    cot_load = local(cot_own.at[known:], cot_ref.at[me, known:], load_sems.at[4])
    cot_load.start()
    for load in loads:
        load.start()
    second_ref[...] = jnp.zeros_like(second_ref)
    greet(*line_peers(size))

    def project_out(j):
        rows = u_ref[:, j].reshape(group, u_ref.shape[3])

        @pl.loop(0, d // tile)
        def _(n):
            cols = pl.ds(pl.multiple_of(n * tile, tile), tile)
            part[j, :, :, cols] = mul(rows, out_w[:, cols], NN).astype(bf16).reshape(size, m, tile)

        scatter.start(j)

    def res_copy(j):
        return local(res_ref.at[j], res_out.at[j], res_sems.at[j])

    def back_copy(j):
        return local(back_ref, back_out.at[j], back_sems.at[0])

    def e_copy(j):
        return local(e_ref.at[:, j], e_out.at[:, j], e_sems.at[j])

    def ub_copy(j):
        return local(ub_ref, ub_out.at[:, j], ub_sem.at[0])

    def down_copy(j):
        return local(down_ref, down_out.at[:, j], down_sem.at[0])

    def norm(j):
        @pl.loop(0, m // 16)
        def _(g):
            r = pl.ds(pl.multiple_of(g * 16, 16), 16)
            residual = x_ref[j, r, :].astype(f32) + total[r, :]
            res_ref[j, r, :] = residual
            scale = lax.rsqrt(jnp.mean(residual * residual, axis=-1, keepdims=True) + epsilon)
            b_ref[me, j, r, :] = (residual * scale * gain).astype(bf16)

        gather.start(j)
        res_copy(j).start()

    def feed(j, piece):
        rows = b_ref[:, j].reshape(group, d)
        cot = cot_ref[:, j].reshape(group, d)
        step = 256
        starts = list(range(0, ff, step))
        for low in starts[len(starts) * piece // PIECES : len(starts) * (piece + 1) // PIECES]:
            cols = slice(low, min(low + step, ff))
            width = cols.stop - cols.start
            gate = mul(rows, gate_w[:, cols], NN)
            up = mul(rows, up_w[:, cols], NN)
            hb = mul(cot, down_w[cols, :], NT)
            sig = jax.nn.sigmoid(gate)
            act = gate * sig
            shape = (size, m, width)
            hidden[:, j, :, cols] = (act * up).astype(bf16).reshape(shape)
            up_back[:, j, :, cols] = (hb * act).astype(bf16).reshape(shape)
            gate_back[:, j, :, cols] = (hb * up * (sig * (1.0 + gate * (1.0 - sig)))).astype(bf16).reshape(shape)

    def feed_back(j):
        scatter.drain(j)
        gates = gate_back[:, j].reshape(group, ff)
        ups = up_back[:, j].reshape(group, ff)

        @pl.loop(0, d // tile)
        def _(n):
            cols = pl.ds(pl.multiple_of(n * tile, tile), tile)
            sums = mul(gates, gate_w[cols, :], NT) + mul(ups, up_w[cols, :], NT)
            part[j, :, :, cols] = sums.astype(bf16).reshape(size, m, tile)

        scatter_back.start(j)

    def feed_out(j):
        rows = hidden[:, j].reshape(group, ff)

        @pl.loop(0, d // tile)
        def _(n):
            cols = pl.ds(pl.multiple_of(n * tile, tile), tile)
            down_ref[:, :, cols] = mul(rows, down_w[:, cols], NN).astype(bf16).reshape(size, m, tile)

        down_copy(j).start()

    def norm_back(j):
        @pl.loop(0, m // 16)
        def _(g):
            r = pl.ds(pl.multiple_of(g * 16, 16), 16)
            b_back, residual = total[r, :], res_ref[j, r, :]
            scale = lax.rsqrt(jnp.mean(residual * residual, axis=-1, keepdims=True) + epsilon)
            normed = residual * scale
            second_ref[...] += jnp.sum(b_back * normed, axis=0, keepdims=True)
            inner = b_back * gain
            back = cot_ref[me, j, r, :].astype(f32) + scale * (
                inner - normed * jnp.mean(inner * normed, axis=-1, keepdims=True)
            )
            back_ref[r, :] = back
            e_ref[me, j, r, :] = back.astype(bf16)

        gather_back.start(j)
        back_copy(j).start()

    def unproject(j):
        e_copy(j).start()
        rows = e_ref[:, j].reshape(group, d)
        ub_ref[...] = mul(rows, out_w[...], NT).reshape(size, m, out_w.shape[0])
        ub_copy(j).start()

    depth = tiles[0].shape[0]
    count = d // depth

    def tile_copies(n):
        rows = pl.ds(n * depth, depth)
        return [local(src, dst.at[rows, :], tile_sems.at[k]) for k, (src, dst) in enumerate(zip(tiles, grad_outs))]

    def weight_tile(n):
        cols = pl.ds(n * depth, depth)
        for left, right, out in zip((b_ref, b_ref, cot_ref), (gate_back, up_back, hidden), tiles):
            rows = left[:, :, :, cols].reshape(rounds * group, depth)
            out[...] = mul(rows, right[...].reshape(rounds * group, ff), TN).astype(bf16)
        for copy in tile_copies(n):
            copy.start()

    cot_load.wait()
    held = {}

    def then(kind, copies):
        for copy in held.get(kind, []):
            copy.wait()
        held[kind] = copies

    shares = sum(name[0] == "W" for name in STEPS)
    for name in STEPS:
        kind, j, t = name[0], int(name[1]), int(name[2:] or 0)
        if kind == "A":
            project_out(j)
        elif kind == "C":
            gather_cot.step(j, t) if t else gather_cot.start(j)
        elif kind == "S" and t < size - 1:
            scatter.step(j, t)
        elif kind == "S":
            scatter.finish(j)
            norm(j)
        elif kind == "G":
            gather.step(j, t)
        elif kind == "F":
            then("loads", loads if "loads" not in held else [])
            then("loads", [])
            feed(j, t)
        elif kind == "B":
            feed_back(j)
        elif kind == "O":
            then(kind, [])
            feed_out(j)
            then(kind, [down_copy(j)])
        elif kind == "T" and t < size - 1:
            scatter_back.step(j, t)
        elif kind == "T":
            then(kind, [])
            scatter_back.finish(j)
            norm_back(j)
            then(kind, [back_copy(j)])
        elif kind == "E":
            gather_back.step(j, t)
        elif kind == "U":
            then(kind, [])
            unproject(j)
            then(kind, [ub_copy(j)])
        elif kind == "W":
            for n in range(count * j // shares, count * (j + 1) // shares):
                then(kind, [])
                weight_tile(n)
                then(kind, tile_copies(n))
    for kind in list(held):
        then(kind, [])
    width = u_ref.shape[3]

    def out_tile(n, slot):
        rows = pl.ds(pl.multiple_of(n * depth, depth), depth)
        source = tiles[slot].at[:, pl.ds(0, width)]
        return local(source, out_grad.at[rows, :], tile_sems.at[slot])

    slots = len(tiles) - 1

    @pl.loop(0, count // slots)
    def _(n):
        for slot in range(slots):
            at = n * slots + slot

            @pl.when(n > 0)
            def _():
                out_tile(at - slots, slot).wait()

            cols = pl.ds(pl.multiple_of(at * depth, depth), depth)
            rows = e_ref[:, :, :, cols].reshape(rounds * group, depth)
            tiles[slot][:, :width] = mul(rows, u_ref[...].reshape(rounds * group, width), TN).astype(bf16)
            out_tile(at, slot).start()

    for slot in range(slots):
        out_tile(count - slots + slot, slot).wait()

    @pl.loop(0, rounds)
    def _(j):
        res_copy(j).wait()
        e_copy(j).wait()

        @pl.when(j >= known)
        def _():
            gather_cot.drain(j)

        gather.drain(j)
        scatter_back.drain(j)
        gather_back.drain(j)


def middle(size, rounds, u, x, cot_some, cot, gain, out_w, gate_w, up_w, down_w):
    rows, d = x.shape
    m = rows // rounds
    c, ff = out_w.shape[0], gate_w.shape[1]
    shape = (size, rounds, m)
    sems = DMA((2, rounds, size))
    spec, far = pl.BlockSpec(memory_space=VM), pl.BlockSpec(memory_space=pl.ANY)
    depth = min(256, d)
    outs = pl.pallas_call(
        partial(middle_kernel, size, rounds),
        out_shape=[
            jax.ShapeDtypeStruct((rounds, m, d), f32),
            jax.ShapeDtypeStruct((rounds, m, d), f32),
            jax.ShapeDtypeStruct(shape + (d,), bf16),
            jax.ShapeDtypeStruct(shape + (c,), f32),
            jax.ShapeDtypeStruct((1, d), f32),
            jax.ShapeDtypeStruct(shape + (d,), bf16),
            jax.ShapeDtypeStruct((d, c), bf16),
        ]
        + [jax.ShapeDtypeStruct((d, ff), bf16)] * 3,
        in_specs=[spec] * 4 + [far] * 5,
        out_specs=[far] * 4 + [spec] + [far] * 5,
        scratch_shapes=[
            VM(gate_w.shape, bf16),
            VM(up_w.shape, bf16),
            VM(down_w.shape, bf16),
            VM(shape + (d,), bf16),
            VM(shape + (d,), bf16),
            VM(shape + (d,), bf16),
            VM((rounds, m, d), f32),
            VM((m, d), f32),
            VM((size, m, c), f32),
            VM((rounds, size, m, d), bf16),
            VM((2, rounds, size - 1, m, d), bf16),
            VM((m, d), f32),
        ]
        + [VM(shape + (ff,), bf16)] * 3
        + [VM((size, m, d), bf16)]
        + [VM((depth, ff), bf16)] * 3
        + [DMA((5,)), DMA((rounds,)), DMA((1,)), DMA((rounds,)), DMA((1,)), DMA((1,)), DMA((3,))]
        + [sems] * 10,
        compiler_params=pltpu.CompilerParams(collective_id=3, has_side_effects=True, vmem_limit_bytes=63 * MIB),
        cost_estimate=pl.CostEstimate(
            flops=2 * size * rows * d * (2 * c + 9 * ff), bytes_accessed=56 * MIB, transcendentals=size * rows * ff
        ),
        name="middle",
    )(
        u.reshape(shape + (c,)),
        x.reshape(rounds, m, d),
        gain.reshape(1, d),
        out_w,
        gate_w,
        up_w,
        down_w,
        cot_some,
        cot.reshape(rounds, m, d),
    )
    res, back, e, ub, second, down, *grads = outs
    total = size * rows
    return (
        res.reshape(rows, d),
        back.reshape(rows, d),
        ub.reshape(total, c),
        second,
        down.reshape(total, d),
        *grads,
    )


class Everyone:
    def __init__(self, size, axis, mine, land, sems):
        self.size, self.axis = size, axis
        self.here = lax.axis_index(axis)
        self.mine, self.land, self.sems = mine, land, sems

    def copy(self, slot, peer):
        return remote(self.mine, self.land.at[slot], self.sems.at[0, peer], self.sems.at[1, slot], self.axis, peer)

    def others(self):
        for k in range(self.size):
            yield k, self.here != k

    def start(self):
        for k, other in self.others():

            @pl.when(other)
            def _():
                self.copy(self.here, k).start()

    def finish(self, out):
        out[...] = self.mine[...]
        for k, other in self.others():

            @pl.when(other)
            def _():
                self.copy(k, k).wait_recv()
                out[...] = out[...] + self.land[k]

    def drain(self):
        for k, other in self.others():

            @pl.when(other)
            def _():
                self.copy(self.here, k).wait_send()


def everyone_scratch(size, rows):
    return [VM((rows, WIDTH), f32), VM((size, rows, WIDTH), f32), DMA((2, size))]


def stack(vector, into, at):
    for k in range(vector.shape[1] // WIDTH):
        into[at + k : at + k + 1, :] = vector[:, k * WIDTH : (k + 1) * WIDTH]


def last_kernel(size, groups, rounds, count, mixed, *refs):
    take = taker(refs)
    backs = take(4)
    x_ref, gain_ref, second_ref, small_ref, first_ref, back_in, a_in, part_in = take(8)
    grads = take(count)
    tokens_far, small_out = take(2)
    grad_outs = take(count + (4 if mixed else 0))
    part, land, total, s_send, s_recv = take(5)
    small_seq, gains_tp, sides = take(3), take(3), take(1)[0]
    nears = take(4 if mixed else 0)
    a_ref, tokens_out, load_sems, store_sems = take(4)
    sums = group_sums(groups, grads + nears, grad_outs, take)
    early, late = sums[:2], sums[2:]

    seq, seq_count = group_peers(groups, "seq")
    tp, tp_count = group_peers(size, "tp")
    greet(seq + tp, seq_count + tp_count)

    for each in sums[:count]:
        each.start()
    m, d = x_ref.shape[1:]
    tile = min(512, d)
    local = pltpu.make_async_copy

    def part_load(j):
        return local(part_in.at[j], part.at[j], load_sems.at[2 + j])

    a_load = local(a_in, a_ref, load_sems.at[1])
    back_load = local(back_in, tokens_out, load_sems.at[0])

    for j in range(rounds):
        part_load(j).start()
    a_load.start()
    back_load.start()

    def store(j):
        return local(tokens_out.at[j], tokens_far.at[j], store_sems.at[j])

    group = size * m
    scatter = Scatter(size, s_send, s_recv, part, land, total)
    gain = gain_ref[...]

    seq_small = Everyone(groups, "seq", *small_seq)
    tp_gains = Everyone(size, "tp", *gains_tp)
    lines, smalls = d // WIDTH, small_ref.shape[0]

    def mix(back, each):
        rows = back[...].reshape(rounds * group, back.shape[3])
        depth = each.own.shape[1]
        for side, into in ((1 - each.side, each.grad), (each.side, each.own)):

            @pl.loop(0, each.half)
            def _(k):
                cols = pl.ds(pl.multiple_of((2 * k + side) * depth, depth), depth)
                left = a_ref[:, :, :, cols].reshape(rounds * group, depth)
                into[k] = mul(left, rows, TN).astype(bf16)

            if into is each.grad:
                each.start()

    def norm_back(j):
        @pl.loop(0, m // 16)
        def _(g):
            r = pl.ds(pl.multiple_of(g * 16, 16), 16)
            a_back, x = total[r, :], x_ref[j, r, :].astype(f32)
            scale = lax.rsqrt(jnp.mean(x * x, axis=-1, keepdims=True) + epsilon)
            normed = x * scale
            inner = a_back * gain
            tokens_out[j, r, :] = tokens_out[j, r, :] + scale * (
                inner - normed * jnp.mean(inner * normed, axis=-1, keepdims=True)
            )

    def steps(j, low, high):
        for t in range(low, high):
            if t < size - 1:
                scatter.step(j, t)
            else:
                scatter.finish(j)
                norm_back(j)
                store(j).start()

    stack(second_ref[...], gains_tp[0], 0)
    stack(first_ref[...], gains_tp[0], lines)
    tp_gains.start()
    for j in range(rounds):
        part_load(j).wait()
        scatter.start(j)
    tp_gains.finish(sides)
    small_seq[0][: 2 * lines, :] = sides[...]
    small_seq[0][2 * lines : 2 * lines + smalls, :] = small_ref[...]
    seq_small.start()
    for each in early:
        each.middle()
    a_load.wait()
    steps(0, 1, 2)
    back_load.wait()
    if mixed:
        for at, (back, each) in enumerate(zip(backs, late)):
            mix(back, each)
            steps(0, 2, 3) if at == 0 else None
            steps(0, 3, size) if at == 2 else None
    else:
        steps(0, 2, size)
    for each in early:
        each.relay()
    for each in late:
        each.middle()
    steps(1, 1, 3)
    steps(1, 3, size)
    for each in late[:2]:
        each.relay()
    steps(2, 1, 3)
    for each in late[2:]:
        each.relay()
    steps(2, 3, size)
    for each in early:
        each.finish()
    seq_small.finish(small_out)
    for j in range(3, rounds):
        steps(j, 1, size)
    for each in late:
        each.finish()

    for each in sums + [seq_small, tp_gains]:
        each.drain()

    @pl.loop(0, rounds)
    def _(j):
        scatter.drain(j)
        store(j).wait()


def last(size, groups, rounds, backs, part, a, x, back, gain, second, first, small, grads, turned):
    mixed = len(turned) > len(grads)
    rows, d = x.shape
    m = rows // rounds
    c = backs[0].shape[1]
    shape = (size, rounds, m)
    lines = d // WIDTH
    sems = DMA((2, rounds, size))
    spec = pl.BlockSpec(memory_space=VM)
    small_rows = 2 * lines + small.shape[0]
    shapes = [grad.shape for grad in grads] + ([(groups, d // groups, c)] * 4 if mixed else [])
    outs = pl.pallas_call(
        partial(last_kernel, size, groups, rounds, len(grads), mixed),
        out_shape=[
            jax.ShapeDtypeStruct((rounds, m, d), f32),
            jax.ShapeDtypeStruct((small_rows, WIDTH), f32),
        ]
        + sum_shapes(shapes, turned),
        in_specs=[spec] * 9 + [pl.BlockSpec(memory_space=pl.ANY)] * (3 + len(grads)),
        out_specs=[pl.BlockSpec(memory_space=pl.ANY)] + [spec] * (1 + len(shapes)),
        scratch_shapes=[
            VM((rounds, size, m, d), bf16),
            VM((2, rounds, size - 1, m, d), bf16),
            VM((m, d), f32),
            sems,
            sems,
        ]
        + everyone_scratch(groups, small_rows)
        + everyone_scratch(size, 2 * lines)
        + [VM((2 * lines, WIDTH), f32)]
        + ([VM((groups // 2, d // groups, c), bf16)] * 4 if mixed else [])
        + [VM(shape + (d,), bf16)]
        + [VM((rounds, m, d), f32), DMA((2 + rounds,)), DMA((rounds,))]
        + group_sums_scratch(shapes),
        compiler_params=pltpu.CompilerParams(collective_id=4, has_side_effects=True, vmem_limit_bytes=63 * MIB),
        cost_estimate=pl.CostEstimate(flops=16 * size * rows * d * c, bytes_accessed=56 * MIB, transcendentals=0),
        name="last",
    )(
        *[part.reshape(shape + (c,)) for part in backs],
        x.reshape(rounds, m, d),
        gain.reshape(1, d),
        second,
        small,
        first,
        back.reshape(rounds, m, d),
        a.reshape(shape + (d,)),
        part,
        *[in_pairs(grad) for grad in grads],
    )
    sides = outs[1]
    return (outs[0].reshape(rows, d), sides[:lines], sides[lines : 2 * lines], sides[2 * lines :]) + tuple(outs[2:])


def per_device(
    size,
    groups,
    tokens,
    lengths,
    cotangent,
    first_gain,
    query_weight,
    forget_weight,
    input_weight,
    swish_weight,
    bound_logit,
    group_gain,
    out_weight,
    second_gain,
    gate_weight,
    up_weight,
    down_weight,
):
    weights = (query_weight, forget_weight, input_weight, swish_weight)
    ends = jnp.cumsum(lengths).astype(jnp.int32)
    bound, head_gain = bound_logit.reshape(1, -1), group_gain.reshape(1, -1)
    a, q, f, i, s, cot_some, o, u, starts = front(
        size, groups, ROUNDS, tokens, cotangent, first_gain, weights, ends, bound, head_gain
    )
    residual, back, ub, second, down, *wide = middle(
        size, ROUNDS, u, tokens, cot_some, cotangent, second_gain, out_weight, gate_weight, up_weight, down_weight
    )
    down, ub = lax.optimization_barrier((down, ub))
    down = lax.psum_scatter(down, "tp", scatter_dimension=0, tiled=True)
    output = (residual + down.astype(f32)).astype(bf16)
    d = tokens.shape[1]

    def chunks(grad):
        return grad.reshape(groups, grad.shape[0] // groups, grad.shape[1])

    def grad_of(left, right):
        return chunks(lax.dot_general(left, right, TN, preferred_element_type=f32).astype(bf16))

    outs, gates, ups, downs = (chunks(grad) for grad in wide)
    dq, df, di, ds, small, first, part, gate_grad, up_grad = scan_backward(
        groups,
        size,
        ROUNDS,
        ends,
        bound,
        head_gain,
        q,
        f,
        i,
        s,
        o,
        ub,
        starts,
        first_gain,
        a,
        weights,
        [gates, ups],
    )
    back_rows = (dq, df, di, ds)
    here_too = groups == 8
    others = [downs, outs] + ([] if here_too else [grad_of(a, part) for part in back_rows])
    tokens_grad, second_sum, first_sum, small_sum, *sums = last(
        size,
        groups,
        ROUNDS,
        back_rows,
        part,
        a,
        tokens,
        back,
        first_gain,
        second,
        first,
        small,
        others,
        [True, True] + [False] * 4,
    )
    down_grad, out_grad, query_grad, forget_grad, input_grad, swish_grad = sums
    heads = bound_logit.shape[0]
    here = lax.axis_index("seq")
    place = here * size + lax.axis_index("tp")
    each = d // (groups * size)
    wide = WIDTH // groups
    first_grad = lax.dynamic_slice_in_dim(first_sum.reshape(-1), place * each, each)
    second_grad = lax.dynamic_slice_in_dim(second_sum.reshape(-1), place * each, each)
    bound_grad = lax.dynamic_slice_in_dim(small_sum[:heads], here * wide, wide, axis=1)
    head_grad = lax.dynamic_slice_in_dim(small_sum[heads:], here * wide, wide, axis=1)
    return (
        output,
        tokens_grad,
        first_grad,
        query_grad,
        forget_grad,
        input_grad,
        swish_grad,
        bound_grad,
        head_grad,
        out_grad,
        second_grad,
        gate_grad,
        up_grad,
        down_grad,
    )


def solution(mesh):
    rows, both, cols, lines = P(("seq", "tp"), None), P(("seq", "tp")), P(None, "tp"), P("tp", None)
    in_specs = (rows, P(), rows, P(), cols, cols, cols, cols, lines, lines, lines, P(), cols, cols, lines)
    down, across = P("seq", "tp"), P("tp", "seq")
    out_specs = (rows, rows, both, down, down, down, down, across, across, across, both, down, down, across)
    return jax.shard_map(
        partial(per_device, mesh.shape["tp"], mesh.shape["seq"]),
        mesh=mesh,
        in_specs=in_specs,
        out_specs=out_specs,
        check_vma=False,
    )
```

```python
from functools import partial

import jax
import jax.numpy as jnp
from jax import lax
from jax.experimental import pallas as pl
from jax.experimental.pallas import tpu as pltpu
from jax.sharding import PartitionSpec as P

WIDTH = 128
ROUNDS = 4
KNOWN = 1
PIECES = 3
STEPS = (
    "C10", "C11", "C20", "A0", "C12", "A1", "C21", "C22", "C13", "S01", "C30", "S11", "S02", "S03", "C23", "A2",
    "C31", "A3", "G01", "G02", "S21", "S22", "S12", "S23", "G03", "F00", "F01", "F02", "O0", "S13", "B0", "C32",
    "C33", "G11", "G12", "G13", "T01", "S31", "F10", "F11", "F12", "O1", "T02", "G21", "T03", "B1", "S32", "G22",
    "G23", "F20", "E01", "S33", "E02", "E03", "F21", "F22", "T11", "T12", "T13", "G31", "O2", "B2", "E11", "U0",
    "T21", "G32", "G33", "F30", "F31", "T22", "F32", "O3", "E12", "T23", "B3", "W0", "E21", "E13", "U1", "T31",
    "T32", "E22", "W1", "W2", "T33", "W3", "E23", "W5", "E31", "W6", "W4", "U2", "W7", "E32", "E33", "U3",
)
MIB = 1 << 20
epsilon = 1e-05

f32 = jnp.float32
bf16 = jnp.bfloat16
NN = (((1,), (0,)), ((), ()))
NT = (((1,), (1,)), ((), ()))
TN = (((0,), (0,)), ((), ()))
VM = pltpu.VMEM
DMA = pltpu.SemaphoreType.DMA
MESH = pl.DeviceIdType.MESH


def mul(left, right, dims):
    return lax.dot_general(left, right, dims, preferred_element_type=f32)


def silu_slope(value):
    gate = jax.nn.sigmoid(value)
    return gate * (1.0 + value * (1.0 - gate))


def remote(src, dst, send, recv, axis, peer):
    return pltpu.make_async_remote_copy(
        src_ref=src,
        dst_ref=dst,
        send_sem=send,
        recv_sem=recv,
        device_id={axis: peer},
        device_id_type=MESH,
    )


def greet(peers, count):
    barrier = pltpu.get_barrier_semaphore()
    for axis, peer, wanted in peers:

        @pl.when(wanted)
        def _():
            pl.semaphore_signal(barrier, inc=1, device_id={axis: peer}, device_id_type=MESH)

    pl.semaphore_wait(barrier, count)


def line_peers(size):
    me = lax.axis_index("tp")
    peers = [("tp", lax.rem(me + 1, size), me < size - 1), ("tp", lax.rem(me + size - 1, size), me > 0)]
    return peers, jnp.where(me < size - 1, 1, 0) + jnp.where(me > 0, 1, 0)


def group_peers(size, axis):
    me = lax.axis_index(axis)
    return [(axis, lax.rem(me + k, size), True) for k in range(1, size)], size - 1


class Line:
    def __init__(self, size, send, recv):
        self.size = size
        self.me = lax.axis_index("tp")
        self.right = lax.rem(self.me + 1, size)
        self.left = lax.rem(self.me + size - 1, size)
        self.send, self.recv = send, recv

    def hop(self, way, src, dst, j, at):
        peer = self.right if way == 0 else self.left
        return remote(src, dst, self.send.at[way, j, at], self.recv.at[way, j, at], "tp", peer)


class Scatter(Line):
    def __init__(self, size, send, recv, part, land, total):
        super().__init__(size, send, recv)
        self.part, self.land, self.total = part, land, total

    def copy(self, way, j, to):
        return self.hop(way, self.part.at[j, to], self.slot(way, j, to), j, to)

    def slot(self, way, j, to):
        return self.land.at[way, j, to - 1 + way]

    def start(self, j):
        last = self.size - 1

        @pl.when(self.me == 0)
        def _():
            for to in range(last, 0, -1):
                self.copy(0, j, to).start()

        @pl.when(self.me == last)
        def _():
            for to in range(last):
                self.copy(1, j, to).start()

    def step(self, j, t):
        last = self.size - 1
        for way in (0, 1):
            place = self.me if way == 0 else last - self.me
            to = last - t + place
            to = to if way == 0 else last - to

            @pl.when((place >= 1) & (place <= t))
            def _():
                copy = self.copy(way, j, to)
                copy.wait_recv()
                self.add(self.part.at[j, to], self.slot(way, j, to))
                copy.start()

    def add(self, into, more):
        rows = into.shape[0]

        @pl.loop(0, rows // 16)
        def _(g):
            r = pl.ds(pl.multiple_of(g * 16, 16), 16)
            into[r, :] = (into[r, :].astype(f32) + more[r, :].astype(f32)).astype(bf16)

    def finish(self, j):
        me, last = self.me, self.size - 1
        rows = self.total.shape[0]

        def over(body):
            @pl.loop(0, rows // 16)
            def _(g):
                body(pl.ds(pl.multiple_of(g * 16, 16), 16))

        def first(r):
            self.total[r, :] = self.part[j, me, r, :].astype(f32)

        over(first)
        for way, there in ((0, me >= 1), (1, me < last)):

            @pl.when(there)
            def _():
                self.copy(way, j, me).wait_recv()

                def more(r):
                    self.total[r, :] = self.total[r, :] + self.land[way, j, me - 1 + way, r, :].astype(f32)

                over(more)

    def drain(self, j):
        for to in range(self.size):

            @pl.when(self.me < to)
            def _():
                self.copy(0, j, to).wait_send()

            @pl.when(self.me > to)
            def _():
                self.copy(1, j, to).wait_send()


class Gather(Line):
    def __init__(self, size, send, recv, whole):
        super().__init__(size, send, recv)
        self.whole = whole

    def copy(self, way, j, source):
        block = self.whole.at[source, j]
        return self.hop(way, block, block, j, source)

    def start(self, j):
        @pl.when(self.me < self.size - 1)
        def _():
            self.copy(0, j, self.me).start()

        @pl.when(self.me > 0)
        def _():
            self.copy(1, j, self.me).start()

    def step(self, j, t):
        last = self.size - 1

        @pl.when(self.me >= t)
        def _():
            copy = self.copy(0, j, self.me - t)
            copy.wait_recv()

            @pl.when(self.me < last)
            def _():
                copy.start()

        @pl.when(self.me + t <= last)
        def _():
            copy = self.copy(1, j, self.me + t)
            copy.wait_recv()

            @pl.when(self.me > 0)
            def _():
                copy.start()

    def drain(self, j):
        last = self.size - 1
        for source in range(self.size):

            @pl.when((self.me >= source) & (self.me < last))
            def _():
                self.copy(0, j, source).wait_send()

            @pl.when((self.me <= source) & (self.me > 0))
            def _():
                self.copy(1, j, source).wait_send()


def add_rows(into, left, right):
    rows = into.shape[0]

    @pl.loop(0, rows // 16)
    def _(g):
        r = pl.ds(pl.multiple_of(g * 16, 16), 16)
        into[r, :] = (left[r, :].astype(f32) + right[r, :].astype(f32)).astype(bf16)


class GroupSum:
    refs = 6

    def __init__(self, size, grad, out, own, got, land, *sems):
        self.half = size // 2
        here = lax.axis_index("seq")
        self.side = lax.rem(here, 2)
        self.mine = here // 2
        self.sibling = here + 1 - 2 * self.side
        self.grad, self.own, self.got, self.land, self.out = grad, own, got, land, out
        self.near_sems, *self.sems = sems
        self.loads = len(grad.shape) == 4
        self.turned = out.shape != own.shape[1:]

    @staticmethod
    def scratch(shape):
        half = shape[0]
        return [VM(shape, bf16)] * 3 + [DMA((3, half)), DMA((half,)), DMA((half,))]

    def near(self, k):
        sems = self.near_sems
        source = self.grad.at[k, 1 - self.side] if self.loads else self.grad.at[k]
        return remote(source, self.got.at[k], sems.at[0, k], sems.at[1, k], "seq", self.sibling)

    def load(self, k):
        return pltpu.make_async_copy(self.grad.at[k, self.side], self.own.at[k], self.near_sems.at[2, k])

    def start(self):
        for k in range(self.half):
            self.near(k).start()
            if self.loads:
                self.load(k).start()

    def pair(self, k, into):
        if self.loads:
            self.load(k).wait()
        self.near(k).wait_recv()
        add_rows(into, self.own.at[k], self.got.at[k])

    def far(self, k):
        send, recv = self.sems
        return remote(self.own.at[k], self.land.at[self.mine], send.at[k], recv.at[self.mine], "seq", 2 * k + self.side)

    def arrival(self, k):
        send, recv = self.sems
        return remote(self.own.at[k], self.land.at[k], send.at[k], recv.at[k], "seq", 2 * k + self.side)

    def middle(self):
        for k in range(self.half):

            @pl.when(k == self.mine)
            def _():
                self.pair(k, self.land.at[k])

            @pl.when(k != self.mine)
            def _():
                self.pair(k, self.own.at[k])
                self.far(k).start()

    def relay(self):
        pass

    def arrive(self):
        for k in range(self.half):

            @pl.when(k != self.mine)
            def _():
                self.arrival(k).wait_recv()

    def terms(self):
        return [self.land.at[k] for k in range(self.half)]

    def finish(self):
        self.arrive()
        rows, cols = self.own.shape[1:]

        def total(r, c):
            acc = None
            for term in self.terms():
                part = term[r, c].astype(f32)
                acc = part if acc is None else acc + part
            return acc

        if self.turned:

            @pl.loop(0, cols // WIDTH)
            def _(g):
                c = pl.ds(pl.multiple_of(g * WIDTH, WIDTH), WIDTH)
                self.out[c, :] = total(slice(None), c).T

        else:

            @pl.loop(0, rows // 16)
            def _(g):
                r = pl.ds(pl.multiple_of(g * 16, 16), 16)
                self.out[r, :] = total(r, slice(None))

    def drain(self):
        for k in range(self.half):
            self.near(k).wait_send()
        self.drain_far()

    def drain_far(self):
        for k in range(self.half):

            @pl.when(k != self.mine)
            def _():
                self.far(k).wait_send()


class SquareSum(GroupSum):
    refs = 6

    def __init__(self, *args):
        super().__init__(*args)
        self.hop, self.far_sems = self.sems
        x, y = lax.rem(self.mine, 2), self.mine // 2
        self.beside = (2 * y + 1 - x, 2 * (1 - y) + x)
        self.opposite = 2 * (1 - y) + 1 - x
        rows = self.own.shape[1] // 2
        self.halves = (pl.ds(0, rows), pl.ds(rows, rows))

    @staticmethod
    def scratch(shape):
        half, rows, cols = shape
        return [
            VM(shape, bf16),
            VM(shape, bf16),
            VM((2, rows, cols), bf16),
            DMA((3, half)),
            VM((2, rows // 2, cols), bf16),
            DMA((2, 6)),
        ]

    def over(self, way, at, source, target):
        sems = self.far_sems
        return remote(source, target, sems.at[0, at], sems.at[1, at], "seq", 2 * self.beside[way] + self.side)

    def pass_on(self, way):
        return self.over(way, way, self.own.at[self.opposite, self.halves[way]], self.hop.at[way])

    def deliver(self, way, half):
        source = self.own.at[self.beside[way], self.halves[half]]
        return self.over(way, 2 + 2 * way + half, source, self.land.at[way, self.halves[half]])

    def middle(self):
        self.pair(self.opposite, self.own.at[self.opposite])
        for way in (0, 1):
            self.pass_on(way).start()
        for way in (0, 1):
            self.pair(self.beside[way], self.own.at[self.beside[way]])
            self.deliver(way, way).start()
        self.pair(self.mine, self.own.at[self.mine])

    def relay(self):
        for way in (0, 1):
            self.pass_on(way).wait_recv()
            into = self.own.at[self.beside[1 - way], self.halves[way]]
            add_rows(into, into, self.hop.at[way])
            self.deliver(1 - way, way).start()

    def arrive(self):
        for way in (0, 1):
            for half in (0, 1):
                self.deliver(way, half).wait_recv()

    def terms(self):
        return [self.own.at[self.mine], self.land.at[0], self.land.at[1]]

    def drain_far(self):
        for way in (0, 1):
            self.pass_on(way).wait_send()
            for half in (0, 1):
                self.deliver(way, half).wait_send()


def summer(size):
    return SquareSum if size == 8 else GroupSum


def group_sums(size, grads, outs, take):
    kind = summer(size)
    return [kind(size, grad, out, *take(kind.refs)) for grad, out in zip(grads, outs)]


def group_sums_scratch(shapes):
    scratch = []
    for size, rows, cols in shapes:
        scratch += summer(size).scratch((size // 2, rows, cols))
    return scratch


def sum_shapes(shapes, turned):
    shapes = [shape[:0:-1] if turn else shape[1:] for shape, turn in zip(shapes, turned)]
    return [jax.ShapeDtypeStruct(shape, f32) for shape in shapes]


def in_pairs(grad):
    return grad.reshape((grad.shape[0] // 2, 2) + grad.shape[1:])


def taker(refs):
    refs = list(refs)

    def take(count):
        taken, refs[:count] = refs[:count], []
        return taken

    return take


def document(rows, ends_ref):
    total = jnp.where(rows >= ends_ref[0], 1, 0)
    for k in range(1, ends_ref.shape[0]):
        total = total + jnp.where(rows >= ends_ref[k], 1, 0)
    return total


def block_masks(first, ends_ref):
    shape = (WIDTH, WIDTH)
    down = lax.broadcasted_iota(jnp.int32, shape, 0)
    along = lax.broadcasted_iota(jnp.int32, shape, 1)
    docs = document(first + down, ends_ref)
    same = (docs == document(first + along, ends_ref)) & (down >= along)
    before = jnp.where(first > 0, document(first - 1, ends_ref), -1)
    final = document(first + WIDTH - 1, ends_ref)
    carry = jnp.where(docs == before, 1.0, 0.0)
    tail = jnp.where(docs == final, 1.0, 0.0)
    keep = jnp.where(final == before, 1.0, 0.0)
    return same, carry, tail, keep


def running(log_forget):
    shape = (WIDTH, WIDTH)
    lower = lax.broadcasted_iota(jnp.int32, shape, 0) >= lax.broadcasted_iota(jnp.int32, shape, 1)
    ones = jnp.where(lower, 1.0, 0.0).astype(bf16)
    high = log_forget.astype(bf16)
    low = (log_forget - high.astype(f32)).astype(bf16)
    return mul(ones, high, NN) + mul(ones, low, NN)


def decay_parts(forget_pre, bound):
    away = jax.nn.sigmoid(-forget_pre)
    key = jax.nn.sigmoid(-bound) * away
    return key, running(jnp.log(1.0 - key)), away


class States:
    def __init__(self, size, out_state, out_decay, land_state, land_decay, sems):
        self.size = size
        self.here = lax.axis_index("seq")
        self.out_state, self.out_decay = out_state, out_decay
        self.land_state, self.land_decay = land_state, land_decay
        self.sems = sems

    def pair(self, slot, peer):
        s = self.sems
        return (
            remote(self.out_state, self.land_state.at[slot], s.at[0, peer], s.at[1, slot], "seq", peer),
            remote(self.out_decay, self.land_decay.at[slot], s.at[2, peer], s.at[3, slot], "seq", peer),
        )

    def sends(self, later):
        for k in range(self.size):
            yield k, (self.here < k if later else self.here > k)

    def start(self, later):
        for k, wanted in self.sends(later):

            @pl.when(wanted)
            def _():
                for copy in self.pair(self.here, k):
                    copy.start()

    def compose(self, later, state):
        state[...] = jnp.zeros_like(state)
        order = range(self.size) if later else range(self.size - 1, -1, -1)
        for k in order:

            @pl.when(self.here > k if later else self.here < k)
            def _():
                for copy in self.pair(k, k):
                    copy.wait_recv()
                for h in range(state.shape[0]):
                    decay = self.land_decay[k, h : h + 1, :]
                    state[h] = decay * state[h] + self.land_state[k, h].astype(f32)

    def drain(self, later):
        for k, wanted in self.sends(later):

            @pl.when(wanted)
            def _():
                for copy in self.pair(self.here, k):
                    copy.wait_send()


def states_scratch(size, heads):
    return [
        VM((heads, WIDTH, WIDTH), f32),
        VM((heads, WIDTH, WIDTH), bf16),
        VM((8, WIDTH), f32),
        VM((size, heads, WIDTH, WIDTH), bf16),
        VM((size, 8, WIDTH), f32),
        DMA((4, size)),
    ]


def front_kernel(size, groups, rounds, *refs):
    take = taker(refs)
    ends_ref, x_ref, norm_gain_ref, bound_ref, gain_ref, cot_in, *loaded = take(10)
    a_out, q_out, f_out, i_out, s_out, cot_out, o_ref, u_ref, starts_ref = take(9)
    *weights, a_ref, q_ref, f_ref, i_ref, s_ref, cot_ref = take(10)
    qd_ref, kd_ref, qe_ref, adds, decays = take(5)
    state, out_state, out_decay, land_state, land_decay, sems = take(6)
    load_sems, store_sems, a_send, a_recv, c_send, c_recv = take(6)
    me = lax.axis_index("tp")
    m, d = x_ref.shape[1:]
    known = cot_ref.shape[1]
    local = pltpu.make_async_copy
    cot_load = local(cot_in.at[:known], cot_ref.at[me], load_sems.at[4])
    cot_load.start()
    loads = [local(source, target, load_sems.at[k]) for k, (source, target) in enumerate(zip(loaded, weights))]
    for load in loads:
        load.start()
    line, line_count = line_peers(size)
    seq, seq_count = group_peers(groups, "seq")
    greet(line + seq, line_count + seq_count)

    gather = Gather(size, a_send, a_recv, a_ref)
    gather_cot = Gather(size, c_send, c_recv, cot_ref)
    norm_gain = norm_gain_ref[...]

    @pl.loop(0, rounds)
    def _(j):
        @pl.loop(0, m // 16)
        def _(g):
            r = pl.ds(pl.multiple_of(g * 16, 16), 16)
            x = x_ref[j, r, :].astype(f32)
            scale = lax.rsqrt(jnp.mean(x * x, axis=-1, keepdims=True) + epsilon)
            a_ref[me, j, r, :] = (x * scale * norm_gain).astype(bf16)

        gather.start(j)

    for load in loads:
        load.wait()
    cot_load.wait()
    pres = (q_ref, f_ref, i_ref, s_ref)

    rows, c = q_ref.shape
    blocks, heads = rows // WIDTH, c // WIDTH
    base = lax.axis_index("seq") * rows
    states = States(groups, out_state, out_decay, land_state, land_decay, sems)
    state[...] = jnp.zeros_like(state)
    out_decay[...] = jnp.ones_like(out_decay)

    def cot_steps(t):
        @pl.loop(0, known)
        def _(j):
            gather_cot.step(j, t)

    def block(b):
        r = pl.ds(pl.multiple_of(b * WIDTH, WIDTH), WIDTH)
        same, carry, tail, keep = block_masks(base + b * WIDTH, ends_ref)
        for h in range(heads):
            cols = slice(h * WIDTH, (h + 1) * WIDTH)
            q = q_ref[r, cols]
            q = q * jax.nn.sigmoid(q)
            key, run, _ = decay_parts(f_ref[r, cols], bound_ref[:, cols])
            middle, last = run[WIDTH // 2 - 1 : WIDTH // 2, :], run[WIDTH - 1 :, :]
            qd_ref[r, cols] = (q * jnp.exp(run - middle)).astype(bf16)
            kd_ref[r, cols] = (key * jnp.exp(middle - run)).astype(bf16)
            qe_ref[r, cols] = (q * jnp.exp(run) * carry).astype(bf16)
            key_tail = (key * jnp.exp(last - run) * tail).astype(bf16)
            adds[b, h] = mul(i_ref[r, cols].astype(bf16), key_tail, TN)
            decays[b, h : h + 1, :] = jnp.exp(last) * keep

    def near_part(b):
        r = pl.ds(pl.multiple_of(b * WIDTH, WIDTH), WIDTH)
        same, carry, tail, keep = block_masks(base + b * WIDTH, ends_ref)
        for h in range(heads):
            cols = slice(h * WIDTH, (h + 1) * WIDTH)
            scores = jnp.where(same, mul(qd_ref[r, cols], kd_ref[r, cols], NT), 0.0).astype(bf16)
            o_ref[r, cols] = mul(scores, i_ref[r, cols].astype(bf16), NN)

    own_rows = rounds * m
    per = own_rows // WIDTH if own_rows % WIDTH == 0 and WIDTH % m == 0 else 0
    early = [z * per + k for z in range(size) for k in range(per - 1)] if per > 1 else []
    late = [b for b in range(blocks) if b not in early]
    ready = (per - 1) * WIDTH // m if early else rounds

    def some_blocks(chosen, body):
        if chosen is early and early:

            @pl.loop(0, size)
            def _(z):
                for k in range(per - 1):
                    body(z * per + k)

        elif early:

            @pl.loop(0, size)
            def _(z):
                body(z * per + per - 1)

        elif chosen is late:
            pl.loop(0, blocks)(body)

    def project(j):
        block_rows = a_ref[:, j].reshape(size * m, d)
        for weight, out in zip(weights, pres):
            product = mul(block_rows, weight[...], NN)
            for z in range(size):
                at = pl.multiple_of(z * own_rows + j * m, 16)
                out[pl.ds(at, m), :] = product[z * m : (z + 1) * m]

    @pl.loop(0, rounds)
    def _(j):
        for t in range(1, size):
            gather.step(j, t)
            if early and t == 1:

                @pl.when(j == ready)
                def _():
                    some_blocks(early, block)

            if early and t == 2:

                @pl.when(j == ready)
                def _():
                    some_blocks(early, near_part)

        @pl.when(j >= rounds - known)
        def _():
            gather_cot.start(j - (rounds - known))

        project(j)

    stores = [
        local(source, target, store_sems.at[k])
        for k, (source, target) in enumerate(zip((a_ref, *pres), (a_out, q_out, f_out, i_out, s_out)))
    ]
    for store in stores:
        store.start()

    some_blocks(late, block)

    @pl.loop(0, blocks)
    def _(b):
        for h in range(heads):
            decay = decays[b, h : h + 1, :]
            state[h] = decay * state[h] + adds[b, h]
            out_decay[h : h + 1, :] = out_decay[h : h + 1, :] * decay

    out_state[...] = state[...].astype(bf16)
    states.start(True)
    cot_steps(1)
    some_blocks(late, near_part)

    states.compose(True, state)
    for t in range(2, size - 1):
        cot_steps(t)

    @pl.loop(0, blocks)
    def _(b):
        r = pl.ds(pl.multiple_of(b * WIDTH, WIDTH), WIDTH)
        places = base + b * WIDTH + lax.broadcasted_iota(jnp.int32, (WIDTH, WIDTH), 0)
        valid = jnp.where(places < ends_ref[ends_ref.shape[0] - 1], 1.0, 0.0)
        for h in range(heads):
            cols = slice(h * WIDTH, (h + 1) * WIDTH)
            low = state[h].astype(bf16)
            starts_ref[b, h] = low
            o = o_ref[r, cols] + mul(qe_ref[r, cols], low, NT)
            o_ref[r, cols] = o
            state[h] = decays[b, h : h + 1, :] * state[h] + adds[b, h]
            scale = lax.rsqrt(jnp.mean(o * o, axis=-1, keepdims=True) + epsilon)
            s = s_ref[r, cols]
            z = s * jax.nn.sigmoid(s) * valid
            u_ref[r, cols] = (o * scale * gain_ref[:, cols] * z).astype(bf16)

    cot_steps(size - 1)
    cot_store = local(cot_ref, cot_out, load_sems.at[4])
    cot_store.start()
    states.drain(True)

    @pl.loop(0, rounds)
    def _(j):
        gather.drain(j)

    @pl.loop(0, known)
    def _(j):
        gather_cot.drain(j)

    for store in stores:
        store.wait()
    cot_store.wait()


def front(size, groups, rounds, tokens, cot, norm_gain, weights, ends, bound, gain):
    own, d = tokens.shape
    m, c = own // rounds, weights[0].shape[1]
    rows = size * own
    blocks, heads = rows // WIDTH, c // WIDTH
    known = KNOWN
    shape, some = (size, rounds, m, d), (size, known, m, d)
    wide, low = jax.ShapeDtypeStruct((rows, c), f32), VM((rows, c), bf16)
    spec, far = pl.BlockSpec(memory_space=VM), pl.BlockSpec(memory_space=pl.ANY)
    sems = DMA((2, rounds, size))
    outs = pl.pallas_call(
        partial(front_kernel, size, groups, rounds),
        out_shape=[
            jax.ShapeDtypeStruct(shape, bf16),
            wide,
            wide,
            wide,
            wide,
            jax.ShapeDtypeStruct(some, bf16),
            wide,
            jax.ShapeDtypeStruct((rows, c), bf16),
            jax.ShapeDtypeStruct((blocks, heads, WIDTH, WIDTH), bf16),
        ],
        in_specs=[pl.BlockSpec(memory_space=pltpu.SMEM)] + [spec] * 4 + [far] * 5,
        out_specs=[far] * 6 + [spec] * 3,
        scratch_shapes=[VM((d, c), bf16)] * 4
        + [VM(shape, bf16)]
        + [VM((rows, c), f32)] * 4
        + [VM(some, bf16)]
        + [low] * 3
        + [VM((blocks, heads, WIDTH, WIDTH), f32), VM((blocks, 8, WIDTH), f32)]
        + states_scratch(groups, heads)
        + [DMA((5,)), DMA((5,)), sems, sems, sems, sems],
        compiler_params=pltpu.CompilerParams(collective_id=0, has_side_effects=True, vmem_limit_bytes=60 * MIB),
        cost_estimate=pl.CostEstimate(flops=8 * rows * d * c, bytes_accessed=36 * MIB, transcendentals=8 * rows * c),
        name="front",
    )(
        ends,
        tokens.reshape(rounds, m, d),
        norm_gain.reshape(1, d),
        bound,
        gain,
        cot.reshape(rounds, m, d),
        *weights,
    )
    return [outs[0].reshape(rows, d)] + list(outs[1:])


def scan_back_kernel(size, line, rounds, count, *refs):
    take = taker(refs)
    ends_ref, bound_ref, gain_ref, norm_gain_ref, *loaded = take(16)
    grads = take(count)
    *back_outs, small_ref, first_ref, part_out = take(7)
    grad_outs = take(count)
    qd_ref, kd_ref, qe_ref, kt_ref, do_ref, run_ref, adds, decays = take(8)
    state, out_state, out_decay, land_state, land_decay, sems = take(6)
    *inputs, load_sems = take(13)
    q_ref, f_ref, i_ref, s_ref, o_ref, ub_ref, starts_ref, *weights, a_ref = inputs
    *loaded, a_in = loaded
    stage, stage_sems, a_sems, *backs, back_sems = take(8)
    dq_ref, df_ref, di_ref, ds_ref = backs
    loads = [
        pltpu.make_async_copy(source, target, load_sems.at[k]) for k, (source, target) in enumerate(zip(loaded, inputs))
    ]
    soon, later = [loads[k] for k in (4, 3, 5, 0, 1)], [loads[k] for k in (2, 6)]
    for load in soon + later:
        load.start()
    sums = group_sums(size, grads, grad_outs, take)
    greet(*group_peers(size, "seq"))
    rows, c = q_ref.shape
    blocks, heads = rows // WIDTH, c // WIDTH
    base = lax.axis_index("seq") * rows
    states = States(size, out_state, out_decay, land_state, land_decay, sems)
    for each in sums:
        each.start()
    state[...] = jnp.zeros_like(state)
    out_decay[...] = jnp.ones_like(out_decay)
    small_ref[...] = jnp.zeros_like(small_ref)
    for load in soon:
        load.wait()

    @pl.loop(0, blocks)
    def _(back):
        for each in sums[:1]:

            @pl.when(back == 1)
            def _():
                each.middle()

        b = blocks - 1 - back
        r = pl.ds(pl.multiple_of(b * WIDTH, WIDTH), WIDTH)
        same, carry, tail, keep = block_masks(base + b * WIDTH, ends_ref)
        places = base + b * WIDTH + lax.broadcasted_iota(jnp.int32, (WIDTH, WIDTH), 0)
        valid = jnp.where(places < ends_ref[ends_ref.shape[0] - 1], 1.0, 0.0)
        for h in range(heads):
            cols = slice(h * WIDTH, (h + 1) * WIDTH)
            o, s, ub, gain = o_ref[r, cols], s_ref[r, cols], ub_ref[r, cols], gain_ref[:, cols]
            scale = lax.rsqrt(jnp.mean(o * o, axis=-1, keepdims=True) + epsilon)
            normed = o * scale
            gate = jax.nn.sigmoid(s)
            uz = ub * (s * gate * valid)
            small_ref[heads + h : heads + h + 1, :] += jnp.sum(uz * normed, axis=0, keepdims=True)
            nb = uz * gain
            ds_ref[r, cols] = (ub * normed * gain * valid * (gate * (1.0 + s * (1.0 - gate)))).astype(bf16)
            do = (scale * (nb - normed * jnp.mean(nb * normed, axis=-1, keepdims=True))).astype(bf16)
            do_ref[r, cols] = do
            q = q_ref[r, cols]
            q = q * jax.nn.sigmoid(q)
            key, run, _ = decay_parts(f_ref[r, cols], bound_ref[:, cols])
            middle, last = run[WIDTH // 2 - 1 : WIDTH // 2, :], run[WIDTH - 1 :, :]
            run_ref[r, cols] = run
            qd_ref[r, cols] = (q * jnp.exp(run - middle)).astype(bf16)
            kd_ref[r, cols] = (key * jnp.exp(middle - run)).astype(bf16)
            kt_ref[r, cols] = (key * jnp.exp(last - run) * tail).astype(bf16)
            qe = (q * jnp.exp(run) * carry).astype(bf16)
            qe_ref[r, cols] = qe
            add = mul(do, qe, TN)
            decay = jnp.exp(last) * keep
            adds[b, h] = add
            decays[b, h : h + 1, :] = decay
            state[h] = decay * state[h] + add
            out_decay[h : h + 1, :] = out_decay[h : h + 1, :] * decay

    out_state[...] = state[...].astype(bf16)
    states.start(False)
    for load in later:
        load.wait()
    for load in loads[7:]:
        load.start()
    for each in sums[:1]:
        each.relay()
    for each in sums[1:]:
        each.middle()
    states.compose(False, state)

    @pl.loop(0, blocks)
    def _(back):
        for each in sums[1:]:

            @pl.when(back == blocks // 2)
            def _():
                each.relay()
        b = blocks - 1 - back
        r = pl.ds(pl.multiple_of(b * WIDTH, WIDTH), WIDTH)
        same, carry, tail, keep = block_masks(base + b * WIDTH, ends_ref)
        shape = (WIDTH, WIDTH)
        down, along = lax.broadcasted_iota(jnp.int32, shape, 0), lax.broadcasted_iota(jnp.int32, shape, 1)
        from_here = jnp.where(along >= down, 1.0, 0.0).astype(bf16)
        ahead = jnp.where(along < down, 1.0, 0.0).astype(bf16)
        for h in range(heads):
            cols = slice(h * WIDTH, (h + 1) * WIDTH)
            do, v = do_ref[r, cols], i_ref[r, cols].astype(bf16)
            low, start = state[h].astype(bf16), starts_ref[b, h]
            dq_state = mul(do, start, NN)
            dk_state = mul(v, low, NN)
            kt = kt_ref[r, cols]
            qd, kd = qd_ref[r, cols], kd_ref[r, cols]
            scores = jnp.where(same, mul(qd, kd, NT), 0.0).astype(bf16)
            slopes = jnp.where(same, mul(do, v, NT), 0.0).astype(bf16)
            dq_near = mul(slopes, kd, NN)
            dk_near = mul(slopes, qd, TN)
            di_ref[r, cols] = (mul(scores, do, TN) + mul(kt, low, NT)).astype(bf16)
            run = run_ref[r, cols]
            middle, last = run[WIDTH // 2 - 1 : WIDTH // 2, :], run[WIDTH - 1 :, :]
            q_back = dq_near * jnp.exp(run - middle) + dq_state * (jnp.exp(run) * carry)
            k_back = dk_near * jnp.exp(middle - run) + dk_state * (jnp.exp(last - run) * tail)
            later = (
                qe_ref[r, cols].astype(f32) * dq_state
                + qd.astype(f32) * dq_near
                - kd.astype(f32) * dk_near
            )
            earlier = kt.astype(f32) * dk_state
            decay = decays[b, h : h + 1, :]
            log_back = decay * jnp.sum(low.astype(f32) * start.astype(f32), axis=0, keepdims=True)
            for ones, part in ((from_here, later), (ahead, earlier)):
                high = part.astype(bf16)
                log_back = log_back + mul(ones, high, NN)
                log_back = log_back + mul(ones, (part - high.astype(f32)).astype(bf16), NN)
            f_pre = f_ref[r, cols]
            away, near = jax.nn.sigmoid(-f_pre), jax.nn.sigmoid(f_pre)
            upper = jax.nn.sigmoid(-bound_ref[:, cols])
            lower = jax.nn.sigmoid(bound_ref[:, cols])
            forget_back = log_back / (1.0 - upper * away) - k_back
            slope = forget_back * away * upper
            df_ref[r, cols] = (slope * near).astype(bf16)
            small_ref[h : h + 1, :] += jnp.sum(slope, axis=0, keepdims=True) * lower
            dq_ref[r, cols] = (q_back * silu_slope(q_ref[r, cols])).astype(bf16)
            state[h] = adds[b, h] + decay * state[h]

    stores = [
        pltpu.make_async_copy(source, target, back_sems.at[k]) for k, (source, target) in enumerate(zip(backs, back_outs))
    ]
    for store in stores:
        store.start()
    for load in loads[7:]:
        load.wait()
    m, d = a_ref.shape[2:]

    def a_load(j):
        slot = lax.rem(j, 2)
        return pltpu.make_async_copy(a_in.at[:, j], a_ref.at[slot], a_sems.at[slot])

    for j in range(min(2, rounds)):
        a_load(j).start()
    tile = min(512, d)
    first_ref[...] = jnp.zeros_like(first_ref)

    def part_copy(j):
        return pltpu.make_async_copy(stage.at[lax.rem(j, 2)], part_out.at[j], stage_sems.at[lax.rem(j, 2)])

    @pl.loop(0, rounds)
    def _(j):
        @pl.when(j > 1)
        def _():
            part_copy(j - 2).wait()

        a_load(j).wait()

        def round_rows(ref):
            places = [pl.multiple_of(z * rounds * m + j * m, 16) for z in range(line)]
            return jnp.concatenate([ref[pl.ds(at, m), :] for at in places], axis=0)

        @pl.loop(0, d // tile)
        def _(n):
            cols = pl.ds(pl.multiple_of(n * tile, tile), tile)
            acc = None
            for back, weight in zip((dq_ref, df_ref, di_ref, ds_ref), weights):
                term = mul(round_rows(back), weight[cols, :], NT)
                acc = term if acc is None else acc + term
            normed = a_ref[lax.rem(j, 2), :, :, cols].reshape(line * m, tile).astype(f32)
            first_ref[:, cols] += jnp.sum(acc * normed, axis=0, keepdims=True)
            stage[lax.rem(j, 2), :, :, cols] = acc.astype(bf16).reshape(line, m, tile)

        part_copy(j).start()

        @pl.when(j + 2 < rounds)
        def _():
            a_load(j + 2).start()

    first_ref[...] = first_ref[...] / norm_gain_ref[...]
    for each in sums:
        each.finish()
    for j in range(max(0, rounds - 2), rounds):
        part_copy(j).wait()
    for store in stores:
        store.wait()
    states.drain(False)
    for each in sums:
        each.drain()


def scan_backward(size, line, rounds, ends, bound, gain, q, f, i, s, o, ub, starts, norm_gain, a, weights, grads):
    rows, c = q.shape
    d = a.shape[1]
    shape = (line, rounds, rows // line // rounds, d)
    part = (rounds, line) + shape[2:]
    blocks, heads = rows // WIDTH, c // WIDTH
    low, wide = VM((rows, c), bf16), VM((rows, c), f32)
    spec = pl.BlockSpec(memory_space=VM)
    return pl.pallas_call(
        partial(scan_back_kernel, size, line, rounds, len(grads)),
        out_shape=[jax.ShapeDtypeStruct((rows, c), bf16)] * 4
        + [jax.ShapeDtypeStruct((2 * heads, WIDTH), f32), jax.ShapeDtypeStruct((1, d), f32)]
        + [jax.ShapeDtypeStruct(part, bf16)]
        + sum_shapes([grad.shape for grad in grads], [False] * len(grads)),
        in_specs=[pl.BlockSpec(memory_space=pltpu.SMEM)]
        + [spec] * 3
        + [pl.BlockSpec(memory_space=pl.ANY)] * (12 + len(grads)),
        out_specs=[pl.BlockSpec(memory_space=pl.ANY)] * 4
        + [spec] * 2
        + [pl.BlockSpec(memory_space=pl.ANY)]
        + [spec] * len(grads),
        scratch_shapes=[low] * 5
        + [wide, VM((blocks, heads, WIDTH, WIDTH), f32), VM((blocks, 8, WIDTH), f32)]
        + states_scratch(size, heads)
        + [wide] * 6
        + [VM(starts.shape, bf16)]
        + [VM((d, c), bf16)] * 4
        + [VM((2,) + part[1:], bf16), DMA((11,)), VM((2,) + part[1:], bf16), DMA((2,)), DMA((2,))]
        + [low] * 4
        + [DMA((4,))]
        + group_sums_scratch([grad.shape for grad in grads]),
        compiler_params=pltpu.CompilerParams(collective_id=2, has_side_effects=True, vmem_limit_bytes=63 * MIB),
        cost_estimate=pl.CostEstimate(flops=8 * rows * c * d, bytes_accessed=40 * MIB, transcendentals=16 * rows * c),
        name="scan_backward",
    )(
        ends,
        bound,
        gain,
        norm_gain.reshape(1, d),
        q,
        f,
        i,
        s,
        o,
        ub,
        starts,
        *weights,
        a.reshape(shape),
        *[in_pairs(grad) for grad in grads],
    )


def middle_kernel(size, rounds, *refs):
    take = taker(refs)
    u_ref, x_ref, gain_ref, out_w, *loaded, cot_some, cot_own = take(9)
    res_out, back_out, e_out, ub_out, second_ref, down_out, out_grad, *grad_outs = take(10)
    gate_w, up_w, down_w = weights = take(3)
    cot_ref = take(1)[0]
    b_ref, e_ref, res_ref, back_ref, ub_ref, part, land, total = take(8)
    wide = take(3)
    down_ref, *tiles = take(4)
    load_sems, res_sems, back_sems, e_sems, ub_sem, down_sem, tile_sems = take(7)
    lines = [take(2) for _ in range(5)]
    hidden, gate_back, up_back = wide
    me = lax.axis_index("tp")
    m, d = x_ref.shape[1:]
    ff = gate_w.shape[1]
    group = size * m
    scatter = Scatter(size, *lines[0], part, land, total)
    gather = Gather(size, *lines[1], b_ref)
    scatter_back = Scatter(size, *lines[2], part, land, total)
    gather_back = Gather(size, *lines[3], e_ref)
    gather_cot = Gather(size, *lines[4], cot_ref)
    known = cot_some.shape[1]
    gain = gain_ref[...]
    tile = min(512, d)
    local = pltpu.make_async_copy
    loads = [local(src, dst, load_sems.at[k]) for k, (src, dst) in enumerate(zip(loaded, weights))]
    loads.append(local(cot_some, cot_ref.at[:, :known], load_sems.at[3]))
    cot_load = local(cot_own.at[known:], cot_ref.at[me, known:], load_sems.at[4])
    cot_load.start()
    for load in loads:
        load.start()
    second_ref[...] = jnp.zeros_like(second_ref)
    greet(*line_peers(size))

    def project_out(j):
        rows = u_ref[:, j].reshape(group, u_ref.shape[3])

        @pl.loop(0, d // tile)
        def _(n):
            cols = pl.ds(pl.multiple_of(n * tile, tile), tile)
            part[j, :, :, cols] = mul(rows, out_w[:, cols], NN).astype(bf16).reshape(size, m, tile)

        scatter.start(j)

    def res_copy(j):
        return local(res_ref.at[j], res_out.at[j], res_sems.at[j])

    def back_copy(j):
        return local(back_ref, back_out.at[j], back_sems.at[0])

    def e_copy(j):
        return local(e_ref.at[:, j], e_out.at[:, j], e_sems.at[j])

    def ub_copy(j):
        return local(ub_ref, ub_out.at[:, j], ub_sem.at[0])

    def down_copy(j):
        return local(down_ref, down_out.at[:, j], down_sem.at[0])

    def norm(j):
        @pl.loop(0, m // 16)
        def _(g):
            r = pl.ds(pl.multiple_of(g * 16, 16), 16)
            residual = x_ref[j, r, :].astype(f32) + total[r, :]
            res_ref[j, r, :] = residual
            scale = lax.rsqrt(jnp.mean(residual * residual, axis=-1, keepdims=True) + epsilon)
            b_ref[me, j, r, :] = (residual * scale * gain).astype(bf16)

        gather.start(j)
        res_copy(j).start()

    def feed(j, piece):
        rows = b_ref[:, j].reshape(group, d)
        cot = cot_ref[:, j].reshape(group, d)
        step = 256
        starts = list(range(0, ff, step))
        for low in starts[len(starts) * piece // PIECES : len(starts) * (piece + 1) // PIECES]:
            cols = slice(low, min(low + step, ff))
            width = cols.stop - cols.start
            gate = mul(rows, gate_w[:, cols], NN)
            up = mul(rows, up_w[:, cols], NN)
            hb = mul(cot, down_w[cols, :], NT)
            sig = jax.nn.sigmoid(gate)
            act = gate * sig
            shape = (size, m, width)
            hidden[:, j, :, cols] = (act * up).astype(bf16).reshape(shape)
            up_back[:, j, :, cols] = (hb * act).astype(bf16).reshape(shape)
            gate_back[:, j, :, cols] = (hb * up * (sig * (1.0 + gate * (1.0 - sig)))).astype(bf16).reshape(shape)

    def feed_back(j):
        scatter.drain(j)
        gates = gate_back[:, j].reshape(group, ff)
        ups = up_back[:, j].reshape(group, ff)

        @pl.loop(0, d // tile)
        def _(n):
            cols = pl.ds(pl.multiple_of(n * tile, tile), tile)
            sums = mul(gates, gate_w[cols, :], NT) + mul(ups, up_w[cols, :], NT)
            part[j, :, :, cols] = sums.astype(bf16).reshape(size, m, tile)

        scatter_back.start(j)

    def feed_out(j):
        rows = hidden[:, j].reshape(group, ff)

        @pl.loop(0, d // tile)
        def _(n):
            cols = pl.ds(pl.multiple_of(n * tile, tile), tile)
            down_ref[:, :, cols] = mul(rows, down_w[:, cols], NN).astype(bf16).reshape(size, m, tile)

        down_copy(j).start()

    def norm_back(j):
        @pl.loop(0, m // 16)
        def _(g):
            r = pl.ds(pl.multiple_of(g * 16, 16), 16)
            b_back, residual = total[r, :], res_ref[j, r, :]
            scale = lax.rsqrt(jnp.mean(residual * residual, axis=-1, keepdims=True) + epsilon)
            normed = residual * scale
            second_ref[...] += jnp.sum(b_back * normed, axis=0, keepdims=True)
            inner = b_back * gain
            back = cot_ref[me, j, r, :].astype(f32) + scale * (
                inner - normed * jnp.mean(inner * normed, axis=-1, keepdims=True)
            )
            back_ref[r, :] = back
            e_ref[me, j, r, :] = back.astype(bf16)

        gather_back.start(j)
        back_copy(j).start()

    def unproject(j):
        e_copy(j).start()
        rows = e_ref[:, j].reshape(group, d)
        ub_ref[...] = mul(rows, out_w[...], NT).reshape(size, m, out_w.shape[0])
        ub_copy(j).start()

    depth = tiles[0].shape[0]
    count = d // depth

    def tile_copies(n):
        rows = pl.ds(n * depth, depth)
        return [local(src, dst.at[rows, :], tile_sems.at[k]) for k, (src, dst) in enumerate(zip(tiles, grad_outs))]

    def weight_tile(n):
        cols = pl.ds(n * depth, depth)
        for left, right, out in zip((b_ref, b_ref, cot_ref), (gate_back, up_back, hidden), tiles):
            rows = left[:, :, :, cols].reshape(rounds * group, depth)
            out[...] = mul(rows, right[...].reshape(rounds * group, ff), TN).astype(bf16)
        for copy in tile_copies(n):
            copy.start()

    cot_load.wait()
    held = {}

    def then(kind, copies):
        for copy in held.get(kind, []):
            copy.wait()
        held[kind] = copies

    shares = sum(name[0] == "W" for name in STEPS)
    for name in STEPS:
        kind, j, t = name[0], int(name[1]), int(name[2:] or 0)
        if kind == "A":
            project_out(j)
        elif kind == "C":
            gather_cot.step(j, t) if t else gather_cot.start(j)
        elif kind == "S" and t < size - 1:
            scatter.step(j, t)
        elif kind == "S":
            scatter.finish(j)
            norm(j)
        elif kind == "G":
            gather.step(j, t)
        elif kind == "F":
            then("loads", loads if "loads" not in held else [])
            then("loads", [])
            feed(j, t)
        elif kind == "B":
            feed_back(j)
        elif kind == "O":
            then(kind, [])
            feed_out(j)
            then(kind, [down_copy(j)])
        elif kind == "T" and t < size - 1:
            scatter_back.step(j, t)
        elif kind == "T":
            then(kind, [])
            scatter_back.finish(j)
            norm_back(j)
            then(kind, [back_copy(j)])
        elif kind == "E":
            gather_back.step(j, t)
        elif kind == "U":
            then(kind, [])
            unproject(j)
            then(kind, [ub_copy(j)])
        elif kind == "W":
            for n in range(count * j // shares, count * (j + 1) // shares):
                then(kind, [])
                weight_tile(n)
                then(kind, tile_copies(n))
    for kind in list(held):
        then(kind, [])
    width = u_ref.shape[3]

    def out_tile(n, slot):
        rows = pl.ds(pl.multiple_of(n * depth, depth), depth)
        source = tiles[slot].at[:, pl.ds(0, width)]
        return local(source, out_grad.at[rows, :], tile_sems.at[slot])

    slots = len(tiles) - 1

    @pl.loop(0, count // slots)
    def _(n):
        for slot in range(slots):
            at = n * slots + slot

            @pl.when(n > 0)
            def _():
                out_tile(at - slots, slot).wait()

            cols = pl.ds(pl.multiple_of(at * depth, depth), depth)
            rows = e_ref[:, :, :, cols].reshape(rounds * group, depth)
            tiles[slot][:, :width] = mul(rows, u_ref[...].reshape(rounds * group, width), TN).astype(bf16)
            out_tile(at, slot).start()

    for slot in range(slots):
        out_tile(count - slots + slot, slot).wait()

    @pl.loop(0, rounds)
    def _(j):
        res_copy(j).wait()
        e_copy(j).wait()

        @pl.when(j >= known)
        def _():
            gather_cot.drain(j)

        gather.drain(j)
        scatter_back.drain(j)
        gather_back.drain(j)


def middle(size, rounds, u, x, cot_some, cot, gain, out_w, gate_w, up_w, down_w):
    rows, d = x.shape
    m = rows // rounds
    c, ff = out_w.shape[0], gate_w.shape[1]
    shape = (size, rounds, m)
    sems = DMA((2, rounds, size))
    spec, far = pl.BlockSpec(memory_space=VM), pl.BlockSpec(memory_space=pl.ANY)
    depth = min(256, d)
    outs = pl.pallas_call(
        partial(middle_kernel, size, rounds),
        out_shape=[
            jax.ShapeDtypeStruct((rounds, m, d), f32),
            jax.ShapeDtypeStruct((rounds, m, d), f32),
            jax.ShapeDtypeStruct(shape + (d,), bf16),
            jax.ShapeDtypeStruct(shape + (c,), f32),
            jax.ShapeDtypeStruct((1, d), f32),
            jax.ShapeDtypeStruct(shape + (d,), bf16),
            jax.ShapeDtypeStruct((d, c), bf16),
        ]
        + [jax.ShapeDtypeStruct((d, ff), bf16)] * 3,
        in_specs=[spec] * 4 + [far] * 5,
        out_specs=[far] * 4 + [spec] + [far] * 5,
        scratch_shapes=[
            VM(gate_w.shape, bf16),
            VM(up_w.shape, bf16),
            VM(down_w.shape, bf16),
            VM(shape + (d,), bf16),
            VM(shape + (d,), bf16),
            VM(shape + (d,), bf16),
            VM((rounds, m, d), f32),
            VM((m, d), f32),
            VM((size, m, c), f32),
            VM((rounds, size, m, d), bf16),
            VM((2, rounds, size - 1, m, d), bf16),
            VM((m, d), f32),
        ]
        + [VM(shape + (ff,), bf16)] * 3
        + [VM((size, m, d), bf16)]
        + [VM((depth, ff), bf16)] * 3
        + [DMA((5,)), DMA((rounds,)), DMA((1,)), DMA((rounds,)), DMA((1,)), DMA((1,)), DMA((3,))]
        + [sems] * 10,
        compiler_params=pltpu.CompilerParams(collective_id=3, has_side_effects=True, vmem_limit_bytes=63 * MIB),
        cost_estimate=pl.CostEstimate(
            flops=2 * size * rows * d * (2 * c + 9 * ff), bytes_accessed=56 * MIB, transcendentals=size * rows * ff
        ),
        name="middle",
    )(
        u.reshape(shape + (c,)),
        x.reshape(rounds, m, d),
        gain.reshape(1, d),
        out_w,
        gate_w,
        up_w,
        down_w,
        cot_some,
        cot.reshape(rounds, m, d),
    )
    res, back, e, ub, second, down, *grads = outs
    total = size * rows
    return (
        res.reshape(rows, d),
        back.reshape(rows, d),
        ub.reshape(total, c),
        second,
        down.reshape(total, d),
        *grads,
    )


class Everyone:
    def __init__(self, size, axis, mine, land, sems):
        self.size, self.axis = size, axis
        self.here = lax.axis_index(axis)
        self.mine, self.land, self.sems = mine, land, sems

    def copy(self, slot, peer):
        return remote(self.mine, self.land.at[slot], self.sems.at[0, peer], self.sems.at[1, slot], self.axis, peer)

    def others(self):
        for k in range(self.size):
            yield k, self.here != k

    def start(self):
        for k, other in self.others():

            @pl.when(other)
            def _():
                self.copy(self.here, k).start()

    def finish(self, out):
        out[...] = self.mine[...]
        for k, other in self.others():

            @pl.when(other)
            def _():
                self.copy(k, k).wait_recv()
                out[...] = out[...] + self.land[k]

    def drain(self):
        for k, other in self.others():

            @pl.when(other)
            def _():
                self.copy(self.here, k).wait_send()


def everyone_scratch(size, rows):
    return [VM((rows, WIDTH), f32), VM((size, rows, WIDTH), f32), DMA((2, size))]


def stack(vector, into, at):
    for k in range(vector.shape[1] // WIDTH):
        into[at + k : at + k + 1, :] = vector[:, k * WIDTH : (k + 1) * WIDTH]


def last_kernel(size, groups, rounds, count, mixed, *refs):
    take = taker(refs)
    backs = take(4)
    x_ref, gain_ref, second_ref, small_ref, first_ref, back_in, a_in, part_in, res_in, down_in = take(10)
    grads = take(count)
    tokens_far, small_out, output_ref = take(3)
    grad_outs = take(count + (4 if mixed else 0))
    part, land, total, s_send, s_recv = take(5)
    small_seq, gains_tp, sides = take(3), take(3), take(1)[0]
    nears = take(4 if mixed else 0)
    a_ref, tokens_out, res_ref, down_ref, load_sems, store_sems = take(6)
    sums = group_sums(groups, grads + nears, grad_outs, take)
    early, late = sums[:2], sums[2:]

    seq, seq_count = group_peers(groups, "seq")
    tp, tp_count = group_peers(size, "tp")
    greet(seq + tp, seq_count + tp_count)

    for each in sums[:count]:
        each.start()
    m, d = x_ref.shape[1:]
    tile = min(512, d)
    local = pltpu.make_async_copy

    def part_load(j):
        return local(part_in.at[j], part.at[j], load_sems.at[2 + j])

    a_load = local(a_in, a_ref, load_sems.at[1])
    back_load = local(back_in, tokens_out, load_sems.at[0])

    for j in range(rounds):
        part_load(j).start()
    a_load.start()
    back_load.start()
    output_loads = [
        local(source, target, load_sems.at[2 + rounds + k])
        for k, (source, target) in enumerate(((res_in, res_ref), (down_in, down_ref)))
    ]
    for load in output_loads:
        load.start()

    def store(j):
        return local(tokens_out.at[j], tokens_far.at[j], store_sems.at[j])

    group = size * m
    scatter = Scatter(size, s_send, s_recv, part, land, total)
    gain = gain_ref[...]

    seq_small = Everyone(groups, "seq", *small_seq)
    tp_gains = Everyone(size, "tp", *gains_tp)
    lines, smalls = d // WIDTH, small_ref.shape[0]

    def mix(back, each):
        rows = back[...].reshape(rounds * group, back.shape[3])
        depth = each.own.shape[1]
        for side, into in ((1 - each.side, each.grad), (each.side, each.own)):

            @pl.loop(0, each.half)
            def _(k):
                cols = pl.ds(pl.multiple_of((2 * k + side) * depth, depth), depth)
                left = a_ref[:, :, :, cols].reshape(rounds * group, depth)
                into[k] = mul(left, rows, TN).astype(bf16)

            if into is each.grad:
                each.start()

    def norm_back(j):
        @pl.loop(0, m // 16)
        def _(g):
            r = pl.ds(pl.multiple_of(g * 16, 16), 16)
            a_back, x = total[r, :], x_ref[j, r, :].astype(f32)
            scale = lax.rsqrt(jnp.mean(x * x, axis=-1, keepdims=True) + epsilon)
            normed = x * scale
            inner = a_back * gain
            tokens_out[j, r, :] = tokens_out[j, r, :] + scale * (
                inner - normed * jnp.mean(inner * normed, axis=-1, keepdims=True)
            )

    def steps(j, low, high):
        for t in range(low, high):
            if t < size - 1:
                scatter.step(j, t)
            else:
                scatter.finish(j)
                norm_back(j)
                store(j).start()

    stack(second_ref[...], gains_tp[0], 0)
    stack(first_ref[...], gains_tp[0], lines)
    tp_gains.start()
    for j in range(rounds):
        part_load(j).wait()
        scatter.start(j)
    tp_gains.finish(sides)
    small_seq[0][: 2 * lines, :] = sides[...]
    small_seq[0][2 * lines : 2 * lines + smalls, :] = small_ref[...]
    seq_small.start()
    for each in early:
        each.middle()
    a_load.wait()
    steps(0, 1, 2)
    back_load.wait()
    if mixed:
        for at, (back, each) in enumerate(zip(backs, late)):
            mix(back, each)
            steps(0, 2, 3) if at == 0 else None
            steps(0, 3, size) if at == 2 else None
    else:
        steps(0, 2, size)
    for each in early:
        each.relay()
    for each in late:
        each.middle()
    for load in output_loads:
        load.wait()

    @pl.loop(0, rounds * m // 16)
    def _(g):
        r = pl.ds(pl.multiple_of(g * 16, 16), 16)
        output_ref[r, :] = (res_ref[r, :] + down_ref[r, :].astype(f32)).astype(bf16)

    steps(1, 1, 3)
    steps(1, 3, size)
    for each in late[:2]:
        each.relay()
    steps(2, 1, 3)
    for each in late[2:]:
        each.relay()
    steps(2, 3, size)
    for each in early:
        each.finish()
    seq_small.finish(small_out)
    for j in range(3, rounds):
        steps(j, 1, size)
    for each in late:
        each.finish()

    for each in sums + [seq_small, tp_gains]:
        each.drain()

    @pl.loop(0, rounds)
    def _(j):
        scatter.drain(j)
        store(j).wait()


def last(size, groups, rounds, backs, part, a, x, back, gain, second, first, small, residual, down, grads, turned):
    mixed = len(turned) > len(grads)
    rows, d = x.shape
    m = rows // rounds
    c = backs[0].shape[1]
    shape = (size, rounds, m)
    lines = d // WIDTH
    sems = DMA((2, rounds, size))
    spec = pl.BlockSpec(memory_space=VM)
    small_rows = 2 * lines + small.shape[0]
    shapes = [grad.shape for grad in grads] + ([(groups, d // groups, c)] * 4 if mixed else [])
    outs = pl.pallas_call(
        partial(last_kernel, size, groups, rounds, len(grads), mixed),
        out_shape=[
            jax.ShapeDtypeStruct((rounds, m, d), f32),
            jax.ShapeDtypeStruct((small_rows, WIDTH), f32),
            jax.ShapeDtypeStruct((rows, d), bf16),
        ]
        + sum_shapes(shapes, turned),
        in_specs=[spec] * 9 + [pl.BlockSpec(memory_space=pl.ANY)] * (5 + len(grads)),
        out_specs=[pl.BlockSpec(memory_space=pl.ANY)] + [spec] * (2 + len(shapes)),
        scratch_shapes=[
            VM((rounds, size, m, d), bf16),
            VM((2, rounds, size - 1, m, d), bf16),
            VM((m, d), f32),
            sems,
            sems,
        ]
        + everyone_scratch(groups, small_rows)
        + everyone_scratch(size, 2 * lines)
        + [VM((2 * lines, WIDTH), f32)]
        + ([VM((groups // 2, d // groups, c), bf16)] * 4 if mixed else [])
        + [VM(shape + (d,), bf16)]
        + [VM((rounds, m, d), f32), VM((rows, d), f32), VM((rows, d), bf16), DMA((4 + rounds,)), DMA((rounds,))]
        + group_sums_scratch(shapes),
        compiler_params=pltpu.CompilerParams(collective_id=4, has_side_effects=True, vmem_limit_bytes=63 * MIB),
        cost_estimate=pl.CostEstimate(flops=16 * size * rows * d * c, bytes_accessed=56 * MIB, transcendentals=0),
        name="last",
    )(
        *[part.reshape(shape + (c,)) for part in backs],
        x.reshape(rounds, m, d),
        gain.reshape(1, d),
        second,
        small,
        first,
        back.reshape(rounds, m, d),
        a.reshape(shape + (d,)),
        part,
        residual,
        down,
        *[in_pairs(grad) for grad in grads],
    )
    sides = outs[1]
    return (outs[0].reshape(rows, d), sides[:lines], sides[lines : 2 * lines], sides[2 * lines :]) + tuple(outs[2:])


def per_device(
    size,
    groups,
    tokens,
    lengths,
    cotangent,
    first_gain,
    query_weight,
    forget_weight,
    input_weight,
    swish_weight,
    bound_logit,
    group_gain,
    out_weight,
    second_gain,
    gate_weight,
    up_weight,
    down_weight,
):
    weights = (query_weight, forget_weight, input_weight, swish_weight)
    ends = jnp.cumsum(lengths).astype(jnp.int32)
    bound, head_gain = bound_logit.reshape(1, -1), group_gain.reshape(1, -1)
    a, q, f, i, s, cot_some, o, u, starts = front(
        size, groups, ROUNDS, tokens, cotangent, first_gain, weights, ends, bound, head_gain
    )
    residual, back, ub, second, down, *wide = middle(
        size, ROUNDS, u, tokens, cot_some, cotangent, second_gain, out_weight, gate_weight, up_weight, down_weight
    )
    down, ub = lax.optimization_barrier((down, ub))
    down = lax.psum_scatter(down, "tp", scatter_dimension=0, tiled=True)
    d = tokens.shape[1]

    def chunks(grad):
        return grad.reshape(groups, grad.shape[0] // groups, grad.shape[1])

    def grad_of(left, right):
        return chunks(lax.dot_general(left, right, TN, preferred_element_type=f32).astype(bf16))

    outs, gates, ups, downs = (chunks(grad) for grad in wide)
    dq, df, di, ds, small, first, part, gate_grad, up_grad = scan_backward(
        groups,
        size,
        ROUNDS,
        ends,
        bound,
        head_gain,
        q,
        f,
        i,
        s,
        o,
        ub,
        starts,
        first_gain,
        a,
        weights,
        [gates, ups],
    )
    back_rows = (dq, df, di, ds)
    here_too = groups == 8
    others = [downs, outs] + ([] if here_too else [grad_of(a, part) for part in back_rows])
    tokens_grad, second_sum, first_sum, small_sum, output, *sums = last(
        size,
        groups,
        ROUNDS,
        back_rows,
        part,
        a,
        tokens,
        back,
        first_gain,
        second,
        first,
        small,
        residual,
        down,
        others,
        [True, True] + [False] * 4,
    )
    down_grad, out_grad, query_grad, forget_grad, input_grad, swish_grad = sums
    heads = bound_logit.shape[0]
    here = lax.axis_index("seq")
    place = here * size + lax.axis_index("tp")
    each = d // (groups * size)
    wide = WIDTH // groups
    first_grad = lax.dynamic_slice_in_dim(first_sum.reshape(-1), place * each, each)
    second_grad = lax.dynamic_slice_in_dim(second_sum.reshape(-1), place * each, each)
    bound_grad = lax.dynamic_slice_in_dim(small_sum[:heads], here * wide, wide, axis=1)
    head_grad = lax.dynamic_slice_in_dim(small_sum[heads:], here * wide, wide, axis=1)
    return (
        output,
        tokens_grad,
        first_grad,
        query_grad,
        forget_grad,
        input_grad,
        swish_grad,
        bound_grad,
        head_grad,
        out_grad,
        second_grad,
        gate_grad,
        up_grad,
        down_grad,
    )


def solution(mesh):
    rows, both, cols, lines = P(("seq", "tp"), None), P(("seq", "tp")), P(None, "tp"), P("tp", None)
    in_specs = (rows, P(), rows, P(), cols, cols, cols, cols, lines, lines, lines, P(), cols, cols, lines)
    down, across = P("seq", "tp"), P("tp", "seq")
    out_specs = (rows, rows, both, down, down, down, down, across, across, across, both, down, down, across)
    return jax.shard_map(
        partial(per_device, mesh.shape["tp"], mesh.shape["seq"]),
        mesh=mesh,
        in_specs=in_specs,
        out_specs=out_specs,
        check_vma=False,
    )
```

```python
from functools import partial

import jax
import jax.numpy as jnp
from jax import lax
from jax.experimental import pallas as pl
from jax.experimental.pallas import tpu as pltpu
from jax.sharding import PartitionSpec as P

WIDTH = 128
ROUNDS = 4
KNOWN = 1
PIECES = 3
STEPS = (
    "C10", "C11", "C20", "A0", "C12", "A1", "C21", "C22", "C13", "S01", "C30", "S11", "S02", "S03", "C23", "A2",
    "C31", "A3", "G01", "G02", "S21", "S22", "S12", "S23", "G03", "F00", "F01", "F02", "O0", "S13", "B0", "C32",
    "C33", "G11", "G12", "G13", "T01", "S31", "F10", "F11", "F12", "O1", "T02", "G21", "T03", "B1", "S32", "G22",
    "G23", "F20", "E01", "S33", "E02", "E03", "F21", "F22", "T11", "T12", "T13", "G31", "O2", "B2", "E11", "U0",
    "T21", "G32", "G33", "F30", "F31", "T22", "F32", "O3", "E12", "T23", "B3", "W0", "E21", "E13", "U1", "T31",
    "T32", "E22", "W1", "W2", "T33", "W3", "E23", "W5", "E31", "W6", "W4", "U2", "W7", "E32", "E33", "U3",
)
MIB = 1 << 20
epsilon = 1e-05

f32 = jnp.float32
bf16 = jnp.bfloat16
NN = (((1,), (0,)), ((), ()))
NT = (((1,), (1,)), ((), ()))
TN = (((0,), (0,)), ((), ()))
VM = pltpu.VMEM
DMA = pltpu.SemaphoreType.DMA
MESH = pl.DeviceIdType.MESH


def mul(left, right, dims):
    return lax.dot_general(left, right, dims, preferred_element_type=f32)


def silu_slope(value):
    gate = jax.nn.sigmoid(value)
    return gate * (1.0 + value * (1.0 - gate))


def remote(src, dst, send, recv, axis, peer):
    return pltpu.make_async_remote_copy(
        src_ref=src,
        dst_ref=dst,
        send_sem=send,
        recv_sem=recv,
        device_id={axis: peer},
        device_id_type=MESH,
    )


def greet(peers, count):
    barrier = pltpu.get_barrier_semaphore()
    for axis, peer, wanted in peers:

        @pl.when(wanted)
        def _():
            pl.semaphore_signal(barrier, inc=1, device_id={axis: peer}, device_id_type=MESH)

    pl.semaphore_wait(barrier, count)


def line_peers(size):
    me = lax.axis_index("tp")
    peers = [("tp", lax.rem(me + 1, size), me < size - 1), ("tp", lax.rem(me + size - 1, size), me > 0)]
    return peers, jnp.where(me < size - 1, 1, 0) + jnp.where(me > 0, 1, 0)


def group_peers(size, axis):
    me = lax.axis_index(axis)
    return [(axis, lax.rem(me + k, size), True) for k in range(1, size)], size - 1


class Line:
    def __init__(self, size, send, recv):
        self.size = size
        self.me = lax.axis_index("tp")
        self.right = lax.rem(self.me + 1, size)
        self.left = lax.rem(self.me + size - 1, size)
        self.send, self.recv = send, recv

    def hop(self, way, src, dst, j, at):
        peer = self.right if way == 0 else self.left
        return remote(src, dst, self.send.at[way, j, at], self.recv.at[way, j, at], "tp", peer)


class Scatter(Line):
    def __init__(self, size, send, recv, part, land, total):
        super().__init__(size, send, recv)
        self.part, self.land, self.total = part, land, total

    def copy(self, way, j, to):
        return self.hop(way, self.part.at[j, to], self.slot(way, j, to), j, to)

    def slot(self, way, j, to):
        return self.land.at[way, j, to - 1 + way]

    def start(self, j):
        last = self.size - 1

        @pl.when(self.me == 0)
        def _():
            for to in range(last, 0, -1):
                self.copy(0, j, to).start()

        @pl.when(self.me == last)
        def _():
            for to in range(last):
                self.copy(1, j, to).start()

    def step(self, j, t):
        last = self.size - 1
        for way in (0, 1):
            place = self.me if way == 0 else last - self.me
            to = last - t + place
            to = to if way == 0 else last - to

            @pl.when((place >= 1) & (place <= t))
            def _():
                copy = self.copy(way, j, to)
                copy.wait_recv()
                self.add(self.part.at[j, to], self.slot(way, j, to))
                copy.start()

    def add(self, into, more):
        rows = into.shape[0]

        @pl.loop(0, rows // 16)
        def _(g):
            r = pl.ds(pl.multiple_of(g * 16, 16), 16)
            into[r, :] = (into[r, :].astype(f32) + more[r, :].astype(f32)).astype(bf16)

    def finish(self, j):
        me, last = self.me, self.size - 1
        rows = self.total.shape[0]

        def over(body):
            @pl.loop(0, rows // 16)
            def _(g):
                body(pl.ds(pl.multiple_of(g * 16, 16), 16))

        def first(r):
            self.total[r, :] = self.part[j, me, r, :].astype(f32)

        over(first)
        for way, there in ((0, me >= 1), (1, me < last)):

            @pl.when(there)
            def _():
                self.copy(way, j, me).wait_recv()

                def more(r):
                    self.total[r, :] = self.total[r, :] + self.land[way, j, me - 1 + way, r, :].astype(f32)

                over(more)

    def drain(self, j):
        for to in range(self.size):

            @pl.when(self.me < to)
            def _():
                self.copy(0, j, to).wait_send()

            @pl.when(self.me > to)
            def _():
                self.copy(1, j, to).wait_send()


class Gather(Line):
    def __init__(self, size, send, recv, whole):
        super().__init__(size, send, recv)
        self.whole = whole

    def copy(self, way, j, source):
        block = self.whole.at[source, j]
        return self.hop(way, block, block, j, source)

    def start(self, j):
        @pl.when(self.me < self.size - 1)
        def _():
            self.copy(0, j, self.me).start()

        @pl.when(self.me > 0)
        def _():
            self.copy(1, j, self.me).start()

    def step(self, j, t):
        last = self.size - 1

        @pl.when(self.me >= t)
        def _():
            copy = self.copy(0, j, self.me - t)
            copy.wait_recv()

            @pl.when(self.me < last)
            def _():
                copy.start()

        @pl.when(self.me + t <= last)
        def _():
            copy = self.copy(1, j, self.me + t)
            copy.wait_recv()

            @pl.when(self.me > 0)
            def _():
                copy.start()

    def drain(self, j):
        last = self.size - 1
        for source in range(self.size):

            @pl.when((self.me >= source) & (self.me < last))
            def _():
                self.copy(0, j, source).wait_send()

            @pl.when((self.me <= source) & (self.me > 0))
            def _():
                self.copy(1, j, source).wait_send()


def add_rows(into, left, right):
    rows = into.shape[0]

    @pl.loop(0, rows // 16)
    def _(g):
        r = pl.ds(pl.multiple_of(g * 16, 16), 16)
        into[r, :] = (left[r, :].astype(f32) + right[r, :].astype(f32)).astype(bf16)


class GroupSum:
    refs = 6

    def __init__(self, size, grad, out, own, got, land, *sems):
        self.half = size // 2
        here = lax.axis_index("seq")
        self.side = lax.rem(here, 2)
        self.mine = here // 2
        self.sibling = here + 1 - 2 * self.side
        self.grad, self.own, self.got, self.land, self.out = grad, own, got, land, out
        self.near_sems, *self.sems = sems
        self.loads = len(grad.shape) == 4
        self.turned = out.shape != own.shape[1:]

    @staticmethod
    def scratch(shape):
        half = shape[0]
        return [VM(shape, bf16)] * 3 + [DMA((3, half)), DMA((half,)), DMA((half,))]

    def near(self, k):
        sems = self.near_sems
        source = self.grad.at[k, 1 - self.side] if self.loads else self.grad.at[k]
        return remote(source, self.got.at[k], sems.at[0, k], sems.at[1, k], "seq", self.sibling)

    def load(self, k):
        return pltpu.make_async_copy(self.grad.at[k, self.side], self.own.at[k], self.near_sems.at[2, k])

    def start(self):
        for k in range(self.half):
            self.near(k).start()
            if self.loads:
                self.load(k).start()

    def pair(self, k, into):
        if self.loads:
            self.load(k).wait()
        self.near(k).wait_recv()
        add_rows(into, self.own.at[k], self.got.at[k])

    def far(self, k):
        send, recv = self.sems
        return remote(self.own.at[k], self.land.at[self.mine], send.at[k], recv.at[self.mine], "seq", 2 * k + self.side)

    def arrival(self, k):
        send, recv = self.sems
        return remote(self.own.at[k], self.land.at[k], send.at[k], recv.at[k], "seq", 2 * k + self.side)

    def middle(self):
        for k in range(self.half):

            @pl.when(k == self.mine)
            def _():
                self.pair(k, self.land.at[k])

            @pl.when(k != self.mine)
            def _():
                self.pair(k, self.own.at[k])
                self.far(k).start()

    def relay(self):
        pass

    def arrive(self):
        for k in range(self.half):

            @pl.when(k != self.mine)
            def _():
                self.arrival(k).wait_recv()

    def terms(self):
        return [self.land.at[k] for k in range(self.half)]

    def finish(self):
        self.arrive()
        rows, cols = self.own.shape[1:]

        def total(r, c):
            acc = None
            for term in self.terms():
                part = term[r, c].astype(f32)
                acc = part if acc is None else acc + part
            return acc

        if self.turned:

            @pl.loop(0, cols // WIDTH)
            def _(g):
                c = pl.ds(pl.multiple_of(g * WIDTH, WIDTH), WIDTH)
                self.out[c, :] = total(slice(None), c).T

        else:

            @pl.loop(0, rows // 16)
            def _(g):
                r = pl.ds(pl.multiple_of(g * 16, 16), 16)
                self.out[r, :] = total(r, slice(None))

    def drain(self):
        for k in range(self.half):
            self.near(k).wait_send()
        self.drain_far()

    def drain_far(self):
        for k in range(self.half):

            @pl.when(k != self.mine)
            def _():
                self.far(k).wait_send()


class SquareSum(GroupSum):
    refs = 6

    def __init__(self, *args):
        super().__init__(*args)
        self.hop, self.far_sems = self.sems
        x, y = lax.rem(self.mine, 2), self.mine // 2
        self.beside = (2 * y + 1 - x, 2 * (1 - y) + x)
        self.opposite = 2 * (1 - y) + 1 - x
        rows = self.own.shape[1] // 2
        self.halves = (pl.ds(0, rows), pl.ds(rows, rows))

    @staticmethod
    def scratch(shape):
        half, rows, cols = shape
        return [
            VM(shape, bf16),
            VM(shape, bf16),
            VM((2, rows, cols), bf16),
            DMA((3, half)),
            VM((2, rows // 2, cols), bf16),
            DMA((2, 6)),
        ]

    def over(self, way, at, source, target):
        sems = self.far_sems
        return remote(source, target, sems.at[0, at], sems.at[1, at], "seq", 2 * self.beside[way] + self.side)

    def pass_on(self, way):
        return self.over(way, way, self.own.at[self.opposite, self.halves[way]], self.hop.at[way])

    def deliver(self, way, half):
        source = self.own.at[self.beside[way], self.halves[half]]
        return self.over(way, 2 + 2 * way + half, source, self.land.at[way, self.halves[half]])

    def middle(self):
        self.pair(self.opposite, self.own.at[self.opposite])
        for way in (0, 1):
            self.pass_on(way).start()
        for way in (0, 1):
            self.pair(self.beside[way], self.own.at[self.beside[way]])
            self.deliver(way, way).start()
        self.pair(self.mine, self.own.at[self.mine])

    def relay(self):
        for way in (0, 1):
            self.pass_on(way).wait_recv()
            into = self.own.at[self.beside[1 - way], self.halves[way]]
            add_rows(into, into, self.hop.at[way])
            self.deliver(1 - way, way).start()

    def arrive(self):
        for way in (0, 1):
            for half in (0, 1):
                self.deliver(way, half).wait_recv()

    def terms(self):
        return [self.own.at[self.mine], self.land.at[0], self.land.at[1]]

    def drain_far(self):
        for way in (0, 1):
            self.pass_on(way).wait_send()
            for half in (0, 1):
                self.deliver(way, half).wait_send()


def summer(size):
    return SquareSum if size == 8 else GroupSum


def group_sums(size, grads, outs, take):
    kind = summer(size)
    return [kind(size, grad, out, *take(kind.refs)) for grad, out in zip(grads, outs)]


def group_sums_scratch(shapes):
    scratch = []
    for size, rows, cols in shapes:
        scratch += summer(size).scratch((size // 2, rows, cols))
    return scratch


def sum_shapes(shapes, turned):
    shapes = [shape[:0:-1] if turn else shape[1:] for shape, turn in zip(shapes, turned)]
    return [jax.ShapeDtypeStruct(shape, f32) for shape in shapes]


def in_pairs(grad):
    return grad.reshape((grad.shape[0] // 2, 2) + grad.shape[1:])


def taker(refs):
    refs = list(refs)

    def take(count):
        taken, refs[:count] = refs[:count], []
        return taken

    return take


def document(rows, ends_ref):
    total = jnp.where(rows >= ends_ref[0], 1, 0)
    for k in range(1, ends_ref.shape[0]):
        total = total + jnp.where(rows >= ends_ref[k], 1, 0)
    return total


def block_masks(first, ends_ref):
    shape = (WIDTH, WIDTH)
    down = lax.broadcasted_iota(jnp.int32, shape, 0)
    along = lax.broadcasted_iota(jnp.int32, shape, 1)
    docs = document(first + down, ends_ref)
    same = (docs == document(first + along, ends_ref)) & (down >= along)
    before = jnp.where(first > 0, document(first - 1, ends_ref), -1)
    final = document(first + WIDTH - 1, ends_ref)
    carry = jnp.where(docs == before, 1.0, 0.0)
    tail = jnp.where(docs == final, 1.0, 0.0)
    keep = jnp.where(final == before, 1.0, 0.0)
    return same, carry, tail, keep


def running(log_forget):
    shape = (WIDTH, WIDTH)
    lower = lax.broadcasted_iota(jnp.int32, shape, 0) >= lax.broadcasted_iota(jnp.int32, shape, 1)
    ones = jnp.where(lower, 1.0, 0.0).astype(bf16)
    high = log_forget.astype(bf16)
    low = (log_forget - high.astype(f32)).astype(bf16)
    return mul(ones, high, NN) + mul(ones, low, NN)


def decay_parts(forget_pre, bound):
    away = jax.nn.sigmoid(-forget_pre)
    key = jax.nn.sigmoid(-bound) * away
    return key, running(jnp.log(1.0 - key)), away


class States:
    def __init__(self, size, out_state, out_decay, land_state, land_decay, sems):
        self.size = size
        self.here = lax.axis_index("seq")
        self.out_state, self.out_decay = out_state, out_decay
        self.land_state, self.land_decay = land_state, land_decay
        self.sems = sems

    def pair(self, slot, peer):
        s = self.sems
        return (
            remote(self.out_state, self.land_state.at[slot], s.at[0, peer], s.at[1, slot], "seq", peer),
            remote(self.out_decay, self.land_decay.at[slot], s.at[2, peer], s.at[3, slot], "seq", peer),
        )

    def sends(self, later):
        for k in range(self.size):
            yield k, (self.here < k if later else self.here > k)

    def start(self, later):
        for k, wanted in self.sends(later):

            @pl.when(wanted)
            def _():
                for copy in self.pair(self.here, k):
                    copy.start()

    def compose(self, later, state):
        state[...] = jnp.zeros_like(state)
        order = range(self.size) if later else range(self.size - 1, -1, -1)
        for k in order:

            @pl.when(self.here > k if later else self.here < k)
            def _():
                for copy in self.pair(k, k):
                    copy.wait_recv()
                for h in range(state.shape[0]):
                    decay = self.land_decay[k, h : h + 1, :]
                    state[h] = decay * state[h] + self.land_state[k, h].astype(f32)

    def drain(self, later):
        for k, wanted in self.sends(later):

            @pl.when(wanted)
            def _():
                for copy in self.pair(self.here, k):
                    copy.wait_send()


def states_scratch(size, heads):
    return [
        VM((heads, WIDTH, WIDTH), f32),
        VM((heads, WIDTH, WIDTH), bf16),
        VM((8, WIDTH), f32),
        VM((size, heads, WIDTH, WIDTH), bf16),
        VM((size, 8, WIDTH), f32),
        DMA((4, size)),
    ]


def front_kernel(size, groups, rounds, *refs):
    take = taker(refs)
    ends_ref, x_ref, norm_gain_ref, bound_ref, gain_ref, cot_in, *loaded = take(10)
    a_out, q_out, f_out, i_out, s_out, cot_out, o_ref, u_ref, starts_ref = take(9)
    *weights, a_ref, q_ref, f_ref, i_ref, s_ref, cot_ref = take(10)
    qd_ref, kd_ref, qe_ref, adds, decays = take(5)
    state, out_state, out_decay, land_state, land_decay, sems = take(6)
    load_sems, store_sems, a_send, a_recv, c_send, c_recv = take(6)
    me = lax.axis_index("tp")
    m, d = x_ref.shape[1:]
    known = cot_ref.shape[1]
    local = pltpu.make_async_copy
    cot_load = local(cot_in.at[:known], cot_ref.at[me], load_sems.at[4])
    cot_load.start()
    loads = [local(source, target, load_sems.at[k]) for k, (source, target) in enumerate(zip(loaded, weights))]
    for load in loads:
        load.start()
    line, line_count = line_peers(size)
    seq, seq_count = group_peers(groups, "seq")
    greet(line + seq, line_count + seq_count)

    gather = Gather(size, a_send, a_recv, a_ref)
    gather_cot = Gather(size, c_send, c_recv, cot_ref)
    norm_gain = norm_gain_ref[...]

    @pl.loop(0, rounds)
    def _(j):
        @pl.loop(0, m // 16)
        def _(g):
            r = pl.ds(pl.multiple_of(g * 16, 16), 16)
            x = x_ref[j, r, :].astype(f32)
            scale = lax.rsqrt(jnp.mean(x * x, axis=-1, keepdims=True) + epsilon)
            a_ref[me, j, r, :] = (x * scale * norm_gain).astype(bf16)

        gather.start(j)

    for load in loads:
        load.wait()
    cot_load.wait()
    pres = (q_ref, f_ref, i_ref, s_ref)

    rows, c = q_ref.shape
    blocks, heads = rows // WIDTH, c // WIDTH
    base = lax.axis_index("seq") * rows
    states = States(groups, out_state, out_decay, land_state, land_decay, sems)
    state[...] = jnp.zeros_like(state)
    out_decay[...] = jnp.ones_like(out_decay)

    def cot_steps(t):
        @pl.loop(0, known)
        def _(j):
            gather_cot.step(j, t)

    def block(b):
        r = pl.ds(pl.multiple_of(b * WIDTH, WIDTH), WIDTH)
        same, carry, tail, keep = block_masks(base + b * WIDTH, ends_ref)
        for h in range(heads):
            cols = slice(h * WIDTH, (h + 1) * WIDTH)
            q = q_ref[r, cols]
            q = q * jax.nn.sigmoid(q)
            key, run, _ = decay_parts(f_ref[r, cols], bound_ref[:, cols])
            middle, last = run[WIDTH // 2 - 1 : WIDTH // 2, :], run[WIDTH - 1 :, :]
            qd_ref[r, cols] = (q * jnp.exp(run - middle)).astype(bf16)
            kd_ref[r, cols] = (key * jnp.exp(middle - run)).astype(bf16)
            qe_ref[r, cols] = (q * jnp.exp(run) * carry).astype(bf16)
            key_tail = (key * jnp.exp(last - run) * tail).astype(bf16)
            adds[b, h] = mul(i_ref[r, cols].astype(bf16), key_tail, TN)
            decays[b, h : h + 1, :] = jnp.exp(last) * keep

    def near_part(b):
        r = pl.ds(pl.multiple_of(b * WIDTH, WIDTH), WIDTH)
        same, carry, tail, keep = block_masks(base + b * WIDTH, ends_ref)
        for h in range(heads):
            cols = slice(h * WIDTH, (h + 1) * WIDTH)
            scores = jnp.where(same, mul(qd_ref[r, cols], kd_ref[r, cols], NT), 0.0).astype(bf16)
            o_ref[r, cols] = mul(scores, i_ref[r, cols].astype(bf16), NN)

    own_rows = rounds * m
    per = own_rows // WIDTH if own_rows % WIDTH == 0 and WIDTH % m == 0 else 0
    early = [z * per + k for z in range(size) for k in range(per - 1)] if per > 1 else []
    late = [b for b in range(blocks) if b not in early]
    ready = (per - 1) * WIDTH // m if early else rounds

    def some_blocks(chosen, body):
        if chosen is early and early:

            @pl.loop(0, size)
            def _(z):
                for k in range(per - 1):
                    body(z * per + k)

        elif early:

            @pl.loop(0, size)
            def _(z):
                body(z * per + per - 1)

        elif chosen is late:
            pl.loop(0, blocks)(body)

    def project(j):
        block_rows = a_ref[:, j].reshape(size * m, d)
        for weight, out in zip(weights, pres):
            product = mul(block_rows, weight[...], NN)
            for z in range(size):
                at = pl.multiple_of(z * own_rows + j * m, 16)
                out[pl.ds(at, m), :] = product[z * m : (z + 1) * m]

    @pl.loop(0, rounds)
    def _(j):
        for t in range(1, size):
            gather.step(j, t)
            if early and t == 1:

                @pl.when(j == ready)
                def _():
                    some_blocks(early, block)

            if early and t == 2:

                @pl.when(j == ready)
                def _():
                    some_blocks(early, near_part)

        @pl.when(j >= rounds - known)
        def _():
            gather_cot.start(j - (rounds - known))

        project(j)

    stores = [
        local(source, target, store_sems.at[k])
        for k, (source, target) in enumerate(zip((a_ref, *pres), (a_out, q_out, f_out, i_out, s_out)))
    ]
    for store in stores:
        store.start()

    some_blocks(late, block)

    @pl.loop(0, blocks)
    def _(b):
        for h in range(heads):
            decay = decays[b, h : h + 1, :]
            state[h] = decay * state[h] + adds[b, h]
            out_decay[h : h + 1, :] = out_decay[h : h + 1, :] * decay

    out_state[...] = state[...].astype(bf16)
    states.start(True)
    cot_steps(1)
    some_blocks(late, near_part)

    states.compose(True, state)
    for t in range(2, size - 1):
        cot_steps(t)

    @pl.loop(0, blocks)
    def _(b):
        r = pl.ds(pl.multiple_of(b * WIDTH, WIDTH), WIDTH)
        places = base + b * WIDTH + lax.broadcasted_iota(jnp.int32, (WIDTH, WIDTH), 0)
        valid = jnp.where(places < ends_ref[ends_ref.shape[0] - 1], 1.0, 0.0)
        for h in range(heads):
            cols = slice(h * WIDTH, (h + 1) * WIDTH)
            low = state[h].astype(bf16)
            starts_ref[b, h] = low
            o = o_ref[r, cols] + mul(qe_ref[r, cols], low, NT)
            o_ref[r, cols] = o
            state[h] = decays[b, h : h + 1, :] * state[h] + adds[b, h]
            scale = lax.rsqrt(jnp.mean(o * o, axis=-1, keepdims=True) + epsilon)
            s = s_ref[r, cols]
            z = s * jax.nn.sigmoid(s) * valid
            u_ref[r, cols] = (o * scale * gain_ref[:, cols] * z).astype(bf16)

    cot_steps(size - 1)
    cot_store = local(cot_ref, cot_out, load_sems.at[4])
    cot_store.start()
    states.drain(True)

    @pl.loop(0, rounds)
    def _(j):
        gather.drain(j)

    @pl.loop(0, known)
    def _(j):
        gather_cot.drain(j)

    for store in stores:
        store.wait()
    cot_store.wait()


def front(size, groups, rounds, tokens, cot, norm_gain, weights, ends, bound, gain):
    own, d = tokens.shape
    m, c = own // rounds, weights[0].shape[1]
    rows = size * own
    blocks, heads = rows // WIDTH, c // WIDTH
    known = KNOWN
    shape, some = (size, rounds, m, d), (size, known, m, d)
    wide, low = jax.ShapeDtypeStruct((rows, c), f32), VM((rows, c), bf16)
    spec, far = pl.BlockSpec(memory_space=VM), pl.BlockSpec(memory_space=pl.ANY)
    sems = DMA((2, rounds, size))
    outs = pl.pallas_call(
        partial(front_kernel, size, groups, rounds),
        out_shape=[
            jax.ShapeDtypeStruct(shape, bf16),
            wide,
            wide,
            wide,
            wide,
            jax.ShapeDtypeStruct(some, bf16),
            wide,
            jax.ShapeDtypeStruct((rows, c), bf16),
            jax.ShapeDtypeStruct((blocks, heads, WIDTH, WIDTH), bf16),
        ],
        in_specs=[pl.BlockSpec(memory_space=pltpu.SMEM)] + [spec] * 4 + [far] * 5,
        out_specs=[far] * 6 + [spec] * 3,
        scratch_shapes=[VM((d, c), bf16)] * 4
        + [VM(shape, bf16)]
        + [VM((rows, c), f32)] * 4
        + [VM(some, bf16)]
        + [low] * 3
        + [VM((blocks, heads, WIDTH, WIDTH), f32), VM((blocks, 8, WIDTH), f32)]
        + states_scratch(groups, heads)
        + [DMA((5,)), DMA((5,)), sems, sems, sems, sems],
        compiler_params=pltpu.CompilerParams(collective_id=0, has_side_effects=True, vmem_limit_bytes=60 * MIB),
        cost_estimate=pl.CostEstimate(flops=8 * rows * d * c, bytes_accessed=36 * MIB, transcendentals=8 * rows * c),
        name="front",
    )(
        ends,
        tokens.reshape(rounds, m, d),
        norm_gain.reshape(1, d),
        bound,
        gain,
        cot.reshape(rounds, m, d),
        *weights,
    )
    return [outs[0].reshape(rows, d)] + list(outs[1:])


def scan_back_kernel(size, line, rounds, count, *refs):
    take = taker(refs)
    ends_ref, bound_ref, gain_ref, norm_gain_ref, *loaded = take(16)
    grads = take(count)
    *back_outs, small_ref, first_ref, part_out = take(7)
    grad_outs = take(count)
    qd_ref, kd_ref, qe_ref, kt_ref, do_ref, run_ref, adds, decays = take(8)
    state, out_state, out_decay, land_state, land_decay, sems = take(6)
    *inputs, load_sems = take(13)
    q_ref, f_ref, i_ref, s_ref, o_ref, ub_ref, starts_ref, *weights, a_ref = inputs
    *loaded, a_in = loaded
    stage, stage_sems, a_sems, *backs, back_sems = take(8)
    dq_ref, df_ref, di_ref, ds_ref = backs
    loads = [
        pltpu.make_async_copy(source, target, load_sems.at[k]) for k, (source, target) in enumerate(zip(loaded, inputs))
    ]
    soon, later = [loads[k] for k in (4, 3, 5, 0, 1)], [loads[k] for k in (2, 6)]
    for load in soon + later:
        load.start()
    sums = group_sums(size, grads, grad_outs, take)
    greet(*group_peers(size, "seq"))
    rows, c = q_ref.shape
    blocks, heads = rows // WIDTH, c // WIDTH
    base = lax.axis_index("seq") * rows
    states = States(size, out_state, out_decay, land_state, land_decay, sems)
    for each in sums:
        each.start()
    state[...] = jnp.zeros_like(state)
    out_decay[...] = jnp.ones_like(out_decay)
    small_ref[...] = jnp.zeros_like(small_ref)
    for load in soon:
        load.wait()

    @pl.loop(0, blocks)
    def _(back):
        for each in sums[:1]:

            @pl.when(back == 1)
            def _():
                each.middle()

        b = blocks - 1 - back
        r = pl.ds(pl.multiple_of(b * WIDTH, WIDTH), WIDTH)
        same, carry, tail, keep = block_masks(base + b * WIDTH, ends_ref)
        places = base + b * WIDTH + lax.broadcasted_iota(jnp.int32, (WIDTH, WIDTH), 0)
        valid = jnp.where(places < ends_ref[ends_ref.shape[0] - 1], 1.0, 0.0)
        for h in range(heads):
            cols = slice(h * WIDTH, (h + 1) * WIDTH)
            o, s, ub, gain = o_ref[r, cols], s_ref[r, cols], ub_ref[r, cols], gain_ref[:, cols]
            scale = lax.rsqrt(jnp.mean(o * o, axis=-1, keepdims=True) + epsilon)
            normed = o * scale
            gate = jax.nn.sigmoid(s)
            uz = ub * (s * gate * valid)
            small_ref[heads + h : heads + h + 1, :] += jnp.sum(uz * normed, axis=0, keepdims=True)
            nb = uz * gain
            ds_ref[r, cols] = (ub * normed * gain * valid * (gate * (1.0 + s * (1.0 - gate)))).astype(bf16)
            do = (scale * (nb - normed * jnp.mean(nb * normed, axis=-1, keepdims=True))).astype(bf16)
            do_ref[r, cols] = do
            q = q_ref[r, cols]
            q = q * jax.nn.sigmoid(q)
            key, run, _ = decay_parts(f_ref[r, cols], bound_ref[:, cols])
            middle, last = run[WIDTH // 2 - 1 : WIDTH // 2, :], run[WIDTH - 1 :, :]
            run_ref[r, cols] = run
            qd_ref[r, cols] = (q * jnp.exp(run - middle)).astype(bf16)
            kd_ref[r, cols] = (key * jnp.exp(middle - run)).astype(bf16)
            kt_ref[r, cols] = (key * jnp.exp(last - run) * tail).astype(bf16)
            qe = (q * jnp.exp(run) * carry).astype(bf16)
            qe_ref[r, cols] = qe
            add = mul(do, qe, TN)
            decay = jnp.exp(last) * keep
            adds[b, h] = add
            decays[b, h : h + 1, :] = decay
            state[h] = decay * state[h] + add
            out_decay[h : h + 1, :] = out_decay[h : h + 1, :] * decay

    out_state[...] = state[...].astype(bf16)
    states.start(False)
    for load in later:
        load.wait()
    for load in loads[7:]:
        load.start()
    for each in sums[:1]:
        each.relay()
    for each in sums[1:]:
        each.middle()
    states.compose(False, state)

    @pl.loop(0, blocks)
    def _(back):
        for each in sums[1:]:

            @pl.when(back == blocks // 2)
            def _():
                each.relay()
        b = blocks - 1 - back
        r = pl.ds(pl.multiple_of(b * WIDTH, WIDTH), WIDTH)
        same, carry, tail, keep = block_masks(base + b * WIDTH, ends_ref)
        shape = (WIDTH, WIDTH)
        down, along = lax.broadcasted_iota(jnp.int32, shape, 0), lax.broadcasted_iota(jnp.int32, shape, 1)
        from_here = jnp.where(along >= down, 1.0, 0.0).astype(bf16)
        ahead = jnp.where(along < down, 1.0, 0.0).astype(bf16)
        for h in range(heads):
            cols = slice(h * WIDTH, (h + 1) * WIDTH)
            do, v = do_ref[r, cols], i_ref[r, cols].astype(bf16)
            low, start = state[h].astype(bf16), starts_ref[b, h]
            dq_state = mul(do, start, NN)
            dk_state = mul(v, low, NN)
            kt = kt_ref[r, cols]
            qd, kd = qd_ref[r, cols], kd_ref[r, cols]
            scores = jnp.where(same, mul(qd, kd, NT), 0.0).astype(bf16)
            slopes = jnp.where(same, mul(do, v, NT), 0.0).astype(bf16)
            dq_near = mul(slopes, kd, NN)
            dk_near = mul(slopes, qd, TN)
            di_ref[r, cols] = (mul(scores, do, TN) + mul(kt, low, NT)).astype(bf16)
            run = run_ref[r, cols]
            middle, last = run[WIDTH // 2 - 1 : WIDTH // 2, :], run[WIDTH - 1 :, :]
            q_back = dq_near * jnp.exp(run - middle) + dq_state * (jnp.exp(run) * carry)
            k_back = dk_near * jnp.exp(middle - run) + dk_state * (jnp.exp(last - run) * tail)
            later = (
                qe_ref[r, cols].astype(f32) * dq_state
                + qd.astype(f32) * dq_near
                - kd.astype(f32) * dk_near
            )
            earlier = kt.astype(f32) * dk_state
            decay = decays[b, h : h + 1, :]
            log_back = decay * jnp.sum(low.astype(f32) * start.astype(f32), axis=0, keepdims=True)
            for ones, part in ((from_here, later), (ahead, earlier)):
                high = part.astype(bf16)
                log_back = log_back + mul(ones, high, NN)
                log_back = log_back + mul(ones, (part - high.astype(f32)).astype(bf16), NN)
            f_pre = f_ref[r, cols]
            away, near = jax.nn.sigmoid(-f_pre), jax.nn.sigmoid(f_pre)
            upper = jax.nn.sigmoid(-bound_ref[:, cols])
            lower = jax.nn.sigmoid(bound_ref[:, cols])
            forget_back = log_back / (1.0 - upper * away) - k_back
            slope = forget_back * away * upper
            df_ref[r, cols] = (slope * near).astype(bf16)
            small_ref[h : h + 1, :] += jnp.sum(slope, axis=0, keepdims=True) * lower
            dq_ref[r, cols] = (q_back * silu_slope(q_ref[r, cols])).astype(bf16)
            state[h] = adds[b, h] + decay * state[h]

    stores = [
        pltpu.make_async_copy(source, target, back_sems.at[k]) for k, (source, target) in enumerate(zip(backs, back_outs))
    ]
    for store in stores:
        store.start()
    for load in loads[7:]:
        load.wait()
    m, d = a_ref.shape[2:]

    def a_load(j):
        slot = lax.rem(j, 2)
        return pltpu.make_async_copy(a_in.at[:, j], a_ref.at[slot], a_sems.at[slot])

    for j in range(min(2, rounds)):
        a_load(j).start()
    tile = min(512, d)
    first_ref[...] = jnp.zeros_like(first_ref)

    def part_copy(j):
        return pltpu.make_async_copy(stage.at[lax.rem(j, 2)], part_out.at[j], stage_sems.at[lax.rem(j, 2)])

    @pl.loop(0, rounds)
    def _(j):
        @pl.when(j > 1)
        def _():
            part_copy(j - 2).wait()

        a_load(j).wait()

        def round_rows(ref):
            places = [pl.multiple_of(z * rounds * m + j * m, 16) for z in range(line)]
            return jnp.concatenate([ref[pl.ds(at, m), :] for at in places], axis=0)

        @pl.loop(0, d // tile)
        def _(n):
            cols = pl.ds(pl.multiple_of(n * tile, tile), tile)
            acc = None
            for back, weight in zip((dq_ref, df_ref, di_ref, ds_ref), weights):
                term = mul(round_rows(back), weight[cols, :], NT)
                acc = term if acc is None else acc + term
            normed = a_ref[lax.rem(j, 2), :, :, cols].reshape(line * m, tile).astype(f32)
            first_ref[:, cols] += jnp.sum(acc * normed, axis=0, keepdims=True)
            stage[lax.rem(j, 2), :, :, cols] = acc.astype(bf16).reshape(line, m, tile)

        part_copy(j).start()

        @pl.when(j + 2 < rounds)
        def _():
            a_load(j + 2).start()

    first_ref[...] = first_ref[...] / norm_gain_ref[...]
    for each in sums:
        each.finish()
    for j in range(max(0, rounds - 2), rounds):
        part_copy(j).wait()
    for store in stores:
        store.wait()
    states.drain(False)
    for each in sums:
        each.drain()


def scan_backward(size, line, rounds, ends, bound, gain, q, f, i, s, o, ub, starts, norm_gain, a, weights, grads):
    rows, c = q.shape
    d = a.shape[1]
    shape = (line, rounds, rows // line // rounds, d)
    part = (rounds, line) + shape[2:]
    blocks, heads = rows // WIDTH, c // WIDTH
    low, wide = VM((rows, c), bf16), VM((rows, c), f32)
    spec = pl.BlockSpec(memory_space=VM)
    return pl.pallas_call(
        partial(scan_back_kernel, size, line, rounds, len(grads)),
        out_shape=[jax.ShapeDtypeStruct((rows, c), bf16)] * 4
        + [jax.ShapeDtypeStruct((2 * heads, WIDTH), f32), jax.ShapeDtypeStruct((1, d), f32)]
        + [jax.ShapeDtypeStruct(part, bf16)]
        + sum_shapes([grad.shape for grad in grads], [False] * len(grads)),
        in_specs=[pl.BlockSpec(memory_space=pltpu.SMEM)]
        + [spec] * 3
        + [pl.BlockSpec(memory_space=pl.ANY)] * (12 + len(grads)),
        out_specs=[pl.BlockSpec(memory_space=pl.ANY)] * 4
        + [spec] * 2
        + [pl.BlockSpec(memory_space=pl.ANY)]
        + [spec] * len(grads),
        scratch_shapes=[low] * 5
        + [wide, VM((blocks, heads, WIDTH, WIDTH), f32), VM((blocks, 8, WIDTH), f32)]
        + states_scratch(size, heads)
        + [wide] * 6
        + [VM(starts.shape, bf16)]
        + [VM((d, c), bf16)] * 4
        + [VM((2,) + part[1:], bf16), DMA((11,)), VM((2,) + part[1:], bf16), DMA((2,)), DMA((2,))]
        + [low] * 4
        + [DMA((4,))]
        + group_sums_scratch([grad.shape for grad in grads]),
        compiler_params=pltpu.CompilerParams(collective_id=2, has_side_effects=True, vmem_limit_bytes=63 * MIB),
        cost_estimate=pl.CostEstimate(flops=8 * rows * c * d, bytes_accessed=40 * MIB, transcendentals=16 * rows * c),
        name="scan_backward",
    )(
        ends,
        bound,
        gain,
        norm_gain.reshape(1, d),
        q,
        f,
        i,
        s,
        o,
        ub,
        starts,
        *weights,
        a.reshape(shape),
        *[in_pairs(grad) for grad in grads],
    )


def middle_kernel(size, rounds, *refs):
    take = taker(refs)
    u_ref, x_ref, gain_ref, out_w, *loaded, cot_some, cot_own = take(9)
    res_out, back_out, e_out, ub_out, second_ref, down_out, out_grad, *grad_outs = take(10)
    gate_w, up_w, down_w = weights = take(3)
    cot_ref = take(1)[0]
    b_ref, e_ref, res_ref, back_ref, ub_ref, part, land, total = take(8)
    wide = take(3)
    down_ref, *tiles = take(4)
    load_sems, res_sems, back_sems, e_sems, ub_sem, down_sem, tile_sems = take(7)
    lines = [take(2) for _ in range(5)]
    hidden, gate_back, up_back = wide
    me = lax.axis_index("tp")
    m, d = x_ref.shape[1:]
    ff = gate_w.shape[1]
    group = size * m
    scatter = Scatter(size, *lines[0], part, land, total)
    gather = Gather(size, *lines[1], b_ref)
    scatter_back = Scatter(size, *lines[2], part, land, total)
    gather_back = Gather(size, *lines[3], e_ref)
    gather_cot = Gather(size, *lines[4], cot_ref)
    known = cot_some.shape[1]
    gain = gain_ref[...]
    tile = min(512, d)
    local = pltpu.make_async_copy
    loads = [local(src, dst, load_sems.at[k]) for k, (src, dst) in enumerate(zip(loaded, weights))]
    loads.append(local(cot_some, cot_ref.at[:, :known], load_sems.at[3]))
    cot_load = local(cot_own.at[known:], cot_ref.at[me, known:], load_sems.at[4])
    cot_load.start()
    for load in loads:
        load.start()
    second_ref[...] = jnp.zeros_like(second_ref)
    greet(*line_peers(size))

    def project_out(j):
        rows = u_ref[:, j].reshape(group, u_ref.shape[3])

        @pl.loop(0, d // tile)
        def _(n):
            cols = pl.ds(pl.multiple_of(n * tile, tile), tile)
            part[j, :, :, cols] = mul(rows, out_w[:, cols], NN).astype(bf16).reshape(size, m, tile)

        scatter.start(j)

    def res_copy(j):
        return local(res_ref.at[j], res_out.at[j], res_sems.at[j])

    def back_copy(j):
        return local(back_ref, back_out.at[j], back_sems.at[0])

    def e_copy(j):
        return local(e_ref.at[:, j], e_out.at[:, j], e_sems.at[j])

    def ub_copy(j):
        return local(ub_ref, ub_out.at[:, j], ub_sem.at[0])

    def down_copy(j):
        return local(down_ref, down_out.at[:, j], down_sem.at[0])

    def norm(j):
        @pl.loop(0, m // 16)
        def _(g):
            r = pl.ds(pl.multiple_of(g * 16, 16), 16)
            residual = x_ref[j, r, :].astype(f32) + total[r, :]
            res_ref[j, r, :] = residual
            scale = lax.rsqrt(jnp.mean(residual * residual, axis=-1, keepdims=True) + epsilon)
            b_ref[me, j, r, :] = (residual * scale * gain).astype(bf16)

        gather.start(j)
        res_copy(j).start()

    def feed(j, piece):
        rows = b_ref[:, j].reshape(group, d)
        cot = cot_ref[:, j].reshape(group, d)
        step = 256
        starts = list(range(0, ff, step))
        for low in starts[len(starts) * piece // PIECES : len(starts) * (piece + 1) // PIECES]:
            cols = slice(low, min(low + step, ff))
            width = cols.stop - cols.start
            gate = mul(rows, gate_w[:, cols], NN)
            up = mul(rows, up_w[:, cols], NN)
            hb = mul(cot, down_w[cols, :], NT)
            sig = jax.nn.sigmoid(gate)
            act = gate * sig
            shape = (size, m, width)
            hidden[:, j, :, cols] = (act * up).astype(bf16).reshape(shape)
            up_back[:, j, :, cols] = (hb * act).astype(bf16).reshape(shape)
            gate_back[:, j, :, cols] = (hb * up * (sig * (1.0 + gate * (1.0 - sig)))).astype(bf16).reshape(shape)

    def feed_back(j):
        scatter.drain(j)
        gates = gate_back[:, j].reshape(group, ff)
        ups = up_back[:, j].reshape(group, ff)

        @pl.loop(0, d // tile)
        def _(n):
            cols = pl.ds(pl.multiple_of(n * tile, tile), tile)
            sums = mul(gates, gate_w[cols, :], NT) + mul(ups, up_w[cols, :], NT)
            part[j, :, :, cols] = sums.astype(bf16).reshape(size, m, tile)

        scatter_back.start(j)

    def feed_out(j):
        rows = hidden[:, j].reshape(group, ff)

        @pl.loop(0, d // tile)
        def _(n):
            cols = pl.ds(pl.multiple_of(n * tile, tile), tile)
            down_ref[:, :, cols] = mul(rows, down_w[:, cols], NN).astype(bf16).reshape(size, m, tile)

        down_copy(j).start()

    def norm_back(j):
        @pl.loop(0, m // 16)
        def _(g):
            r = pl.ds(pl.multiple_of(g * 16, 16), 16)
            b_back, residual = total[r, :], res_ref[j, r, :]
            scale = lax.rsqrt(jnp.mean(residual * residual, axis=-1, keepdims=True) + epsilon)
            normed = residual * scale
            second_ref[...] += jnp.sum(b_back * normed, axis=0, keepdims=True)
            inner = b_back * gain
            back = cot_ref[me, j, r, :].astype(f32) + scale * (
                inner - normed * jnp.mean(inner * normed, axis=-1, keepdims=True)
            )
            back_ref[r, :] = back
            e_ref[me, j, r, :] = back.astype(bf16)

        gather_back.start(j)
        back_copy(j).start()

    def unproject(j):
        e_copy(j).start()
        rows = e_ref[:, j].reshape(group, d)
        ub_ref[...] = mul(rows, out_w[...], NT).reshape(size, m, out_w.shape[0])
        ub_copy(j).start()

    depth = tiles[0].shape[0]
    count = d // depth

    def tile_copies(n):
        rows = pl.ds(n * depth, depth)
        return [local(src, dst.at[rows, :], tile_sems.at[k]) for k, (src, dst) in enumerate(zip(tiles, grad_outs))]

    def weight_tile(n):
        cols = pl.ds(n * depth, depth)
        for left, right, out in zip((b_ref, b_ref, cot_ref), (gate_back, up_back, hidden), tiles):
            rows = left[:, :, :, cols].reshape(rounds * group, depth)
            out[...] = mul(rows, right[...].reshape(rounds * group, ff), TN).astype(bf16)
        for copy in tile_copies(n):
            copy.start()

    cot_load.wait()
    held = {}

    def then(kind, copies):
        for copy in held.get(kind, []):
            copy.wait()
        held[kind] = copies

    shares = sum(name[0] == "W" for name in STEPS)
    for name in STEPS:
        kind, j, t = name[0], int(name[1]), int(name[2:] or 0)
        if kind == "A":
            project_out(j)
        elif kind == "C":
            gather_cot.step(j, t) if t else gather_cot.start(j)
        elif kind == "S" and t < size - 1:
            scatter.step(j, t)
        elif kind == "S":
            scatter.finish(j)
            norm(j)
        elif kind == "G":
            gather.step(j, t)
        elif kind == "F":
            then("loads", loads if "loads" not in held else [])
            then("loads", [])
            feed(j, t)
        elif kind == "B":
            feed_back(j)
        elif kind == "O":
            then(kind, [])
            feed_out(j)
            then(kind, [down_copy(j)])
        elif kind == "T" and t < size - 1:
            scatter_back.step(j, t)
        elif kind == "T":
            then(kind, [])
            scatter_back.finish(j)
            norm_back(j)
            then(kind, [back_copy(j)])
        elif kind == "E":
            gather_back.step(j, t)
        elif kind == "U":
            then(kind, [])
            unproject(j)
            then(kind, [ub_copy(j)])
        elif kind == "W":
            for n in range(count * j // shares, count * (j + 1) // shares):
                then(kind, [])
                weight_tile(n)
                then(kind, tile_copies(n))
    for kind in list(held):
        then(kind, [])
    width = u_ref.shape[3]

    def out_tile(n, slot):
        rows = pl.ds(pl.multiple_of(n * depth, depth), depth)
        source = tiles[slot].at[:, pl.ds(0, width)]
        return local(source, out_grad.at[rows, :], tile_sems.at[slot])

    slots = len(tiles) - 1

    @pl.loop(0, count // slots)
    def _(n):
        for slot in range(slots):
            at = n * slots + slot

            @pl.when(n > 0)
            def _():
                out_tile(at - slots, slot).wait()

            cols = pl.ds(pl.multiple_of(at * depth, depth), depth)
            rows = e_ref[:, :, :, cols].reshape(rounds * group, depth)
            tiles[slot][:, :width] = mul(rows, u_ref[...].reshape(rounds * group, width), TN).astype(bf16)
            out_tile(at, slot).start()

    for slot in range(slots):
        out_tile(count - slots + slot, slot).wait()

    @pl.loop(0, rounds)
    def _(j):
        res_copy(j).wait()
        e_copy(j).wait()

        @pl.when(j >= known)
        def _():
            gather_cot.drain(j)

        gather.drain(j)
        scatter_back.drain(j)
        gather_back.drain(j)


def middle(size, rounds, u, x, cot_some, cot, gain, out_w, gate_w, up_w, down_w):
    rows, d = x.shape
    m = rows // rounds
    c, ff = out_w.shape[0], gate_w.shape[1]
    shape = (size, rounds, m)
    sems = DMA((2, rounds, size))
    spec, far = pl.BlockSpec(memory_space=VM), pl.BlockSpec(memory_space=pl.ANY)
    depth = min(256, d)
    outs = pl.pallas_call(
        partial(middle_kernel, size, rounds),
        out_shape=[
            jax.ShapeDtypeStruct((rounds, m, d), f32),
            jax.ShapeDtypeStruct((rounds, m, d), f32),
            jax.ShapeDtypeStruct(shape + (d,), bf16),
            jax.ShapeDtypeStruct(shape + (c,), f32),
            jax.ShapeDtypeStruct((1, d), f32),
            jax.ShapeDtypeStruct(shape + (d,), bf16),
            jax.ShapeDtypeStruct((d, c), bf16),
        ]
        + [jax.ShapeDtypeStruct((d, ff), bf16)] * 3,
        in_specs=[spec] * 4 + [far] * 5,
        out_specs=[far] * 4 + [spec] + [far] * 5,
        scratch_shapes=[
            VM(gate_w.shape, bf16),
            VM(up_w.shape, bf16),
            VM(down_w.shape, bf16),
            VM(shape + (d,), bf16),
            VM(shape + (d,), bf16),
            VM(shape + (d,), bf16),
            VM((rounds, m, d), f32),
            VM((m, d), f32),
            VM((size, m, c), f32),
            VM((rounds, size, m, d), bf16),
            VM((2, rounds, size - 1, m, d), bf16),
            VM((m, d), f32),
        ]
        + [VM(shape + (ff,), bf16)] * 3
        + [VM((size, m, d), bf16)]
        + [VM((depth, ff), bf16)] * 3
        + [DMA((5,)), DMA((rounds,)), DMA((1,)), DMA((rounds,)), DMA((1,)), DMA((1,)), DMA((3,))]
        + [sems] * 10,
        compiler_params=pltpu.CompilerParams(collective_id=3, has_side_effects=True, vmem_limit_bytes=63 * MIB),
        cost_estimate=pl.CostEstimate(
            flops=2 * size * rows * d * (2 * c + 9 * ff), bytes_accessed=56 * MIB, transcendentals=size * rows * ff
        ),
        name="middle",
    )(
        u.reshape(shape + (c,)),
        x.reshape(rounds, m, d),
        gain.reshape(1, d),
        out_w,
        gate_w,
        up_w,
        down_w,
        cot_some,
        cot.reshape(rounds, m, d),
    )
    res, back, e, ub, second, down, *grads = outs
    total = size * rows
    return (
        res.reshape(rows, d),
        back.reshape(rows, d),
        ub.reshape(total, c),
        second,
        down.reshape(total, d),
        *grads,
    )


class Everyone:
    def __init__(self, size, axis, mine, land, sems):
        self.size, self.axis = size, axis
        self.here = lax.axis_index(axis)
        self.mine, self.land, self.sems = mine, land, sems

    def copy(self, slot, peer):
        return remote(self.mine, self.land.at[slot], self.sems.at[0, peer], self.sems.at[1, slot], self.axis, peer)

    def others(self):
        for k in range(self.size):
            yield k, self.here != k

    def start(self):
        for k, other in self.others():

            @pl.when(other)
            def _():
                self.copy(self.here, k).start()

    def finish(self, out):
        out[...] = self.mine[...]
        for k, other in self.others():

            @pl.when(other)
            def _():
                self.copy(k, k).wait_recv()
                out[...] = out[...] + self.land[k]

    def drain(self):
        for k, other in self.others():

            @pl.when(other)
            def _():
                self.copy(self.here, k).wait_send()


def everyone_scratch(size, rows):
    return [VM((rows, WIDTH), f32), VM((size, rows, WIDTH), f32), DMA((2, size))]


def stack(vector, into, at):
    for k in range(vector.shape[1] // WIDTH):
        into[at + k : at + k + 1, :] = vector[:, k * WIDTH : (k + 1) * WIDTH]


def last_kernel(size, groups, rounds, count, mixed, *refs):
    take = taker(refs)
    backs = take(4)
    x_ref, gain_ref, second_ref, small_ref, first_ref, back_in, a_in, part_in, res_in, down_in = take(10)
    grads = take(count)
    tokens_far, small_out, output_ref = take(3)
    grad_outs = take(count + (4 if mixed else 0))
    part, land, total, s_send, s_recv = take(5)
    small_seq, gains_tp, sides = take(3), take(3), take(1)[0]
    nears = take(4 if mixed else 0)
    a_ref, tokens_out, res_ref, down_ref, load_sems, store_sems = take(6)
    sums = group_sums(groups, grads + nears, grad_outs, take)
    early, late = sums[:2], sums[2:]

    seq, seq_count = group_peers(groups, "seq")
    tp, tp_count = group_peers(size, "tp")
    greet(seq + tp, seq_count + tp_count)

    for each in sums[:count]:
        each.start()
    m, d = x_ref.shape[1:]
    tile = min(512, d)
    local = pltpu.make_async_copy

    def part_load(j):
        return local(part_in.at[j], part.at[j], load_sems.at[2 + j])

    a_load = local(a_in, a_ref, load_sems.at[1])
    back_load = local(back_in, tokens_out, load_sems.at[0])

    for j in range(rounds):
        part_load(j).start()
    a_load.start()
    back_load.start()
    output_loads = [
        local(source, target, load_sems.at[2 + rounds + k])
        for k, (source, target) in enumerate(((res_in, res_ref), (down_in, down_ref)))
    ]
    for load in output_loads:
        load.start()

    def store(j):
        return local(tokens_out.at[j], tokens_far.at[j], store_sems.at[j])

    group = size * m
    scatter = Scatter(size, s_send, s_recv, part, land, total)
    gain = gain_ref[...]

    seq_small = Everyone(groups, "seq", *small_seq)
    tp_gains = Everyone(size, "tp", *gains_tp)
    lines, smalls = d // WIDTH, small_ref.shape[0]

    def mix(back, each):
        rows = back[...].reshape(rounds * group, back.shape[3])
        depth = each.own.shape[1]
        for side, into in ((1 - each.side, each.grad), (each.side, each.own)):

            @pl.loop(0, each.half)
            def _(k):
                cols = pl.ds(pl.multiple_of((2 * k + side) * depth, depth), depth)
                left = a_ref[:, :, :, cols].reshape(rounds * group, depth)
                into[k] = mul(left, rows, TN).astype(bf16)

            if into is each.grad:
                each.start()

    def norm_back(j):
        @pl.loop(0, m // 16)
        def _(g):
            r = pl.ds(pl.multiple_of(g * 16, 16), 16)
            a_back, x = total[r, :], x_ref[j, r, :].astype(f32)
            scale = lax.rsqrt(jnp.mean(x * x, axis=-1, keepdims=True) + epsilon)
            normed = x * scale
            inner = a_back * gain
            tokens_out[j, r, :] = tokens_out[j, r, :] + scale * (
                inner - normed * jnp.mean(inner * normed, axis=-1, keepdims=True)
            )

    def steps(j, low, high):
        for t in range(low, high):
            if t < size - 1:
                scatter.step(j, t)
            else:
                scatter.finish(j)
                norm_back(j)
                store(j).start()

    stack(second_ref[...], gains_tp[0], 0)
    stack(first_ref[...], gains_tp[0], lines)
    tp_gains.start()
    for j in range(rounds):
        part_load(j).wait()
        scatter.start(j)
    tp_gains.finish(sides)
    small_seq[0][: 2 * lines, :] = sides[...]
    small_seq[0][2 * lines : 2 * lines + smalls, :] = small_ref[...]
    seq_small.start()
    for each in early:
        each.middle()
    a_load.wait()
    steps(0, 1, 2)
    back_load.wait()
    if mixed:
        for at, (back, each) in enumerate(zip(backs, late)):
            mix(back, each)
            steps(0, 2, 3) if at == 0 else None
            steps(0, 3, size) if at == 2 else None
    else:
        steps(0, 2, size)
    for each in early:
        each.relay()
    for each in late:
        each.middle()
    for load in output_loads:
        load.wait()

    @pl.loop(0, rounds * m // 16)
    def _(g):
        r = pl.ds(pl.multiple_of(g * 16, 16), 16)
        output_ref[r, :] = (res_ref[r, :] + down_ref[r, :].astype(f32)).astype(bf16)

    steps(1, 1, 3)
    steps(1, 3, size)
    for each in late[:2]:
        each.relay()
    steps(2, 1, 3)
    for each in late[2:]:
        each.relay()
    steps(2, 3, size)
    for each in early:
        each.finish()
    seq_small.finish(small_out)
    for j in range(3, rounds):
        steps(j, 1, size)
    for each in late:
        each.finish()

    for each in sums + [seq_small, tp_gains]:
        each.drain()

    @pl.loop(0, rounds)
    def _(j):
        scatter.drain(j)
        store(j).wait()


def last(size, groups, rounds, backs, part, a, x, back, gain, second, first, small, residual, down, grads, turned):
    mixed = len(turned) > len(grads)
    rows, d = x.shape
    m = rows // rounds
    c = backs[0].shape[1]
    shape = (size, rounds, m)
    lines = d // WIDTH
    sems = DMA((2, rounds, size))
    spec = pl.BlockSpec(memory_space=VM)
    small_rows = 2 * lines + small.shape[0]
    shapes = [grad.shape for grad in grads] + ([(groups, d // groups, c)] * 4 if mixed else [])
    outs = pl.pallas_call(
        partial(last_kernel, size, groups, rounds, len(grads), mixed),
        out_shape=[
            jax.ShapeDtypeStruct((rounds, m, d), f32),
            jax.ShapeDtypeStruct((small_rows, WIDTH), f32),
            jax.ShapeDtypeStruct((rows, d), bf16),
        ]
        + sum_shapes(shapes, turned),
        in_specs=[spec] * 9 + [pl.BlockSpec(memory_space=pl.ANY)] * (5 + len(grads)),
        out_specs=[pl.BlockSpec(memory_space=pl.ANY)] + [spec] * (2 + len(shapes)),
        scratch_shapes=[
            VM((rounds, size, m, d), bf16),
            VM((2, rounds, size - 1, m, d), bf16),
            VM((m, d), f32),
            sems,
            sems,
        ]
        + everyone_scratch(groups, small_rows)
        + everyone_scratch(size, 2 * lines)
        + [VM((2 * lines, WIDTH), f32)]
        + ([VM((groups // 2, d // groups, c), bf16)] * 4 if mixed else [])
        + [VM(shape + (d,), bf16)]
        + [VM((rounds, m, d), f32), VM((rows, d), f32), VM((rows, d), bf16), DMA((4 + rounds,)), DMA((rounds,))]
        + group_sums_scratch(shapes),
        compiler_params=pltpu.CompilerParams(collective_id=4, has_side_effects=True, vmem_limit_bytes=63 * MIB),
        cost_estimate=pl.CostEstimate(flops=16 * size * rows * d * c, bytes_accessed=56 * MIB, transcendentals=0),
        name="last",
    )(
        *[part.reshape(shape + (c,)) for part in backs],
        x.reshape(rounds, m, d),
        gain.reshape(1, d),
        second,
        small,
        first,
        back.reshape(rounds, m, d),
        a.reshape(shape + (d,)),
        part,
        residual,
        down,
        *[in_pairs(grad) for grad in grads],
    )
    sides = outs[1]
    return (outs[0].reshape(rows, d), sides[:lines], sides[lines : 2 * lines], sides[2 * lines :]) + tuple(outs[2:])


def results_kernel(count, places_ref, first_ref, second_ref, small_ref, *refs):
    ins, outs = refs[:count], refs[count : 2 * count]
    first_out, second_out, bound_out, gain_out, *held, sems = refs[2 * count :]
    loads = [pltpu.make_async_copy(a, b, sems.at[0, k]) for k, (a, b) in enumerate(zip(ins, held))]
    stores = [pltpu.make_async_copy(a, b, sems.at[1, k]) for k, (a, b) in enumerate(zip(held, outs))]
    for load in loads:
        load.start()

    def share(rows, at, width):
        picked = rows[:, :width]
        for k in range(1, WIDTH // width):
            picked = jnp.where(at == k, rows[:, k * width : (k + 1) * width], picked)
        return picked

    here, place = places_ref[0], places_ref[1]
    each = first_out.shape[1]
    per = WIDTH // each
    lines = lax.broadcasted_iota(jnp.int32, first_ref.shape, 0)
    for source, target in ((first_ref, first_out), (second_ref, second_out)):
        line = jnp.sum(jnp.where(lines == place // per, source[...], 0.0), axis=0, keepdims=True)
        target[...] = share(line, place % per, each)
    heads, wide = bound_out.shape
    bound_out[...] = share(small_ref[:heads, :], here, wide)
    gain_out[...] = share(small_ref[heads:, :], here, wide)
    for load, store in zip(loads, stores):
        load.wait()
        store.start()
    for store in stores:
        store.wait()


def results(groups, size, first, second, small, arrays):
    here = lax.axis_index("seq")
    places = jnp.stack([here, here * size + lax.axis_index("tp")]).astype(jnp.int32)
    each, heads = first.size // (groups * size), small.shape[0] // 2
    spec, far = pl.BlockSpec(memory_space=VM), pl.BlockSpec(memory_space=pl.ANY)
    outs = pl.pallas_call(
        partial(results_kernel, len(arrays)),
        out_shape=[jax.ShapeDtypeStruct(part.shape, part.dtype) for part in arrays]
        + [jax.ShapeDtypeStruct((1, each), f32)] * 2
        + [jax.ShapeDtypeStruct((heads, WIDTH // groups), f32)] * 2,
        in_specs=[pl.BlockSpec(memory_space=pltpu.SMEM)] + [spec] * 3 + [far] * len(arrays),
        out_specs=[far] * len(arrays) + [spec] * 4,
        scratch_shapes=[VM(part.shape, part.dtype) for part in arrays] + [DMA((2, len(arrays)))],
        compiler_params=pltpu.CompilerParams(vmem_limit_bytes=60 * MIB),
        cost_estimate=pl.CostEstimate(flops=0, bytes_accessed=20 * MIB, transcendentals=0),
        name="results",
    )(places, first, second, small, *arrays)
    copied, (first, second, bound, gain) = outs[: len(arrays)], outs[len(arrays) :]
    return first.reshape(each), second.reshape(each), bound, gain, copied


def per_device(
    size,
    groups,
    tokens,
    lengths,
    cotangent,
    first_gain,
    query_weight,
    forget_weight,
    input_weight,
    swish_weight,
    bound_logit,
    group_gain,
    out_weight,
    second_gain,
    gate_weight,
    up_weight,
    down_weight,
):
    weights = (query_weight, forget_weight, input_weight, swish_weight)
    ends = jnp.cumsum(lengths).astype(jnp.int32)
    bound, head_gain = bound_logit.reshape(1, -1), group_gain.reshape(1, -1)
    a, q, f, i, s, cot_some, o, u, starts = front(
        size, groups, ROUNDS, tokens, cotangent, first_gain, weights, ends, bound, head_gain
    )
    residual, back, ub, second, down, *wide = middle(
        size, ROUNDS, u, tokens, cot_some, cotangent, second_gain, out_weight, gate_weight, up_weight, down_weight
    )
    down, ub = lax.optimization_barrier((down, ub))
    down = lax.psum_scatter(down, "tp", scatter_dimension=0, tiled=True)
    d = tokens.shape[1]

    def chunks(grad):
        return grad.reshape(groups, grad.shape[0] // groups, grad.shape[1])

    def grad_of(left, right):
        return chunks(lax.dot_general(left, right, TN, preferred_element_type=f32).astype(bf16))

    outs, gates, ups, downs = (chunks(grad) for grad in wide)
    dq, df, di, ds, small, first, part, gate_grad, up_grad = scan_backward(
        groups,
        size,
        ROUNDS,
        ends,
        bound,
        head_gain,
        q,
        f,
        i,
        s,
        o,
        ub,
        starts,
        first_gain,
        a,
        weights,
        [gates, ups],
    )
    back_rows = (dq, df, di, ds)
    here_too = groups == 8
    others = [downs, outs] + ([] if here_too else [grad_of(a, part) for part in back_rows])
    tokens_grad, second_sum, first_sum, small_sum, output, *sums = last(
        size,
        groups,
        ROUNDS,
        back_rows,
        part,
        a,
        tokens,
        back,
        first_gain,
        second,
        first,
        small,
        residual,
        down,
        others,
        [True, True] + [False] * 4,
    )
    arrays = [output, tokens_grad, gate_grad, up_grad, *sums]
    first_grad, second_grad, bound_grad, head_grad, copied = results(
        groups, size, first_sum, second_sum, small_sum, arrays
    )
    output, tokens_grad, gate_grad, up_grad, down_grad, out_grad, *mixes = copied
    query_grad, forget_grad, input_grad, swish_grad = mixes
    return (
        output,
        tokens_grad,
        first_grad,
        query_grad,
        forget_grad,
        input_grad,
        swish_grad,
        bound_grad,
        head_grad,
        out_grad,
        second_grad,
        gate_grad,
        up_grad,
        down_grad,
    )


def solution(mesh):
    rows, both, cols, lines = P(("seq", "tp"), None), P(("seq", "tp")), P(None, "tp"), P("tp", None)
    in_specs = (rows, P(), rows, P(), cols, cols, cols, cols, lines, lines, lines, P(), cols, cols, lines)
    down, across = P("seq", "tp"), P("tp", "seq")
    out_specs = (rows, rows, both, down, down, down, down, across, across, across, both, down, down, across)
    return jax.shard_map(
        partial(per_device, mesh.shape["tp"], mesh.shape["seq"]),
        mesh=mesh,
        in_specs=in_specs,
        out_specs=out_specs,
        check_vma=False,
    )
```

```python
from functools import partial

import jax
import jax.numpy as jnp
from jax import lax
from jax.experimental import pallas as pl
from jax.experimental.pallas import tpu as pltpu
from jax.sharding import PartitionSpec as P

WIDTH = 128
ROUNDS = 4
KNOWN = 1
PIECES = 3
STEPS = (
    "C10", "C11", "C20", "A0", "C12", "A1", "C21", "C22", "C13", "S01", "C30", "S11", "S02", "S03", "C23", "A2",
    "C31", "A3", "G01", "G02", "S21", "S22", "S12", "S23", "G03", "F00", "F01", "F02", "O0", "S13", "B0", "C32",
    "C33", "G11", "G12", "G13", "T01", "S31", "F10", "F11", "F12", "O1", "T02", "G21", "T03", "B1", "S32", "G22",
    "G23", "F20", "E01", "S33", "E02", "E03", "F21", "F22", "T11", "T12", "T13", "G31", "O2", "B2", "E11", "U0",
    "T21", "G32", "G33", "F30", "F31", "T22", "F32", "O3", "E12", "T23", "B3", "W0", "E21", "E13", "U1", "T31",
    "T32", "E22", "W1", "W2", "T33", "W3", "E23", "W5", "E31", "W6", "W4", "U2", "W7", "E32", "E33", "U3",
)
MIB = 1 << 20
epsilon = 1e-05

f32 = jnp.float32
bf16 = jnp.bfloat16
NN = (((1,), (0,)), ((), ()))
NT = (((1,), (1,)), ((), ()))
TN = (((0,), (0,)), ((), ()))
VM = pltpu.VMEM
DMA = pltpu.SemaphoreType.DMA
MESH = pl.DeviceIdType.MESH


def mul(left, right, dims):
    return lax.dot_general(left, right, dims, preferred_element_type=f32)


def silu_slope(value):
    gate = jax.nn.sigmoid(value)
    return gate * (1.0 + value * (1.0 - gate))


def remote(src, dst, send, recv, axis, peer):
    return pltpu.make_async_remote_copy(
        src_ref=src,
        dst_ref=dst,
        send_sem=send,
        recv_sem=recv,
        device_id={axis: peer},
        device_id_type=MESH,
    )


def greet(peers, count):
    barrier = pltpu.get_barrier_semaphore()
    for axis, peer, wanted in peers:

        @pl.when(wanted)
        def _():
            pl.semaphore_signal(barrier, inc=1, device_id={axis: peer}, device_id_type=MESH)

    pl.semaphore_wait(barrier, count)


def line_peers(size):
    me = lax.axis_index("tp")
    peers = [("tp", lax.rem(me + 1, size), me < size - 1), ("tp", lax.rem(me + size - 1, size), me > 0)]
    return peers, jnp.where(me < size - 1, 1, 0) + jnp.where(me > 0, 1, 0)


def group_peers(size, axis):
    me = lax.axis_index(axis)
    return [(axis, lax.rem(me + k, size), True) for k in range(1, size)], size - 1


class Line:
    def __init__(self, size, send, recv):
        self.size = size
        self.me = lax.axis_index("tp")
        self.right = lax.rem(self.me + 1, size)
        self.left = lax.rem(self.me + size - 1, size)
        self.send, self.recv = send, recv

    def hop(self, way, src, dst, j, at):
        peer = self.right if way == 0 else self.left
        return remote(src, dst, self.send.at[way, j, at], self.recv.at[way, j, at], "tp", peer)


class Scatter(Line):
    def __init__(self, size, send, recv, part, land, total):
        super().__init__(size, send, recv)
        self.part, self.land, self.total = part, land, total

    def copy(self, way, j, to):
        return self.hop(way, self.part.at[j, to], self.slot(way, j, to), j, to)

    def slot(self, way, j, to):
        return self.land.at[way, j, to - 1 + way]

    def start(self, j):
        last = self.size - 1

        @pl.when(self.me == 0)
        def _():
            for to in range(last, 0, -1):
                self.copy(0, j, to).start()

        @pl.when(self.me == last)
        def _():
            for to in range(last):
                self.copy(1, j, to).start()

    def step(self, j, t):
        last = self.size - 1
        for way in (0, 1):
            place = self.me if way == 0 else last - self.me
            to = last - t + place
            to = to if way == 0 else last - to

            @pl.when((place >= 1) & (place <= t))
            def _():
                copy = self.copy(way, j, to)
                copy.wait_recv()
                self.add(self.part.at[j, to], self.slot(way, j, to))
                copy.start()

    def add(self, into, more):
        rows = into.shape[0]

        @pl.loop(0, rows // 16)
        def _(g):
            r = pl.ds(pl.multiple_of(g * 16, 16), 16)
            into[r, :] = (into[r, :].astype(f32) + more[r, :].astype(f32)).astype(bf16)

    def finish(self, j):
        me, last = self.me, self.size - 1
        rows = self.total.shape[0]

        def over(body):
            @pl.loop(0, rows // 16)
            def _(g):
                body(pl.ds(pl.multiple_of(g * 16, 16), 16))

        def first(r):
            self.total[r, :] = self.part[j, me, r, :].astype(f32)

        over(first)
        for way, there in ((0, me >= 1), (1, me < last)):

            @pl.when(there)
            def _():
                self.copy(way, j, me).wait_recv()

                def more(r):
                    self.total[r, :] = self.total[r, :] + self.land[way, j, me - 1 + way, r, :].astype(f32)

                over(more)

    def drain(self, j):
        for to in range(self.size):

            @pl.when(self.me < to)
            def _():
                self.copy(0, j, to).wait_send()

            @pl.when(self.me > to)
            def _():
                self.copy(1, j, to).wait_send()


class Gather(Line):
    def __init__(self, size, send, recv, whole):
        super().__init__(size, send, recv)
        self.whole = whole

    def copy(self, way, j, source):
        block = self.whole.at[source, j]
        return self.hop(way, block, block, j, source)

    def start(self, j):
        @pl.when(self.me < self.size - 1)
        def _():
            self.copy(0, j, self.me).start()

        @pl.when(self.me > 0)
        def _():
            self.copy(1, j, self.me).start()

    def step(self, j, t):
        last = self.size - 1

        @pl.when(self.me >= t)
        def _():
            copy = self.copy(0, j, self.me - t)
            copy.wait_recv()

            @pl.when(self.me < last)
            def _():
                copy.start()

        @pl.when(self.me + t <= last)
        def _():
            copy = self.copy(1, j, self.me + t)
            copy.wait_recv()

            @pl.when(self.me > 0)
            def _():
                copy.start()

    def drain(self, j):
        last = self.size - 1
        for source in range(self.size):

            @pl.when((self.me >= source) & (self.me < last))
            def _():
                self.copy(0, j, source).wait_send()

            @pl.when((self.me <= source) & (self.me > 0))
            def _():
                self.copy(1, j, source).wait_send()


def add_rows(into, left, right):
    rows = into.shape[0]

    @pl.loop(0, rows // 16)
    def _(g):
        r = pl.ds(pl.multiple_of(g * 16, 16), 16)
        into[r, :] = (left[r, :].astype(f32) + right[r, :].astype(f32)).astype(bf16)


class GroupSum:
    refs = 6

    def __init__(self, size, grad, out, own, got, land, *sems):
        self.half = size // 2
        here = lax.axis_index("seq")
        self.side = lax.rem(here, 2)
        self.mine = here // 2
        self.sibling = here + 1 - 2 * self.side
        self.grad, self.own, self.got, self.land, self.out = grad, own, got, land, out
        self.near_sems, *self.sems = sems
        self.loads = len(grad.shape) == 4
        self.turned = out.shape != own.shape[1:]

    @staticmethod
    def scratch(shape):
        half = shape[0]
        return [VM(shape, bf16)] * 3 + [DMA((3, half)), DMA((half,)), DMA((half,))]

    def near(self, k):
        sems = self.near_sems
        source = self.grad.at[k, 1 - self.side] if self.loads else self.grad.at[k]
        return remote(source, self.got.at[k], sems.at[0, k], sems.at[1, k], "seq", self.sibling)

    def load(self, k):
        return pltpu.make_async_copy(self.grad.at[k, self.side], self.own.at[k], self.near_sems.at[2, k])

    def start(self):
        for k in range(self.half):
            self.near(k).start()
            if self.loads:
                self.load(k).start()

    def pair(self, k, into):
        if self.loads:
            self.load(k).wait()
        self.near(k).wait_recv()
        add_rows(into, self.own.at[k], self.got.at[k])

    def far(self, k):
        send, recv = self.sems
        return remote(self.own.at[k], self.land.at[self.mine], send.at[k], recv.at[self.mine], "seq", 2 * k + self.side)

    def arrival(self, k):
        send, recv = self.sems
        return remote(self.own.at[k], self.land.at[k], send.at[k], recv.at[k], "seq", 2 * k + self.side)

    def middle(self):
        for k in range(self.half):

            @pl.when(k == self.mine)
            def _():
                self.pair(k, self.land.at[k])

            @pl.when(k != self.mine)
            def _():
                self.pair(k, self.own.at[k])
                self.far(k).start()

    def relay(self):
        pass

    def arrive(self):
        for k in range(self.half):

            @pl.when(k != self.mine)
            def _():
                self.arrival(k).wait_recv()

    def terms(self):
        return [self.land.at[k] for k in range(self.half)]

    def finish(self):
        self.arrive()
        rows, cols = self.own.shape[1:]

        def total(r, c):
            acc = None
            for term in self.terms():
                part = term[r, c].astype(f32)
                acc = part if acc is None else acc + part
            return acc

        if self.turned:

            @pl.loop(0, cols // WIDTH)
            def _(g):
                c = pl.ds(pl.multiple_of(g * WIDTH, WIDTH), WIDTH)
                self.out[c, :] = total(slice(None), c).T

        else:

            @pl.loop(0, rows // 16)
            def _(g):
                r = pl.ds(pl.multiple_of(g * 16, 16), 16)
                self.out[r, :] = total(r, slice(None))

    def drain(self):
        for k in range(self.half):
            self.near(k).wait_send()
        self.drain_far()

    def drain_far(self):
        for k in range(self.half):

            @pl.when(k != self.mine)
            def _():
                self.far(k).wait_send()


class SquareSum(GroupSum):
    refs = 6

    def __init__(self, *args):
        super().__init__(*args)
        self.hop, self.far_sems = self.sems
        x, y = lax.rem(self.mine, 2), self.mine // 2
        self.beside = (2 * y + 1 - x, 2 * (1 - y) + x)
        self.opposite = 2 * (1 - y) + 1 - x
        rows = self.own.shape[1] // 2
        self.halves = (pl.ds(0, rows), pl.ds(rows, rows))

    @staticmethod
    def scratch(shape):
        half, rows, cols = shape
        return [
            VM(shape, bf16),
            VM(shape, bf16),
            VM((2, rows, cols), bf16),
            DMA((3, half)),
            VM((2, rows // 2, cols), bf16),
            DMA((2, 6)),
        ]

    def over(self, way, at, source, target):
        sems = self.far_sems
        return remote(source, target, sems.at[0, at], sems.at[1, at], "seq", 2 * self.beside[way] + self.side)

    def pass_on(self, way):
        return self.over(way, way, self.own.at[self.opposite, self.halves[way]], self.hop.at[way])

    def deliver(self, way, half):
        source = self.own.at[self.beside[way], self.halves[half]]
        return self.over(way, 2 + 2 * way + half, source, self.land.at[way, self.halves[half]])

    def middle(self):
        self.pair(self.opposite, self.own.at[self.opposite])
        for way in (0, 1):
            self.pass_on(way).start()
        for way in (0, 1):
            self.pair(self.beside[way], self.own.at[self.beside[way]])
            self.deliver(way, way).start()
        self.pair(self.mine, self.own.at[self.mine])

    def relay(self):
        for way in (0, 1):
            self.pass_on(way).wait_recv()
            into = self.own.at[self.beside[1 - way], self.halves[way]]
            add_rows(into, into, self.hop.at[way])
            self.deliver(1 - way, way).start()

    def arrive(self):
        for way in (0, 1):
            for half in (0, 1):
                self.deliver(way, half).wait_recv()

    def terms(self):
        return [self.own.at[self.mine], self.land.at[0], self.land.at[1]]

    def drain_far(self):
        for way in (0, 1):
            self.pass_on(way).wait_send()
            for half in (0, 1):
                self.deliver(way, half).wait_send()


def summer(size):
    return SquareSum if size == 8 else GroupSum


def group_sums(size, grads, outs, take):
    kind = summer(size)
    return [kind(size, grad, out, *take(kind.refs)) for grad, out in zip(grads, outs)]


def group_sums_scratch(shapes):
    scratch = []
    for size, rows, cols in shapes:
        scratch += summer(size).scratch((size // 2, rows, cols))
    return scratch


def sum_shapes(shapes, turned):
    shapes = [shape[:0:-1] if turn else shape[1:] for shape, turn in zip(shapes, turned)]
    return [jax.ShapeDtypeStruct(shape, f32) for shape in shapes]


def in_pairs(grad):
    return grad.reshape((grad.shape[0] // 2, 2) + grad.shape[1:])


def taker(refs):
    refs = list(refs)

    def take(count):
        taken, refs[:count] = refs[:count], []
        return taken

    return take


def running_ends(lengths_ref):
    ends = [lengths_ref[0]]
    for k in range(1, lengths_ref.shape[0]):
        ends.append(ends[-1] + lengths_ref[k])
    return ends


def document(rows, ends):
    total = jnp.where(rows >= ends[0], 1, 0)
    for end in ends[1:]:
        total = total + jnp.where(rows >= end, 1, 0)
    return total


def block_masks(first, ends):
    shape = (WIDTH, WIDTH)
    down = lax.broadcasted_iota(jnp.int32, shape, 0)
    along = lax.broadcasted_iota(jnp.int32, shape, 1)
    docs = document(first + down, ends)
    same = (docs == document(first + along, ends)) & (down >= along)
    before = jnp.where(first > 0, document(first - 1, ends), -1)
    final = document(first + WIDTH - 1, ends)
    carry = jnp.where(docs == before, 1.0, 0.0)
    tail = jnp.where(docs == final, 1.0, 0.0)
    keep = jnp.where(final == before, 1.0, 0.0)
    return same, carry, tail, keep


def running(log_forget):
    shape = (WIDTH, WIDTH)
    lower = lax.broadcasted_iota(jnp.int32, shape, 0) >= lax.broadcasted_iota(jnp.int32, shape, 1)
    ones = jnp.where(lower, 1.0, 0.0).astype(bf16)
    high = log_forget.astype(bf16)
    low = (log_forget - high.astype(f32)).astype(bf16)
    return mul(ones, high, NN) + mul(ones, low, NN)


def decay_parts(forget_pre, bound):
    away = jax.nn.sigmoid(-forget_pre)
    key = jax.nn.sigmoid(-bound) * away
    return key, running(jnp.log(1.0 - key)), away


class States:
    def __init__(self, size, out_state, out_decay, land_state, land_decay, sems):
        self.size = size
        self.here = lax.axis_index("seq")
        self.out_state, self.out_decay = out_state, out_decay
        self.land_state, self.land_decay = land_state, land_decay
        self.sems = sems

    def pair(self, slot, peer):
        s = self.sems
        return (
            remote(self.out_state, self.land_state.at[slot], s.at[0, peer], s.at[1, slot], "seq", peer),
            remote(self.out_decay, self.land_decay.at[slot], s.at[2, peer], s.at[3, slot], "seq", peer),
        )

    def sends(self, later):
        for k in range(self.size):
            yield k, (self.here < k if later else self.here > k)

    def start(self, later):
        for k, wanted in self.sends(later):

            @pl.when(wanted)
            def _():
                for copy in self.pair(self.here, k):
                    copy.start()

    def compose(self, later, state):
        state[...] = jnp.zeros_like(state)
        order = range(self.size) if later else range(self.size - 1, -1, -1)
        for k in order:

            @pl.when(self.here > k if later else self.here < k)
            def _():
                for copy in self.pair(k, k):
                    copy.wait_recv()
                for h in range(state.shape[0]):
                    decay = self.land_decay[k, h : h + 1, :]
                    state[h] = decay * state[h] + self.land_state[k, h].astype(f32)

    def drain(self, later):
        for k, wanted in self.sends(later):

            @pl.when(wanted)
            def _():
                for copy in self.pair(self.here, k):
                    copy.wait_send()


def states_scratch(size, heads):
    return [
        VM((heads, WIDTH, WIDTH), f32),
        VM((heads, WIDTH, WIDTH), bf16),
        VM((8, WIDTH), f32),
        VM((size, heads, WIDTH, WIDTH), bf16),
        VM((size, 8, WIDTH), f32),
        DMA((4, size)),
    ]


def front_kernel(size, groups, rounds, *refs):
    take = taker(refs)
    lengths_ref, x_ref, norm_gain_ref, bound_ref, gain_ref, cot_in, *loaded = take(10)
    ends = running_ends(lengths_ref)
    a_out, q_out, f_out, i_out, s_out, cot_out, o_ref, u_ref, starts_ref = take(9)
    *weights, a_ref, q_ref, f_ref, i_ref, s_ref, cot_ref = take(10)
    qd_ref, kd_ref, qe_ref, adds, decays = take(5)
    state, out_state, out_decay, land_state, land_decay, sems = take(6)
    load_sems, store_sems, a_send, a_recv, c_send, c_recv = take(6)
    me = lax.axis_index("tp")
    m, d = x_ref.shape[1:]
    known = cot_ref.shape[1]
    local = pltpu.make_async_copy
    cot_load = local(cot_in.at[:known], cot_ref.at[me], load_sems.at[4])
    cot_load.start()
    loads = [local(source, target, load_sems.at[k]) for k, (source, target) in enumerate(zip(loaded, weights))]
    for load in loads:
        load.start()
    line, line_count = line_peers(size)
    seq, seq_count = group_peers(groups, "seq")
    greet(line + seq, line_count + seq_count)

    gather = Gather(size, a_send, a_recv, a_ref)
    gather_cot = Gather(size, c_send, c_recv, cot_ref)
    norm_gain = norm_gain_ref[...]

    @pl.loop(0, rounds)
    def _(j):
        @pl.loop(0, m // 16)
        def _(g):
            r = pl.ds(pl.multiple_of(g * 16, 16), 16)
            x = x_ref[j, r, :].astype(f32)
            scale = lax.rsqrt(jnp.mean(x * x, axis=-1, keepdims=True) + epsilon)
            a_ref[me, j, r, :] = (x * scale * norm_gain).astype(bf16)

        gather.start(j)

    for load in loads:
        load.wait()
    cot_load.wait()
    pres = (q_ref, f_ref, i_ref, s_ref)

    rows, c = q_ref.shape
    blocks, heads = rows // WIDTH, c // WIDTH
    base = lax.axis_index("seq") * rows
    states = States(groups, out_state, out_decay, land_state, land_decay, sems)
    state[...] = jnp.zeros_like(state)
    out_decay[...] = jnp.ones_like(out_decay)

    def cot_steps(t):
        @pl.loop(0, known)
        def _(j):
            gather_cot.step(j, t)

    def block(b):
        r = pl.ds(pl.multiple_of(b * WIDTH, WIDTH), WIDTH)
        same, carry, tail, keep = block_masks(base + b * WIDTH, ends)
        for h in range(heads):
            cols = slice(h * WIDTH, (h + 1) * WIDTH)
            q = q_ref[r, cols]
            q = q * jax.nn.sigmoid(q)
            key, run, _ = decay_parts(f_ref[r, cols], bound_ref[:, cols])
            middle, last = run[WIDTH // 2 - 1 : WIDTH // 2, :], run[WIDTH - 1 :, :]
            qd_ref[r, cols] = (q * jnp.exp(run - middle)).astype(bf16)
            kd_ref[r, cols] = (key * jnp.exp(middle - run)).astype(bf16)
            qe_ref[r, cols] = (q * jnp.exp(run) * carry).astype(bf16)
            key_tail = (key * jnp.exp(last - run) * tail).astype(bf16)
            adds[b, h] = mul(i_ref[r, cols].astype(bf16), key_tail, TN)
            decays[b, h : h + 1, :] = jnp.exp(last) * keep

    def near_part(b):
        r = pl.ds(pl.multiple_of(b * WIDTH, WIDTH), WIDTH)
        same, carry, tail, keep = block_masks(base + b * WIDTH, ends)
        for h in range(heads):
            cols = slice(h * WIDTH, (h + 1) * WIDTH)
            scores = jnp.where(same, mul(qd_ref[r, cols], kd_ref[r, cols], NT), 0.0).astype(bf16)
            o_ref[r, cols] = mul(scores, i_ref[r, cols].astype(bf16), NN)

    own_rows = rounds * m
    per = own_rows // WIDTH if own_rows % WIDTH == 0 and WIDTH % m == 0 else 0
    early = [z * per + k for z in range(size) for k in range(per - 1)] if per > 1 else []
    late = [b for b in range(blocks) if b not in early]
    ready = (per - 1) * WIDTH // m if early else rounds

    def some_blocks(chosen, body):
        if chosen is early and early:

            @pl.loop(0, size)
            def _(z):
                for k in range(per - 1):
                    body(z * per + k)

        elif early:

            @pl.loop(0, size)
            def _(z):
                body(z * per + per - 1)

        elif chosen is late:
            pl.loop(0, blocks)(body)

    def project(j):
        block_rows = a_ref[:, j].reshape(size * m, d)
        for weight, out in zip(weights, pres):
            product = mul(block_rows, weight[...], NN)
            for z in range(size):
                at = pl.multiple_of(z * own_rows + j * m, 16)
                out[pl.ds(at, m), :] = product[z * m : (z + 1) * m]

    @pl.loop(0, rounds)
    def _(j):
        for t in range(1, size):
            gather.step(j, t)
            if early and t == 1:

                @pl.when(j == ready)
                def _():
                    some_blocks(early, block)

            if early and t == 2:

                @pl.when(j == ready)
                def _():
                    some_blocks(early, near_part)

        @pl.when(j >= rounds - known)
        def _():
            gather_cot.start(j - (rounds - known))

        project(j)

    stores = [
        local(source, target, store_sems.at[k])
        for k, (source, target) in enumerate(zip((a_ref, *pres), (a_out, q_out, f_out, i_out, s_out)))
    ]
    for store in stores:
        store.start()

    some_blocks(late, block)

    @pl.loop(0, blocks)
    def _(b):
        for h in range(heads):
            decay = decays[b, h : h + 1, :]
            state[h] = decay * state[h] + adds[b, h]
            out_decay[h : h + 1, :] = out_decay[h : h + 1, :] * decay

    out_state[...] = state[...].astype(bf16)
    states.start(True)
    cot_steps(1)
    some_blocks(late, near_part)

    states.compose(True, state)
    for t in range(2, size - 1):
        cot_steps(t)

    @pl.loop(0, blocks)
    def _(b):
        r = pl.ds(pl.multiple_of(b * WIDTH, WIDTH), WIDTH)
        places = base + b * WIDTH + lax.broadcasted_iota(jnp.int32, (WIDTH, WIDTH), 0)
        valid = jnp.where(places < ends[-1], 1.0, 0.0)
        for h in range(heads):
            cols = slice(h * WIDTH, (h + 1) * WIDTH)
            low = state[h].astype(bf16)
            starts_ref[b, h] = low
            o = o_ref[r, cols] + mul(qe_ref[r, cols], low, NT)
            o_ref[r, cols] = o
            state[h] = decays[b, h : h + 1, :] * state[h] + adds[b, h]
            scale = lax.rsqrt(jnp.mean(o * o, axis=-1, keepdims=True) + epsilon)
            s = s_ref[r, cols]
            z = s * jax.nn.sigmoid(s) * valid
            u_ref[r, cols] = (o * scale * gain_ref[:, cols] * z).astype(bf16)

    cot_steps(size - 1)
    cot_store = local(cot_ref, cot_out, load_sems.at[4])
    cot_store.start()
    states.drain(True)

    @pl.loop(0, rounds)
    def _(j):
        gather.drain(j)

    @pl.loop(0, known)
    def _(j):
        gather_cot.drain(j)

    for store in stores:
        store.wait()
    cot_store.wait()


def front(size, groups, rounds, tokens, cot, norm_gain, weights, ends, bound, gain):
    own, d = tokens.shape
    m, c = own // rounds, weights[0].shape[1]
    rows = size * own
    blocks, heads = rows // WIDTH, c // WIDTH
    known = KNOWN
    shape, some = (size, rounds, m, d), (size, known, m, d)
    wide, low = jax.ShapeDtypeStruct((rows, c), f32), VM((rows, c), bf16)
    spec, far = pl.BlockSpec(memory_space=VM), pl.BlockSpec(memory_space=pl.ANY)
    sems = DMA((2, rounds, size))
    outs = pl.pallas_call(
        partial(front_kernel, size, groups, rounds),
        out_shape=[
            jax.ShapeDtypeStruct(shape, bf16),
            wide,
            wide,
            wide,
            wide,
            jax.ShapeDtypeStruct(some, bf16),
            wide,
            jax.ShapeDtypeStruct((rows, c), bf16),
            jax.ShapeDtypeStruct((blocks, heads, WIDTH, WIDTH), bf16),
        ],
        in_specs=[pl.BlockSpec(memory_space=pltpu.SMEM)] + [spec] * 4 + [far] * 5,
        out_specs=[far] * 6 + [spec] * 3,
        scratch_shapes=[VM((d, c), bf16)] * 4
        + [VM(shape, bf16)]
        + [VM((rows, c), f32)] * 4
        + [VM(some, bf16)]
        + [low] * 3
        + [VM((blocks, heads, WIDTH, WIDTH), f32), VM((blocks, 8, WIDTH), f32)]
        + states_scratch(groups, heads)
        + [DMA((5,)), DMA((5,)), sems, sems, sems, sems],
        compiler_params=pltpu.CompilerParams(collective_id=0, has_side_effects=True, vmem_limit_bytes=60 * MIB),
        cost_estimate=pl.CostEstimate(flops=8 * rows * d * c, bytes_accessed=36 * MIB, transcendentals=8 * rows * c),
        name="front",
    )(
        ends,
        tokens.reshape(rounds, m, d),
        norm_gain.reshape(1, d),
        bound,
        gain,
        cot.reshape(rounds, m, d),
        *weights,
    )
    return [outs[0].reshape(rows, d)] + list(outs[1:])


def scan_back_kernel(size, line, rounds, count, *refs):
    take = taker(refs)
    lengths_ref, bound_ref, gain_ref, norm_gain_ref, *loaded = take(16)
    ends = running_ends(lengths_ref)
    grads = take(count)
    *back_outs, small_ref, first_ref, part_out = take(7)
    grad_outs = take(count)
    qd_ref, kd_ref, qe_ref, kt_ref, do_ref, run_ref, adds, decays = take(8)
    state, out_state, out_decay, land_state, land_decay, sems = take(6)
    *inputs, load_sems = take(13)
    q_ref, f_ref, i_ref, s_ref, o_ref, ub_ref, starts_ref, *weights, a_ref = inputs
    *loaded, a_in = loaded
    stage, stage_sems, a_sems, *backs, back_sems = take(8)
    dq_ref, df_ref, di_ref, ds_ref = backs
    loads = [
        pltpu.make_async_copy(source, target, load_sems.at[k]) for k, (source, target) in enumerate(zip(loaded, inputs))
    ]
    soon, later = [loads[k] for k in (4, 3, 5, 0, 1)], [loads[k] for k in (2, 6)]
    for load in soon + later:
        load.start()
    sums = group_sums(size, grads, grad_outs, take)
    greet(*group_peers(size, "seq"))
    rows, c = q_ref.shape
    blocks, heads = rows // WIDTH, c // WIDTH
    base = lax.axis_index("seq") * rows
    states = States(size, out_state, out_decay, land_state, land_decay, sems)
    for each in sums:
        each.start()
    state[...] = jnp.zeros_like(state)
    out_decay[...] = jnp.ones_like(out_decay)
    small_ref[...] = jnp.zeros_like(small_ref)
    for load in soon:
        load.wait()

    @pl.loop(0, blocks)
    def _(back):
        for each in sums[:1]:

            @pl.when(back == 1)
            def _():
                each.middle()

        b = blocks - 1 - back
        r = pl.ds(pl.multiple_of(b * WIDTH, WIDTH), WIDTH)
        same, carry, tail, keep = block_masks(base + b * WIDTH, ends)
        places = base + b * WIDTH + lax.broadcasted_iota(jnp.int32, (WIDTH, WIDTH), 0)
        valid = jnp.where(places < ends[-1], 1.0, 0.0)
        for h in range(heads):
            cols = slice(h * WIDTH, (h + 1) * WIDTH)
            o, s, ub, gain = o_ref[r, cols], s_ref[r, cols], ub_ref[r, cols], gain_ref[:, cols]
            scale = lax.rsqrt(jnp.mean(o * o, axis=-1, keepdims=True) + epsilon)
            normed = o * scale
            gate = jax.nn.sigmoid(s)
            uz = ub * (s * gate * valid)
            small_ref[heads + h : heads + h + 1, :] += jnp.sum(uz * normed, axis=0, keepdims=True)
            nb = uz * gain
            ds_ref[r, cols] = (ub * normed * gain * valid * (gate * (1.0 + s * (1.0 - gate)))).astype(bf16)
            do = (scale * (nb - normed * jnp.mean(nb * normed, axis=-1, keepdims=True))).astype(bf16)
            do_ref[r, cols] = do
            q = q_ref[r, cols]
            q = q * jax.nn.sigmoid(q)
            key, run, _ = decay_parts(f_ref[r, cols], bound_ref[:, cols])
            middle, last = run[WIDTH // 2 - 1 : WIDTH // 2, :], run[WIDTH - 1 :, :]
            run_ref[r, cols] = run
            qd_ref[r, cols] = (q * jnp.exp(run - middle)).astype(bf16)
            kd_ref[r, cols] = (key * jnp.exp(middle - run)).astype(bf16)
            kt_ref[r, cols] = (key * jnp.exp(last - run) * tail).astype(bf16)
            qe = (q * jnp.exp(run) * carry).astype(bf16)
            qe_ref[r, cols] = qe
            add = mul(do, qe, TN)
            decay = jnp.exp(last) * keep
            adds[b, h] = add
            decays[b, h : h + 1, :] = decay
            state[h] = decay * state[h] + add
            out_decay[h : h + 1, :] = out_decay[h : h + 1, :] * decay

    out_state[...] = state[...].astype(bf16)
    states.start(False)
    for load in later:
        load.wait()
    for load in loads[7:]:
        load.start()
    for each in sums[:1]:
        each.relay()
    for each in sums[1:]:
        each.middle()
    states.compose(False, state)

    @pl.loop(0, blocks)
    def _(back):
        for each in sums[1:]:

            @pl.when(back == blocks // 2)
            def _():
                each.relay()
        b = blocks - 1 - back
        r = pl.ds(pl.multiple_of(b * WIDTH, WIDTH), WIDTH)
        same, carry, tail, keep = block_masks(base + b * WIDTH, ends)
        shape = (WIDTH, WIDTH)
        down, along = lax.broadcasted_iota(jnp.int32, shape, 0), lax.broadcasted_iota(jnp.int32, shape, 1)
        from_here = jnp.where(along >= down, 1.0, 0.0).astype(bf16)
        ahead = jnp.where(along < down, 1.0, 0.0).astype(bf16)
        for h in range(heads):
            cols = slice(h * WIDTH, (h + 1) * WIDTH)
            do, v = do_ref[r, cols], i_ref[r, cols].astype(bf16)
            low, start = state[h].astype(bf16), starts_ref[b, h]
            dq_state = mul(do, start, NN)
            dk_state = mul(v, low, NN)
            kt = kt_ref[r, cols]
            qd, kd = qd_ref[r, cols], kd_ref[r, cols]
            scores = jnp.where(same, mul(qd, kd, NT), 0.0).astype(bf16)
            slopes = jnp.where(same, mul(do, v, NT), 0.0).astype(bf16)
            dq_near = mul(slopes, kd, NN)
            dk_near = mul(slopes, qd, TN)
            di_ref[r, cols] = (mul(scores, do, TN) + mul(kt, low, NT)).astype(bf16)
            run = run_ref[r, cols]
            middle, last = run[WIDTH // 2 - 1 : WIDTH // 2, :], run[WIDTH - 1 :, :]
            q_back = dq_near * jnp.exp(run - middle) + dq_state * (jnp.exp(run) * carry)
            k_back = dk_near * jnp.exp(middle - run) + dk_state * (jnp.exp(last - run) * tail)
            later = (
                qe_ref[r, cols].astype(f32) * dq_state
                + qd.astype(f32) * dq_near
                - kd.astype(f32) * dk_near
            )
            earlier = kt.astype(f32) * dk_state
            decay = decays[b, h : h + 1, :]
            log_back = decay * jnp.sum(low.astype(f32) * start.astype(f32), axis=0, keepdims=True)
            for ones, part in ((from_here, later), (ahead, earlier)):
                high = part.astype(bf16)
                log_back = log_back + mul(ones, high, NN)
                log_back = log_back + mul(ones, (part - high.astype(f32)).astype(bf16), NN)
            f_pre = f_ref[r, cols]
            away, near = jax.nn.sigmoid(-f_pre), jax.nn.sigmoid(f_pre)
            upper = jax.nn.sigmoid(-bound_ref[:, cols])
            lower = jax.nn.sigmoid(bound_ref[:, cols])
            forget_back = log_back / (1.0 - upper * away) - k_back
            slope = forget_back * away * upper
            df_ref[r, cols] = (slope * near).astype(bf16)
            small_ref[h : h + 1, :] += jnp.sum(slope, axis=0, keepdims=True) * lower
            dq_ref[r, cols] = (q_back * silu_slope(q_ref[r, cols])).astype(bf16)
            state[h] = adds[b, h] + decay * state[h]

    stores = [
        pltpu.make_async_copy(source, target, back_sems.at[k]) for k, (source, target) in enumerate(zip(backs, back_outs))
    ]
    for store in stores:
        store.start()
    for load in loads[7:]:
        load.wait()
    m, d = a_ref.shape[2:]

    def a_load(j):
        slot = lax.rem(j, 2)
        return pltpu.make_async_copy(a_in.at[:, j], a_ref.at[slot], a_sems.at[slot])

    for j in range(min(2, rounds)):
        a_load(j).start()
    tile = min(512, d)
    first_ref[...] = jnp.zeros_like(first_ref)

    def part_copy(j):
        return pltpu.make_async_copy(stage.at[lax.rem(j, 2)], part_out.at[j], stage_sems.at[lax.rem(j, 2)])

    @pl.loop(0, rounds)
    def _(j):
        @pl.when(j > 1)
        def _():
            part_copy(j - 2).wait()

        a_load(j).wait()

        def round_rows(ref):
            places = [pl.multiple_of(z * rounds * m + j * m, 16) for z in range(line)]
            return jnp.concatenate([ref[pl.ds(at, m), :] for at in places], axis=0)

        @pl.loop(0, d // tile)
        def _(n):
            cols = pl.ds(pl.multiple_of(n * tile, tile), tile)
            acc = None
            for back, weight in zip((dq_ref, df_ref, di_ref, ds_ref), weights):
                term = mul(round_rows(back), weight[cols, :], NT)
                acc = term if acc is None else acc + term
            normed = a_ref[lax.rem(j, 2), :, :, cols].reshape(line * m, tile).astype(f32)
            first_ref[:, cols] += jnp.sum(acc * normed, axis=0, keepdims=True)
            stage[lax.rem(j, 2), :, :, cols] = acc.astype(bf16).reshape(line, m, tile)

        part_copy(j).start()

        @pl.when(j + 2 < rounds)
        def _():
            a_load(j + 2).start()

    first_ref[...] = first_ref[...] / norm_gain_ref[...]
    for each in sums:
        each.finish()
    for j in range(max(0, rounds - 2), rounds):
        part_copy(j).wait()
    for store in stores:
        store.wait()
    states.drain(False)
    for each in sums:
        each.drain()


def scan_backward(size, line, rounds, ends, bound, gain, q, f, i, s, o, ub, starts, norm_gain, a, weights, grads):
    rows, c = q.shape
    d = a.shape[1]
    shape = (line, rounds, rows // line // rounds, d)
    part = (rounds, line) + shape[2:]
    blocks, heads = rows // WIDTH, c // WIDTH
    low, wide = VM((rows, c), bf16), VM((rows, c), f32)
    spec = pl.BlockSpec(memory_space=VM)
    return pl.pallas_call(
        partial(scan_back_kernel, size, line, rounds, len(grads)),
        out_shape=[jax.ShapeDtypeStruct((rows, c), bf16)] * 4
        + [jax.ShapeDtypeStruct((2 * heads, WIDTH), f32), jax.ShapeDtypeStruct((1, d), f32)]
        + [jax.ShapeDtypeStruct(part, bf16)]
        + sum_shapes([grad.shape for grad in grads], [False] * len(grads)),
        in_specs=[pl.BlockSpec(memory_space=pltpu.SMEM)]
        + [spec] * 3
        + [pl.BlockSpec(memory_space=pl.ANY)] * (12 + len(grads)),
        out_specs=[pl.BlockSpec(memory_space=pl.ANY)] * 4
        + [spec] * 2
        + [pl.BlockSpec(memory_space=pl.ANY)]
        + [spec] * len(grads),
        scratch_shapes=[low] * 5
        + [wide, VM((blocks, heads, WIDTH, WIDTH), f32), VM((blocks, 8, WIDTH), f32)]
        + states_scratch(size, heads)
        + [wide] * 6
        + [VM(starts.shape, bf16)]
        + [VM((d, c), bf16)] * 4
        + [VM((2,) + part[1:], bf16), DMA((11,)), VM((2,) + part[1:], bf16), DMA((2,)), DMA((2,))]
        + [low] * 4
        + [DMA((4,))]
        + group_sums_scratch([grad.shape for grad in grads]),
        compiler_params=pltpu.CompilerParams(collective_id=2, has_side_effects=True, vmem_limit_bytes=63 * MIB),
        cost_estimate=pl.CostEstimate(flops=8 * rows * c * d, bytes_accessed=40 * MIB, transcendentals=16 * rows * c),
        name="scan_backward",
    )(
        ends,
        bound,
        gain,
        norm_gain.reshape(1, d),
        q,
        f,
        i,
        s,
        o,
        ub,
        starts,
        *weights,
        a.reshape(shape),
        *[in_pairs(grad) for grad in grads],
    )


def middle_kernel(size, rounds, *refs):
    take = taker(refs)
    u_ref, x_ref, gain_ref, out_w, *loaded, cot_some, cot_own = take(9)
    res_out, back_out, e_out, ub_out, second_ref, down_out, out_grad, *grad_outs = take(10)
    gate_w, up_w, down_w = weights = take(3)
    cot_ref = take(1)[0]
    b_ref, e_ref, res_ref, back_ref, ub_ref, part, land, total = take(8)
    wide = take(3)
    down_ref, *tiles = take(4)
    load_sems, res_sems, back_sems, e_sems, ub_sem, down_sem, tile_sems = take(7)
    lines = [take(2) for _ in range(5)]
    hidden, gate_back, up_back = wide
    me = lax.axis_index("tp")
    m, d = x_ref.shape[1:]
    ff = gate_w.shape[1]
    group = size * m
    scatter = Scatter(size, *lines[0], part, land, total)
    gather = Gather(size, *lines[1], b_ref)
    scatter_back = Scatter(size, *lines[2], part, land, total)
    gather_back = Gather(size, *lines[3], e_ref)
    gather_cot = Gather(size, *lines[4], cot_ref)
    known = cot_some.shape[1]
    gain = gain_ref[...]
    tile = min(512, d)
    local = pltpu.make_async_copy
    loads = [local(src, dst, load_sems.at[k]) for k, (src, dst) in enumerate(zip(loaded, weights))]
    loads.append(local(cot_some, cot_ref.at[:, :known], load_sems.at[3]))
    cot_load = local(cot_own.at[known:], cot_ref.at[me, known:], load_sems.at[4])
    cot_load.start()
    for load in loads:
        load.start()
    second_ref[...] = jnp.zeros_like(second_ref)
    greet(*line_peers(size))

    def project_out(j):
        rows = u_ref[:, j].reshape(group, u_ref.shape[3])

        @pl.loop(0, d // tile)
        def _(n):
            cols = pl.ds(pl.multiple_of(n * tile, tile), tile)
            part[j, :, :, cols] = mul(rows, out_w[:, cols], NN).astype(bf16).reshape(size, m, tile)

        scatter.start(j)

    def res_copy(j):
        return local(res_ref.at[j], res_out.at[j], res_sems.at[j])

    def back_copy(j):
        return local(back_ref, back_out.at[j], back_sems.at[0])

    def e_copy(j):
        return local(e_ref.at[:, j], e_out.at[:, j], e_sems.at[j])

    def ub_copy(j):
        return local(ub_ref, ub_out.at[:, j], ub_sem.at[0])

    def down_copy(j):
        return local(down_ref, down_out.at[:, j], down_sem.at[0])

    def norm(j):
        @pl.loop(0, m // 16)
        def _(g):
            r = pl.ds(pl.multiple_of(g * 16, 16), 16)
            residual = x_ref[j, r, :].astype(f32) + total[r, :]
            res_ref[j, r, :] = residual
            scale = lax.rsqrt(jnp.mean(residual * residual, axis=-1, keepdims=True) + epsilon)
            b_ref[me, j, r, :] = (residual * scale * gain).astype(bf16)

        gather.start(j)
        res_copy(j).start()

    def feed(j, piece):
        rows = b_ref[:, j].reshape(group, d)
        cot = cot_ref[:, j].reshape(group, d)
        step = 256
        starts = list(range(0, ff, step))
        for low in starts[len(starts) * piece // PIECES : len(starts) * (piece + 1) // PIECES]:
            cols = slice(low, min(low + step, ff))
            width = cols.stop - cols.start
            gate = mul(rows, gate_w[:, cols], NN)
            up = mul(rows, up_w[:, cols], NN)
            hb = mul(cot, down_w[cols, :], NT)
            sig = jax.nn.sigmoid(gate)
            act = gate * sig
            shape = (size, m, width)
            hidden[:, j, :, cols] = (act * up).astype(bf16).reshape(shape)
            up_back[:, j, :, cols] = (hb * act).astype(bf16).reshape(shape)
            gate_back[:, j, :, cols] = (hb * up * (sig * (1.0 + gate * (1.0 - sig)))).astype(bf16).reshape(shape)

    def feed_back(j):
        scatter.drain(j)
        gates = gate_back[:, j].reshape(group, ff)
        ups = up_back[:, j].reshape(group, ff)

        @pl.loop(0, d // tile)
        def _(n):
            cols = pl.ds(pl.multiple_of(n * tile, tile), tile)
            sums = mul(gates, gate_w[cols, :], NT) + mul(ups, up_w[cols, :], NT)
            part[j, :, :, cols] = sums.astype(bf16).reshape(size, m, tile)

        scatter_back.start(j)

    def feed_out(j):
        rows = hidden[:, j].reshape(group, ff)

        @pl.loop(0, d // tile)
        def _(n):
            cols = pl.ds(pl.multiple_of(n * tile, tile), tile)
            down_ref[:, :, cols] = mul(rows, down_w[:, cols], NN).astype(bf16).reshape(size, m, tile)

        down_copy(j).start()

    def norm_back(j):
        @pl.loop(0, m // 16)
        def _(g):
            r = pl.ds(pl.multiple_of(g * 16, 16), 16)
            b_back, residual = total[r, :], res_ref[j, r, :]
            scale = lax.rsqrt(jnp.mean(residual * residual, axis=-1, keepdims=True) + epsilon)
            normed = residual * scale
            second_ref[...] += jnp.sum(b_back * normed, axis=0, keepdims=True)
            inner = b_back * gain
            back = cot_ref[me, j, r, :].astype(f32) + scale * (
                inner - normed * jnp.mean(inner * normed, axis=-1, keepdims=True)
            )
            back_ref[r, :] = back
            e_ref[me, j, r, :] = back.astype(bf16)

        gather_back.start(j)
        back_copy(j).start()

    def unproject(j):
        e_copy(j).start()
        rows = e_ref[:, j].reshape(group, d)
        ub_ref[...] = mul(rows, out_w[...], NT).reshape(size, m, out_w.shape[0])
        ub_copy(j).start()

    depth = tiles[0].shape[0]
    count = d // depth

    def tile_copies(n):
        rows = pl.ds(n * depth, depth)
        return [local(src, dst.at[rows, :], tile_sems.at[k]) for k, (src, dst) in enumerate(zip(tiles, grad_outs))]

    def weight_tile(n):
        cols = pl.ds(n * depth, depth)
        for left, right, out in zip((b_ref, b_ref, cot_ref), (gate_back, up_back, hidden), tiles):
            rows = left[:, :, :, cols].reshape(rounds * group, depth)
            out[...] = mul(rows, right[...].reshape(rounds * group, ff), TN).astype(bf16)
        for copy in tile_copies(n):
            copy.start()

    cot_load.wait()
    held = {}

    def then(kind, copies):
        for copy in held.get(kind, []):
            copy.wait()
        held[kind] = copies

    shares = sum(name[0] == "W" for name in STEPS)
    for name in STEPS:
        kind, j, t = name[0], int(name[1]), int(name[2:] or 0)
        if kind == "A":
            project_out(j)
        elif kind == "C":
            gather_cot.step(j, t) if t else gather_cot.start(j)
        elif kind == "S" and t < size - 1:
            scatter.step(j, t)
        elif kind == "S":
            scatter.finish(j)
            norm(j)
        elif kind == "G":
            gather.step(j, t)
        elif kind == "F":
            then("loads", loads if "loads" not in held else [])
            then("loads", [])
            feed(j, t)
        elif kind == "B":
            feed_back(j)
        elif kind == "O":
            then(kind, [])
            feed_out(j)
            then(kind, [down_copy(j)])
        elif kind == "T" and t < size - 1:
            scatter_back.step(j, t)
        elif kind == "T":
            then(kind, [])
            scatter_back.finish(j)
            norm_back(j)
            then(kind, [back_copy(j)])
        elif kind == "E":
            gather_back.step(j, t)
        elif kind == "U":
            then(kind, [])
            unproject(j)
            then(kind, [ub_copy(j)])
        elif kind == "W":
            for n in range(count * j // shares, count * (j + 1) // shares):
                then(kind, [])
                weight_tile(n)
                then(kind, tile_copies(n))
    for kind in list(held):
        then(kind, [])
    width = u_ref.shape[3]

    def out_tile(n, slot):
        rows = pl.ds(pl.multiple_of(n * depth, depth), depth)
        source = tiles[slot].at[:, pl.ds(0, width)]
        return local(source, out_grad.at[rows, :], tile_sems.at[slot])

    slots = len(tiles) - 1

    @pl.loop(0, count // slots)
    def _(n):
        for slot in range(slots):
            at = n * slots + slot

            @pl.when(n > 0)
            def _():
                out_tile(at - slots, slot).wait()

            cols = pl.ds(pl.multiple_of(at * depth, depth), depth)
            rows = e_ref[:, :, :, cols].reshape(rounds * group, depth)
            tiles[slot][:, :width] = mul(rows, u_ref[...].reshape(rounds * group, width), TN).astype(bf16)
            out_tile(at, slot).start()

    for slot in range(slots):
        out_tile(count - slots + slot, slot).wait()

    @pl.loop(0, rounds)
    def _(j):
        res_copy(j).wait()
        e_copy(j).wait()

        @pl.when(j >= known)
        def _():
            gather_cot.drain(j)

        gather.drain(j)
        scatter_back.drain(j)
        gather_back.drain(j)


def middle(size, rounds, u, x, cot_some, cot, gain, out_w, gate_w, up_w, down_w):
    rows, d = x.shape
    m = rows // rounds
    c, ff = out_w.shape[0], gate_w.shape[1]
    shape = (size, rounds, m)
    sems = DMA((2, rounds, size))
    spec, far = pl.BlockSpec(memory_space=VM), pl.BlockSpec(memory_space=pl.ANY)
    depth = min(256, d)
    outs = pl.pallas_call(
        partial(middle_kernel, size, rounds),
        out_shape=[
            jax.ShapeDtypeStruct((rounds, m, d), f32),
            jax.ShapeDtypeStruct((rounds, m, d), f32),
            jax.ShapeDtypeStruct(shape + (d,), bf16),
            jax.ShapeDtypeStruct(shape + (c,), f32),
            jax.ShapeDtypeStruct((1, d), f32),
            jax.ShapeDtypeStruct(shape + (d,), bf16),
            jax.ShapeDtypeStruct((d, c), bf16),
        ]
        + [jax.ShapeDtypeStruct((d, ff), bf16)] * 3,
        in_specs=[spec] * 4 + [far] * 5,
        out_specs=[far] * 4 + [spec] + [far] * 5,
        scratch_shapes=[
            VM(gate_w.shape, bf16),
            VM(up_w.shape, bf16),
            VM(down_w.shape, bf16),
            VM(shape + (d,), bf16),
            VM(shape + (d,), bf16),
            VM(shape + (d,), bf16),
            VM((rounds, m, d), f32),
            VM((m, d), f32),
            VM((size, m, c), f32),
            VM((rounds, size, m, d), bf16),
            VM((2, rounds, size - 1, m, d), bf16),
            VM((m, d), f32),
        ]
        + [VM(shape + (ff,), bf16)] * 3
        + [VM((size, m, d), bf16)]
        + [VM((depth, ff), bf16)] * 3
        + [DMA((5,)), DMA((rounds,)), DMA((1,)), DMA((rounds,)), DMA((1,)), DMA((1,)), DMA((3,))]
        + [sems] * 10,
        compiler_params=pltpu.CompilerParams(collective_id=3, has_side_effects=True, vmem_limit_bytes=63 * MIB),
        cost_estimate=pl.CostEstimate(
            flops=2 * size * rows * d * (2 * c + 9 * ff), bytes_accessed=56 * MIB, transcendentals=size * rows * ff
        ),
        name="middle",
    )(
        u.reshape(shape + (c,)),
        x.reshape(rounds, m, d),
        gain.reshape(1, d),
        out_w,
        gate_w,
        up_w,
        down_w,
        cot_some,
        cot.reshape(rounds, m, d),
    )
    res, back, e, ub, second, down, *grads = outs
    total = size * rows
    return (
        res.reshape(rows, d),
        back.reshape(rows, d),
        ub.reshape(total, c),
        second,
        down.reshape(total, d),
        *grads,
    )


class Everyone:
    def __init__(self, size, axis, mine, land, sems):
        self.size, self.axis = size, axis
        self.here = lax.axis_index(axis)
        self.mine, self.land, self.sems = mine, land, sems

    def copy(self, slot, peer):
        return remote(self.mine, self.land.at[slot], self.sems.at[0, peer], self.sems.at[1, slot], self.axis, peer)

    def others(self):
        for k in range(self.size):
            yield k, self.here != k

    def start(self):
        for k, other in self.others():

            @pl.when(other)
            def _():
                self.copy(self.here, k).start()

    def finish(self, out):
        out[...] = self.mine[...]
        for k, other in self.others():

            @pl.when(other)
            def _():
                self.copy(k, k).wait_recv()
                out[...] = out[...] + self.land[k]

    def drain(self):
        for k, other in self.others():

            @pl.when(other)
            def _():
                self.copy(self.here, k).wait_send()


def everyone_scratch(size, rows):
    return [VM((rows, WIDTH), f32), VM((size, rows, WIDTH), f32), DMA((2, size))]


def stack(vector, into, at):
    for k in range(vector.shape[1] // WIDTH):
        into[at + k : at + k + 1, :] = vector[:, k * WIDTH : (k + 1) * WIDTH]


def last_kernel(size, groups, rounds, count, mixed, *refs):
    take = taker(refs)
    backs = take(4)
    x_ref, gain_ref, second_ref, small_ref, first_ref, back_in, a_in, part_in, res_in, down_in = take(10)
    grads = take(count)
    tokens_far, small_out, output_ref = take(3)
    grad_outs = take(count + (4 if mixed else 0))
    part, land, total, s_send, s_recv = take(5)
    small_seq, gains_tp, sides = take(3), take(3), take(1)[0]
    nears = take(4 if mixed else 0)
    a_ref, tokens_out, res_ref, down_ref, load_sems, store_sems = take(6)
    sums = group_sums(groups, grads + nears, grad_outs, take)
    early, late = sums[:2], sums[2:]

    seq, seq_count = group_peers(groups, "seq")
    tp, tp_count = group_peers(size, "tp")
    greet(seq + tp, seq_count + tp_count)

    for each in sums[:count]:
        each.start()
    m, d = x_ref.shape[1:]
    tile = min(512, d)
    local = pltpu.make_async_copy

    def part_load(j):
        return local(part_in.at[j], part.at[j], load_sems.at[2 + j])

    a_load = local(a_in, a_ref, load_sems.at[1])
    back_load = local(back_in, tokens_out, load_sems.at[0])

    for j in range(rounds):
        part_load(j).start()
    a_load.start()
    back_load.start()
    output_loads = [
        local(source, target, load_sems.at[2 + rounds + k])
        for k, (source, target) in enumerate(((res_in, res_ref), (down_in, down_ref)))
    ]
    for load in output_loads:
        load.start()

    def store(j):
        return local(tokens_out.at[j], tokens_far.at[j], store_sems.at[j])

    group = size * m
    scatter = Scatter(size, s_send, s_recv, part, land, total)
    gain = gain_ref[...]

    seq_small = Everyone(groups, "seq", *small_seq)
    tp_gains = Everyone(size, "tp", *gains_tp)
    lines, smalls = d // WIDTH, small_ref.shape[0]

    def mix(back, each):
        rows = back[...].reshape(rounds * group, back.shape[3])
        depth = each.own.shape[1]
        for side, into in ((1 - each.side, each.grad), (each.side, each.own)):

            @pl.loop(0, each.half)
            def _(k):
                cols = pl.ds(pl.multiple_of((2 * k + side) * depth, depth), depth)
                left = a_ref[:, :, :, cols].reshape(rounds * group, depth)
                into[k] = mul(left, rows, TN).astype(bf16)

            if into is each.grad:
                each.start()

    def norm_back(j):
        @pl.loop(0, m // 16)
        def _(g):
            r = pl.ds(pl.multiple_of(g * 16, 16), 16)
            a_back, x = total[r, :], x_ref[j, r, :].astype(f32)
            scale = lax.rsqrt(jnp.mean(x * x, axis=-1, keepdims=True) + epsilon)
            normed = x * scale
            inner = a_back * gain
            tokens_out[j, r, :] = tokens_out[j, r, :] + scale * (
                inner - normed * jnp.mean(inner * normed, axis=-1, keepdims=True)
            )

    def steps(j, low, high):
        for t in range(low, high):
            if t < size - 1:
                scatter.step(j, t)
            else:
                scatter.finish(j)
                norm_back(j)
                store(j).start()

    stack(second_ref[...], gains_tp[0], 0)
    stack(first_ref[...], gains_tp[0], lines)
    tp_gains.start()
    for j in range(rounds):
        part_load(j).wait()
        scatter.start(j)
    tp_gains.finish(sides)
    small_seq[0][: 2 * lines, :] = sides[...]
    small_seq[0][2 * lines : 2 * lines + smalls, :] = small_ref[...]
    seq_small.start()
    for each in early:
        each.middle()
    a_load.wait()
    steps(0, 1, 2)
    back_load.wait()
    if mixed:
        for at, (back, each) in enumerate(zip(backs, late)):
            mix(back, each)
            steps(0, 2, 3) if at == 0 else None
            steps(0, 3, size) if at == 2 else None
    else:
        steps(0, 2, size)
    for each in early:
        each.relay()
    for each in late:
        each.middle()
    for load in output_loads:
        load.wait()

    @pl.loop(0, rounds * m // 16)
    def _(g):
        r = pl.ds(pl.multiple_of(g * 16, 16), 16)
        output_ref[r, :] = (res_ref[r, :] + down_ref[r, :].astype(f32)).astype(bf16)

    steps(1, 1, 3)
    steps(1, 3, size)
    for each in late[:2]:
        each.relay()
    steps(2, 1, 3)
    for each in late[2:]:
        each.relay()
    steps(2, 3, size)
    for each in early:
        each.finish()
    seq_small.finish(small_out)
    for j in range(3, rounds):
        steps(j, 1, size)
    for each in late:
        each.finish()

    for each in sums + [seq_small, tp_gains]:
        each.drain()

    @pl.loop(0, rounds)
    def _(j):
        scatter.drain(j)
        store(j).wait()


def last(size, groups, rounds, backs, part, a, x, back, gain, second, first, small, residual, down, grads, turned):
    mixed = len(turned) > len(grads)
    rows, d = x.shape
    m = rows // rounds
    c = backs[0].shape[1]
    shape = (size, rounds, m)
    lines = d // WIDTH
    sems = DMA((2, rounds, size))
    spec = pl.BlockSpec(memory_space=VM)
    small_rows = 2 * lines + small.shape[0]
    shapes = [grad.shape for grad in grads] + ([(groups, d // groups, c)] * 4 if mixed else [])
    outs = pl.pallas_call(
        partial(last_kernel, size, groups, rounds, len(grads), mixed),
        out_shape=[
            jax.ShapeDtypeStruct((rounds, m, d), f32),
            jax.ShapeDtypeStruct((small_rows, WIDTH), f32),
            jax.ShapeDtypeStruct((rows, d), bf16),
        ]
        + sum_shapes(shapes, turned),
        in_specs=[spec] * 9 + [pl.BlockSpec(memory_space=pl.ANY)] * (5 + len(grads)),
        out_specs=[pl.BlockSpec(memory_space=pl.ANY)] + [spec] * (2 + len(shapes)),
        scratch_shapes=[
            VM((rounds, size, m, d), bf16),
            VM((2, rounds, size - 1, m, d), bf16),
            VM((m, d), f32),
            sems,
            sems,
        ]
        + everyone_scratch(groups, small_rows)
        + everyone_scratch(size, 2 * lines)
        + [VM((2 * lines, WIDTH), f32)]
        + ([VM((groups // 2, d // groups, c), bf16)] * 4 if mixed else [])
        + [VM(shape + (d,), bf16)]
        + [VM((rounds, m, d), f32), VM((rows, d), f32), VM((rows, d), bf16), DMA((4 + rounds,)), DMA((rounds,))]
        + group_sums_scratch(shapes),
        compiler_params=pltpu.CompilerParams(collective_id=4, has_side_effects=True, vmem_limit_bytes=63 * MIB),
        cost_estimate=pl.CostEstimate(flops=16 * size * rows * d * c, bytes_accessed=56 * MIB, transcendentals=0),
        name="last",
    )(
        *[part.reshape(shape + (c,)) for part in backs],
        x.reshape(rounds, m, d),
        gain.reshape(1, d),
        second,
        small,
        first,
        back.reshape(rounds, m, d),
        a.reshape(shape + (d,)),
        part,
        residual,
        down,
        *[in_pairs(grad) for grad in grads],
    )
    return (outs[0].reshape(rows, d),) + tuple(outs[1:])


def results_kernel(count, size, small_ref, *refs):
    ins, outs = refs[:count], refs[count : 2 * count]
    first_out, second_out, bound_out, gain_out, *held, sems = refs[2 * count :]
    loads = [pltpu.make_async_copy(a, b, sems.at[0, k]) for k, (a, b) in enumerate(zip(ins, held))]
    stores = [pltpu.make_async_copy(a, b, sems.at[1, k]) for k, (a, b) in enumerate(zip(held, outs))]
    for load in loads:
        load.start()

    def share(rows, at, width):
        picked = rows[:, :width]
        for k in range(1, WIDTH // width):
            picked = jnp.where(at == k, rows[:, k * width : (k + 1) * width], picked)
        return picked

    here = lax.axis_index("seq")
    place = here * size + lax.axis_index("tp")
    each = first_out.shape[1]
    per = WIDTH // each
    heads, wide = bound_out.shape
    lines = (small_ref.shape[0] - 2 * heads) // 2
    at = lax.broadcasted_iota(jnp.int32, (lines, WIDTH), 0)
    for source, target in ((small_ref[:lines], second_out), (small_ref[lines : 2 * lines], first_out)):
        line = jnp.sum(jnp.where(at == place // per, source, 0.0), axis=0, keepdims=True)
        target[...] = share(line, place % per, each)
    bound_out[...] = share(small_ref[2 * lines : 2 * lines + heads, :], here, wide)
    gain_out[...] = share(small_ref[2 * lines + heads :, :], here, wide)
    for load, store in zip(loads, stores):
        load.wait()
        store.start()
    for store in stores:
        store.wait()


def results(groups, size, small, heads, arrays):
    each = (small.shape[0] - 2 * heads) // 2 * WIDTH // (groups * size)
    spec, far = pl.BlockSpec(memory_space=VM), pl.BlockSpec(memory_space=pl.ANY)
    outs = pl.pallas_call(
        partial(results_kernel, len(arrays), size),
        out_shape=[jax.ShapeDtypeStruct(part.shape, part.dtype) for part in arrays]
        + [jax.ShapeDtypeStruct((1, each), f32)] * 2
        + [jax.ShapeDtypeStruct((heads, WIDTH // groups), f32)] * 2,
        in_specs=[spec] + [far] * len(arrays),
        out_specs=[far] * len(arrays) + [spec] * 4,
        scratch_shapes=[VM(part.shape, part.dtype) for part in arrays] + [DMA((2, len(arrays)))],
        compiler_params=pltpu.CompilerParams(vmem_limit_bytes=60 * MIB),
        cost_estimate=pl.CostEstimate(flops=0, bytes_accessed=20 * MIB, transcendentals=0),
        name="results",
    )(small, *arrays)
    copied, (first, second, bound, gain) = outs[: len(arrays)], outs[len(arrays) :]
    return first.reshape(each), second.reshape(each), bound, gain, copied


def per_device(
    size,
    groups,
    tokens,
    lengths,
    cotangent,
    first_gain,
    query_weight,
    forget_weight,
    input_weight,
    swish_weight,
    bound_logit,
    group_gain,
    out_weight,
    second_gain,
    gate_weight,
    up_weight,
    down_weight,
):
    weights = (query_weight, forget_weight, input_weight, swish_weight)
    ends = lengths.astype(jnp.int32)
    bound, head_gain = bound_logit.reshape(1, -1), group_gain.reshape(1, -1)
    a, q, f, i, s, cot_some, o, u, starts = front(
        size, groups, ROUNDS, tokens, cotangent, first_gain, weights, ends, bound, head_gain
    )
    residual, back, ub, second, down, *wide = middle(
        size, ROUNDS, u, tokens, cot_some, cotangent, second_gain, out_weight, gate_weight, up_weight, down_weight
    )
    down, ub = lax.optimization_barrier((down, ub))
    down = lax.psum_scatter(down, "tp", scatter_dimension=0, tiled=True)
    d = tokens.shape[1]

    def chunks(grad):
        return grad.reshape(groups, grad.shape[0] // groups, grad.shape[1])

    def grad_of(left, right):
        return chunks(lax.dot_general(left, right, TN, preferred_element_type=f32).astype(bf16))

    outs, gates, ups, downs = (chunks(grad) for grad in wide)
    dq, df, di, ds, small, first, part, gate_grad, up_grad = scan_backward(
        groups,
        size,
        ROUNDS,
        ends,
        bound,
        head_gain,
        q,
        f,
        i,
        s,
        o,
        ub,
        starts,
        first_gain,
        a,
        weights,
        [gates, ups],
    )
    back_rows = (dq, df, di, ds)
    here_too = groups == 8
    others = [downs, outs] + ([] if here_too else [grad_of(a, part) for part in back_rows])
    tokens_grad, small_sum, output, *sums = last(
        size,
        groups,
        ROUNDS,
        back_rows,
        part,
        a,
        tokens,
        back,
        first_gain,
        second,
        first,
        small,
        residual,
        down,
        others,
        [True, True] + [False] * 4,
    )
    arrays = [output, tokens_grad, gate_grad, up_grad, *sums]
    first_grad, second_grad, bound_grad, head_grad, copied = results(
        groups, size, small_sum, bound_logit.shape[0], arrays
    )
    output, tokens_grad, gate_grad, up_grad, down_grad, out_grad, *mixes = copied
    query_grad, forget_grad, input_grad, swish_grad = mixes
    return (
        output,
        tokens_grad,
        first_grad,
        query_grad,
        forget_grad,
        input_grad,
        swish_grad,
        bound_grad,
        head_grad,
        out_grad,
        second_grad,
        gate_grad,
        up_grad,
        down_grad,
    )


def solution(mesh):
    rows, both, cols, lines = P(("seq", "tp"), None), P(("seq", "tp")), P(None, "tp"), P("tp", None)
    in_specs = (rows, P(), rows, P(), cols, cols, cols, cols, lines, lines, lines, P(), cols, cols, lines)
    down, across = P("seq", "tp"), P("tp", "seq")
    out_specs = (rows, rows, both, down, down, down, down, across, across, across, both, down, down, across)
    return jax.shard_map(
        partial(per_device, mesh.shape["tp"], mesh.shape["seq"]),
        mesh=mesh,
        in_specs=in_specs,
        out_specs=out_specs,
        check_vma=False,
    )
```

```python
from functools import partial

import jax
import jax.numpy as jnp
from jax import lax
from jax.experimental import pallas as pl
from jax.experimental.pallas import tpu as pltpu
from jax.sharding import PartitionSpec as P

WIDTH = 128
ROUNDS = 4
KNOWN = 1
PIECES = 3
STEPS = (
    "C10", "C11", "C20", "A0", "C12", "A1", "C21", "C22", "C13", "S01", "C30", "S11", "S02", "S03", "C23", "A2",
    "C31", "A3", "G01", "G02", "S21", "S22", "S12", "S23", "G03", "F00", "F01", "F02", "O0", "S13", "B0", "C32",
    "C33", "G11", "G12", "G13", "T01", "S31", "F10", "F11", "F12", "O1", "T02", "G21", "T03", "B1", "S32", "G22",
    "G23", "F20", "E01", "S33", "E02", "E03", "F21", "F22", "T11", "T12", "T13", "G31", "O2", "B2", "E11", "U0",
    "T21", "G32", "G33", "F30", "F31", "T22", "F32", "O3", "E12", "T23", "B3", "W0", "E21", "E13", "U1", "T31",
    "T32", "E22", "W1", "W2", "T33", "W3", "E23", "W5", "E31", "W6", "W4", "U2", "W7", "E32", "E33", "U3",
)
MIB = 1 << 20
epsilon = 1e-05

f32 = jnp.float32
bf16 = jnp.bfloat16
NN = (((1,), (0,)), ((), ()))
NT = (((1,), (1,)), ((), ()))
TN = (((0,), (0,)), ((), ()))
VM = pltpu.VMEM
DMA = pltpu.SemaphoreType.DMA
MESH = pl.DeviceIdType.MESH


def mul(left, right, dims):
    return lax.dot_general(left, right, dims, preferred_element_type=f32)


def silu_slope(value):
    gate = jax.nn.sigmoid(value)
    return gate * (1.0 + value * (1.0 - gate))


def remote(src, dst, send, recv, axis, peer):
    return pltpu.make_async_remote_copy(
        src_ref=src,
        dst_ref=dst,
        send_sem=send,
        recv_sem=recv,
        device_id={axis: peer},
        device_id_type=MESH,
    )


def greet(peers, count):
    barrier = pltpu.get_barrier_semaphore()
    for axis, peer, wanted in peers:

        @pl.when(wanted)
        def _():
            pl.semaphore_signal(barrier, inc=1, device_id={axis: peer}, device_id_type=MESH)

    pl.semaphore_wait(barrier, count)


def line_peers(size):
    me = lax.axis_index("tp")
    peers = [("tp", lax.rem(me + 1, size), me < size - 1), ("tp", lax.rem(me + size - 1, size), me > 0)]
    return peers, jnp.where(me < size - 1, 1, 0) + jnp.where(me > 0, 1, 0)


def group_peers(size, axis):
    me = lax.axis_index(axis)
    return [(axis, lax.rem(me + k, size), True) for k in range(1, size)], size - 1


class Line:
    def __init__(self, size, send, recv):
        self.size = size
        self.me = lax.axis_index("tp")
        self.right = lax.rem(self.me + 1, size)
        self.left = lax.rem(self.me + size - 1, size)
        self.send, self.recv = send, recv

    def hop(self, way, src, dst, j, at):
        peer = self.right if way == 0 else self.left
        return remote(src, dst, self.send.at[way, j, at], self.recv.at[way, j, at], "tp", peer)


class Scatter(Line):
    def __init__(self, size, send, recv, part, land, total):
        super().__init__(size, send, recv)
        self.part, self.land, self.total = part, land, total

    def copy(self, way, j, to):
        return self.hop(way, self.part.at[j, to], self.slot(way, j, to), j, to)

    def slot(self, way, j, to):
        return self.land.at[way, j, to - 1 + way]

    def start(self, j):
        last = self.size - 1

        @pl.when(self.me == 0)
        def _():
            for to in range(last, 0, -1):
                self.copy(0, j, to).start()

        @pl.when(self.me == last)
        def _():
            for to in range(last):
                self.copy(1, j, to).start()

    def step(self, j, t):
        last = self.size - 1
        for way in (0, 1):
            place = self.me if way == 0 else last - self.me
            to = last - t + place
            to = to if way == 0 else last - to

            @pl.when((place >= 1) & (place <= t))
            def _():
                copy = self.copy(way, j, to)
                copy.wait_recv()
                self.add(self.part.at[j, to], self.slot(way, j, to))
                copy.start()

    def add(self, into, more):
        rows = into.shape[0]

        @pl.loop(0, rows // 16)
        def _(g):
            r = pl.ds(pl.multiple_of(g * 16, 16), 16)
            into[r, :] = (into[r, :].astype(f32) + more[r, :].astype(f32)).astype(bf16)

    def finish(self, j):
        me, last = self.me, self.size - 1
        rows = self.total.shape[0]

        def over(body):
            @pl.loop(0, rows // 16)
            def _(g):
                body(pl.ds(pl.multiple_of(g * 16, 16), 16))

        def first(r):
            self.total[r, :] = self.part[j, me, r, :].astype(f32)

        over(first)
        for way, there in ((0, me >= 1), (1, me < last)):

            @pl.when(there)
            def _():
                self.copy(way, j, me).wait_recv()

                def more(r):
                    self.total[r, :] = self.total[r, :] + self.land[way, j, me - 1 + way, r, :].astype(f32)

                over(more)

    def drain(self, j):
        for to in range(self.size):

            @pl.when(self.me < to)
            def _():
                self.copy(0, j, to).wait_send()

            @pl.when(self.me > to)
            def _():
                self.copy(1, j, to).wait_send()


class Gather(Line):
    def __init__(self, size, send, recv, whole):
        super().__init__(size, send, recv)
        self.whole = whole

    def copy(self, way, j, source):
        block = self.whole.at[source, j]
        return self.hop(way, block, block, j, source)

    def start(self, j):
        @pl.when(self.me < self.size - 1)
        def _():
            self.copy(0, j, self.me).start()

        @pl.when(self.me > 0)
        def _():
            self.copy(1, j, self.me).start()

    def step(self, j, t):
        last = self.size - 1

        @pl.when(self.me >= t)
        def _():
            copy = self.copy(0, j, self.me - t)
            copy.wait_recv()

            @pl.when(self.me < last)
            def _():
                copy.start()

        @pl.when(self.me + t <= last)
        def _():
            copy = self.copy(1, j, self.me + t)
            copy.wait_recv()

            @pl.when(self.me > 0)
            def _():
                copy.start()

    def drain(self, j):
        last = self.size - 1
        for source in range(self.size):

            @pl.when((self.me >= source) & (self.me < last))
            def _():
                self.copy(0, j, source).wait_send()

            @pl.when((self.me <= source) & (self.me > 0))
            def _():
                self.copy(1, j, source).wait_send()


def add_rows(into, left, right):
    rows = into.shape[0]

    @pl.loop(0, rows // 16)
    def _(g):
        r = pl.ds(pl.multiple_of(g * 16, 16), 16)
        into[r, :] = (left[r, :].astype(f32) + right[r, :].astype(f32)).astype(bf16)


class GroupSum:
    refs = 6

    def __init__(self, size, grad, out, own, got, land, *sems):
        self.half = size // 2
        here = lax.axis_index("seq")
        self.side = lax.rem(here, 2)
        self.mine = here // 2
        self.sibling = here + 1 - 2 * self.side
        self.grad, self.own, self.got, self.land, self.out = grad, own, got, land, out
        self.near_sems, *self.sems = sems
        self.loads = len(grad.shape) == 4
        self.turned = out.shape != own.shape[1:]

    @staticmethod
    def scratch(shape):
        half = shape[0]
        return [VM(shape, bf16)] * 3 + [DMA((3, half)), DMA((half,)), DMA((half,))]

    def near(self, k):
        sems = self.near_sems
        source = self.grad.at[k, 1 - self.side] if self.loads else self.grad.at[k]
        return remote(source, self.got.at[k], sems.at[0, k], sems.at[1, k], "seq", self.sibling)

    def load(self, k):
        return pltpu.make_async_copy(self.grad.at[k, self.side], self.own.at[k], self.near_sems.at[2, k])

    def start(self):
        for k in range(self.half):
            self.near(k).start()
            if self.loads:
                self.load(k).start()

    def pair(self, k, into):
        if self.loads:
            self.load(k).wait()
        self.near(k).wait_recv()
        add_rows(into, self.own.at[k], self.got.at[k])

    def far(self, k):
        send, recv = self.sems
        return remote(self.own.at[k], self.land.at[self.mine], send.at[k], recv.at[self.mine], "seq", 2 * k + self.side)

    def arrival(self, k):
        send, recv = self.sems
        return remote(self.own.at[k], self.land.at[k], send.at[k], recv.at[k], "seq", 2 * k + self.side)

    def middle(self):
        for k in range(self.half):

            @pl.when(k == self.mine)
            def _():
                self.pair(k, self.land.at[k])

            @pl.when(k != self.mine)
            def _():
                self.pair(k, self.own.at[k])
                self.far(k).start()

    def relay(self):
        pass

    def arrive(self):
        for k in range(self.half):

            @pl.when(k != self.mine)
            def _():
                self.arrival(k).wait_recv()

    def terms(self):
        return [self.land.at[k] for k in range(self.half)]

    def finish(self):
        self.arrive()
        rows, cols = self.own.shape[1:]

        def total(r, c):
            acc = None
            for term in self.terms():
                part = term[r, c].astype(f32)
                acc = part if acc is None else acc + part
            return acc

        if self.turned:

            @pl.loop(0, cols // WIDTH)
            def _(g):
                c = pl.ds(pl.multiple_of(g * WIDTH, WIDTH), WIDTH)
                self.out[c, :] = total(slice(None), c).T

        else:

            @pl.loop(0, rows // 16)
            def _(g):
                r = pl.ds(pl.multiple_of(g * 16, 16), 16)
                self.out[r, :] = total(r, slice(None))

    def drain(self):
        for k in range(self.half):
            self.near(k).wait_send()
        self.drain_far()

    def drain_far(self):
        for k in range(self.half):

            @pl.when(k != self.mine)
            def _():
                self.far(k).wait_send()


class SquareSum(GroupSum):
    refs = 6

    def __init__(self, *args):
        super().__init__(*args)
        self.hop, self.far_sems = self.sems
        x, y = lax.rem(self.mine, 2), self.mine // 2
        self.beside = (2 * y + 1 - x, 2 * (1 - y) + x)
        self.opposite = 2 * (1 - y) + 1 - x
        rows = self.own.shape[1] // 2
        self.halves = (pl.ds(0, rows), pl.ds(rows, rows))

    @staticmethod
    def scratch(shape):
        half, rows, cols = shape
        return [
            VM(shape, bf16),
            VM(shape, bf16),
            VM((2, rows, cols), bf16),
            DMA((3, half)),
            VM((2, rows // 2, cols), bf16),
            DMA((2, 6)),
        ]

    def over(self, way, at, source, target):
        sems = self.far_sems
        return remote(source, target, sems.at[0, at], sems.at[1, at], "seq", 2 * self.beside[way] + self.side)

    def pass_on(self, way):
        return self.over(way, way, self.own.at[self.opposite, self.halves[way]], self.hop.at[way])

    def deliver(self, way, half):
        source = self.own.at[self.beside[way], self.halves[half]]
        return self.over(way, 2 + 2 * way + half, source, self.land.at[way, self.halves[half]])

    def middle(self):
        self.pair(self.opposite, self.own.at[self.opposite])
        for way in (0, 1):
            self.pass_on(way).start()
        for way in (0, 1):
            self.pair(self.beside[way], self.own.at[self.beside[way]])
            self.deliver(way, way).start()
        self.pair(self.mine, self.own.at[self.mine])

    def relay(self):
        for way in (0, 1):
            self.pass_on(way).wait_recv()
            into = self.own.at[self.beside[1 - way], self.halves[way]]
            add_rows(into, into, self.hop.at[way])
            self.deliver(1 - way, way).start()

    def arrive(self):
        for way in (0, 1):
            for half in (0, 1):
                self.deliver(way, half).wait_recv()

    def terms(self):
        return [self.own.at[self.mine], self.land.at[0], self.land.at[1]]

    def drain_far(self):
        for way in (0, 1):
            self.pass_on(way).wait_send()
            for half in (0, 1):
                self.deliver(way, half).wait_send()


def summer(size):
    return SquareSum if size == 8 else GroupSum


def group_sums(size, grads, outs, take):
    kind = summer(size)
    return [kind(size, grad, out, *take(kind.refs)) for grad, out in zip(grads, outs)]


def group_sums_scratch(shapes):
    scratch = []
    for size, rows, cols in shapes:
        scratch += summer(size).scratch((size // 2, rows, cols))
    return scratch


def sum_shapes(shapes, turned):
    shapes = [shape[:0:-1] if turn else shape[1:] for shape, turn in zip(shapes, turned)]
    return [jax.ShapeDtypeStruct(shape, f32) for shape in shapes]


def in_pairs(grad):
    return grad.reshape((grad.shape[0] // 2, 2) + grad.shape[1:])


def taker(refs):
    refs = list(refs)

    def take(count):
        taken, refs[:count] = refs[:count], []
        return taken

    return take


def running_ends(lengths_ref):
    ends = [lengths_ref[0]]
    for k in range(1, lengths_ref.shape[0]):
        ends.append(ends[-1] + lengths_ref[k])
    return ends


def document(rows, ends):
    total = jnp.where(rows >= ends[0], 1, 0)
    for end in ends[1:]:
        total = total + jnp.where(rows >= end, 1, 0)
    return total


def block_masks(first, ends):
    shape = (WIDTH, WIDTH)
    down = lax.broadcasted_iota(jnp.int32, shape, 0)
    along = lax.broadcasted_iota(jnp.int32, shape, 1)
    docs = document(first + down, ends)
    same = (docs == document(first + along, ends)) & (down >= along)
    before = jnp.where(first > 0, document(first - 1, ends), -1)
    final = document(first + WIDTH - 1, ends)
    carry = jnp.where(docs == before, 1.0, 0.0)
    tail = jnp.where(docs == final, 1.0, 0.0)
    keep = jnp.where(final == before, 1.0, 0.0)
    return same, carry, tail, keep


def running(log_forget):
    shape = (WIDTH, WIDTH)
    lower = lax.broadcasted_iota(jnp.int32, shape, 0) >= lax.broadcasted_iota(jnp.int32, shape, 1)
    ones = jnp.where(lower, 1.0, 0.0).astype(bf16)
    high = log_forget.astype(bf16)
    low = (log_forget - high.astype(f32)).astype(bf16)
    return mul(ones, high, NN) + mul(ones, low, NN)


def decay_parts(forget_pre, bound):
    away = jax.nn.sigmoid(-forget_pre)
    key = jax.nn.sigmoid(-bound) * away
    return key, running(jnp.log(1.0 - key)), away


class States:
    def __init__(self, size, out_state, out_decay, land_state, land_decay, sems):
        self.size = size
        self.here = lax.axis_index("seq")
        self.out_state, self.out_decay = out_state, out_decay
        self.land_state, self.land_decay = land_state, land_decay
        self.sems = sems

    def pair(self, slot, peer):
        s = self.sems
        return (
            remote(self.out_state, self.land_state.at[slot], s.at[0, peer], s.at[1, slot], "seq", peer),
            remote(self.out_decay, self.land_decay.at[slot], s.at[2, peer], s.at[3, slot], "seq", peer),
        )

    def sends(self, later):
        for k in range(self.size):
            yield k, (self.here < k if later else self.here > k)

    def start(self, later):
        for k, wanted in self.sends(later):

            @pl.when(wanted)
            def _():
                for copy in self.pair(self.here, k):
                    copy.start()

    def compose(self, later, state):
        state[...] = jnp.zeros_like(state)
        order = range(self.size) if later else range(self.size - 1, -1, -1)
        for k in order:

            @pl.when(self.here > k if later else self.here < k)
            def _():
                for copy in self.pair(k, k):
                    copy.wait_recv()
                for h in range(state.shape[0]):
                    decay = self.land_decay[k, h : h + 1, :]
                    state[h] = decay * state[h] + self.land_state[k, h].astype(f32)

    def drain(self, later):
        for k, wanted in self.sends(later):

            @pl.when(wanted)
            def _():
                for copy in self.pair(self.here, k):
                    copy.wait_send()


def states_scratch(size, heads):
    return [
        VM((heads, WIDTH, WIDTH), f32),
        VM((heads, WIDTH, WIDTH), bf16),
        VM((8, WIDTH), f32),
        VM((size, heads, WIDTH, WIDTH), bf16),
        VM((size, 8, WIDTH), f32),
        DMA((4, size)),
    ]


def front_kernel(size, groups, rounds, *refs):
    take = taker(refs)
    lengths_ref, x_ref, norm_gain_ref, bound_ref, gain_ref, cot_in, *loaded = take(10)
    ends = running_ends(lengths_ref)
    a_out, q_out, f_out, i_out, s_out, cot_out, o_ref, u_ref, starts_ref = take(9)
    *weights, a_ref, q_ref, f_ref, i_ref, s_ref, cot_ref = take(10)
    qd_ref, kd_ref, qe_ref, adds, decays = take(5)
    state, out_state, out_decay, land_state, land_decay, sems = take(6)
    load_sems, store_sems, a_send, a_recv, c_send, c_recv = take(6)
    me = lax.axis_index("tp")
    m, d = x_ref.shape[1:]
    known = cot_ref.shape[1]
    local = pltpu.make_async_copy
    cot_load = local(cot_in.at[:known], cot_ref.at[me], load_sems.at[4])
    cot_load.start()
    loads = [local(source, target, load_sems.at[k]) for k, (source, target) in enumerate(zip(loaded, weights))]
    for load in loads:
        load.start()
    line, line_count = line_peers(size)
    seq, seq_count = group_peers(groups, "seq")
    greet(line + seq, line_count + seq_count)

    gather = Gather(size, a_send, a_recv, a_ref)
    gather_cot = Gather(size, c_send, c_recv, cot_ref)
    norm_gain = norm_gain_ref[...]

    @pl.loop(0, rounds)
    def _(j):
        @pl.loop(0, m // 16)
        def _(g):
            r = pl.ds(pl.multiple_of(g * 16, 16), 16)
            x = x_ref[j, r, :].astype(f32)
            scale = lax.rsqrt(jnp.mean(x * x, axis=-1, keepdims=True) + epsilon)
            a_ref[me, j, r, :] = (x * scale * norm_gain).astype(bf16)

        gather.start(j)

    for load in loads:
        load.wait()
    cot_load.wait()
    pres = (q_ref, f_ref, i_ref, s_ref)

    rows, c = q_ref.shape
    blocks, heads = rows // WIDTH, c // WIDTH
    base = lax.axis_index("seq") * rows
    states = States(groups, out_state, out_decay, land_state, land_decay, sems)
    state[...] = jnp.zeros_like(state)
    out_decay[...] = jnp.ones_like(out_decay)

    def cot_steps(t):
        @pl.loop(0, known)
        def _(j):
            gather_cot.step(j, t)

    def block(b):
        r = pl.ds(pl.multiple_of(b * WIDTH, WIDTH), WIDTH)
        same, carry, tail, keep = block_masks(base + b * WIDTH, ends)
        for h in range(heads):
            cols = slice(h * WIDTH, (h + 1) * WIDTH)
            q = q_ref[r, cols]
            q = q * jax.nn.sigmoid(q)
            key, run, _ = decay_parts(f_ref[r, cols], bound_ref[:, cols])
            middle, last = run[WIDTH // 2 - 1 : WIDTH // 2, :], run[WIDTH - 1 :, :]
            qd_ref[r, cols] = (q * jnp.exp(run - middle)).astype(bf16)
            kd_ref[r, cols] = (key * jnp.exp(middle - run)).astype(bf16)
            qe_ref[r, cols] = (q * jnp.exp(run) * carry).astype(bf16)
            key_tail = (key * jnp.exp(last - run) * tail).astype(bf16)
            adds[b, h] = mul(i_ref[r, cols].astype(bf16), key_tail, TN)
            decays[b, h : h + 1, :] = jnp.exp(last) * keep

    def near_part(b):
        r = pl.ds(pl.multiple_of(b * WIDTH, WIDTH), WIDTH)
        same, carry, tail, keep = block_masks(base + b * WIDTH, ends)
        for h in range(heads):
            cols = slice(h * WIDTH, (h + 1) * WIDTH)
            scores = jnp.where(same, mul(qd_ref[r, cols], kd_ref[r, cols], NT), 0.0).astype(bf16)
            o_ref[r, cols] = mul(scores, i_ref[r, cols].astype(bf16), NN)

    own_rows = rounds * m
    per = own_rows // WIDTH if own_rows % WIDTH == 0 and WIDTH % m == 0 else 0
    early = [z * per + k for z in range(size) for k in range(per - 1)] if per > 1 else []
    late = [b for b in range(blocks) if b not in early]
    ready = (per - 1) * WIDTH // m if early else rounds

    def some_blocks(chosen, body):
        if chosen is early and early:

            @pl.loop(0, size)
            def _(z):
                for k in range(per - 1):
                    body(z * per + k)

        elif early:

            @pl.loop(0, size)
            def _(z):
                body(z * per + per - 1)

        elif chosen is late:
            pl.loop(0, blocks)(body)

    def project(j):
        block_rows = a_ref[:, j].reshape(size * m, d)
        for weight, out in zip(weights, pres):
            product = mul(block_rows, weight[...], NN)
            for z in range(size):
                at = pl.multiple_of(z * own_rows + j * m, 16)
                out[pl.ds(at, m), :] = product[z * m : (z + 1) * m]

    @pl.loop(0, rounds)
    def _(j):
        for t in range(1, size):
            gather.step(j, t)
            if early and t == 1:

                @pl.when(j == ready)
                def _():
                    some_blocks(early, block)

            if early and t == 2:

                @pl.when(j == ready)
                def _():
                    some_blocks(early, near_part)

        @pl.when(j >= rounds - known)
        def _():
            gather_cot.start(j - (rounds - known))

        project(j)

    stores = [
        local(source, target, store_sems.at[k])
        for k, (source, target) in enumerate(zip((a_ref, *pres), (a_out, q_out, f_out, i_out, s_out)))
    ]
    for store in stores:
        store.start()

    some_blocks(late, block)

    @pl.loop(0, blocks)
    def _(b):
        for h in range(heads):
            decay = decays[b, h : h + 1, :]
            state[h] = decay * state[h] + adds[b, h]
            out_decay[h : h + 1, :] = out_decay[h : h + 1, :] * decay

    out_state[...] = state[...].astype(bf16)
    states.start(True)
    cot_steps(1)
    some_blocks(late, near_part)

    states.compose(True, state)
    for t in range(2, size - 1):
        cot_steps(t)

    @pl.loop(0, blocks)
    def _(b):
        r = pl.ds(pl.multiple_of(b * WIDTH, WIDTH), WIDTH)
        places = base + b * WIDTH + lax.broadcasted_iota(jnp.int32, (WIDTH, WIDTH), 0)
        valid = jnp.where(places < ends[-1], 1.0, 0.0)
        for h in range(heads):
            cols = slice(h * WIDTH, (h + 1) * WIDTH)
            low = state[h].astype(bf16)
            starts_ref[b, h] = low
            o = o_ref[r, cols] + mul(qe_ref[r, cols], low, NT)
            o_ref[r, cols] = o
            state[h] = decays[b, h : h + 1, :] * state[h] + adds[b, h]
            scale = lax.rsqrt(jnp.mean(o * o, axis=-1, keepdims=True) + epsilon)
            s = s_ref[r, cols]
            z = s * jax.nn.sigmoid(s) * valid
            u_ref[r, cols] = (o * scale * gain_ref[:, cols] * z).astype(bf16)

    cot_steps(size - 1)
    cot_store = local(cot_ref, cot_out, load_sems.at[4])
    cot_store.start()
    states.drain(True)

    @pl.loop(0, rounds)
    def _(j):
        gather.drain(j)

    @pl.loop(0, known)
    def _(j):
        gather_cot.drain(j)

    for store in stores:
        store.wait()
    cot_store.wait()


def front(size, groups, rounds, tokens, cot, norm_gain, weights, ends, bound, gain):
    own, d = tokens.shape
    m, c = own // rounds, weights[0].shape[1]
    rows = size * own
    blocks, heads = rows // WIDTH, c // WIDTH
    known = KNOWN
    shape, some = (size, rounds, m, d), (size, known, m, d)
    wide, low = jax.ShapeDtypeStruct((rows, c), f32), VM((rows, c), bf16)
    spec, far = pl.BlockSpec(memory_space=VM), pl.BlockSpec(memory_space=pl.ANY)
    sems = DMA((2, rounds, size))
    outs = pl.pallas_call(
        partial(front_kernel, size, groups, rounds),
        out_shape=[
            jax.ShapeDtypeStruct(shape, bf16),
            wide,
            wide,
            wide,
            wide,
            jax.ShapeDtypeStruct(some, bf16),
            wide,
            jax.ShapeDtypeStruct((rows, c), bf16),
            jax.ShapeDtypeStruct((blocks, heads, WIDTH, WIDTH), bf16),
        ],
        in_specs=[pl.BlockSpec(memory_space=pltpu.SMEM)] + [spec] * 4 + [far] * 5,
        out_specs=[far] * 6 + [spec] * 3,
        scratch_shapes=[VM((d, c), bf16)] * 4
        + [VM(shape, bf16)]
        + [VM((rows, c), f32)] * 4
        + [VM(some, bf16)]
        + [low] * 3
        + [VM((blocks, heads, WIDTH, WIDTH), f32), VM((blocks, 8, WIDTH), f32)]
        + states_scratch(groups, heads)
        + [DMA((5,)), DMA((5,)), sems, sems, sems, sems],
        compiler_params=pltpu.CompilerParams(collective_id=0, has_side_effects=True, vmem_limit_bytes=60 * MIB),
        cost_estimate=pl.CostEstimate(flops=8 * rows * d * c, bytes_accessed=36 * MIB, transcendentals=8 * rows * c),
        name="front",
    )(
        ends,
        tokens.reshape(rounds, m, d),
        norm_gain.reshape(1, d),
        bound,
        gain,
        cot.reshape(rounds, m, d),
        *weights,
    )
    return [outs[0].reshape(rows, d)] + list(outs[1:])


def scan_back_kernel(size, line, rounds, count, *refs):
    take = taker(refs)
    lengths_ref, bound_ref, gain_ref, norm_gain_ref, *loaded = take(16)
    ends = running_ends(lengths_ref)
    grads = take(count)
    *back_outs, small_ref, first_ref, part_out = take(7)
    grad_outs = take(count)
    qd_ref, kd_ref, qe_ref, kt_ref, do_ref, run_ref, adds, decays = take(8)
    state, out_state, out_decay, land_state, land_decay, sems = take(6)
    *inputs, load_sems = take(13)
    q_ref, f_ref, i_ref, s_ref, o_ref, ub_ref, starts_ref, *weights, a_ref = inputs
    *loaded, a_in = loaded
    stage, stage_sems, a_sems, *backs, back_sems = take(8)
    dq_ref, df_ref, di_ref, ds_ref = backs
    loads = [
        pltpu.make_async_copy(source, target, load_sems.at[k]) for k, (source, target) in enumerate(zip(loaded, inputs))
    ]
    soon, later = [loads[k] for k in (4, 3, 5, 0, 1)], [loads[k] for k in (2, 6)]
    for load in soon + later:
        load.start()
    sums = group_sums(size, grads, grad_outs, take)
    greet(*group_peers(size, "seq"))
    rows, c = q_ref.shape
    blocks, heads = rows // WIDTH, c // WIDTH
    base = lax.axis_index("seq") * rows
    states = States(size, out_state, out_decay, land_state, land_decay, sems)
    for each in sums:
        each.start()
    state[...] = jnp.zeros_like(state)
    out_decay[...] = jnp.ones_like(out_decay)
    small_ref[...] = jnp.zeros_like(small_ref)
    for load in soon:
        load.wait()

    @pl.loop(0, blocks)
    def _(back):
        for each in sums[:1]:

            @pl.when(back == 1)
            def _():
                each.middle()

        b = blocks - 1 - back
        r = pl.ds(pl.multiple_of(b * WIDTH, WIDTH), WIDTH)
        same, carry, tail, keep = block_masks(base + b * WIDTH, ends)
        places = base + b * WIDTH + lax.broadcasted_iota(jnp.int32, (WIDTH, WIDTH), 0)
        valid = jnp.where(places < ends[-1], 1.0, 0.0)
        for h in range(heads):
            cols = slice(h * WIDTH, (h + 1) * WIDTH)
            o, s, ub, gain = o_ref[r, cols], s_ref[r, cols], ub_ref[r, cols], gain_ref[:, cols]
            scale = lax.rsqrt(jnp.mean(o * o, axis=-1, keepdims=True) + epsilon)
            normed = o * scale
            gate = jax.nn.sigmoid(s)
            uz = ub * (s * gate * valid)
            small_ref[heads + h : heads + h + 1, :] += jnp.sum(uz * normed, axis=0, keepdims=True)
            nb = uz * gain
            ds_ref[r, cols] = (ub * normed * gain * valid * (gate * (1.0 + s * (1.0 - gate)))).astype(bf16)
            do = (scale * (nb - normed * jnp.mean(nb * normed, axis=-1, keepdims=True))).astype(bf16)
            do_ref[r, cols] = do
            q = q_ref[r, cols]
            q = q * jax.nn.sigmoid(q)
            key, run, _ = decay_parts(f_ref[r, cols], bound_ref[:, cols])
            middle, last = run[WIDTH // 2 - 1 : WIDTH // 2, :], run[WIDTH - 1 :, :]
            run_ref[r, cols] = run
            qd_ref[r, cols] = (q * jnp.exp(run - middle)).astype(bf16)
            kd_ref[r, cols] = (key * jnp.exp(middle - run)).astype(bf16)
            kt_ref[r, cols] = (key * jnp.exp(last - run) * tail).astype(bf16)
            qe = (q * jnp.exp(run) * carry).astype(bf16)
            qe_ref[r, cols] = qe
            add = mul(do, qe, TN)
            decay = jnp.exp(last) * keep
            adds[b, h] = add
            decays[b, h : h + 1, :] = decay
            state[h] = decay * state[h] + add
            out_decay[h : h + 1, :] = out_decay[h : h + 1, :] * decay

    out_state[...] = state[...].astype(bf16)
    states.start(False)
    for load in later:
        load.wait()
    for load in loads[7:]:
        load.start()
    for each in sums[:1]:
        each.relay()
    for each in sums[1:]:
        each.middle()
    states.compose(False, state)

    @pl.loop(0, blocks)
    def _(back):
        for each in sums[1:]:

            @pl.when(back == blocks // 2)
            def _():
                each.relay()
        b = blocks - 1 - back
        r = pl.ds(pl.multiple_of(b * WIDTH, WIDTH), WIDTH)
        same, carry, tail, keep = block_masks(base + b * WIDTH, ends)
        shape = (WIDTH, WIDTH)
        down, along = lax.broadcasted_iota(jnp.int32, shape, 0), lax.broadcasted_iota(jnp.int32, shape, 1)
        from_here = jnp.where(along >= down, 1.0, 0.0).astype(bf16)
        ahead = jnp.where(along < down, 1.0, 0.0).astype(bf16)
        for h in range(heads):
            cols = slice(h * WIDTH, (h + 1) * WIDTH)
            do, v = do_ref[r, cols], i_ref[r, cols].astype(bf16)
            low, start = state[h].astype(bf16), starts_ref[b, h]
            dq_state = mul(do, start, NN)
            dk_state = mul(v, low, NN)
            kt = kt_ref[r, cols]
            qd, kd = qd_ref[r, cols], kd_ref[r, cols]
            scores = jnp.where(same, mul(qd, kd, NT), 0.0).astype(bf16)
            slopes = jnp.where(same, mul(do, v, NT), 0.0).astype(bf16)
            dq_near = mul(slopes, kd, NN)
            dk_near = mul(slopes, qd, TN)
            di_ref[r, cols] = (mul(scores, do, TN) + mul(kt, low, NT)).astype(bf16)
            run = run_ref[r, cols]
            middle, last = run[WIDTH // 2 - 1 : WIDTH // 2, :], run[WIDTH - 1 :, :]
            q_back = dq_near * jnp.exp(run - middle) + dq_state * (jnp.exp(run) * carry)
            k_back = dk_near * jnp.exp(middle - run) + dk_state * (jnp.exp(last - run) * tail)
            later = (
                qe_ref[r, cols].astype(f32) * dq_state
                + qd.astype(f32) * dq_near
                - kd.astype(f32) * dk_near
            )
            earlier = kt.astype(f32) * dk_state
            decay = decays[b, h : h + 1, :]
            log_back = decay * jnp.sum(low.astype(f32) * start.astype(f32), axis=0, keepdims=True)
            for ones, part in ((from_here, later), (ahead, earlier)):
                high = part.astype(bf16)
                log_back = log_back + mul(ones, high, NN)
                log_back = log_back + mul(ones, (part - high.astype(f32)).astype(bf16), NN)
            f_pre = f_ref[r, cols]
            away, near = jax.nn.sigmoid(-f_pre), jax.nn.sigmoid(f_pre)
            upper = jax.nn.sigmoid(-bound_ref[:, cols])
            lower = jax.nn.sigmoid(bound_ref[:, cols])
            forget_back = log_back / (1.0 - upper * away) - k_back
            slope = forget_back * away * upper
            df_ref[r, cols] = (slope * near).astype(bf16)
            small_ref[h : h + 1, :] += jnp.sum(slope, axis=0, keepdims=True) * lower
            dq_ref[r, cols] = (q_back * silu_slope(q_ref[r, cols])).astype(bf16)
            state[h] = adds[b, h] + decay * state[h]

    stores = [
        pltpu.make_async_copy(source, target, back_sems.at[k]) for k, (source, target) in enumerate(zip(backs, back_outs))
    ]
    for store in stores:
        store.start()
    for load in loads[7:]:
        load.wait()
    m, d = a_ref.shape[2:]

    def a_load(j):
        slot = lax.rem(j, 2)
        return pltpu.make_async_copy(a_in.at[:, j], a_ref.at[slot], a_sems.at[slot])

    for j in range(min(2, rounds)):
        a_load(j).start()
    tile = min(512, d)
    first_ref[...] = jnp.zeros_like(first_ref)

    def part_copy(j):
        return pltpu.make_async_copy(stage.at[lax.rem(j, 2)], part_out.at[j], stage_sems.at[lax.rem(j, 2)])

    @pl.loop(0, rounds)
    def _(j):
        @pl.when(j > 1)
        def _():
            part_copy(j - 2).wait()

        a_load(j).wait()

        def round_rows(ref):
            places = [pl.multiple_of(z * rounds * m + j * m, 16) for z in range(line)]
            return jnp.concatenate([ref[pl.ds(at, m), :] for at in places], axis=0)

        @pl.loop(0, d // tile)
        def _(n):
            cols = pl.ds(pl.multiple_of(n * tile, tile), tile)
            acc = None
            for back, weight in zip((dq_ref, df_ref, di_ref, ds_ref), weights):
                term = mul(round_rows(back), weight[cols, :], NT)
                acc = term if acc is None else acc + term
            normed = a_ref[lax.rem(j, 2), :, :, cols].reshape(line * m, tile).astype(f32)
            first_ref[:, cols] += jnp.sum(acc * normed, axis=0, keepdims=True)
            stage[lax.rem(j, 2), :, :, cols] = acc.astype(bf16).reshape(line, m, tile)

        part_copy(j).start()

        @pl.when(j + 2 < rounds)
        def _():
            a_load(j + 2).start()

    first_ref[...] = first_ref[...] / norm_gain_ref[...]
    for each in sums:
        each.finish()
    for j in range(max(0, rounds - 2), rounds):
        part_copy(j).wait()
    for store in stores:
        store.wait()
    states.drain(False)
    for each in sums:
        each.drain()


def scan_backward(size, line, rounds, ends, bound, gain, q, f, i, s, o, ub, starts, norm_gain, a, weights, grads):
    rows, c = q.shape
    d = a.shape[1]
    shape = (line, rounds, rows // line // rounds, d)
    part = (rounds, line) + shape[2:]
    blocks, heads = rows // WIDTH, c // WIDTH
    low, wide = VM((rows, c), bf16), VM((rows, c), f32)
    spec = pl.BlockSpec(memory_space=VM)
    return pl.pallas_call(
        partial(scan_back_kernel, size, line, rounds, len(grads)),
        out_shape=[jax.ShapeDtypeStruct((rows, c), bf16)] * 4
        + [jax.ShapeDtypeStruct((2 * heads, WIDTH), f32), jax.ShapeDtypeStruct((1, d), f32)]
        + [jax.ShapeDtypeStruct(part, bf16)]
        + sum_shapes([grad.shape for grad in grads], [False] * len(grads)),
        in_specs=[pl.BlockSpec(memory_space=pltpu.SMEM)]
        + [spec] * 3
        + [pl.BlockSpec(memory_space=pl.ANY)] * (12 + len(grads)),
        out_specs=[pl.BlockSpec(memory_space=pl.ANY)] * 4
        + [spec] * 2
        + [pl.BlockSpec(memory_space=pl.ANY)]
        + [spec] * len(grads),
        scratch_shapes=[low] * 5
        + [wide, VM((blocks, heads, WIDTH, WIDTH), f32), VM((blocks, 8, WIDTH), f32)]
        + states_scratch(size, heads)
        + [wide] * 6
        + [VM(starts.shape, bf16)]
        + [VM((d, c), bf16)] * 4
        + [VM((2,) + part[1:], bf16), DMA((11,)), VM((2,) + part[1:], bf16), DMA((2,)), DMA((2,))]
        + [low] * 4
        + [DMA((4,))]
        + group_sums_scratch([grad.shape for grad in grads]),
        compiler_params=pltpu.CompilerParams(collective_id=2, has_side_effects=True, vmem_limit_bytes=63 * MIB),
        cost_estimate=pl.CostEstimate(flops=8 * rows * c * d, bytes_accessed=40 * MIB, transcendentals=16 * rows * c),
        name="scan_backward",
    )(
        ends,
        bound,
        gain,
        norm_gain.reshape(1, d),
        q,
        f,
        i,
        s,
        o,
        ub,
        starts,
        *weights,
        a.reshape(shape),
        *[in_pairs(grad) for grad in grads],
    )


def middle_kernel(size, rounds, *refs):
    take = taker(refs)
    u_ref, x_ref, gain_ref, out_w, *loaded, cot_some, cot_own = take(9)
    res_out, back_out, e_out, ub_out, second_ref, down_out, out_grad, *grad_outs = take(10)
    gate_w, up_w, down_w = weights = take(3)
    cot_ref = take(1)[0]
    b_ref, e_ref, res_ref, back_ref, ub_ref, part, land, total = take(8)
    wide = take(3)
    down_ref, *tiles = take(4)
    load_sems, res_sems, back_sems, e_sems, ub_sem, down_sem, tile_sems = take(7)
    lines = [take(2) for _ in range(5)]
    hidden, gate_back, up_back = wide
    me = lax.axis_index("tp")
    m, d = x_ref.shape[1:]
    ff = gate_w.shape[1]
    group = size * m
    scatter = Scatter(size, *lines[0], part, land, total)
    gather = Gather(size, *lines[1], b_ref)
    scatter_back = Scatter(size, *lines[2], part, land, total)
    gather_back = Gather(size, *lines[3], e_ref)
    gather_cot = Gather(size, *lines[4], cot_ref)
    known = cot_some.shape[1]
    gain = gain_ref[...]
    tile = min(512, d)
    local = pltpu.make_async_copy
    loads = [local(src, dst, load_sems.at[k]) for k, (src, dst) in enumerate(zip(loaded, weights))]
    loads.append(local(cot_some, cot_ref.at[:, :known], load_sems.at[3]))
    cot_load = local(cot_own.at[known:], cot_ref.at[me, known:], load_sems.at[4])
    cot_load.start()
    for load in loads:
        load.start()
    second_ref[...] = jnp.zeros_like(second_ref)
    greet(*line_peers(size))

    def project_out(j):
        rows = u_ref[:, j].reshape(group, u_ref.shape[3])

        @pl.loop(0, d // tile)
        def _(n):
            cols = pl.ds(pl.multiple_of(n * tile, tile), tile)
            part[j, :, :, cols] = mul(rows, out_w[:, cols], NN).astype(bf16).reshape(size, m, tile)

        scatter.start(j)

    def res_copy(j):
        return local(res_ref.at[j], res_out.at[j], res_sems.at[j])

    def back_copy(j):
        return local(back_ref, back_out.at[j], back_sems.at[0])

    def e_copy(j):
        return local(e_ref.at[:, j], e_out.at[:, j], e_sems.at[j])

    def ub_copy(j):
        return local(ub_ref, ub_out.at[:, j], ub_sem.at[0])

    def down_copy(j):
        return local(down_ref, down_out.at[:, j], down_sem.at[0])

    def norm(j):
        @pl.loop(0, m // 16)
        def _(g):
            r = pl.ds(pl.multiple_of(g * 16, 16), 16)
            residual = x_ref[j, r, :].astype(f32) + total[r, :]
            res_ref[j, r, :] = residual
            scale = lax.rsqrt(jnp.mean(residual * residual, axis=-1, keepdims=True) + epsilon)
            b_ref[me, j, r, :] = (residual * scale * gain).astype(bf16)

        gather.start(j)
        res_copy(j).start()

    def feed(j, piece):
        rows = b_ref[:, j].reshape(group, d)
        cot = cot_ref[:, j].reshape(group, d)
        step = 256
        starts = list(range(0, ff, step))
        for low in starts[len(starts) * piece // PIECES : len(starts) * (piece + 1) // PIECES]:
            cols = slice(low, min(low + step, ff))
            width = cols.stop - cols.start
            gate = mul(rows, gate_w[:, cols], NN)
            up = mul(rows, up_w[:, cols], NN)
            hb = mul(cot, down_w[cols, :], NT)
            sig = jax.nn.sigmoid(gate)
            act = gate * sig
            shape = (size, m, width)
            hidden[:, j, :, cols] = (act * up).astype(bf16).reshape(shape)
            up_back[:, j, :, cols] = (hb * act).astype(bf16).reshape(shape)
            gate_back[:, j, :, cols] = (hb * up * (sig * (1.0 + gate * (1.0 - sig)))).astype(bf16).reshape(shape)

    def feed_back(j):
        scatter.drain(j)
        gates = gate_back[:, j].reshape(group, ff)
        ups = up_back[:, j].reshape(group, ff)

        @pl.loop(0, d // tile)
        def _(n):
            cols = pl.ds(pl.multiple_of(n * tile, tile), tile)
            sums = mul(gates, gate_w[cols, :], NT) + mul(ups, up_w[cols, :], NT)
            part[j, :, :, cols] = sums.astype(bf16).reshape(size, m, tile)

        scatter_back.start(j)

    def feed_out(j):
        rows = hidden[:, j].reshape(group, ff)

        @pl.loop(0, d // tile)
        def _(n):
            cols = pl.ds(pl.multiple_of(n * tile, tile), tile)
            down_ref[:, :, cols] = mul(rows, down_w[:, cols], NN).astype(bf16).reshape(size, m, tile)

        down_copy(j).start()

    def norm_back(j):
        @pl.loop(0, m // 16)
        def _(g):
            r = pl.ds(pl.multiple_of(g * 16, 16), 16)
            b_back, residual = total[r, :], res_ref[j, r, :]
            scale = lax.rsqrt(jnp.mean(residual * residual, axis=-1, keepdims=True) + epsilon)
            normed = residual * scale
            second_ref[...] += jnp.sum(b_back * normed, axis=0, keepdims=True)
            inner = b_back * gain
            back = cot_ref[me, j, r, :].astype(f32) + scale * (
                inner - normed * jnp.mean(inner * normed, axis=-1, keepdims=True)
            )
            back_ref[r, :] = back
            e_ref[me, j, r, :] = back.astype(bf16)

        gather_back.start(j)
        back_copy(j).start()

    def unproject(j):
        e_copy(j).start()
        rows = e_ref[:, j].reshape(group, d)
        ub_ref[...] = mul(rows, out_w[...], NT).reshape(size, m, out_w.shape[0])
        ub_copy(j).start()

    depth = tiles[0].shape[0]
    count = d // depth

    def tile_copies(n):
        rows = pl.ds(n * depth, depth)
        return [local(src, dst.at[rows, :], tile_sems.at[k]) for k, (src, dst) in enumerate(zip(tiles, grad_outs))]

    def weight_tile(n):
        cols = pl.ds(n * depth, depth)
        for left, right, out in zip((b_ref, b_ref, cot_ref), (gate_back, up_back, hidden), tiles):
            rows = left[:, :, :, cols].reshape(rounds * group, depth)
            out[...] = mul(rows, right[...].reshape(rounds * group, ff), TN).astype(bf16)
        for copy in tile_copies(n):
            copy.start()

    cot_load.wait()
    held = {}

    def then(kind, copies):
        for copy in held.get(kind, []):
            copy.wait()
        held[kind] = copies

    shares = sum(name[0] == "W" for name in STEPS)
    for name in STEPS:
        kind, j, t = name[0], int(name[1]), int(name[2:] or 0)
        if kind == "A":
            project_out(j)
        elif kind == "C":
            gather_cot.step(j, t) if t else gather_cot.start(j)
        elif kind == "S" and t < size - 1:
            scatter.step(j, t)
        elif kind == "S":
            scatter.finish(j)
            norm(j)
        elif kind == "G":
            gather.step(j, t)
        elif kind == "F":
            then("loads", loads if "loads" not in held else [])
            then("loads", [])
            feed(j, t)
        elif kind == "B":
            feed_back(j)
        elif kind == "O":
            then(kind, [])
            feed_out(j)
            then(kind, [down_copy(j)])
        elif kind == "T" and t < size - 1:
            scatter_back.step(j, t)
        elif kind == "T":
            then(kind, [])
            scatter_back.finish(j)
            norm_back(j)
            then(kind, [back_copy(j)])
        elif kind == "E":
            gather_back.step(j, t)
        elif kind == "U":
            then(kind, [])
            unproject(j)
            then(kind, [ub_copy(j)])
        elif kind == "W":
            for n in range(count * j // shares, count * (j + 1) // shares):
                then(kind, [])
                weight_tile(n)
                then(kind, tile_copies(n))
    for kind in list(held):
        then(kind, [])
    width = u_ref.shape[3]

    def out_tile(n, slot):
        rows = pl.ds(pl.multiple_of(n * depth, depth), depth)
        source = tiles[slot].at[:, pl.ds(0, width)]
        return local(source, out_grad.at[rows, :], tile_sems.at[slot])

    slots = len(tiles) - 1

    @pl.loop(0, count // slots)
    def _(n):
        for slot in range(slots):
            at = n * slots + slot

            @pl.when(n > 0)
            def _():
                out_tile(at - slots, slot).wait()

            cols = pl.ds(pl.multiple_of(at * depth, depth), depth)
            rows = e_ref[:, :, :, cols].reshape(rounds * group, depth)
            tiles[slot][:, :width] = mul(rows, u_ref[...].reshape(rounds * group, width), TN).astype(bf16)
            out_tile(at, slot).start()

    for slot in range(slots):
        out_tile(count - slots + slot, slot).wait()

    @pl.loop(0, rounds)
    def _(j):
        res_copy(j).wait()
        e_copy(j).wait()

        @pl.when(j >= known)
        def _():
            gather_cot.drain(j)

        gather.drain(j)
        scatter_back.drain(j)
        gather_back.drain(j)


def middle(size, rounds, u, x, cot_some, cot, gain, out_w, gate_w, up_w, down_w):
    rows, d = x.shape
    m = rows // rounds
    c, ff = out_w.shape[0], gate_w.shape[1]
    shape = (size, rounds, m)
    sems = DMA((2, rounds, size))
    spec, far = pl.BlockSpec(memory_space=VM), pl.BlockSpec(memory_space=pl.ANY)
    depth = min(256, d)
    outs = pl.pallas_call(
        partial(middle_kernel, size, rounds),
        out_shape=[
            jax.ShapeDtypeStruct((rounds, m, d), f32),
            jax.ShapeDtypeStruct((rounds, m, d), f32),
            jax.ShapeDtypeStruct(shape + (d,), bf16),
            jax.ShapeDtypeStruct(shape + (c,), f32),
            jax.ShapeDtypeStruct((1, d), f32),
            jax.ShapeDtypeStruct(shape + (d,), bf16),
            jax.ShapeDtypeStruct((d, c), bf16),
        ]
        + [jax.ShapeDtypeStruct((d, ff), bf16)] * 3,
        in_specs=[spec] * 4 + [far] * 5,
        out_specs=[far] * 4 + [spec] + [far] * 5,
        scratch_shapes=[
            VM(gate_w.shape, bf16),
            VM(up_w.shape, bf16),
            VM(down_w.shape, bf16),
            VM(shape + (d,), bf16),
            VM(shape + (d,), bf16),
            VM(shape + (d,), bf16),
            VM((rounds, m, d), f32),
            VM((m, d), f32),
            VM((size, m, c), f32),
            VM((rounds, size, m, d), bf16),
            VM((2, rounds, size - 1, m, d), bf16),
            VM((m, d), f32),
        ]
        + [VM(shape + (ff,), bf16)] * 3
        + [VM((size, m, d), bf16)]
        + [VM((depth, ff), bf16)] * 3
        + [DMA((5,)), DMA((rounds,)), DMA((1,)), DMA((rounds,)), DMA((1,)), DMA((1,)), DMA((3,))]
        + [sems] * 10,
        compiler_params=pltpu.CompilerParams(collective_id=3, has_side_effects=True, vmem_limit_bytes=63 * MIB),
        cost_estimate=pl.CostEstimate(
            flops=2 * size * rows * d * (2 * c + 9 * ff), bytes_accessed=56 * MIB, transcendentals=size * rows * ff
        ),
        name="middle",
    )(
        u.reshape(shape + (c,)),
        x.reshape(rounds, m, d),
        gain.reshape(1, d),
        out_w,
        gate_w,
        up_w,
        down_w,
        cot_some,
        cot.reshape(rounds, m, d),
    )
    res, back, e, ub, second, down, *grads = outs
    total = size * rows
    return (
        res.reshape(rows, d),
        back.reshape(rows, d),
        ub.reshape(total, c),
        second,
        down.reshape(total, d),
        *grads,
    )


class Everyone:
    def __init__(self, size, axis, mine, land, sems):
        self.size, self.axis = size, axis
        self.here = lax.axis_index(axis)
        self.mine, self.land, self.sems = mine, land, sems

    def copy(self, slot, peer):
        return remote(self.mine, self.land.at[slot], self.sems.at[0, peer], self.sems.at[1, slot], self.axis, peer)

    def others(self):
        for k in range(self.size):
            yield k, self.here != k

    def start(self):
        for k, other in self.others():

            @pl.when(other)
            def _():
                self.copy(self.here, k).start()

    def finish(self, out):
        out[...] = self.mine[...]
        for k, other in self.others():

            @pl.when(other)
            def _():
                self.copy(k, k).wait_recv()
                out[...] = out[...] + self.land[k]

    def drain(self):
        for k, other in self.others():

            @pl.when(other)
            def _():
                self.copy(self.here, k).wait_send()


def everyone_scratch(size, rows):
    return [VM((rows, WIDTH), f32), VM((size, rows, WIDTH), f32), DMA((2, size))]


def stack(vector, into, at):
    for k in range(vector.shape[1] // WIDTH):
        into[at + k : at + k + 1, :] = vector[:, k * WIDTH : (k + 1) * WIDTH]


def last_kernel(size, groups, rounds, count, mixed, *refs):
    take = taker(refs)
    backs_in = take(4)
    x_ref, gain_ref, second_ref, small_ref, first_ref, back_in, a_in, part_in, res_in, down_in = take(10)
    grads = take(count)
    tokens_far, small_out, output_ref = take(3)
    grad_outs = take(count + (4 if mixed else 0))
    part, land, total, s_send, s_recv = take(5)
    small_seq, gains_tp, sides = take(3), take(3), take(1)[0]
    nears = take(4 if mixed else 0)
    a_ref, *backs, tokens_out, res_ref, down_ref, load_sems, store_sems = take(10)
    sums = group_sums(groups, grads + nears, grad_outs, take)
    early, late = sums[:2], sums[2:]

    seq, seq_count = group_peers(groups, "seq")
    tp, tp_count = group_peers(size, "tp")
    greet(seq + tp, seq_count + tp_count)

    for each in sums[:count]:
        each.start()
    m, d = x_ref.shape[1:]
    tile = min(512, d)
    local = pltpu.make_async_copy

    def part_load(j):
        return local(part_in.at[j], part.at[j], load_sems.at[2 + j])

    a_load = local(a_in, a_ref, load_sems.at[1])
    back_load = local(back_in, tokens_out, load_sems.at[0])

    for j in range(rounds):
        part_load(j).start()
    a_load.start()
    backs_loads = [
        local(source, target, load_sems.at[4 + rounds + k]) for k, (source, target) in enumerate(zip(backs_in, backs))
    ]
    for load in backs_loads:
        load.start()
    back_load.start()
    output_loads = [
        local(source, target, load_sems.at[2 + rounds + k])
        for k, (source, target) in enumerate(((res_in, res_ref), (down_in, down_ref)))
    ]
    for load in output_loads:
        load.start()

    def store(j):
        return local(tokens_out.at[j], tokens_far.at[j], store_sems.at[j])

    group = size * m
    scatter = Scatter(size, s_send, s_recv, part, land, total)
    gain = gain_ref[...]

    seq_small = Everyone(groups, "seq", *small_seq)
    tp_gains = Everyone(size, "tp", *gains_tp)
    lines, smalls = d // WIDTH, small_ref.shape[0]

    def mix(back, each):
        rows = back[...].reshape(rounds * group, back.shape[3])
        depth = each.own.shape[1]
        for side, into in ((1 - each.side, each.grad), (each.side, each.own)):

            @pl.loop(0, each.half)
            def _(k):
                cols = pl.ds(pl.multiple_of((2 * k + side) * depth, depth), depth)
                left = a_ref[:, :, :, cols].reshape(rounds * group, depth)
                into[k] = mul(left, rows, TN).astype(bf16)

            if into is each.grad:
                each.start()

    def norm_back(j):
        @pl.loop(0, m // 16)
        def _(g):
            r = pl.ds(pl.multiple_of(g * 16, 16), 16)
            a_back, x = total[r, :], x_ref[j, r, :].astype(f32)
            scale = lax.rsqrt(jnp.mean(x * x, axis=-1, keepdims=True) + epsilon)
            normed = x * scale
            inner = a_back * gain
            tokens_out[j, r, :] = tokens_out[j, r, :] + scale * (
                inner - normed * jnp.mean(inner * normed, axis=-1, keepdims=True)
            )

    def steps(j, low, high):
        for t in range(low, high):
            if t < size - 1:
                scatter.step(j, t)
            else:
                scatter.finish(j)
                norm_back(j)
                store(j).start()

    stack(second_ref[...], gains_tp[0], 0)
    stack(first_ref[...], gains_tp[0], lines)
    tp_gains.start()
    for j in range(rounds):
        part_load(j).wait()
        scatter.start(j)
    tp_gains.finish(sides)
    small_seq[0][: 2 * lines, :] = sides[...]
    small_seq[0][2 * lines : 2 * lines + smalls, :] = small_ref[...]
    seq_small.start()
    for each in early:
        each.middle()
    a_load.wait()
    for load in backs_loads:
        load.wait()
    steps(0, 1, 2)
    back_load.wait()
    if mixed:
        for at, (back, each) in enumerate(zip(backs, late)):
            mix(back, each)
            steps(0, 2, 3) if at == 0 else None
            steps(0, 3, size) if at == 2 else None
    else:
        steps(0, 2, size)
    for each in early:
        each.relay()
    for each in late:
        each.middle()
    for load in output_loads:
        load.wait()

    @pl.loop(0, rounds * m // 16)
    def _(g):
        r = pl.ds(pl.multiple_of(g * 16, 16), 16)
        output_ref[r, :] = (res_ref[r, :] + down_ref[r, :].astype(f32)).astype(bf16)

    steps(1, 1, 3)
    steps(1, 3, size)
    for each in late[:2]:
        each.relay()
    steps(2, 1, 3)
    for each in late[2:]:
        each.relay()
    steps(2, 3, size)
    for each in early:
        each.finish()
    seq_small.finish(small_out)
    for j in range(3, rounds):
        steps(j, 1, size)
    for each in late:
        each.finish()

    for each in sums + [seq_small, tp_gains]:
        each.drain()

    @pl.loop(0, rounds)
    def _(j):
        scatter.drain(j)
        store(j).wait()


def last(size, groups, rounds, backs, part, a, x, back, gain, second, first, small, residual, down, grads, turned):
    mixed = len(turned) > len(grads)
    rows, d = x.shape
    m = rows // rounds
    c = backs[0].shape[1]
    shape = (size, rounds, m)
    lines = d // WIDTH
    sems = DMA((2, rounds, size))
    spec = pl.BlockSpec(memory_space=VM)
    small_rows = 2 * lines + small.shape[0]
    shapes = [grad.shape for grad in grads] + ([(groups, d // groups, c)] * 4 if mixed else [])
    outs = pl.pallas_call(
        partial(last_kernel, size, groups, rounds, len(grads), mixed),
        out_shape=[
            jax.ShapeDtypeStruct((rounds, m, d), f32),
            jax.ShapeDtypeStruct((small_rows, WIDTH), f32),
            jax.ShapeDtypeStruct((rows, d), bf16),
        ]
        + sum_shapes(shapes, turned),
        in_specs=[pl.BlockSpec(memory_space=pl.ANY)] * 4
        + [spec] * 5
        + [pl.BlockSpec(memory_space=pl.ANY)] * (5 + len(grads)),
        out_specs=[pl.BlockSpec(memory_space=pl.ANY)] + [spec] * (2 + len(shapes)),
        scratch_shapes=[
            VM((rounds, size, m, d), bf16),
            VM((2, rounds, size - 1, m, d), bf16),
            VM((m, d), f32),
            sems,
            sems,
        ]
        + everyone_scratch(groups, small_rows)
        + everyone_scratch(size, 2 * lines)
        + [VM((2 * lines, WIDTH), f32)]
        + ([VM((groups // 2, d // groups, c), bf16)] * 4 if mixed else [])
        + [VM(shape + (d,), bf16)]
        + [VM(shape + (c,), bf16)] * 4
        + [VM((rounds, m, d), f32), VM((rows, d), f32), VM((rows, d), bf16), DMA((8 + rounds,)), DMA((rounds,))]
        + group_sums_scratch(shapes),
        compiler_params=pltpu.CompilerParams(collective_id=4, has_side_effects=True, vmem_limit_bytes=63 * MIB),
        cost_estimate=pl.CostEstimate(flops=16 * size * rows * d * c, bytes_accessed=56 * MIB, transcendentals=0),
        name="last",
    )(
        *[part.reshape(shape + (c,)) for part in backs],
        x.reshape(rounds, m, d),
        gain.reshape(1, d),
        second,
        small,
        first,
        back.reshape(rounds, m, d),
        a.reshape(shape + (d,)),
        part,
        residual,
        down,
        *[in_pairs(grad) for grad in grads],
    )
    return (outs[0].reshape(rows, d),) + tuple(outs[1:])


def results_kernel(count, size, small_ref, *refs):
    ins, outs = refs[:count], refs[count : 2 * count]
    first_out, second_out, bound_out, gain_out, *held, sems = refs[2 * count :]
    loads = [pltpu.make_async_copy(a, b, sems.at[0, k]) for k, (a, b) in enumerate(zip(ins, held))]
    stores = [pltpu.make_async_copy(a, b, sems.at[1, k]) for k, (a, b) in enumerate(zip(held, outs))]
    for load in loads:
        load.start()

    def share(rows, at, width):
        picked = rows[:, :width]
        for k in range(1, WIDTH // width):
            picked = jnp.where(at == k, rows[:, k * width : (k + 1) * width], picked)
        return picked

    here = lax.axis_index("seq")
    place = here * size + lax.axis_index("tp")
    each = first_out.shape[1]
    per = WIDTH // each
    heads, wide = bound_out.shape
    lines = (small_ref.shape[0] - 2 * heads) // 2
    at = lax.broadcasted_iota(jnp.int32, (lines, WIDTH), 0)
    for source, target in ((small_ref[:lines], second_out), (small_ref[lines : 2 * lines], first_out)):
        line = jnp.sum(jnp.where(at == place // per, source, 0.0), axis=0, keepdims=True)
        target[...] = share(line, place % per, each)
    bound_out[...] = share(small_ref[2 * lines : 2 * lines + heads, :], here, wide)
    gain_out[...] = share(small_ref[2 * lines + heads :, :], here, wide)
    for load, store in zip(loads, stores):
        load.wait()
        store.start()
    for store in stores:
        store.wait()


def results(groups, size, small, heads, arrays):
    each = (small.shape[0] - 2 * heads) // 2 * WIDTH // (groups * size)
    spec, far = pl.BlockSpec(memory_space=VM), pl.BlockSpec(memory_space=pl.ANY)
    outs = pl.pallas_call(
        partial(results_kernel, len(arrays), size),
        out_shape=[jax.ShapeDtypeStruct(part.shape, part.dtype) for part in arrays]
        + [jax.ShapeDtypeStruct((1, each), f32)] * 2
        + [jax.ShapeDtypeStruct((heads, WIDTH // groups), f32)] * 2,
        in_specs=[spec] + [far] * len(arrays),
        out_specs=[far] * len(arrays) + [spec] * 4,
        scratch_shapes=[VM(part.shape, part.dtype) for part in arrays] + [DMA((2, len(arrays)))],
        compiler_params=pltpu.CompilerParams(vmem_limit_bytes=60 * MIB),
        cost_estimate=pl.CostEstimate(flops=0, bytes_accessed=20 * MIB, transcendentals=0),
        name="results",
    )(small, *arrays)
    copied, (first, second, bound, gain) = outs[: len(arrays)], outs[len(arrays) :]
    return first.reshape(each), second.reshape(each), bound, gain, copied


def per_device(
    size,
    groups,
    tokens,
    lengths,
    cotangent,
    first_gain,
    query_weight,
    forget_weight,
    input_weight,
    swish_weight,
    bound_logit,
    group_gain,
    out_weight,
    second_gain,
    gate_weight,
    up_weight,
    down_weight,
):
    weights = (query_weight, forget_weight, input_weight, swish_weight)
    ends = lengths.astype(jnp.int32)
    bound, head_gain = bound_logit.reshape(1, -1), group_gain.reshape(1, -1)
    a, q, f, i, s, cot_some, o, u, starts = front(
        size, groups, ROUNDS, tokens, cotangent, first_gain, weights, ends, bound, head_gain
    )
    residual, back, ub, second, down, *wide = middle(
        size, ROUNDS, u, tokens, cot_some, cotangent, second_gain, out_weight, gate_weight, up_weight, down_weight
    )
    down, ub = lax.optimization_barrier((down, ub))
    down = lax.psum_scatter(down, "tp", scatter_dimension=0, tiled=True)
    d = tokens.shape[1]

    def chunks(grad):
        return grad.reshape(groups, grad.shape[0] // groups, grad.shape[1])

    def grad_of(left, right):
        return chunks(lax.dot_general(left, right, TN, preferred_element_type=f32).astype(bf16))

    outs, gates, ups, downs = (chunks(grad) for grad in wide)
    dq, df, di, ds, small, first, part, gate_grad, up_grad = scan_backward(
        groups,
        size,
        ROUNDS,
        ends,
        bound,
        head_gain,
        q,
        f,
        i,
        s,
        o,
        ub,
        starts,
        first_gain,
        a,
        weights,
        [gates, ups],
    )
    back_rows = (dq, df, di, ds)
    here_too = groups == 8
    others = [downs, outs] + ([] if here_too else [grad_of(a, part) for part in back_rows])
    tokens_grad, small_sum, output, *sums = last(
        size,
        groups,
        ROUNDS,
        back_rows,
        part,
        a,
        tokens,
        back,
        first_gain,
        second,
        first,
        small,
        residual,
        down,
        others,
        [True, True] + [False] * 4,
    )
    arrays = [output, tokens_grad, gate_grad, up_grad, *sums]
    first_grad, second_grad, bound_grad, head_grad, copied = results(
        groups, size, small_sum, bound_logit.shape[0], arrays
    )
    output, tokens_grad, gate_grad, up_grad, down_grad, out_grad, *mixes = copied
    query_grad, forget_grad, input_grad, swish_grad = mixes
    return (
        output,
        tokens_grad,
        first_grad,
        query_grad,
        forget_grad,
        input_grad,
        swish_grad,
        bound_grad,
        head_grad,
        out_grad,
        second_grad,
        gate_grad,
        up_grad,
        down_grad,
    )


def solution(mesh):
    rows, both, cols, lines = P(("seq", "tp"), None), P(("seq", "tp")), P(None, "tp"), P("tp", None)
    in_specs = (rows, P(), rows, P(), cols, cols, cols, cols, lines, lines, lines, P(), cols, cols, lines)
    down, across = P("seq", "tp"), P("tp", "seq")
    out_specs = (rows, rows, both, down, down, down, down, across, across, across, both, down, down, across)
    return jax.shard_map(
        partial(per_device, mesh.shape["tp"], mesh.shape["seq"]),
        mesh=mesh,
        in_specs=in_specs,
        out_specs=out_specs,
        check_vma=False,
    )
```
